32 devices in a mesh: section: 4 (over y, core), dp: 8 (over z, x).
Axes of the slice: x: 2, y: 2, z: 4, core: 2. Of those that a mesh axis runs over, the one named last changes fastest.
Arguments:
- patches: bfloat16 [2048, 192], P('dp'), may hold values from -6 to 6
- var_ids: int32 [48], replicated, may hold values from 0 to 47, each once
- segment_ids: int32 [16, 128], P('dp'), may hold values from 0 to 7, never falling along the last dimension, each value on 1 to 32 neighbouring positions
- embed_weight: bfloat16 [1024, 192], P('dp'), may hold values from -3 to 3
- var_embed: float32 [48, 1024], replicated, may hold values from -3 to 3
- agg_query: float32 [1024], replicated, may hold values from -6 to 6
- agg_wq: bfloat16 [1024, 1024], P('dp'), may hold values from -0.1875 to 0.1875
- agg_bq: float32 [1024], replicated, may hold values from -3 to 3
- agg_wk: bfloat16 [1024, 1024], P('dp'), may hold values from -0.1875 to 0.1875
- agg_wv: bfloat16 [1024, 1024], P('dp'), may hold values from -0.1875 to 0.1875
- agg_bv: float32 [1024], replicated, may hold values from -2 to 2
- agg_wo: bfloat16 [1024, 1024], P('dp'), may hold values from -0.1875 to 0.1875
- agg_bo: float32 [1024], replicated, may hold values from -2 to 2
- attn_norm_gain: float32 [1024], replicated, may hold values from 0.1 to 1.9
- attn_norm_bias: float32 [1024], replicated, may hold values from -2 to 2
- attn_wqkv: bfloat16 [1024, 3072], P('dp'), may hold values from -0.1875 to 0.1875
- attn_bq: float32 [1024], replicated, may hold values from -2 to 2
- attn_bv: float32 [1024], replicated, may hold values from -2 to 2
- attn_wo: bfloat16 [1024, 1024], P('dp'), may hold values from -1 to 1
- attn_bo: float32 [1024], replicated, may hold values from -2 to 2
- mlp_norm_gain: float32 [1024], replicated, may hold values from 0.1 to 1.9
- mlp_norm_bias: float32 [1024], replicated, may hold values from -2 to 2
- mlp_up: bfloat16 [1024, 4096], P('dp'), may hold values from -0.1875 to 0.1875
- mlp_bup: float32 [4096], replicated, may hold values from -2 to 2
- mlp_down: bfloat16 [1024, 4096], P('dp'), may hold values from -0.125 to 0.125
- mlp_bdown: float32 [1024], replicated, may hold values from -2 to 2
- cotangent: bfloat16 [2048, 1024], P('dp', 'section'), may hold values from -8 to 8
Outputs:
- activations: bfloat16 [2048, 1024], P('dp', 'section')
- patches_grad: bfloat16 [2048, 192], P('dp', 'section')
- embed_weight_grad: float32 [1024, 192], P('dp')
- var_embed_grad: float32 [48, 1024], P(None, 'dp')
- agg_query_grad: float32 [1024], P('dp')
- agg_wq_grad: float32 [1024, 1024], P('dp')
- agg_bq_grad: float32 [1024], P('dp')
- agg_wk_grad: float32 [1024, 1024], P('dp')
- agg_wv_grad: float32 [1024, 1024], P('dp')
- agg_bv_grad: float32 [1024], P('dp')
- agg_wo_grad: float32 [1024, 1024], P('dp')
- agg_bo_grad: float32 [1024], P('dp')
- attn_norm_gain_grad: float32 [1024], P('dp')
- attn_norm_bias_grad: float32 [1024], P('dp')
- attn_wqkv_grad: float32 [1024, 3072], P('dp')
- attn_bq_grad: float32 [1024], P('dp')
- attn_bv_grad: float32 [1024], P('dp')
- attn_wo_grad: float32 [1024, 1024], P('dp')
- attn_bo_grad: float32 [1024], P('dp')
- mlp_norm_gain_grad: float32 [1024], P('dp')
- mlp_norm_bias_grad: float32 [1024], P('dp')
- mlp_up_grad: float32 [1024, 4096], P('dp')
- mlp_bup_grad: float32 [4096], P('dp')
- mlp_down_grad: float32 [1024, 4096], P('dp')
- mlp_bdown_grad: float32 [1024], P('dp')
The draws below stay inside these ranges and needn't reach their ends.
Inputs may be any that keep to these rules, and one draw needn't show every extreme that they name: `segment_ids`: in every sequence the ids never decrease, each of the 8 subgrids holds one to a quarter of 128 patches, and one holds exactly a quarter. `var_ids`: each of the 48 variables belongs to exactly one input channel.
All inputs are finite; a program needn't handle non-finite values.
Results may differ from the reference program's by a relative error of at most 0.028.
Values may be sent and summed in bfloat16 or wider, within the bound.
A program may use at most 320 MiB of HBM per device.

```python
import math
import jax
import jax.numpy as jnp
import numpy as np
from jax import lax

D = 1024
HEADS = 16
HEAD = 64
FF = 4096
VARS = 48
PIX = 4
LEN = 128
SEGS = 8
SEQS = 16
TOKENS = 2048


def raised(array, key, source, target, blocks, factor):
    owner, partner = [(jnp.arange(array.shape[position]) // (array.shape[position] // blocks)).reshape([-1 if axis == position else 1 for axis in range(array.ndim)]) for position in (source, target)]
    chosen = jax.random.permutation(key, blocks)[partner]
    strong = (owner == chosen) | (owner == (partner + blocks // 2) % blocks)
    return jnp.where(strong, factor * array, array)


def steps_of(rng, dims, cuts, low, high):
    gain, own = 1.0, jax.random.fold_in(rng, 6)
    for dim, parts in cuts:
        steps = jnp.exp(jax.random.uniform(jax.random.fold_in(own, dim), (parts,), jnp.float32, low / len(cuts), high / len(cuts)))
        gain = gain * jnp.repeat(steps, dims[dim] // parts).reshape([-1 if axis == dim else 1 for axis in range(len(dims))])
    return gain


def length_profile(number_of, total, most, slope):
    loads = [(1 << 20) // math.isqrt(rank ** slope) + 1 for rank in range(2, number_of + 1)]
    surplus, given = total - most - (number_of - 1), [1] * (number_of - 1)
    while surplus > 0:
        candidates = [i for i in range(number_of - 1) if given[i] < most]
        whole, left = sum([loads[i] for i in candidates]), surplus
        for i in candidates:
            extra = min(most - given[i], max(1, left * loads[i] // whole), surplus)
            given[i] = given[i] + extra
            surplus = surplus - extra
    return np.array([most] + given)


def uneven_parts(rng, count, total, limit, lean):
    if count == 2:
        one = jax.random.randint(rng, (), max(1, total - limit), min(limit, total - 1) + 1)
        return jnp.stack([one, total - one])
    lengths = jnp.asarray(length_profile(count, total, limit, lean), jnp.int32)
    pairs = (count - 1) // 2
    giver, receiver = lengths[1:1 + 2 * pairs:2], lengths[2:2 + 2 * pairs:2]
    room = jnp.minimum(giver - 1, limit - receiver)
    passed = jax.random.randint(jax.random.fold_in(rng, 1), (pairs,), 0, 1 << 20) % (room + 1)
    lengths = lengths.at[1:1 + 2 * pairs:2].set(giver - passed).at[2:2 + 2 * pairs:2].set(receiver + passed)
    return lengths[jax.random.permutation(jax.random.fold_in(rng, 2), count)]


def scatter_about(own_key, extent, scale, bound, cuts=(), dtype=jnp.bfloat16):
    array = scale * jax.random.normal(own_key, extent, jnp.float32)
    if cuts:
        array = array * steps_of(own_key, extent, cuts, -0.22, 0.18)
    return jnp.clip(array, -bound, bound).astype(dtype)


def gaussian_with(key, dims, spread, reach, shards, heavy, kind=jnp.bfloat16):
    values = spread * jax.random.normal(key, dims, jnp.float32)
    if shards:
        values = values * steps_of(key, dims, shards, -0.22, 0.18)
    return jnp.clip(raised(values, jax.random.fold_in(key, 3), *heavy), -reach, reach).astype(kind)


def setup_inputs(seed: int = 0) -> dict:
    seeds = jax.random.split(jax.random.key(seed), 28)
    patches = scatter_about(seeds[0], (TOKENS, VARS * PIX), 1.0, 6.0, ((0, 8),))
    var_ids = jax.random.permutation(seeds[1], VARS).astype(jnp.int32)
    segment_ids = jax.vmap(lambda own: jnp.searchsorted(jnp.cumsum(uneven_parts(own, SEGS, LEN, LEN // 4, 1)), jnp.arange(LEN), side="right"))(jax.random.split(seeds[2], SEQS)).reshape((SEQS, LEN)).astype(jnp.int32)
    embed_weight = scatter_about(seeds[3], (D, VARS * PIX), PIX ** -0.5, 3.0, ((0, 8),))
    var_embed = scatter_about(seeds[4], (VARS, D), 0.5, 3.0, (), jnp.float32)
    agg_query = scatter_about(seeds[5], (D,), 1.0, 6.0, (), jnp.float32)
    agg_wq = scatter_about(seeds[6], (D, D), D ** -0.5, 0.1875, ((0, 8),))
    agg_bq = scatter_about(seeds[7], (D,), 0.5, 3.0, (), jnp.float32)
    agg_wk = scatter_about(seeds[8], (D, D), D ** -0.5, 0.1875, ((0, 8),))
    agg_wv = scatter_about(seeds[9], (D, D), D ** -0.5, 0.1875, ((0, 8),))
    agg_bv = scatter_about(seeds[10], (D,), 0.3, 2.0, (), jnp.float32)
    agg_wo = scatter_about(seeds[11], (D, D), D ** -0.5, 0.1875, ((0, 8),))
    agg_bo = scatter_about(seeds[12], (D,), 0.3, 2.0, (), jnp.float32)
    attn_norm_gain = jnp.clip(1.0 + 0.18 * jax.random.normal(seeds[13], (D,), jnp.float32), 0.1, 1.9)
    attn_norm_bias = scatter_about(seeds[14], (D,), 0.3, 2.0, (), jnp.float32)
    attn_wqkv = scatter_about(seeds[15], (D, 3 * D), D ** -0.5, 0.1875, ((0, 8),))
    attn_bq = scatter_about(seeds[16], (D,), 0.3, 2.0, (), jnp.float32)
    attn_bv = scatter_about(seeds[17], (D,), 0.3, 2.0, (), jnp.float32)
    attn_wo = scatter_about(seeds[18], (D, D), (D // 32) ** -0.5, 1.0, ((0, 8),))
    attn_bo = scatter_about(seeds[19], (D,), 0.3, 2.0, (), jnp.float32)
    mlp_norm_gain = jnp.clip(1.0 + 0.18 * jax.random.normal(seeds[20], (D,), jnp.float32), 0.1, 1.9)
    mlp_norm_bias = scatter_about(seeds[21], (D,), 0.3, 2.0, (), jnp.float32)
    mlp_up = scatter_about(seeds[22], (D, FF), D ** -0.5, 0.1875, ((0, 8),))
    mlp_bup = scatter_about(seeds[23], (FF,), 0.3, 2.0, (), jnp.float32)
    mlp_down = scatter_about(seeds[24], (D, FF), (FF // 2) ** -0.5, 0.125, ((0, 8),))
    mlp_bdown = scatter_about(seeds[25], (D,), 0.3, 2.0, (), jnp.float32)
    cotangent = gaussian_with(seeds[26], (TOKENS, D), 1.0, 8.0, ((0, 8), (1, 4)), (0, 1, 8, 2.0))
    return {"patches": patches, "var_ids": var_ids, "segment_ids": segment_ids, "embed_weight": embed_weight, "var_embed": var_embed, "agg_query": agg_query, "agg_wq": agg_wq, "agg_bq": agg_bq, "agg_wk": agg_wk, "agg_wv": agg_wv, "agg_bv": agg_bv, "agg_wo": agg_wo, "agg_bo": agg_bo, "attn_norm_gain": attn_norm_gain, "attn_norm_bias": attn_norm_bias, "attn_wqkv": attn_wqkv, "attn_bq": attn_bq, "attn_bv": attn_bv, "attn_wo": attn_wo, "attn_bo": attn_bo, "mlp_norm_gain": mlp_norm_gain, "mlp_norm_bias": mlp_norm_bias, "mlp_up": mlp_up, "mlp_bup": mlp_bup, "mlp_down": mlp_down, "mlp_bdown": mlp_bdown, "cotangent": cotangent}


highest = lax.Precision.HIGHEST
blocked = -1000000000.0
epsilon = 1e-05

@jax.custom_vjp
def low(v):
    return lax.optimization_barrier(v.astype(jnp.bfloat16)).astype(jnp.float32)

@jax.custom_vjp
def low_back(v):
    return v

def low_keep(v):
    return (low(v), None)

def low_pass(kept, grad):
    return (grad,)

def back_keep(v):
    return (v, None)

def back_low(kept, grad):
    return (low(grad),)
low.defvjp(low_keep, low_pass)
low_back.defvjp(back_keep, back_low)

def matmul(left_rows, right_matrix):
    return jnp.dot(left_rows, right_matrix, precision=highest)

def layer_norm(row_block, norm_gain, shift_vec):
    averaged = lax.optimization_barrier(jnp.mean(row_block, axis=-1, keepdims=True))
    centred = row_block - averaged
    variance = lax.optimization_barrier(jnp.mean(centred * centred, axis=-1, keepdims=True))
    return centred * lax.rsqrt(variance + epsilon) * norm_gain + shift_vec

def aggregate(embedded, key_query, value_w, value_b, out_w, out_b):
    scores = low_back(jnp.einsum('tcd,dh->tch', embedded, key_query, precision=highest))
    weights = low(jax.nn.softmax(scores, axis=1))
    mixture = low_back(low(jnp.einsum('tch,tcd->thd', weights, embedded, precision=highest)))
    context = jnp.einsum('thd,dhj->thj', mixture, value_w.reshape(D, HEADS, HEAD), precision=highest)
    context = low_back(low(context.reshape(LEN, D) + value_b))
    return low_back(low(matmul(context, out_w) + out_b))

def attention_block(inputs, segments, norm_gain, shift_vec, qkv_w, query_b, value_b, out_w, out_b):
    normed = low(layer_norm(inputs, norm_gain, shift_vec))
    projected = matmul(normed, qkv_w)
    queries = low_back(low(projected[:, :D] + query_b)).reshape(LEN, HEADS, HEAD)
    keys_rows = low_back(low(projected[:, D:2 * D])).reshape(LEN, HEADS, HEAD)
    values = low_back(low(projected[:, 2 * D:] + value_b)).reshape(LEN, HEADS, HEAD)
    scores = low_back(jnp.einsum('thj,uhj->htu', queries, keys_rows, precision=highest) * HEAD ** (-0.5))
    same_segment = segments[:, None] == segments[None, :]
    probabilities = low(jax.nn.softmax(jnp.where(same_segment[None], scores, blocked), axis=-1))
    attended = jnp.einsum('htu,uhj->thj', probabilities, values, precision=highest).reshape(LEN, D)
    attended = low_back(low(attended))
    return low_back(low(inputs + matmul(attended, out_w) + out_b))

def mlp_block(inputs, norm_gain, shift_vec, up_w, up_b, down_w, down_b):
    normed = low(layer_norm(inputs, norm_gain, shift_vec))
    hidden = low_back(matmul(normed, up_w) + up_b)
    activated = low(jax.nn.gelu(hidden, approximate=False))
    return inputs + matmul(activated, down_w.T) + down_b

def reference(patches, var_ids, segment_ids, embed_weight, var_embed, agg_query, agg_wq, agg_bq, agg_wk, agg_wv, agg_bv, agg_wo, agg_bo, attn_norm_gain, attn_norm_bias, attn_wqkv, attn_bq, attn_bv, attn_wo, attn_bo, mlp_norm_gain, mlp_norm_bias, mlp_up, mlp_bup, mlp_down, mlp_bdown, cotangent):
    floats = (patches, embed_weight, var_embed, agg_query, agg_wq, agg_bq, agg_wk, agg_wv, agg_bv, agg_wo, agg_bo, attn_norm_gain, attn_norm_bias, attn_wqkv, attn_bq, attn_bv, attn_wo, attn_bo, mlp_norm_gain, mlp_norm_bias, mlp_up, mlp_bup, mlp_down, mlp_bdown)
    floats = tuple((array_in.astype(jnp.float32) for array_in in floats))

    def forward(params):
        patch_all, embed_w, var_table, query_vec, query_w, query_b, key_w, value_w, value_b, out_w, out_b, attn_gain, attn_shift, qkv_w, attn_qb, attn_vb, attn_ow, attn_ob, mlp_gain, mlp_shift, up_w, up_b, down_w, down_b = params
        picked_weight = embed_w.reshape(D, VARS, PIX)[:, var_ids, :]
        picked_embed = var_table[var_ids]
        query_proj = matmul(low(query_vec)[None, :], query_w)[0] + query_b
        key_query = jnp.einsum('dhj,hj->dh', key_w.reshape(D, HEADS, HEAD), query_proj.reshape(HEADS, HEAD), precision=highest)
        key_query = low(key_query * HEAD ** (-0.5))

        def one_sequence(carry_in, inputs):
            patch_rows, segments = inputs
            embedded = jnp.einsum('tcp,dcp->tcd', patch_rows.reshape(LEN, VARS, PIX), picked_weight, precision=highest)
            embedded = low_back(low(embedded + picked_embed[None]))
            aggregated = aggregate(embedded, key_query, value_w, value_b, out_w, out_b)
            block_mid = attention_block(aggregated, segments, attn_gain, attn_shift, qkv_w, attn_qb, attn_vb, attn_ow, attn_ob)
            result = mlp_block(block_mid, mlp_gain, mlp_shift, up_w, up_b, down_w, down_b)
            return (carry_in, result)
        carry_out, outputs = lax.scan(jax.checkpoint(one_sequence), jnp.zeros((), jnp.float32), (patch_all.reshape(SEQS, LEN, VARS * PIX), segment_ids))
        return outputs.reshape(TOKENS, D)
    output_rows, pullback = jax.vjp(forward, floats)
    grads, = pullback(cotangent.astype(jnp.float32))
    patches_grad, embed_weight_grad, var_embed_grad, agg_query_grad, agg_wq_grad, agg_bq_grad, agg_wk_grad, agg_wv_grad, agg_bv_grad, agg_wo_grad, agg_bo_grad, attn_norm_gain_grad, attn_norm_bias_grad, attn_wqkv_grad, attn_bq_grad, attn_bv_grad, attn_wo_grad, attn_bo_grad, mlp_norm_gain_grad, mlp_norm_bias_grad, mlp_up_grad, mlp_bup_grad, mlp_down_grad, mlp_bdown_grad = grads
    return (output_rows.astype(jnp.bfloat16), patches_grad.astype(jnp.bfloat16), embed_weight_grad, var_embed_grad, agg_query_grad, agg_wq_grad, agg_bq_grad, agg_wk_grad, agg_wv_grad, agg_bv_grad, agg_wo_grad, agg_bo_grad, attn_norm_gain_grad, attn_norm_bias_grad, attn_wqkv_grad, attn_bq_grad, attn_bv_grad, attn_wo_grad, attn_bo_grad, mlp_norm_gain_grad, mlp_norm_bias_grad, mlp_up_grad, mlp_bup_grad, mlp_down_grad, mlp_bdown_grad)
```

```python
from functools import partial

import jax
import jax.numpy as jnp
from jax import lax
from jax.sharding import PartitionSpec as P

D = 1024
HEADS = 16
HEAD = 64
FF = 4096
VARS = 48
PIX = 4
LEN = 128


highest = lax.Precision.HIGHEST
blocked = -1000000000.0
epsilon = 1e-05


def project(row_block, matrix):
    return jnp.dot(row_block, matrix, preferred_element_type=jnp.float32)


def project_back(row_block, matrix):
    return jnp.einsum("ta,ba->tb", row_block, matrix, preferred_element_type=jnp.float32)


def outer_sum(left_rows, right_rows):
    return jnp.einsum("ta,tb->ab", left_rows, right_rows, preferred_element_type=jnp.float32)


def layer_norm(row_block, norm_gain, shift_vec):
    averaged = jnp.mean(row_block, axis=-1, keepdims=True)
    centred = row_block - averaged
    variance = jnp.mean(centred * centred, axis=-1, keepdims=True)
    return centred * lax.rsqrt(variance + epsilon) * norm_gain + shift_vec


def on_device(
    patches,
    var_ids,
    segment_ids,
    embed_weight,
    var_embed,
    agg_query,
    agg_wq,
    agg_bq,
    agg_wk,
    agg_wv,
    agg_bv,
    agg_wo,
    agg_bo,
    attn_norm_gain,
    attn_norm_bias,
    attn_wqkv,
    attn_bq,
    attn_bv,
    attn_wo,
    attn_bo,
    mlp_norm_gain,
    mlp_norm_bias,
    mlp_up,
    mlp_bup,
    mlp_down,
    mlp_bdown,
    cotangent,
):
    s = lax.axis_index("section")
    r = lax.axis_index("dp")
    ns = lax.axis_size("section")
    nd = lax.axis_size("dp")
    rows = agg_wv.shape[0]
    tokens = patches.shape[0]
    seqs = tokens // LEN
    hl = HEADS // ns
    wl = D // ns
    fl = FF // ns
    cp = VARS * PIX

    def mine(array, axis, index, size):
        return lax.dynamic_slice_in_dim(array, index * size, size, axis)

    qkv_cols = mine(attn_wqkv.reshape(rows, 3, D), 2, s, wl).reshape(rows, 3 * wl)
    first = jnp.concatenate([mine(agg_wo, 1, s, wl), mine(attn_wo, 1, s, wl), qkv_cols], axis=1)
    second = jnp.concatenate([mine(mlp_up, 1, s, fl), mine(mlp_down, 1, s, fl)], axis=1)
    first = lax.all_gather(first, "dp", axis=0, tiled=True)
    second = lax.all_gather(second, "dp", axis=0, tiled=True)
    g_all = lax.all_gather(cotangent, "section", axis=1, tiled=True)
    out_ws = lax.all_to_all(first[:, : 2 * wl].reshape(ns, wl, 2 * wl), "section", 0, 0, tiled=True)
    agg_wo_rows = out_ws[:, :, :wl].transpose(1, 0, 2).reshape(wl, D)
    attn_wo_rows = out_ws[:, :, wl:].transpose(1, 0, 2).reshape(wl, D)
    qkv_w = first[:, 2 * wl :]
    up_w, down_w = second[:, :fl], second[:, fl:]

    var_row = var_ids[:, None] == jnp.arange(VARS, dtype=jnp.int32)[None, :]
    place = jnp.kron(var_row.astype(jnp.bfloat16), jnp.eye(PIX, dtype=jnp.bfloat16))
    spread = jnp.kron(jnp.eye(VARS, dtype=jnp.bfloat16), jnp.ones((1, PIX), jnp.bfloat16))
    pixels = project(patches, place).astype(jnp.bfloat16)

    basis = jnp.concatenate(
        [embed_weight.astype(jnp.float32), mine(var_embed, 1, r, rows).T], axis=1
    )
    wq_part = jnp.dot(
        mine(agg_query, 0, r, rows).astype(jnp.bfloat16)[None],
        agg_wq,
        preferred_element_type=jnp.float32,
    )
    wk_s, wv_s = mine(agg_wk, 1, s, wl), mine(agg_wv, 1, s, wl)
    kv = jnp.concatenate([wk_s, wv_s], axis=1).astype(jnp.float32)
    bkv = jnp.einsum("dc,dn->cn", basis, kv, precision=highest)
    bkv, query_proj = lax.psum((bkv, wq_part), "dp")
    query_proj = query_proj[0] + agg_bq
    query_s = mine(query_proj, 0, s, wl)
    score_scale = HEAD ** (-0.5)
    score_basis = (bkv[:, :wl] * query_s).reshape(-1, hl, HEAD).sum(-1) * score_scale
    value_basis = bkv[:, wl:].astype(jnp.bfloat16)
    key_query = (wk_s.astype(jnp.float32) * query_s).reshape(rows, hl, HEAD).sum(-1) * score_scale

    head_basis = score_basis[:cp, None, :] * spread.T.astype(jnp.float32)[:, :, None]
    head_basis = jnp.concatenate([head_basis, score_basis[cp:, None, :] * jnp.eye(VARS)[:, :, None]], 0)
    head_basis = head_basis.transpose(0, 2, 1).reshape(-1, hl * VARS)
    base = head_basis[cp:].sum(0)
    scores = jnp.dot(pixels.astype(jnp.float32), head_basis[:cp], precision=highest) + base
    probs = jax.nn.softmax(scores.reshape(tokens, hl, VARS), axis=-1)
    probs_low = probs.astype(jnp.bfloat16)
    wrep = jnp.einsum("thc,cq->thq", probs_low, spread, preferred_element_type=jnp.float32)
    mixed = jnp.concatenate(
        [(wrep * pixels[:, None, :].astype(jnp.float32)).astype(jnp.bfloat16), probs_low], axis=-1
    )
    value_heads = value_basis.reshape(-1, hl, HEAD)
    context = jnp.einsum("thq,qhj->thj", mixed, value_heads, preferred_element_type=jnp.float32)
    context = (context.reshape(tokens, wl) + mine(agg_bv, 0, s, wl)).astype(jnp.bfloat16)

    def section_sum(part):
        return lax.psum(part, "section")

    aggregated = section_sum(project(context, agg_wo_rows))
    aggregated = (aggregated + agg_bo).astype(jnp.bfloat16)
    context_all = lax.all_gather(context, "section", axis=1, tiled=True)

    agg_float = aggregated.astype(jnp.float32)
    normed_float, norm_pull = jax.vjp(layer_norm, agg_float, attn_norm_gain, attn_norm_bias)
    normed = normed_float.astype(jnp.bfloat16)
    projected = project(normed, qkv_w)
    shaped = (seqs, LEN, hl, HEAD)
    queries = (projected[:, :wl] + mine(attn_bq, 0, s, wl)).astype(jnp.bfloat16).reshape(shaped)
    keys = projected[:, wl : 2 * wl].astype(jnp.bfloat16).reshape(shaped)
    values = (projected[:, 2 * wl :] + mine(attn_bv, 0, s, wl)).astype(jnp.bfloat16).reshape(shaped)
    f32 = dict(preferred_element_type=jnp.float32)
    att = jnp.einsum("bthj,buhj->bhtu", queries, keys, **f32) * score_scale
    same = segment_ids[:, :, None] == segment_ids[:, None, :]
    att = jnp.where(same[:, None], att, blocked)
    att = jax.nn.softmax(att, axis=-1)
    att_low = att.astype(jnp.bfloat16)
    attended = jnp.einsum("bhtu,buhj->bthj", att_low, values, **f32).reshape(tokens, wl)
    attended = attended.astype(jnp.bfloat16)
    mid = section_sum(project(attended, attn_wo_rows))
    mid = (agg_float + mid + attn_bo).astype(jnp.bfloat16)
    attended_all = lax.all_gather(attended, "section", axis=1, tiled=True)

    mid_float = mid.astype(jnp.float32)
    mnormed_float, mnorm_pull = jax.vjp(layer_norm, mid_float, mlp_norm_gain, mlp_norm_bias)
    mnormed = mnormed_float.astype(jnp.bfloat16)
    hidden = project(mnormed, up_w) + mine(mlp_bup, 0, s, fl)
    act_float, gelu_pull = jax.vjp(partial(jax.nn.gelu, approximate=False), hidden)
    act = act_float.astype(jnp.bfloat16)
    out_part = project_back(act, down_w)
    out_cols = lax.psum_scatter(out_part, "section", scatter_dimension=1, tiled=True)
    activations = mine(mid_float, 1, s, wl) + out_cols + mine(mlp_bdown, 0, s, wl)
    activations = activations.astype(jnp.bfloat16)

    g_float = g_all.astype(jnp.float32)
    grad_down = outer_sum(g_all, act)
    grad_bdown = jnp.sum(g_float, axis=0)
    d_hidden = gelu_pull(project(g_all, down_w))[0].astype(jnp.bfloat16)
    grad_bup = jnp.sum(d_hidden.astype(jnp.float32), axis=0)
    grad_up = outer_sum(mnormed, d_hidden)
    grad_mlp = lax.psum_scatter(
        jnp.concatenate([grad_up, grad_down], axis=1), "dp", scatter_dimension=0, tiled=True
    )
    d_mnormed = section_sum(project_back(d_hidden, up_w))
    d_mid, grad_mgain, grad_mbias = mnorm_pull(d_mnormed)
    d_mid = (g_float + d_mid).astype(jnp.bfloat16)

    grad_attn_wo = outer_sum(attended_all, mine(d_mid, 1, s, wl))
    grad_attn_bo = jnp.sum(d_mid.astype(jnp.float32), axis=0)
    d_att = project_back(d_mid, attn_wo_rows).astype(jnp.bfloat16).reshape(shaped)
    d_values = jnp.einsum("bhtu,bthj->buhj", att_low, d_att, **f32).astype(jnp.bfloat16)
    d_probs = jnp.einsum("bthj,buhj->bhtu", d_att, values, **f32)
    d_scores = att * (d_probs - jnp.sum(att * d_probs, axis=-1, keepdims=True))
    d_scores = d_scores.astype(jnp.bfloat16)
    d_queries = jnp.einsum("bhtu,buhj->bthj", d_scores, keys, **f32) * score_scale
    d_keys = jnp.einsum("bhtu,bthj->buhj", d_scores, queries, **f32) * score_scale
    d_queries = d_queries.astype(jnp.bfloat16).reshape(tokens, wl)
    d_keys = d_keys.astype(jnp.bfloat16).reshape(tokens, wl)
    d_values = d_values.reshape(tokens, wl)
    grad_bq = jnp.sum(d_queries.astype(jnp.float32), axis=0)
    grad_bv = jnp.sum(d_values.astype(jnp.float32), axis=0)
    d_qkv = jnp.concatenate([d_queries, d_keys, d_values], axis=1)
    grad_qkv = outer_sum(normed, d_qkv)
    d_normed = section_sum(project_back(d_qkv, qkv_w))
    d_agg, grad_again, grad_abias = norm_pull(d_normed)
    d_agg = (d_mid.astype(jnp.float32) + d_agg).astype(jnp.bfloat16)

    grad_agg_wo = outer_sum(context_all, mine(d_agg, 1, s, wl))
    grad_agg_bo = jnp.sum(d_agg.astype(jnp.float32), axis=0)
    d_context = project_back(d_agg, agg_wo_rows).astype(jnp.bfloat16)
    grad_agg_bv = jnp.sum(d_context.astype(jnp.float32), axis=0)
    d_ctx_heads = d_context.reshape(tokens, hl, HEAD)
    cross = jnp.einsum("thj,thq->hjq", d_ctx_heads, mixed, **f32).reshape(wl, -1)
    pulled = jnp.einsum("thj,qhj->thq", d_ctx_heads, value_heads, **f32)
    d_weights = jnp.einsum(
        "thq,cq->thc",
        pulled[:, :, :cp] * pixels[:, None, :].astype(jnp.float32),
        spread.astype(jnp.float32),
        precision=highest,
    ) + pulled[:, :, cp:]
    d_sc = probs * (d_weights - jnp.sum(probs * d_weights, axis=-1, keepdims=True))
    d_sc = d_sc.astype(jnp.bfloat16)
    srep = jnp.einsum("thc,cq->thq", d_sc, spread, **f32)
    key_terms = jnp.concatenate(
        [
            jnp.sum(srep * pixels[:, None, :].astype(jnp.float32), axis=0),
            jnp.sum(d_sc.astype(jnp.float32), axis=0),
        ],
        axis=-1,
    )
    grad_pix = jnp.sum(wrep * pulled[:, :, :cp] + srep * score_basis[:cp].T[None], axis=1)
    grad_pix = section_sum(grad_pix).astype(jnp.bfloat16)
    patches_grad = mine(project_back(grad_pix, place).astype(jnp.bfloat16), 1, s, cp // ns)

    grad_attn = lax.psum_scatter(
        jnp.concatenate([grad_agg_wo, grad_attn_wo, grad_qkv], axis=1),
        "dp",
        scatter_dimension=0,
        tiled=True,
    )
    full_small = jnp.stack([grad_bdown, grad_mgain, grad_mbias, grad_attn_bo, grad_again, grad_abias, grad_agg_bo])
    part_small = jnp.concatenate([grad_bup, grad_bq, grad_bv, grad_agg_bv])
    cross, key_terms, full_small, part_small = lax.psum((cross, key_terms, full_small, part_small), "dp")

    grad_wv = jnp.dot(basis, cross.T, precision=highest)
    grad_basis = jnp.dot(wv_s.astype(jnp.float32), cross, precision=highest) + jnp.dot(
        key_query, key_terms, precision=highest
    )
    d_key_query = jnp.einsum("dq,hq->dh", basis, key_terms, precision=highest)
    grad_wk = (d_key_query[:, :, None] * query_s.reshape(hl, HEAD)[None]).reshape(rows, wl) * score_scale
    d_query = jnp.einsum("qhj,hq->hj", bkv[:, :wl].reshape(-1, hl, HEAD), key_terms, precision=highest)
    d_query = d_query.reshape(wl) * score_scale
    grad_basis = section_sum(grad_basis)
    d_query = lax.all_gather(d_query, "section", axis=0, tiled=True)
    part_small = lax.all_gather(part_small, "section", axis=0)
    grad_wq = mine(agg_query, 0, r, rows).astype(jnp.bfloat16).astype(jnp.float32)[:, None] * d_query
    grad_query = jnp.dot(agg_wq.astype(jnp.float32), d_query, precision=highest)
    joined = jnp.concatenate([grad_attn, grad_wv, grad_wk, grad_mlp], axis=1).astype(jnp.bfloat16)
    joined = lax.all_gather(joined, "section", axis=0)

    def columns(start, width):
        part = joined[:, :, start : start + width].astype(jnp.float32)
        return part.transpose(1, 0, 2).reshape(rows, ns * width)

    grad_qkv = joined[:, :, 2 * wl : 5 * wl].astype(jnp.float32).reshape(ns, rows, 3, wl)
    grad_qkv = grad_qkv.transpose(1, 2, 0, 3).reshape(rows, 3 * D)
    small = mine(full_small, 1, r, rows)
    bup = mine(part_small[:, :fl].reshape(-1), 0, r, FF // nd)
    bq = mine(part_small[:, fl : fl + wl].reshape(-1), 0, r, rows)
    bv = mine(part_small[:, fl + wl : fl + 2 * wl].reshape(-1), 0, r, rows)
    abv = mine(part_small[:, fl + 2 * wl :].reshape(-1), 0, r, rows)
    return (
        activations,
        patches_grad,
        grad_basis[:, :cp],
        grad_basis[:, cp:].T,
        grad_query,
        grad_wq,
        mine(d_query, 0, r, rows),
        columns(6 * wl, wl),
        columns(5 * wl, wl),
        abv,
        columns(0, wl),
        small[6],
        small[4],
        small[5],
        grad_qkv,
        bq,
        bv,
        columns(wl, wl),
        small[3],
        small[1],
        small[2],
        columns(7 * wl, fl),
        bup,
        columns(7 * wl + fl, fl),
        small[0],
    )


def solution(mesh):
    in_specs = (
        P("dp", None),
        P(),
        P("dp", None),
        P("dp", None),
        P(),
        P(),
        P("dp", None),
        P(),
        P("dp", None),
        P("dp", None),
        P(),
        P("dp", None),
        P(),
        P(),
        P(),
        P("dp", None),
        P(),
        P(),
        P("dp", None),
        P(),
        P(),
        P(),
        P("dp", None),
        P(),
        P("dp", None),
        P(),
        P("dp", "section"),
    )
    out_specs = (
        P("dp", "section"),
        P("dp", "section"),
        P("dp", None),
        P(None, "dp"),
        P("dp"),
        P("dp", None),
        P("dp"),
        P("dp", None),
        P("dp", None),
        P("dp"),
        P("dp", None),
        P("dp"),
        P("dp"),
        P("dp"),
        P("dp", None),
        P("dp"),
        P("dp"),
        P("dp", None),
        P("dp"),
        P("dp"),
        P("dp"),
        P("dp", None),
        P("dp"),
        P("dp", None),
        P("dp"),
    )
    return jax.shard_map(
        on_device, mesh=mesh, in_specs=in_specs, out_specs=out_specs, check_vma=False
    )
```

```python
from functools import partial
from types import SimpleNamespace

import jax
import jax.numpy as jnp
from jax import lax
from jax.experimental import pallas as pl
from jax.experimental.pallas import tpu as pltpu
from jax.sharding import PartitionSpec as P

D = 1024
HEADS = 16
HEAD = 64
FF = 4096
VARS = 48
PIX = 4
LEN = 128

highest = lax.Precision.HIGHEST
blocked = -1000000000.0
epsilon = 1e-05
MESH = pl.DeviceIdType.MESH
BF = jnp.bfloat16
F32 = jnp.float32
CHUNK = 256
CP = VARS * PIX
LANES = 128


def nn(a, b):
    return jnp.dot(a, b, preferred_element_type=F32)


def nt(a, b):
    return lax.dot_general(a, b, (((1,), (1,)), ((), ())), preferred_element_type=F32)


def tn(a, b):
    return lax.dot_general(a, b, (((0,), (0,)), ((), ())), preferred_element_type=F32)


def split(x):
    high = x.astype(BF)
    return high, (x - high.astype(F32)).astype(BF)


def iota(shape, dim):
    return lax.broadcasted_iota(jnp.int32, shape, dim)


def colsum(x):
    return jnp.sum(x.astype(F32), axis=0, keepdims=True)


def each(low, high, body):
    if high - low <= 8:
        for k in range(low, high):
            body(k)
    else:

        def step(k, carry):
            body(k)
            return carry

        lax.fori_loop(low, high, step, 0)


class Transfer:
    def __init__(self, make, low, high):
        self.make, self.low, self.high = make, low, high

    def start(self):
        each(self.low, self.high, lambda k: self.make(k).start())
        return self

    def wait_recv(self):
        each(self.low, self.high, lambda k: self.make(k).wait_recv())

    def wait_send(self):
        each(self.low, self.high, lambda k: self.make(k).wait_send())


def kernel(ns, nd, refs_in, refs_out, sc):
    s = lax.axis_index("section")
    r = lax.axis_index("dp")
    nx = 2
    nz = nd // nx
    z, x = lax.div(r, nx), lax.rem(r, nx)
    i, o = refs_in, refs_out
    rows = D // nd
    tokens = i.patches.shape[0]
    shard = tokens // ns
    wl, fl, hl = D // ns, FF // ns, HEADS // ns
    zq = nz // ns
    own_cols = pl.ds(pl.multiple_of(s * wl, LANES), wl)
    own_ff = pl.ds(pl.multiple_of(s * fl, LANES), fl)
    own_rows = pl.ds(pl.multiple_of(s * shard, 16), shard)
    scale = HEAD ** (-0.5)
    send, recv = sc.send, sc.recv
    used = {"n": 0}
    pending = []

    def sems(count):
        base = used["n"]
        used["n"] += count
        return base

    def remote(src, dst, sem, device):
        return pltpu.make_async_remote_copy(
            src_ref=src,
            dst_ref=dst,
            send_sem=send.at[sem],
            recv_sem=recv.at[sem],
            device_id=device,
            device_id_type=MESH,
        )

    def over_section(src, dst):
        base = sems(ns)

        def make(k):
            t = lax.rem(s + k, ns)
            return remote(src(t), dst, base + k, (t, r))

        transfer = Transfer(make, 1, ns).start()
        pending.append(transfer)
        return transfer

    def over_dp(src, dst):
        base = sems(nd)

        def make(k):
            t = lax.rem(r + k, nd)
            return remote(src(t), dst, base + k, (s, t))

        transfer = Transfer(make, 1, nd).start()
        pending.append(transfer)
        return transfer

    def over_z(src, dst):
        base = sems(nz)

        def make(k):
            t = lax.rem(z + k, nz)
            return remote(src(t), dst, base + k, (s, t * nx + x))

        transfer = Transfer(make, 1, nz).start()
        pending.append(transfer)
        return transfer

    def over_x(src, dst):
        base = sems(1)
        transfer = Transfer(lambda k: remote(src, dst, base, (s, z * nx + 1 - x)), 0, 1).start()
        pending.append(transfer)
        return transfer

    local_used = {"n": 0}

    def local(src, dst):
        sem = local_used["n"]
        local_used["n"] += 1
        copy = pltpu.make_async_copy(src, dst, sc.local.at[sem])
        copy.start()
        return copy

    small_loads = [
        local(i.agg_wq.at[:, own_cols], sc.wq),
        local(i.agg_wk.at[:, own_cols], sc.wk),
        local(i.agg_wv.at[:, own_cols], sc.wv),
    ]
    qkv_loads = [
        local(
            i.attn_wqkv.at[:, pl.ds(pl.multiple_of(j * D + s * wl, LANES), wl)],
            sc.qkv_w.at[z, x, :, pl.ds(j * wl, wl)],
        )
        for j in range(3)
    ]
    up_load = local(i.mlp_up.at[:, own_ff], sc.up_w.at[z, x])
    down_load = local(i.mlp_down.at[:, own_ff], sc.down_w.at[z, x])
    cot_load = local(i.cotangent, sc.g_full.at[:, own_cols])

    barrier = pltpu.get_barrier_semaphore()
    for k in range(1, ns):
        pl.semaphore_signal(barrier, inc=1, device_id=(lax.rem(s + k, ns), r), device_id_type=MESH)
    each(
        1,
        nd,
        lambda k: pl.semaphore_signal(
            barrier, inc=1, device_id=(s, lax.rem(r + k, nd)), device_id_type=MESH
        ),
    )

    chan = (iota((CP, VARS), 0) >> 2 == iota((CP, VARS), 1)).astype(F32).astype(BF)
    ids = jnp.broadcast_to(i.var_ids[...].astype(F32), (CHUNK, VARS)).astype(BF)
    ids = nt(chan, ids)
    lane = iota((CP, CHUNK), 1)
    row = iota((CP, CHUNK), 0)
    hit = ((lane >> 2).astype(F32) == ids) & ((lane & 3) == (row & 3)) & (lane < CP)
    place = hit.astype(F32).astype(BF)
    sc.place[...] = place
    lane = iota((tokens, CHUNK), 1)
    ones = ((lane >= CP) & (lane < CP + VARS)).astype(F32)
    sc.pix[...] = (nn(i.patches[...], place) + ones).astype(BF)
    row = iota((CHUNK, LANES), 0)
    lane = iota((CHUNK, LANES), 1)
    owner = jnp.where(row < CP, row >> 2, row - CP)
    sc.fold[...] = ((owner == lane) & (lane < VARS)).astype(F32).astype(BF)
    chosen = (iota((rows, D), 1) == iota((rows, D), 0) + r * rows).astype(F32).astype(BF)
    lane = iota((CP, CHUNK), 1)
    row = iota((CP, CHUNK), 0)
    widen = (lane == row).astype(F32).astype(BF)
    lane = iota((VARS, CHUNK), 1)
    row = iota((VARS, CHUNK), 0)
    widen_var = (lane == row + CP).astype(F32).astype(BF)
    var_rows = nt(chosen, i.var_embed[...].astype(BF)).astype(BF)
    sc.basis[...] = (nn(i.embed_weight[...], widen) + nn(var_rows, widen_var)).astype(BF)
    query = jnp.broadcast_to(i.agg_query[...].astype(BF).astype(F32), (16, D))
    query = jnp.where(iota((16, D), 0) == 0, query, 0.0).astype(BF)
    query_rows = nt(query, chosen).astype(BF)
    sc.vecs[...] = jnp.zeros_like(sc.vecs)
    sc.bup[...] = jnp.zeros_like(sc.bup)

    for copy in small_loads:
        copy.wait()
    sc.q_src[...] = nn(query_rows, sc.wq[...])[0:8]
    value_part = tn(sc.basis[...], sc.wv[...])
    blk = CHUNK // nd
    for t in range(nd):
        sc.bv_src[t] = value_part[t * blk : (t + 1) * blk]
    cot_load.wait()

    pl.semaphore_wait(barrier, ns - 1 + nd - 1)

    def push(src, dst):
        transfer = over_dp(lambda t: src, dst.at[r])
        dst[r] = src[...]
        return transfer

    def summed(dst, count):
        total = dst[0]
        for k in range(1, count):
            total = total + dst[k]
        return total

    q_push = push(sc.q_src, sc.q_recv)
    bv_rs = over_dp(lambda t: sc.bv_src.at[t], sc.bv_recv.at[r])
    sc.bv_recv[r] = sc.bv_src[r]
    g_gather = over_section(lambda t: sc.g_full.at[:, own_cols], sc.g_full.at[:, own_cols])

    def rows_out(whole, dst):
        base = sems(zq)
        base_send = sems(nz)
        local_base = local_used["n"]
        local_used["n"] += zq

        def make(j, k):
            t = lax.rem(z + k, nz)
            return pltpu.make_async_remote_copy(
                src_ref=whole,
                dst_ref=dst.at[j, x],
                send_sem=send.at[base_send + k],
                recv_sem=recv.at[base + j],
                device_id=(s, t * nx + x),
                device_id_type=MESH,
            )

        def go(j):
            @pl.when(z == s * zq + j)
            def _():
                pltpu.make_async_copy(whole, dst.at[j, x], sc.local.at[local_base + j]).start()
                each(1, nz, lambda k: make(j, k).start())

        def arrive(j):
            @pl.when(z == s * zq + j)
            def _():
                pltpu.make_async_copy(whole, dst.at[j, x], sc.local.at[local_base + j]).wait()

            @pl.when(z != s * zq + j)
            def _():
                make(j, 1).wait_recv()

        def finish(j):
            @pl.when(z == s * zq + j)
            def _():
                each(1, nz, lambda k: make(j, k).wait_send())

        def start():
            each(0, zq, go)

        def forward():
            each(0, zq, arrive)
            return over_x(dst.at[:, x], dst.at[:, x])

        return start, forward, lambda: each(0, zq, finish)

    awo_start, awo_forward, awo_finish = rows_out(i.agg_wo, sc.awo)
    two_start, two_forward, two_finish = rows_out(i.attn_wo, sc.two)
    awo_start()
    for copy in qkv_loads:
        copy.wait()
    qkv_z = over_z(lambda t: sc.qkv_w.at[z, x], sc.qkv_w.at[z, x])
    two_start()

    q_push.wait_recv()
    query_proj = summed(sc.q_recv, nd)[0:1] + i.agg_bq[:, own_cols]
    sc.query_proj[...] = query_proj
    head_rows = (iota((16, wl), 1) >> 6 == iota((16, wl), 0)).astype(F32)
    high, low = split(head_rows * (query_proj * scale))
    key_query = (nt(high, sc.wk[...]) + nt(low, sc.wk[...])).astype(BF)
    sc.key_query[...] = key_query
    sc.s_src[...] = nn(key_query, sc.basis[...])[0:8]
    s_push = push(sc.s_src, sc.s_recv)
    bv_rs.wait_recv()
    sc.bv_own[...] = summed(sc.bv_recv, nd)
    bv_ag = push(sc.bv_own, sc.bv_all)
    up_load.wait()
    up_z = over_z(lambda t: sc.up_w.at[z, x], sc.up_w.at[z, x])

    s_push.wait_recv()
    score_rows = summed(sc.s_recv, nd)
    sc.score_rows[...] = score_rows
    fold = sc.fold[...]
    lane_ok = iota((tokens, LANES), 1) < VARS
    for h in range(hl):
        pix = sc.pix[...].astype(F32)
        high, low = split(pix * score_rows[h : h + 1])
        scores = nn(high, fold) + nn(low, fold)
        scores = jnp.where(lane_ok, scores, -1e30)
        scores = jnp.exp(scores - jnp.max(scores, axis=-1, keepdims=True))
        probs = scores / jnp.sum(scores, axis=-1, keepdims=True)
        sc.probs[h] = probs
        wrep = nt(probs.astype(BF), fold)
        sc.wrep[h] = wrep.astype(BF)
        sc.mixed[h] = (wrep * pix).astype(BF)
    awo_x = awo_forward()
    bv_ag.wait_recv()
    for t in range(nd):
        sc.bv[t * blk : (t + 1) * blk] = sc.bv_all[t]
    value_basis = sc.bv[...].astype(BF)
    head_of = iota((1, wl), 1) >> 6
    context = jnp.broadcast_to(i.agg_bv[:, own_cols], (tokens, wl))
    for h in range(hl):
        context = context + jnp.where(head_of == h, nn(sc.mixed[h], value_basis), 0.0)
    sc.context[...] = context.astype(BF)
    awo_x.wait_recv()

    def weight(ref):
        return ref[...].reshape(ref.shape[0] * ref.shape[1] * ref.shape[2], ref.shape[3])

    def scatter(part, landed, value):
        part[...] = value.astype(BF)
        transfer = over_section(lambda t: part.at[pl.ds(pl.multiple_of(t * shard, 16), shard)], landed.at[s])
        landed[s] = part[own_rows, :]
        return transfer

    def gather(full, value):
        full[own_rows, :] = value.astype(BF)
        return over_section(lambda t: full.at[own_rows], full.at[own_rows])

    def landed_sum(landed):
        total = landed[0].astype(F32)
        for k in range(1, ns):
            total = total + landed[k].astype(F32)
        return total

    def norm(value, gain, bias, kept, rstd_kept):
        centred = value - jnp.mean(value, axis=-1, keepdims=True)
        rstd = lax.rsqrt(jnp.mean(centred * centred, axis=-1, keepdims=True) + epsilon)
        hat = centred * rstd
        kept[...] = hat
        rstd_kept[...] = jnp.broadcast_to(rstd, rstd_kept.shape)
        return hat * gain[...] + bias[...]

    def norm_back(grad, gain, kept, rstd_kept, gain_row, bias_row):
        hat = kept[...]
        sc.vecs[gain_row : gain_row + 1, :] = colsum(grad * hat)
        sc.vecs[bias_row : bias_row + 1, :] = colsum(grad)
        inner = grad * gain[...]
        mean = jnp.mean(inner, axis=-1, keepdims=True)
        dot = jnp.mean(inner * hat, axis=-1, keepdims=True)
        return rstd_kept[:, 0:1] * (inner - mean - hat * dot)

    def transposed(full, dst):
        for j in range(D // CHUNK):
            turned = full[:, j * CHUNK : (j + 1) * CHUNK].astype(F32).T.astype(BF)
            n = dst.shape[0] // (D // CHUNK)
            dst[j * n : (j + 1) * n] = turned.reshape((n,) + dst.shape[1:])

    def head_block(value, dst):
        at = pl.ds(s * zq, zq)
        dst[at] = value.astype(F32).T.astype(BF).reshape((zq,) + dst.shape[1:])
        return over_section(lambda t: dst.at[at], dst.at[at])

    rs1 = scatter(sc.rs1_part, sc.rs1_recv, nn(sc.context[...], weight(sc.awo)))
    context_gather = head_block(sc.context[...], sc.contextT)
    g_gather.wait_recv()
    qkv_z.wait_recv()
    qkv_x = over_x(sc.qkv_w.at[:, x], sc.qkv_w.at[:, x])
    down_load.wait()
    down_z = over_z(lambda t: sc.down_w.at[z, x], sc.down_w.at[z, x])
    rs1.wait_recv()
    agg = (landed_sum(sc.rs1_recv) + i.agg_bo[...]).astype(BF).astype(F32)
    sc.agg[...] = agg
    ag1 = gather(sc.normed, norm(agg, i.attn_norm_gain, i.attn_norm_bias, sc.hat1, sc.rstd1))
    two_x = two_forward()
    transposed(sc.g_full, sc.gT)
    qkv_x.wait_recv()
    ag1.wait_recv()

    normed = sc.normed[...]
    qkv_w = weight(sc.qkv_w)
    for j in range(3):
        part = nn(normed, qkv_w[:, j * wl : (j + 1) * wl])
        if j == 0:
            part = part + i.attn_bq[:, own_cols]
        if j == 2:
            part = part + i.attn_bv[:, own_cols]
        sc.qkv[:, j * wl : (j + 1) * wl] = part.astype(BF)
    lo = (iota((1, LANES), 1) < HEAD).astype(F32)
    first, second = lo.astype(BF), (1.0 - lo).astype(BF)

    def pair(a):
        return jnp.concatenate([a * first, a * second], axis=0)

    def pick(a):
        return jnp.where(iota((LEN, LANES), 1) < HEAD, a[0:LEN], a[LEN:])

    tiles = [(b, p) for b in range(tokens // LEN) for p in range(wl // LANES)]

    def tile(ref, b, p, j=0):
        return ref[b * LEN : (b + 1) * LEN, j * wl + p * LANES : j * wl + (p + 1) * LANES]

    for n, (b, p) in enumerate(tiles):
        q, k, v = [tile(sc.qkv, b, p, j) for j in range(3)]
        ids = jnp.broadcast_to(i.segment_ids[b : b + 1, :].astype(F32), (LEN, LEN))
        same = ids == ids.T
        scores = nt(pair(q), k) * scale
        scores = jnp.where(jnp.concatenate([same, same], axis=0), scores, blocked)
        scores = jnp.exp(scores - jnp.max(scores, axis=-1, keepdims=True))
        probs = scores / jnp.sum(scores, axis=-1, keepdims=True)
        sc.att[n] = probs
        sc.attended[b * LEN : (b + 1) * LEN, p * LANES : (p + 1) * LANES] = pick(
            nn(probs.astype(BF), v)
        ).astype(BF)
    two_x.wait_recv()
    rs2 = scatter(sc.rs2_part, sc.rs2_recv, nn(sc.attended[...], weight(sc.two)))
    attended_gather = head_block(sc.attended[...], sc.attendedT)
    up_z.wait_recv()
    up_x = over_x(sc.up_w.at[:, x], sc.up_w.at[:, x])
    transposed(sc.normed, sc.normedT)
    rs2.wait_recv()
    mid = (sc.agg[...] + landed_sum(sc.rs2_recv) + i.attn_bo[...]).astype(BF).astype(F32)
    sc.mid[...] = mid
    ag2 = gather(sc.mnormed, norm(mid, i.mlp_norm_gain, i.mlp_norm_bias, sc.hat2, sc.rstd2))
    ag2.wait_recv()
    up_x.wait_recv()

    def columns(ref, j):
        return ref[:, :, :, j * CHUNK : (j + 1) * CHUNK].reshape(D, CHUNK)

    mnormed = sc.mnormed[...]
    for j in range(fl // CHUNK):
        at = slice(j * CHUNK, (j + 1) * CHUNK)
        bias = i.mlp_bup[:, pl.ds(pl.multiple_of(s * fl + j * CHUNK, LANES), CHUNK)]
        hidden = nn(mnormed, columns(sc.up_w, j)) + bias
        phi = 0.5 + 0.5 * lax.erf(hidden * 0.7071067811865476)
        density = jnp.exp(hidden * hidden * -0.5) * 0.3989422804014327
        sc.act[:, at] = (hidden * phi).astype(BF)
        sc.slope[:, at] = phi + hidden * density
    down_z.wait_recv()
    down_x = over_x(sc.down_w.at[:, x], sc.down_w.at[:, x])

    names = (
        [(o.mlp_down, s * fl + j * CHUNK) for j in range(fl // CHUNK)]
        + [(o.mlp_up, s * fl + j * CHUNK) for j in range(fl // CHUNK)]
        + [(o.attn_wo, s * wl)]
        + [(o.attn_wqkv, j * D + s * wl) for j in range(3)]
        + [(o.agg_wo, s * wl)]
    )
    to_x, to_z = {}, {}
    out_copies, out_sends = [], []

    def produce(c, left, right):
        def half(side):
            block = left[:, pl.ds(side, 1)].reshape(nz * rows, tokens)
            return nn(block, right).reshape(nz, rows, CHUNK)

        sc.x_send[c] = half(1 - x).astype(BF)
        to_x[c] = over_x(sc.x_send.at[c], sc.x_recv.at[c])
        sc.keep[c] = half(x)

    def middle(c):
        to_x[c].wait_recv()
        sc.z_send[c] = (sc.keep[c] + sc.x_recv[c].astype(F32)).astype(BF)
        to_z[c] = over_z(lambda t: sc.z_send.at[c, t], sc.z_recv.at[c, z])
        sc.z_recv[c, z] = sc.z_send[c, z]

    def publish(c, array, start):
        dst = array.at[:, pl.ds(pl.multiple_of(start, LANES), CHUNK)]
        out_sends.append(over_section(lambda t: sc.final.at[c], dst))
        out_copies.append(local(sc.final.at[c], dst))

    def finish(c):
        to_z[c].wait_recv()
        total = sc.z_recv[c, 0].astype(F32)
        for k in range(1, nz):
            total = total + sc.z_recv[c, k].astype(F32)
        sc.final[c] = total.astype(BF)
        publish(c, *names[c])

    for j in range(fl // CHUNK):
        produce(j, sc.gT, sc.act[:, j * CHUNK : (j + 1) * CHUNK])
    transposed(sc.mnormed, sc.mnormedT)
    down_x.wait_recv()
    g_full = sc.g_full[...]
    for j in range(fl // CHUNK):
        at = slice(j * CHUNK, (j + 1) * CHUNK)
        d_hidden = nn(g_full, columns(sc.down_w, j)) * sc.slope[:, at]
        sc.d_hidden[:, at] = d_hidden.astype(BF)
    up_w = weight(sc.up_w)
    rs3 = scatter(sc.rs3_part, sc.rs3_recv, nt(sc.d_hidden[...], up_w))
    nmlp = fl // CHUNK
    for j in range(nmlp):
        at = slice(j * CHUNK, (j + 1) * CHUNK)
        produce(nmlp + j, sc.mnormedT, sc.d_hidden[:, at])
    sc.bup[:, own_ff] = colsum(sc.d_hidden[...])
    rs3.wait_recv()
    g_shard = sc.g_full[own_rows, :].astype(F32)
    sc.vecs[0:1, :] = colsum(g_shard)
    d_mid = norm_back(landed_sum(sc.rs3_recv), i.mlp_norm_gain, sc.hat2, sc.rstd2, 1, 2)
    d_mid = (g_shard + d_mid).astype(BF)
    sc.vecs[3:4, :] = colsum(d_mid)
    ag3 = gather(sc.d_mid, d_mid)
    d_mid = d_mid.astype(F32)
    sc.out_part[...] = nt(sc.act[...], weight(sc.down_w))
    sc.out_part[own_rows, :] = sc.out_part[own_rows, :] + sc.mid[...] + i.mlp_bdown[...]
    sc.out_low[...] = sc.out_part[...].astype(BF)
    out_rs = over_section(
        lambda t: sc.out_low.at[:, pl.ds(pl.multiple_of(t * wl, LANES), wl)], sc.out_recv.at[s]
    )
    sc.out_recv[s] = sc.out_low[:, own_cols]
    for c in range(2):
        middle(c)
    ag3.wait_recv()

    d_att = nt(sc.d_mid[...], weight(sc.two)).astype(BF)
    sc.d_att[...] = d_att
    for n, (b, p) in enumerate(tiles):
        q, k, v = [tile(sc.qkv, b, p, j) for j in range(3)]
        q, d_out = pair(q), pair(tile(sc.d_att, b, p))
        probs = sc.att[n]
        d_probs = nt(d_out, v)
        d_scores = probs * (d_probs - jnp.sum(probs * d_probs, axis=-1, keepdims=True))
        d_scores = d_scores.astype(BF)
        parts = (pick(nn(d_scores, k)) * scale, tn(d_scores, q) * scale, tn(probs.astype(BF), d_out))
        for j in range(3):
            lanes = slice(j * wl + p * LANES, j * wl + (p + 1) * LANES)
            sc.d_qkv[b * LEN : (b + 1) * LEN, lanes] = parts[j].astype(BF)
    rs4 = scatter(sc.rs4_part, sc.rs4_recv, nt(sc.d_qkv[...], weight(sc.qkv_w)))
    attended_gather.wait_recv()
    produce(2 * nmlp, sc.attendedT, sc.d_mid[:, own_cols])
    for j in range(3):
        produce(2 * nmlp + 1 + j, sc.normedT, sc.d_qkv[:, j * wl : (j + 1) * wl])
    sc.vecs[7:8, own_cols] = colsum(sc.d_qkv[:, 0:wl])
    sc.vecs[8:9, own_cols] = colsum(sc.d_qkv[:, 2 * wl : 3 * wl])
    for c in range(2, 4):
        middle(c)
    rs4.wait_recv()
    d_agg = norm_back(landed_sum(sc.rs4_recv), i.attn_norm_gain, sc.hat1, sc.rstd1, 4, 5)
    d_agg = (sc.d_mid[own_rows, :].astype(F32) + d_agg).astype(BF)
    sc.vecs[6:7, :] = colsum(d_agg)
    ag4 = gather(sc.d_agg, d_agg)
    for c in range(4, 6):
        middle(c)
    finish(0)
    finish(1)
    ag4.wait_recv()

    context_gather.wait_recv()
    produce(2 * nmlp + 4, sc.contextT, sc.d_agg[:, own_cols])
    d_context = nt(sc.d_agg[...], weight(sc.awo)).astype(BF)
    sc.vecs[9:10, own_cols] = colsum(d_context)
    value_basis = sc.bv[...].astype(BF)
    cross = jnp.zeros((wl, CHUNK), F32)
    grad_pix = jnp.zeros((tokens, CHUNK), F32)
    sc.key_src[...] = jnp.zeros_like(sc.key_src)
    for h in range(hl):
        masked = d_context * (head_of == h).astype(F32).astype(BF)
        pulled = nt(masked, value_basis)
        cross = cross + tn(masked, sc.mixed[h])
        pix = sc.pix[...].astype(F32)
        high, low = split(pulled * pix)
        d_weights = nn(high, fold) + nn(low, fold)
        probs = sc.probs[h]
        d_scores = probs * (d_weights - jnp.sum(probs * d_weights, axis=-1, keepdims=True))
        srep = nt(d_scores.astype(BF), fold)
        sc.key_src[h : h + 1, :] = colsum(srep * pix)
        grad_pix = grad_pix + sc.wrep[h].astype(F32) * pulled
        grad_pix = grad_pix + srep * sc.score_rows[h : h + 1, :]
    key_push = push(sc.key_src, sc.key_recv)
    for t in range(nd):
        sc.m_src[t] = cross[t * blk : (t + 1) * blk]
    m_rs = over_dp(lambda t: sc.m_src.at[t], sc.m_recv.at[r])
    sc.m_recv[r] = sc.m_src[r]
    grad_pix = grad_pix.astype(BF)
    pw = CP // ns
    for t in range(ns):
        sc.pix_src[t, :, 0:pw] = nt(grad_pix, sc.place[t * pw : (t + 1) * pw, :]).astype(BF)
    pix_rs = over_section(lambda t: sc.pix_src.at[t], sc.pix_recv.at[s])
    sc.pix_recv[s] = sc.pix_src[s]
    for t in range(nd):
        sc.small_src[t, 0:10] = sc.vecs[0:10, t * rows : (t + 1) * rows]
        for j in range(FF // D):
            start = (t * (FF // D) + j) * rows
            sc.small_src[t, 10 + j : 11 + j] = sc.bup[:, start : start + rows]
    small_rs = over_dp(lambda t: sc.small_src.at[t], sc.small_recv.at[r])
    sc.small_recv[r] = sc.small_src[r]

    middle(6)
    m_rs.wait_recv()
    sc.m_own[...] = summed(sc.m_recv, nd)
    m_ag = push(sc.m_own, sc.m_all)
    middle(7)
    key_push.wait_recv()
    key_terms = summed(sc.key_recv, nd)
    wide = jnp.concatenate([jnp.broadcast_to(key_terms[h : h + 1], (HEAD, CHUNK)) for h in range(hl)], axis=0)
    d_key = nt(sc.basis[...], wide.astype(BF))
    d_query = jnp.sum(sc.wk[...].astype(F32) * d_key, axis=0, keepdims=True) * scale
    sc.dq_src[...] = jnp.broadcast_to(d_query, sc.dq_src.shape)
    dq_push = push(sc.dq_src, sc.dq_recv)
    count = len(names)
    sc.final[count] = (d_key * (sc.query_proj[...] * scale)).astype(BF)
    publish(count, o.agg_wk, s * wl)
    finish(2)
    small_rs.wait_recv()
    sc.sec_small[s] = summed(sc.small_recv, nd)
    small_ag = over_section(lambda t: sc.sec_small.at[s], sc.sec_small.at[s])
    middle(8)
    finish(3)
    m_ag.wait_recv()
    for t in range(nd):
        sc.cross[t * blk : (t + 1) * blk] = sc.m_all[t]
    cross = sc.cross[...].astype(BF)
    sc.final[count + 1] = nt(sc.basis[...], cross).astype(BF)
    publish(count + 1, o.agg_wv, s * wl)
    key_low = jnp.concatenate([key_terms, jnp.zeros_like(key_terms)], axis=0).astype(BF)
    grad_basis = nn(sc.wv[...], cross) + tn(sc.key_query[...], key_low)
    sc.basis_recv[s] = grad_basis.astype(BF)
    basis_sum = over_section(lambda t: sc.basis_recv.at[s], sc.basis_recv.at[s])
    dq_push.wait_recv()
    o.d_query[s] = summed(sc.dq_recv, nd)
    dq_gather = over_section(lambda t: o.d_query.at[s], o.d_query.at[s])
    middle(9)
    finish(4)
    middle(10)
    finish(5)
    middle(11)
    finish(6)
    middle(12)
    finish(7)
    small_ag.wait_recv()
    o.small[...] = summed(sc.sec_small, ns)
    pix_rs.wait_recv()
    total = sc.pix_recv[0].astype(F32)
    for k in range(1, ns):
        total = total + sc.pix_recv[k].astype(F32)
    o.patches[...] = total.astype(BF)
    out_rs.wait_recv()
    total = sc.out_recv[0].astype(F32)
    for k in range(1, ns):
        total = total + sc.out_recv[k].astype(F32)
    o.activations[...] = total.astype(BF)
    basis_sum.wait_recv()
    total = sc.basis_recv[0].astype(F32)
    for k in range(1, ns):
        total = total + sc.basis_recv[k].astype(F32)
    o.basis[...] = total
    for c in range(8, 13):
        finish(c)
    dq_gather.wait_recv()
    for transfer in out_sends:
        transfer.wait_recv()
    for copy in out_copies:
        copy.wait()
    awo_finish()
    two_finish()
    for transfer in pending:
        transfer.wait_send()
    assert used["n"] <= send.shape[0], used["n"]
    assert local_used["n"] <= sc.local.shape[0]


def scratch(ns, nd, tokens):
    nz, rows = nd // 2, D // nd
    wl, fl, hl = D // ns, FF // ns, HEADS // ns
    shard, zq, blk = tokens // ns, nz // ns, CHUNK // nd
    chunks = 2 * (fl // CHUNK) + 5
    v = pltpu.VMEM
    shapes = dict(
        wq=v((rows, wl), BF),
        wk=v((rows, wl), BF),
        wv=v((rows, wl), BF),
        qkv_w=v((nz, 2, rows, 3 * wl), BF),
        up_w=v((nz, 2, rows, fl), BF),
        down_w=v((nz, 2, rows, fl), BF),
        awo=v((zq, 2, rows, D), BF),
        two=v((zq, 2, rows, D), BF),
        g_full=v((tokens, D), BF),
        place=v((CP, CHUNK), BF),
        pix=v((tokens, CHUNK), BF),
        fold=v((CHUNK, LANES), BF),
        basis=v((rows, CHUNK), BF),
        vecs=v((16, D), F32),
        bup=v((1, FF), F32),
        query_proj=v((1, wl), F32),
        key_query=v((16, rows), BF),
        score_rows=v((8, CHUNK), F32),
        bv_own=v((blk, CHUNK), F32),
        m_own=v((blk, CHUNK), F32),
        bv=v((CHUNK, CHUNK), F32),
        cross=v((CHUNK, CHUNK), F32),
        probs=v((hl, tokens, LANES), F32),
        wrep=v((hl, tokens, CHUNK), BF),
        mixed=v((hl, tokens, CHUNK), BF),
        context=v((tokens, wl), BF),
        agg=v((shard, D), F32),
        mid=v((shard, D), F32),
        hat1=v((shard, D), F32),
        hat2=v((shard, D), F32),
        rstd1=v((shard, LANES), F32),
        rstd2=v((shard, LANES), F32),
        normed=v((tokens, D), BF),
        mnormed=v((tokens, D), BF),
        qkv=v((tokens, 3 * wl), BF),
        d_qkv=v((tokens, 3 * wl), BF),
        att=v((tokens // LEN * (wl // LANES), 2 * LEN, LEN), F32),
        attended=v((tokens, wl), BF),
        d_att=v((tokens, wl), BF),
        act=v((tokens, fl), BF),
        slope=v((tokens, fl), F32),
        d_hidden=v((tokens, fl), BF),
        d_mid=v((tokens, D), BF),
        d_agg=v((tokens, D), BF),
        out_part=v((tokens, D), F32),
        out_low=v((tokens, D), BF),
        out_recv=v((ns, tokens, wl), BF),
        pix_src=v((ns, tokens, LANES), BF),
        pix_recv=v((ns, tokens, LANES), BF),
        small_src=v((nd, 16, rows), F32),
        small_recv=v((nd, 16, rows), F32),
        sec_small=v((ns, 16, rows), F32),
        basis_recv=v((ns, rows, CHUNK), BF),
        x_send=v((chunks, nz, rows, CHUNK), BF),
        x_recv=v((chunks, nz, rows, CHUNK), BF),
        keep=v((chunks, nz, rows, CHUNK), F32),
        z_send=v((chunks, nz, rows, CHUNK), BF),
        z_recv=v((chunks, nz, rows, CHUNK), BF),
        final=v((chunks + 2, rows, CHUNK), BF),
    )
    whole = v((nz, 2, rows, tokens), BF)
    shapes.update(gT=whole, contextT=whole, attendedT=whole, normedT=whole, mnormedT=whole)
    part = v((tokens, D), BF)
    shapes.update(rs1_part=part, rs2_part=part, rs3_part=part, rs4_part=part)
    part = v((ns, shard, D), BF)
    shapes.update(rs1_recv=part, rs2_recv=part, rs3_recv=part, rs4_recv=part)
    part = v((8, CHUNK), F32)
    shapes.update(q_src=part, s_src=part, key_src=part, dq_src=part)
    part = v((nd, 8, CHUNK), F32)
    shapes.update(q_recv=part, s_recv=part, key_recv=part, dq_recv=part)
    part = v((nd, blk, CHUNK), F32)
    shapes.update(bv_src=part, bv_recv=part, bv_all=part, m_src=part, m_recv=part, m_all=part)
    count = 9 * nd + 24 * ns + chunks * (1 + nz) + 6 * nz + 16 + 2 * zq + chunks * ns
    dma = pltpu.SemaphoreType.DMA
    shapes.update(send=dma((count,)), recv=dma((count,)), local=dma((32 + 2 * zq,)))
    return shapes


def fused(ns, nd, near, far):
    tokens = near["patches"].shape[0]
    rows = D // nd
    shapes = scratch(ns, nd, tokens)
    arrays = {**near, **far}
    hbm = pl.BlockSpec(memory_space=pl.ANY)
    vmem = pl.BlockSpec(memory_space=pltpu.VMEM)
    outs = dict(
        activations=((tokens, D // ns), BF, vmem),
        patches=((tokens, LANES), BF, vmem),
        basis=((rows, CHUNK), F32, vmem),
        d_query=((ns, 8, D // ns), F32, vmem),
        small=((16, rows), F32, vmem),
        mlp_up=((rows, FF), BF, hbm),
        mlp_down=((rows, FF), BF, hbm),
        attn_wqkv=((rows, 3 * D), BF, hbm),
        attn_wo=((rows, D), BF, hbm),
        agg_wo=((rows, D), BF, hbm),
        agg_wv=((rows, D), BF, hbm),
        agg_wk=((rows, D), BF, hbm),
    )

    def body(*refs):
        n_in, n_out = len(arrays), len(outs)
        kernel(
            ns,
            nd,
            SimpleNamespace(**dict(zip(arrays, refs[:n_in]))),
            SimpleNamespace(**dict(zip(outs, refs[n_in : n_in + n_out]))),
            SimpleNamespace(**dict(zip(shapes, refs[n_in + n_out :]))),
        )

    result = pl.pallas_call(
        body,
        out_shape=[jax.ShapeDtypeStruct(shape, kind) for shape, kind, _ in outs.values()],
        in_specs=[vmem] * len(near) + [hbm] * len(far),
        out_specs=[spec for _, _, spec in outs.values()],
        scratch_shapes=list(shapes.values()),
        compiler_params=pltpu.CompilerParams(
            collective_id=0, has_side_effects=True, vmem_limit_bytes=60 * 1024 * 1024
        ),
        name="block",
    )(*arrays.values())
    return SimpleNamespace(**dict(zip(outs, result)))


def on_device(
    ns,
    nd,
    patches,
    var_ids,
    segment_ids,
    embed_weight,
    var_embed,
    agg_query,
    agg_wq,
    agg_bq,
    agg_wk,
    agg_wv,
    agg_bv,
    agg_wo,
    agg_bo,
    attn_norm_gain,
    attn_norm_bias,
    attn_wqkv,
    attn_bq,
    attn_bv,
    attn_wo,
    attn_bo,
    mlp_norm_gain,
    mlp_norm_bias,
    mlp_up,
    mlp_bup,
    mlp_down,
    mlp_bdown,
    cotangent,
):
    near = dict(
        patches=patches,
        var_ids=var_ids,
        segment_ids=segment_ids,
        embed_weight=embed_weight,
        var_embed=var_embed,
        agg_query=agg_query,
        agg_bq=agg_bq,
        agg_bv=agg_bv,
        agg_bo=agg_bo,
        attn_norm_gain=attn_norm_gain,
        attn_norm_bias=attn_norm_bias,
        attn_bq=attn_bq,
        attn_bv=attn_bv,
        attn_bo=attn_bo,
        mlp_norm_gain=mlp_norm_gain,
        mlp_norm_bias=mlp_norm_bias,
        mlp_bup=mlp_bup,
        mlp_bdown=mlp_bdown,
    )
    far = dict(
        agg_wq=agg_wq,
        agg_wk=agg_wk,
        agg_wv=agg_wv,
        agg_wo=agg_wo,
        attn_wqkv=attn_wqkv,
        attn_wo=attn_wo,
        mlp_up=mlp_up,
        mlp_down=mlp_down,
        cotangent=cotangent,
    )
    near = {name: a.reshape(1, -1) if a.ndim == 1 else a for name, a in near.items()}
    got = fused(ns, nd, near, far)
    r = lax.axis_index("dp")
    rows = D // nd

    def mine(array, size):
        return lax.dynamic_slice_in_dim(array, r * size, size, 0)

    d_query = got.d_query[:, 0, :].reshape(D)
    query = mine(agg_query, rows).astype(BF).astype(F32)
    small = got.small
    return (
        got.activations,
        got.patches[:, : CP // ns],
        got.basis[:, :CP],
        got.basis[:, CP : CP + VARS].T,
        jnp.sum(agg_wq.astype(F32) * d_query, axis=1),
        query[:, None] * d_query,
        mine(d_query, rows),
        got.agg_wk.astype(F32),
        got.agg_wv.astype(F32),
        small[9],
        got.agg_wo.astype(F32),
        small[6],
        small[4],
        small[5],
        got.attn_wqkv.astype(F32),
        small[7],
        small[8],
        got.attn_wo.astype(F32),
        small[3],
        small[1],
        small[2],
        got.mlp_up.astype(F32),
        small[10 : 10 + FF // D].reshape(-1),
        got.mlp_down.astype(F32),
        small[0],
    )


def solution(mesh):
    in_specs = (
        P("dp", None),
        P(),
        P("dp", None),
        P("dp", None),
        P(),
        P(),
        P("dp", None),
        P(),
        P("dp", None),
        P("dp", None),
        P(),
        P("dp", None),
        P(),
        P(),
        P(),
        P("dp", None),
        P(),
        P(),
        P("dp", None),
        P(),
        P(),
        P(),
        P("dp", None),
        P(),
        P("dp", None),
        P(),
        P("dp", "section"),
    )
    out_specs = (
        P("dp", "section"),
        P("dp", "section"),
        P("dp", None),
        P(None, "dp"),
        P("dp"),
        P("dp", None),
        P("dp"),
        P("dp", None),
        P("dp", None),
        P("dp"),
        P("dp", None),
        P("dp"),
        P("dp"),
        P("dp"),
        P("dp", None),
        P("dp"),
        P("dp"),
        P("dp", None),
        P("dp"),
        P("dp"),
        P("dp"),
        P("dp", None),
        P("dp"),
        P("dp", None),
        P("dp"),
    )
    sizes = (mesh.shape["section"], mesh.shape["dp"])
    return jax.shard_map(
        partial(on_device, *sizes), mesh=mesh, in_specs=in_specs, out_specs=out_specs, check_vma=False
    )
```

```python
from functools import partial
from types import SimpleNamespace

import jax
import jax.numpy as jnp
from jax import lax
from jax.experimental import pallas as pl
from jax.experimental.pallas import tpu as pltpu
from jax.sharding import PartitionSpec as P

D = 1024
HEADS = 16
HEAD = 64
FF = 4096
VARS = 48
PIX = 4
LEN = 128

highest = lax.Precision.HIGHEST
blocked = -1000000000.0
epsilon = 1e-05
MESH = pl.DeviceIdType.MESH
BF = jnp.bfloat16
F32 = jnp.float32
CHUNK = 256
CP = VARS * PIX
LANES = 128


def nn(a, b):
    return jnp.dot(a, b, preferred_element_type=F32)


def nt(a, b):
    return lax.dot_general(a, b, (((1,), (1,)), ((), ())), preferred_element_type=F32)


def tn(a, b):
    return lax.dot_general(a, b, (((0,), (0,)), ((), ())), preferred_element_type=F32)


def split(x):
    high = x.astype(BF)
    return high, (x - high.astype(F32)).astype(BF)


def iota(shape, dim):
    return lax.broadcasted_iota(jnp.int32, shape, dim)


def colsum(x):
    return jnp.sum(x.astype(F32), axis=0, keepdims=True)


def each(low, high, body):
    if high - low <= 8:
        for k in range(low, high):
            body(k)
    else:

        def step(k, carry):
            body(k)
            return carry

        lax.fori_loop(low, high, step, 0)


class Transfer:
    def __init__(self, make, low, high):
        self.make, self.low, self.high = make, low, high

    def start(self):
        each(self.low, self.high, lambda k: self.make(k).start())
        return self

    def wait_recv(self):
        each(self.low, self.high, lambda k: self.make(k).wait_recv())

    def wait_send(self):
        each(self.low, self.high, lambda k: self.make(k).wait_send())


def kernel(ns, nd, refs_in, refs_out, sc):
    s = lax.axis_index("section")
    r = lax.axis_index("dp")
    nx = 2
    nz = nd // nx
    z, x = lax.div(r, nx), lax.rem(r, nx)
    i, o = refs_in, refs_out
    rows = D // nd
    tokens = i.patches.shape[1]
    shard = tokens // ns
    wl, fl, hl = D // ns, FF // ns, HEADS // ns
    zq = nz // ns
    own_cols = pl.ds(pl.multiple_of(s * wl, LANES), wl)
    own_ff = pl.ds(pl.multiple_of(s * fl, LANES), fl)
    own_rows = pl.ds(pl.multiple_of(s * shard, 16), shard)
    scale = HEAD ** (-0.5)
    send, recv = sc.send, sc.recv
    used = {"n": 0}
    pending = []

    def sems(count):
        base = used["n"]
        used["n"] += count
        return base

    def remote(src, dst, sem, device):
        return pltpu.make_async_remote_copy(
            src_ref=src,
            dst_ref=dst,
            send_sem=send.at[sem],
            recv_sem=recv.at[sem],
            device_id=device,
            device_id_type=MESH,
        )

    def over_section(src, dst):
        base = sems(ns)

        def make(k):
            t = lax.rem(s + k, ns)
            return remote(src(t), dst, base + k, (t, r))

        transfer = Transfer(make, 1, ns).start()
        pending.append(transfer)
        return transfer

    def over_dp(src, dst):
        base = sems(nd)

        def make(k):
            t = lax.rem(r + k, nd)
            return remote(src(t), dst, base + k, (s, t))

        transfer = Transfer(make, 1, nd).start()
        pending.append(transfer)
        return transfer

    def over_z(src, dst):
        base = sems(nz)

        def make(k):
            t = lax.rem(z + k, nz)
            return remote(src(t), dst, base + k, (s, t * nx + x))

        transfer = Transfer(make, 1, nz).start()
        pending.append(transfer)
        return transfer

    def over_x(src, dst):
        base = sems(1)
        transfer = Transfer(lambda k: remote(src, dst, base, (s, z * nx + 1 - x)), 0, 1).start()
        pending.append(transfer)
        return transfer

    local_used = {"n": 0}

    def local(src, dst):
        sem = local_used["n"]
        local_used["n"] += 1
        copy = pltpu.make_async_copy(src, dst, sc.local.at[sem])
        copy.start()
        return copy

    small_loads = [
        local(i.agg_wq.at[:, own_cols], sc.wq),
        local(i.agg_wk.at[:, own_cols], sc.wk),
        local(i.agg_wv.at[:, own_cols], sc.wv),
    ]
    sources = [(i.agg_wo, sc.awo_c, 0, s * wl)]
    sources += [(i.attn_wqkv, sc.qkv_w, j * wl, j * D + s * wl) for j in range(3)]
    sources += [(i.attn_wo, sc.two_c, 0, s * wl)]
    sources += [(i.mlp_up, sc.up_w, j * CHUNK, s * fl + j * CHUNK) for j in range(fl // CHUNK)]
    sources += [(i.mlp_down, sc.down_w, j * CHUNK, s * fl + j * CHUNK) for j in range(fl // CHUNK)]
    pieces = [(dst, pl.ds(at, CHUNK)) for _, dst, at, _ in sources]
    piece_loads = [
        local(src.at[:, pl.ds(pl.multiple_of(col, LANES), CHUNK)], dst.at[z, x, :, pl.ds(at, CHUNK)])
        for src, dst, at, col in sources
    ]
    n_pieces = len(pieces)
    from_z, from_x = {}, {}

    def issue_z(count):
        for c in range(len(from_z), min(len(from_z) + count, n_pieces)):
            dst, cols = pieces[c]
            block = dst.at[z, x, :, cols]
            from_z[c] = over_z(lambda t, block=block: block, block)

    def forward(count):
        for c in range(len(from_x), min(len(from_x) + count, n_pieces)):
            from_z[c].wait_recv()
            dst, cols = pieces[c]
            half = dst.at[:, x, :, cols]
            from_x[c] = over_x(half, half)
            issue_z(1)

    cot_load = local(i.cotangent, sc.g_full.at[:, own_cols])

    barrier = pltpu.get_barrier_semaphore()
    for k in range(1, ns):
        pl.semaphore_signal(barrier, inc=1, device_id=(lax.rem(s + k, ns), r), device_id_type=MESH)
    each(
        1,
        nd,
        lambda k: pl.semaphore_signal(
            barrier, inc=1, device_id=(s, lax.rem(r + k, nd)), device_id_type=MESH
        ),
    )

    chan = (iota((CP, VARS), 0) >> 2 == iota((CP, VARS), 1)).astype(F32).astype(BF)
    ids = jnp.broadcast_to(i.var_ids[...].astype(F32), (CHUNK, VARS)).astype(BF)
    ids = nt(chan, ids)
    lane = iota((CP, CHUNK), 1)
    row = iota((CP, CHUNK), 0)
    hit = ((lane >> 2).astype(F32) == ids) & ((lane & 3) == (row & 3)) & (lane < CP)
    place = hit.astype(F32).astype(BF)
    sc.place[...] = place
    lane = iota((tokens, CHUNK), 1)
    ones = ((lane >= CP) & (lane < CP + VARS)).astype(F32)
    sc.pix[...] = (tn(i.patches[...], place) + ones).astype(BF)
    row = iota((CHUNK, LANES), 0)
    lane = iota((CHUNK, LANES), 1)
    owner = jnp.where(row < CP, row >> 2, row - CP)
    sc.fold[...] = ((owner == lane) & (lane < VARS)).astype(F32).astype(BF)
    chosen = (iota((rows, D), 1) == iota((rows, D), 0) + r * rows).astype(F32).astype(BF)
    lane = iota((CP, CHUNK), 1)
    row = iota((CP, CHUNK), 0)
    widen = (lane == row).astype(F32).astype(BF)
    lane = iota((VARS, CHUNK), 1)
    row = iota((VARS, CHUNK), 0)
    widen_var = (lane == row + CP).astype(F32).astype(BF)
    var_rows = nt(chosen, i.var_embed[...].astype(BF)).astype(BF)
    sc.basis[...] = (tn(i.embed_weight[...], widen) + nn(var_rows, widen_var)).astype(BF)
    query = jnp.broadcast_to(i.agg_query[...].astype(BF).astype(F32), (16, D))
    query = jnp.where(iota((16, D), 0) == 0, query, 0.0).astype(BF)
    query_rows = nt(query, chosen).astype(BF)
    o.query_rows[...] = query_rows
    sc.vecs[...] = jnp.zeros_like(sc.vecs)
    sc.bup[...] = jnp.zeros_like(sc.bup)

    for copy in small_loads:
        copy.wait()
    sc.q_src[...] = nn(query_rows, sc.wq[...])[0:8]
    value_part = tn(sc.basis[...], sc.wv[...])
    blk = CHUNK // nd
    for t in range(nd):
        sc.bv_src[t] = value_part[t * blk : (t + 1) * blk]
    cot_load.wait()
    for copy in piece_loads:
        copy.wait()

    pl.semaphore_wait(barrier, ns - 1 + nd - 1)

    def weight(ref):
        return ref[...].reshape(ref.shape[0] * ref.shape[1] * ref.shape[2], ref.shape[3])

    def scatter(part, landed, value):
        part[...] = value.astype(BF)
        transfer = over_section(lambda t: part.at[pl.ds(pl.multiple_of(t * shard, 16), shard)], landed.at[s])
        landed[s] = part[own_rows, :]
        return transfer

    def gather(full, value):
        full[own_rows, :] = value.astype(BF)
        return over_section(lambda t: full.at[own_rows], full.at[own_rows])

    def landed_sum(landed):
        total = landed[0].astype(F32)
        for k in range(1, ns):
            total = total + landed[k].astype(F32)
        return total

    def normal(value):
        centred = value - jnp.mean(value, axis=-1, keepdims=True)
        rstd = lax.rsqrt(jnp.mean(centred * centred, axis=-1, keepdims=True) + epsilon)
        return centred * rstd, rstd

    def whole_norm(full, gain, bias, dst):
        for t in range(ns):
            at = slice(t * shard, (t + 1) * shard)
            hat, _ = normal(full[at, :].astype(F32))
            dst[at, :] = (hat * gain[...] + bias[...]).astype(BF)

    def kept_norm(full, kept, rstd_kept):
        hat, rstd = normal(full[own_rows, :].astype(F32))
        kept[...] = hat
        rstd_kept[...] = jnp.broadcast_to(rstd, rstd_kept.shape)

    def norm_back(grad, gain, kept, rstd_kept, gain_row, bias_row):
        hat = kept[...]
        sc.vecs[gain_row : gain_row + 1, :] = colsum(grad * hat)
        sc.vecs[bias_row : bias_row + 1, :] = colsum(grad)
        inner = grad * gain[...]
        mean = jnp.mean(inner, axis=-1, keepdims=True)
        dot = jnp.mean(inner * hat, axis=-1, keepdims=True)
        return rstd_kept[:, 0:1] * (inner - mean - hat * dot)

    def transposed(full, dst):
        for j in range(D // CHUNK):
            turned = full[:, j * CHUNK : (j + 1) * CHUNK].astype(F32).T.astype(BF)
            n = dst.shape[0] // (D // CHUNK)
            dst[j * n : (j + 1) * n] = turned.reshape((n,) + dst.shape[1:])

    def by_rows(cols, dst):
        at = pl.ds(s * zq, zq)
        dst[:, :, :, own_cols] = cols[at]
        return over_section(
            lambda t: cols.at[pl.ds(t * zq, zq)], dst.at[:, :, :, own_cols]
        )

    def columns(ref, j):
        return ref[:, :, :, j * CHUNK : (j + 1) * CHUNK].reshape(D, CHUNK)

    def push(src, dst):
        transfer = over_dp(lambda t: src, dst.at[r])
        dst[r] = src[...]
        return transfer

    def summed(dst, count):
        total = dst[0]
        for k in range(1, count):
            total = total + dst[k]
        return total

    q_push = push(sc.q_src, sc.q_recv)
    bv_rs = over_dp(lambda t: sc.bv_src.at[t], sc.bv_recv.at[r])
    sc.bv_recv[r] = sc.bv_src[r]
    g_gather = over_section(lambda t: sc.g_full.at[:, own_cols], sc.g_full.at[:, own_cols])

    q_push.wait_recv()
    query_proj = summed(sc.q_recv, nd)[0:1] + i.agg_bq[:, own_cols]
    sc.query_proj[...] = query_proj
    head_rows = (iota((16, wl), 1) >> 6 == iota((16, wl), 0)).astype(F32)
    high, low = split(head_rows * (query_proj * scale))
    key_query = (nt(high, sc.wk[...]) + nt(low, sc.wk[...])).astype(BF)
    sc.key_query[...] = key_query
    sc.s_src[...] = nn(key_query, sc.basis[...])[0:8]
    s_push = push(sc.s_src, sc.s_recv)
    bv_rs.wait_recv()
    sc.bv_own[...] = summed(sc.bv_recv, nd)
    bv_ag = push(sc.bv_own, sc.bv_all)
    issue_z(2)

    s_push.wait_recv()
    score_rows = summed(sc.s_recv, nd)
    sc.score_rows[...] = score_rows
    fold = sc.fold[...]
    lane_ok = iota((tokens, LANES), 1) < VARS
    for h in range(hl):
        pix = sc.pix[...].astype(F32)
        high, low = split(pix * score_rows[h : h + 1])
        scores = nn(high, fold) + nn(low, fold)
        scores = jnp.where(lane_ok, scores, -1e30)
        scores = jnp.exp(scores - jnp.max(scores, axis=-1, keepdims=True))
        probs = scores / jnp.sum(scores, axis=-1, keepdims=True)
        sc.probs[h] = probs
        wrep = nt(probs.astype(BF), fold)
        sc.wrep[h] = wrep.astype(BF)
        sc.mixed[h] = (wrep * pix).astype(BF)
    bv_ag.wait_recv()
    for t in range(nd):
        sc.bv[t * blk : (t + 1) * blk] = sc.bv_all[t]
    value_basis = sc.bv[...].astype(BF)
    head_of = iota((1, wl), 1) >> 6
    context = jnp.broadcast_to(i.agg_bv[:, own_cols], (tokens, wl))
    for h in range(hl):
        context = context + jnp.where(head_of == h, nn(sc.mixed[h], value_basis), 0.0)
    sc.context_full[:, own_cols] = context.astype(BF)
    context_gather = over_section(lambda t: sc.context_full.at[:, own_cols], sc.context_full.at[:, own_cols])
    issue_z(1)
    forward(1)
    g_gather.wait_recv()
    transposed(sc.g_full, sc.gT)
    context_gather.wait_recv()
    forward(1)
    from_x[0].wait_recv()
    part = nn(sc.context_full[...], weight(sc.awo_c)) + i.agg_bo[:, own_cols]
    sc.agg_full[:, own_cols] = part.astype(BF)
    agg_gather = over_section(lambda t: sc.agg_full.at[:, own_cols], sc.agg_full.at[:, own_cols])
    transposed(sc.context_full, sc.contextT)
    forward(1)
    agg_gather.wait_recv()
    whole_norm(sc.agg_full, i.attn_norm_gain, i.attn_norm_bias, sc.normed)
    kept_norm(sc.agg_full, sc.hat1, sc.rstd1)
    transposed(sc.normed, sc.normedT)
    forward(1)
    normed = sc.normed[...]
    for j in range(3):
        from_x[1 + j].wait_recv()
        part = nn(normed, columns(sc.qkv_w, j))
        if j == 0:
            part = part + i.attn_bq[:, own_cols]
        if j == 2:
            part = part + i.attn_bv[:, own_cols]
        sc.qkv[:, j * wl : (j + 1) * wl] = part.astype(BF)
    lo = (iota((1, LANES), 1) < HEAD).astype(F32)
    first, second = lo.astype(BF), (1.0 - lo).astype(BF)

    def pair(a):
        return jnp.concatenate([a * first, a * second], axis=0)

    def pick(a):
        return jnp.where(iota((LEN, LANES), 1) < HEAD, a[0:LEN], a[LEN:])

    tiles = [(b, p) for b in range(tokens // LEN) for p in range(wl // LANES)]

    def tile(ref, b, p, j=0):
        return ref[b * LEN : (b + 1) * LEN, j * wl + p * LANES : j * wl + (p + 1) * LANES]

    for n, (b, p) in enumerate(tiles):
        q, k, v = [tile(sc.qkv, b, p, j) for j in range(3)]
        ids = jnp.broadcast_to(i.segment_ids[b : b + 1, :].astype(F32), (LEN, LEN))
        same = ids == ids.T
        scores = nt(pair(q), k) * scale
        scores = jnp.where(jnp.concatenate([same, same], axis=0), scores, blocked)
        scores = jnp.exp(scores - jnp.max(scores, axis=-1, keepdims=True))
        probs = scores / jnp.sum(scores, axis=-1, keepdims=True)
        sc.att[n] = probs
        sc.attended[b * LEN : (b + 1) * LEN, p * LANES : (p + 1) * LANES] = pick(
            nn(probs.astype(BF), v)
        ).astype(BF)
    sc.attended_full[:, own_cols] = sc.attended[...]
    attended_gather = over_section(
        lambda t: sc.attended_full.at[:, own_cols], sc.attended_full.at[:, own_cols]
    )
    forward(1)
    attended_gather.wait_recv()
    forward(1)
    from_x[4].wait_recv()
    part = nn(sc.attended_full[...], weight(sc.two_c)) + i.attn_bo[:, own_cols]
    sc.mid_full[:, own_cols] = (part + sc.agg_full[:, own_cols].astype(F32)).astype(BF)
    mid_gather = over_section(lambda t: sc.mid_full.at[:, own_cols], sc.mid_full.at[:, own_cols])
    transposed(sc.attended_full, sc.attendedT)
    forward(1)
    mid_gather.wait_recv()
    awo_rows = by_rows(sc.awo_c, sc.awo)
    two_rows = by_rows(sc.two_c, sc.two)
    whole_norm(sc.mid_full, i.mlp_norm_gain, i.mlp_norm_bias, sc.mnormed)
    kept_norm(sc.mid_full, sc.hat2, sc.rstd2)
    transposed(sc.mnormed, sc.mnormedT)
    forward(2)
    mnormed = sc.mnormed[...]
    for j in range(fl // CHUNK):
        at = slice(j * CHUNK, (j + 1) * CHUNK)
        bias = i.mlp_bup[:, pl.ds(pl.multiple_of(s * fl + j * CHUNK, LANES), CHUNK)]
        from_x[5 + j].wait_recv()
        hidden = nn(mnormed, columns(sc.up_w, j)) + bias
        phi = 0.5 + 0.5 * lax.erf(hidden * 0.7071067811865476)
        density = jnp.exp(hidden * hidden * -0.5) * 0.3989422804014327
        sc.act[:, at] = (hidden * phi).astype(BF)
        sc.slope[:, at] = phi + hidden * density
        if j == 0:
            forward(1)
        if j == 2:
            forward(1)
    forward(2)
    names = (
        [(o.mlp_down, s * fl + j * CHUNK) for j in range(fl // CHUNK)]
        + [(o.mlp_up, s * fl + j * CHUNK) for j in range(fl // CHUNK)]
        + [(o.attn_wo, s * wl)]
        + [(o.attn_wqkv, j * D + s * wl) for j in range(3)]
        + [(o.agg_wo, s * wl)]
    )
    to_x, to_z, made, done = {}, {}, [], []
    out_copies, out_sends = [], []

    def produce(c, left, right):
        def half(side):
            block = left[:, pl.ds(side, 1)].reshape(nz * rows, tokens)
            return nn(block, right).reshape(nz, rows, CHUNK)

        sc.x_send[c] = half(1 - x).astype(BF)
        made.append(c)
        sc.keep[c] = half(x)

    def issue_x(count):
        for c in made[len(to_x) : len(to_x) + count]:
            to_x[c] = over_x(sc.x_send.at[c], sc.x_recv.at[c])

    def middle(c):
        to_x[c].wait_recv()
        issue_x(1)
        sc.z_send[c] = (sc.keep[c] + sc.x_recv[c].astype(F32)).astype(BF)
        to_z[c] = over_z(lambda t: sc.z_send.at[c, t], sc.z_recv.at[c, z])
        sc.z_recv[c, z] = sc.z_send[c, z]

    def publish(c, array, start):
        dst = array.at[:, pl.ds(pl.multiple_of(start, LANES), CHUNK)]
        out_sends.append(over_section(lambda t: sc.final.at[c], dst))
        out_copies.append(local(sc.final.at[c], dst))

    def finish(c):
        to_z[c].wait_recv()
        total = sc.z_recv[c, 0].astype(F32)
        for k in range(1, nz):
            total = total + sc.z_recv[c, k].astype(F32)
        sc.final[c] = total.astype(BF)
        publish(c, *names[c])

    def pump(count):
        for _ in range(count):
            c = len(to_z)
            if c < len(names):
                middle(c)
            if len(done) < len(names) and (c == len(names) or len(done) < c - 1):
                finish(len(done))
                done.append(c)

    for j in range(fl // CHUNK):
        produce(j, sc.gT, sc.act[:, j * CHUNK : (j + 1) * CHUNK])
    issue_x(3)
    g_full = sc.g_full[...]
    nmlp = fl // CHUNK
    for j in range(fl // CHUNK):
        at = slice(j * CHUNK, (j + 1) * CHUNK)
        from_x[5 + nmlp + j].wait_recv()
        d_hidden = nn(g_full, columns(sc.down_w, j)) * sc.slope[:, at]
        sc.d_hidden[:, at] = d_hidden.astype(BF)
    up_w = weight(sc.up_w)
    rs3 = scatter(sc.rs3_part, sc.rs3_recv, nt(sc.d_hidden[...], up_w))
    for j in range(nmlp):
        at = slice(j * CHUNK, (j + 1) * CHUNK)
        produce(nmlp + j, sc.mnormedT, sc.d_hidden[:, at])
    sc.bup[:, own_ff] = colsum(sc.d_hidden[...])
    rs3.wait_recv()
    g_shard = sc.g_full[own_rows, :].astype(F32)
    sc.vecs[0:1, :] = colsum(g_shard)
    d_mid = norm_back(landed_sum(sc.rs3_recv), i.mlp_norm_gain, sc.hat2, sc.rstd2, 1, 2)
    d_mid = (g_shard + d_mid).astype(BF)
    sc.vecs[3:4, :] = colsum(d_mid)
    ag3 = gather(sc.d_mid, d_mid)
    d_mid = d_mid.astype(F32)
    sc.out_part[...] = nt(sc.act[...], weight(sc.down_w))
    sc.out_part[own_rows, :] = sc.out_part[own_rows, :] + sc.mid_full[own_rows, :].astype(F32) + i.mlp_bdown[...]
    sc.out_low[...] = sc.out_part[...].astype(BF)
    out_rs = over_section(
        lambda t: sc.out_low.at[:, pl.ds(pl.multiple_of(t * wl, LANES), wl)], sc.out_recv.at[s]
    )
    sc.out_recv[s] = sc.out_low[:, own_cols]
    pump(1)
    ag3.wait_recv()

    two_rows.wait_recv()
    d_att = nt(sc.d_mid[...], weight(sc.two)).astype(BF)
    sc.d_att[...] = d_att
    for n, (b, p) in enumerate(tiles):
        q, k, v = [tile(sc.qkv, b, p, j) for j in range(3)]
        q, d_out = pair(q), pair(tile(sc.d_att, b, p))
        probs = sc.att[n]
        d_probs = nt(d_out, v)
        d_scores = probs * (d_probs - jnp.sum(probs * d_probs, axis=-1, keepdims=True))
        d_scores = d_scores.astype(BF)
        parts = (pick(nn(d_scores, k)) * scale, tn(d_scores, q) * scale, tn(probs.astype(BF), d_out))
        for j in range(3):
            lanes = slice(j * wl + p * LANES, j * wl + (p + 1) * LANES)
            sc.d_qkv[b * LEN : (b + 1) * LEN, lanes] = parts[j].astype(BF)
    rs4 = scatter(sc.rs4_part, sc.rs4_recv, nt(sc.d_qkv[...], weight(sc.qkv_w)))
    produce(2 * nmlp, sc.attendedT, sc.d_mid[:, own_cols])
    for j in range(3):
        produce(2 * nmlp + 1 + j, sc.normedT, sc.d_qkv[:, j * wl : (j + 1) * wl])
    sc.vecs[7:8, own_cols] = colsum(sc.d_qkv[:, 0:wl])
    sc.vecs[8:9, own_cols] = colsum(sc.d_qkv[:, 2 * wl : 3 * wl])
    pump(1)
    rs4.wait_recv()
    d_agg = norm_back(landed_sum(sc.rs4_recv), i.attn_norm_gain, sc.hat1, sc.rstd1, 4, 5)
    d_agg = (sc.d_mid[own_rows, :].astype(F32) + d_agg).astype(BF)
    sc.vecs[6:7, :] = colsum(d_agg)
    ag4 = gather(sc.d_agg, d_agg)
    pump(1)
    ag4.wait_recv()

    awo_rows.wait_recv()
    produce(2 * nmlp + 4, sc.contextT, sc.d_agg[:, own_cols])
    d_context = nt(sc.d_agg[...], weight(sc.awo)).astype(BF)
    sc.vecs[9:10, own_cols] = colsum(d_context)
    value_basis = sc.bv[...].astype(BF)
    cross = jnp.zeros((CHUNK, wl), F32)
    grad_pix = jnp.zeros((tokens, CHUNK), F32)
    sc.key_src[...] = jnp.zeros_like(sc.key_src)
    for h in range(hl):
        masked = d_context * (head_of == h).astype(F32).astype(BF)
        pulled = nt(masked, value_basis)
        cross = cross + tn(sc.mixed[h], masked)
        pix = sc.pix[...].astype(F32)
        high, low = split(pulled * pix)
        d_weights = nn(high, fold) + nn(low, fold)
        probs = sc.probs[h]
        d_scores = probs * (d_weights - jnp.sum(probs * d_weights, axis=-1, keepdims=True))
        srep = nt(d_scores.astype(BF), fold)
        sc.key_src[h : h + 1, :] = colsum(srep * pix)
        grad_pix = grad_pix + sc.wrep[h].astype(F32) * pulled
        grad_pix = grad_pix + srep * sc.score_rows[h : h + 1, :]
    key_push = push(sc.key_src, sc.key_recv)
    for t in range(nd):
        sc.m_src[t] = cross[t * blk : (t + 1) * blk]
    m_rs = over_dp(lambda t: sc.m_src.at[t], sc.m_recv.at[r])
    sc.m_recv[r] = sc.m_src[r]
    grad_pix = grad_pix.astype(BF)
    pw = CP // ns
    for t in range(ns):
        sc.pix_src[t] = nt(sc.place[t * pw : (t + 1) * pw, :], grad_pix).astype(BF)
    pix_rs = over_section(lambda t: sc.pix_src.at[t], sc.pix_recv.at[s])
    sc.pix_recv[s] = sc.pix_src[s]
    for t in range(nd):
        sc.small_src[t, 0:10] = sc.vecs[0:10, t * rows : (t + 1) * rows]
        for j in range(FF // D):
            start = (t * (FF // D) + j) * rows
            sc.small_src[t, 10 + j : 11 + j] = sc.bup[:, start : start + rows]
    small_rs = over_dp(lambda t: sc.small_src.at[t], sc.small_recv.at[r])
    sc.small_recv[r] = sc.small_src[r]

    pump(2)
    m_rs.wait_recv()
    sc.m_own[...] = summed(sc.m_recv, nd)
    m_ag = push(sc.m_own, sc.m_all)
    key_push.wait_recv()
    key_terms = summed(sc.key_recv, nd)
    wide = jnp.concatenate([jnp.broadcast_to(key_terms[h : h + 1], (HEAD, CHUNK)) for h in range(hl)], axis=0)
    d_key = nt(sc.basis[...], wide.astype(BF))
    d_query = jnp.sum(sc.wk[...].astype(F32) * d_key, axis=0, keepdims=True) * scale
    sc.dq_src[...] = jnp.broadcast_to(d_query, sc.dq_src.shape)
    dq_push = push(sc.dq_src, sc.dq_recv)
    count = len(names)
    sc.final[count] = (d_key * (sc.query_proj[...] * scale)).astype(BF)
    publish(count, o.agg_wk, s * wl)
    pump(2)
    small_rs.wait_recv()
    sc.sec_small[s] = summed(sc.small_recv, nd)
    small_ag = over_section(lambda t: sc.sec_small.at[s], sc.sec_small.at[s])
    pump(1)
    m_ag.wait_recv()
    for t in range(nd):
        sc.cross[t * blk : (t + 1) * blk] = sc.m_all[t]
    cross = sc.cross[...].astype(BF)
    sc.final[count + 1] = nn(sc.basis[...], cross).astype(BF)
    publish(count + 1, o.agg_wv, s * wl)
    key_low = jnp.concatenate([key_terms, jnp.zeros_like(key_terms)], axis=0).astype(BF)
    grad_basis = nt(cross, sc.wv[...]) + tn(key_low, sc.key_query[...])
    sc.basis_recv[s] = grad_basis.astype(BF)
    basis_sum = over_section(lambda t: sc.basis_recv.at[s], sc.basis_recv.at[s])
    pump(1)
    dq_push.wait_recv()
    o.d_query[s] = summed(sc.dq_recv, nd)
    dq_gather = over_section(lambda t: o.d_query.at[s], o.d_query.at[s])

    def section_total(ref):
        total = ref[0].astype(F32)
        for k in range(1, ns):
            total = total + ref[k].astype(F32)
        return total

    out_rs.wait_recv()
    o.activations[...] = section_total(sc.out_recv).astype(BF)
    pix_rs.wait_recv()
    o.patches[...] = section_total(sc.pix_recv).astype(BF)
    small_ag.wait_recv()
    o.small[...] = summed(sc.sec_small, ns)
    pump(20)
    basis_sum.wait_recv()
    o.basis[...] = section_total(sc.basis_recv)
    dq_gather.wait_recv()
    for transfer in out_sends:
        transfer.wait_recv()
    for copy in out_copies:
        copy.wait()
    for transfer in pending:
        transfer.wait_send()
    assert used["n"] <= send.shape[0], used["n"]
    assert local_used["n"] <= sc.local.shape[0]


def scratch(ns, nd, tokens):
    nz, rows = nd // 2, D // nd
    wl, fl, hl = D // ns, FF // ns, HEADS // ns
    shard, zq, blk = tokens // ns, nz // ns, CHUNK // nd
    chunks = 2 * (fl // CHUNK) + 5
    v = pltpu.VMEM
    shapes = dict(
        wq=v((rows, wl), BF),
        wk=v((rows, wl), BF),
        wv=v((rows, wl), BF),
        qkv_w=v((nz, 2, rows, 3 * wl), BF),
        up_w=v((nz, 2, rows, fl), BF),
        down_w=v((nz, 2, rows, fl), BF),
        awo_c=v((nz, 2, rows, wl), BF),
        two_c=v((nz, 2, rows, wl), BF),
        awo=v((zq, 2, rows, D), BF),
        two=v((zq, 2, rows, D), BF),
        g_full=v((tokens, D), BF),
        place=v((CP, CHUNK), BF),
        pix=v((tokens, CHUNK), BF),
        fold=v((CHUNK, LANES), BF),
        basis=v((rows, CHUNK), BF),
        vecs=v((16, D), F32),
        bup=v((1, FF), F32),
        query_proj=v((1, wl), F32),
        key_query=v((16, rows), BF),
        score_rows=v((8, CHUNK), F32),
        bv_own=v((blk, CHUNK), F32),
        m_own=v((blk, CHUNK), F32),
        bv=v((CHUNK, CHUNK), F32),
        cross=v((CHUNK, CHUNK), F32),
        probs=v((hl, tokens, LANES), F32),
        wrep=v((hl, tokens, CHUNK), BF),
        mixed=v((hl, tokens, CHUNK), BF),
        context_full=v((tokens, D), BF),
        attended_full=v((tokens, D), BF),
        agg_full=v((tokens, D), BF),
        mid_full=v((tokens, D), BF),
        hat1=v((shard, D), F32),
        hat2=v((shard, D), F32),
        rstd1=v((shard, LANES), F32),
        rstd2=v((shard, LANES), F32),
        normed=v((tokens, D), BF),
        mnormed=v((tokens, D), BF),
        qkv=v((tokens, 3 * wl), BF),
        d_qkv=v((tokens, 3 * wl), BF),
        att=v((tokens // LEN * (wl // LANES), 2 * LEN, LEN), F32),
        attended=v((tokens, wl), BF),
        d_att=v((tokens, wl), BF),
        act=v((tokens, fl), BF),
        slope=v((tokens, fl), F32),
        d_hidden=v((tokens, fl), BF),
        d_mid=v((tokens, D), BF),
        d_agg=v((tokens, D), BF),
        out_part=v((tokens, D), F32),
        out_low=v((tokens, D), BF),
        out_recv=v((ns, tokens, wl), BF),
        pix_src=v((ns, CP // ns, tokens), BF),
        pix_recv=v((ns, CP // ns, tokens), BF),
        small_src=v((nd, 16, rows), F32),
        small_recv=v((nd, 16, rows), F32),
        sec_small=v((ns, 16, rows), F32),
        basis_recv=v((ns, CHUNK, rows), BF),
        x_send=v((chunks, nz, rows, CHUNK), BF),
        x_recv=v((chunks, nz, rows, CHUNK), BF),
        keep=v((chunks, nz, rows, CHUNK), F32),
        z_send=v((chunks, nz, rows, CHUNK), BF),
        z_recv=v((chunks, nz, rows, CHUNK), BF),
        final=v((chunks + 2, rows, CHUNK), BF),
    )
    whole = v((nz, 2, rows, tokens), BF)
    shapes.update(gT=whole, contextT=whole, attendedT=whole, normedT=whole, mnormedT=whole)
    part = v((tokens, D), BF)
    shapes.update(rs3_part=part, rs4_part=part)
    part = v((ns, shard, D), BF)
    shapes.update(rs3_recv=part, rs4_recv=part)
    part = v((8, CHUNK), F32)
    shapes.update(q_src=part, s_src=part, key_src=part, dq_src=part)
    part = v((nd, 8, CHUNK), F32)
    shapes.update(q_recv=part, s_recv=part, key_recv=part, dq_recv=part)
    part = v((nd, blk, CHUNK), F32)
    shapes.update(bv_src=part, bv_recv=part, bv_all=part, m_src=part, m_recv=part, m_all=part)
    count = 9 * nd + 24 * ns + 2 * chunks * (1 + nz) + chunks * ns
    dma = pltpu.SemaphoreType.DMA
    shapes.update(send=dma((count,)), recv=dma((count,)), local=dma((8 + 2 * chunks + 4,)))
    return shapes


def fused(ns, nd, near, far):
    tokens = near["patches"].shape[1]
    rows = D // nd
    shapes = scratch(ns, nd, tokens)
    arrays = {**near, **far}
    hbm = pl.BlockSpec(memory_space=pl.ANY)
    vmem = pl.BlockSpec(memory_space=pltpu.VMEM)
    outs = dict(
        activations=((tokens, D // ns), BF, vmem),
        patches=((CP // ns, tokens), BF, vmem),
        basis=((CHUNK, rows), F32, vmem),
        query_rows=((16, rows), BF, vmem),
        d_query=((ns, 8, D // ns), F32, vmem),
        small=((16, rows), F32, vmem),
        mlp_up=((rows, FF), BF, hbm),
        mlp_down=((rows, FF), BF, hbm),
        attn_wqkv=((rows, 3 * D), BF, hbm),
        attn_wo=((rows, D), BF, hbm),
        agg_wo=((rows, D), BF, hbm),
        agg_wv=((rows, D), BF, hbm),
        agg_wk=((rows, D), BF, hbm),
    )

    def body(*refs):
        n_in, n_out = len(arrays), len(outs)
        kernel(
            ns,
            nd,
            SimpleNamespace(**dict(zip(arrays, refs[:n_in]))),
            SimpleNamespace(**dict(zip(outs, refs[n_in : n_in + n_out]))),
            SimpleNamespace(**dict(zip(shapes, refs[n_in + n_out :]))),
        )

    result = pl.pallas_call(
        body,
        out_shape=[jax.ShapeDtypeStruct(shape, kind) for shape, kind, _ in outs.values()],
        in_specs=[vmem] * len(near) + [hbm] * len(far),
        out_specs=[spec for _, _, spec in outs.values()],
        scratch_shapes=list(shapes.values()),
        compiler_params=pltpu.CompilerParams(
            collective_id=0, has_side_effects=True, vmem_limit_bytes=60 * 1024 * 1024
        ),
        name="block",
    )(*arrays.values())
    return SimpleNamespace(**dict(zip(outs, result)))


def widen(nd, got, agg_wq):
    rows = D // nd
    step = min(rows, 32)
    big = dict(
        mlp_up=got.mlp_up,
        mlp_down=got.mlp_down,
        attn_wqkv=got.attn_wqkv,
        attn_wo=got.attn_wo,
        agg_wo=got.agg_wo,
        agg_wv=got.agg_wv,
        agg_wk=got.agg_wk,
    )
    rest = dict(
        activations=got.activations,
        patches=got.patches,
        basis=got.basis,
        query_rows=got.query_rows,
        d_query=got.d_query,
        small=got.small,
        agg_wq=agg_wq,
    )
    line = (1, rows)
    outs = dict(
        activations=(got.activations.shape, BF),
        patches=(got.patches.shape, BF),
        embed=((CP, rows), F32),
        var=((VARS, rows), F32),
        query=(line, F32),
        wq=((rows, D), F32),
        bq=(line, F32),
        bup=((1, rows * (FF // D)), F32),
    )
    lines = tuple(range(10))

    def body(*refs):
        n = len(big)
        for src, dst in zip(refs[:n], refs[n + len(rest) : 2 * n + len(rest)]):
            dst[...] = src[...].astype(F32)
        i = SimpleNamespace(**dict(zip(rest, refs[n : n + len(rest)])))
        left = refs[2 * n + len(rest) :]
        o = SimpleNamespace(**dict(zip(outs, left)))
        left = left[len(outs) :]
        r = lax.axis_index("dp")

        @pl.when(pl.program_id(0) == 0)
        def _():
            o.activations[...] = i.activations[...]
            o.patches[...] = i.patches[...]
            o.embed[...] = i.basis[0:CP]
            o.var[...] = i.basis[CP : CP + VARS]
            d_query = jnp.concatenate([i.d_query[k] for k in range(i.d_query.shape[0])], axis=1)
            d_query = jnp.concatenate([d_query, d_query], axis=0)
            d_query = jnp.where(iota(d_query.shape, 0) == 0, d_query, 0.0)
            high, low = split(d_query)
            low, rest_low = split(d_query - high.astype(F32))
            chosen = (iota((rows, D), 1) == iota((rows, D), 0) + r * rows).astype(F32).astype(BF)
            o.bq[...] = (nt(high, chosen) + nt(low, chosen) + nt(rest_low, chosen))[0:1]
            weight = i.agg_wq[...]
            o.query[...] = (nt(high, weight) + nt(low, weight) + nt(rest_low, weight))[0:1]
            first = i.query_rows[...]
            o.wq[...] = tn(first, high) + tn(first, low) + tn(first, rest_low)
            o.bup[...] = jnp.concatenate([i.small[10 + k : 11 + k] for k in range(FF // D)], axis=1)
            for k in lines:
                left[k][...] = i.small[k : k + 1]

    def by_step(a):
        return pl.BlockSpec((step, a.shape[1]), lambda g: (g, 0))

    def fixed(shape):
        return pl.BlockSpec(shape, lambda g: (0,) * len(shape))

    shaped = [jax.ShapeDtypeStruct(a.shape, F32) for a in big.values()]
    shaped += [jax.ShapeDtypeStruct(*a) for a in outs.values()]
    shaped += [jax.ShapeDtypeStruct(line, F32) for _ in lines]
    result = pl.pallas_call(
        body,
        grid=(rows // step,),
        out_shape=shaped,
        in_specs=[by_step(a) for a in big.values()] + [fixed(a.shape) for a in rest.values()],
        out_specs=[by_step(a) for a in big.values()] + [fixed(a.shape) for a in shaped[len(big) :]],
        compiler_params=pltpu.CompilerParams(vmem_limit_bytes=48 * 1024 * 1024),
        name="widen",
    )(*big.values(), *rest.values())
    names = list(big) + list(outs)
    return SimpleNamespace(**dict(zip(names, result))), [a.reshape(-1) for a in result[len(names) :]]


def on_device(
    ns,
    nd,
    patches,
    var_ids,
    segment_ids,
    embed_weight,
    var_embed,
    agg_query,
    agg_wq,
    agg_bq,
    agg_wk,
    agg_wv,
    agg_bv,
    agg_wo,
    agg_bo,
    attn_norm_gain,
    attn_norm_bias,
    attn_wqkv,
    attn_bq,
    attn_bv,
    attn_wo,
    attn_bo,
    mlp_norm_gain,
    mlp_norm_bias,
    mlp_up,
    mlp_bup,
    mlp_down,
    mlp_bdown,
    cotangent,
):
    near = dict(
        patches=patches,
        var_ids=var_ids,
        segment_ids=segment_ids,
        embed_weight=embed_weight,
        var_embed=var_embed,
        agg_query=agg_query,
        agg_bq=agg_bq,
        agg_bv=agg_bv,
        agg_bo=agg_bo,
        attn_norm_gain=attn_norm_gain,
        attn_norm_bias=attn_norm_bias,
        attn_bq=attn_bq,
        attn_bv=attn_bv,
        attn_bo=attn_bo,
        mlp_norm_gain=mlp_norm_gain,
        mlp_norm_bias=mlp_norm_bias,
        mlp_bup=mlp_bup,
        mlp_bdown=mlp_bdown,
    )
    far = dict(
        agg_wq=agg_wq,
        agg_wk=agg_wk,
        agg_wv=agg_wv,
        agg_wo=agg_wo,
        attn_wqkv=attn_wqkv,
        attn_wo=attn_wo,
        mlp_up=mlp_up,
        mlp_down=mlp_down,
        cotangent=cotangent,
    )
    near = {name: a.reshape(1, -1) if a.ndim == 1 else a for name, a in near.items()}
    near["patches"], near["embed_weight"] = patches.T, embed_weight.T
    got = fused(ns, nd, near, far)
    out, small = widen(nd, got, agg_wq)
    return (
        out.activations,
        out.patches.T,
        out.embed.T,
        out.var,
        out.query.reshape(-1),
        out.wq,
        out.bq.reshape(-1),
        out.agg_wk,
        out.agg_wv,
        small[9],
        out.agg_wo,
        small[6],
        small[4],
        small[5],
        out.attn_wqkv,
        small[7],
        small[8],
        out.attn_wo,
        small[3],
        small[1],
        small[2],
        out.mlp_up,
        out.bup.reshape(-1),
        out.mlp_down,
        small[0],
    )


def solution(mesh):
    in_specs = (
        P("dp", None),
        P(),
        P("dp", None),
        P("dp", None),
        P(),
        P(),
        P("dp", None),
        P(),
        P("dp", None),
        P("dp", None),
        P(),
        P("dp", None),
        P(),
        P(),
        P(),
        P("dp", None),
        P(),
        P(),
        P("dp", None),
        P(),
        P(),
        P(),
        P("dp", None),
        P(),
        P("dp", None),
        P(),
        P("dp", "section"),
    )
    out_specs = (
        P("dp", "section"),
        P("dp", "section"),
        P("dp", None),
        P(None, "dp"),
        P("dp"),
        P("dp", None),
        P("dp"),
        P("dp", None),
        P("dp", None),
        P("dp"),
        P("dp", None),
        P("dp"),
        P("dp"),
        P("dp"),
        P("dp", None),
        P("dp"),
        P("dp"),
        P("dp", None),
        P("dp"),
        P("dp"),
        P("dp"),
        P("dp", None),
        P("dp"),
        P("dp", None),
        P("dp"),
    )
    sizes = (mesh.shape["section"], mesh.shape["dp"])
    return jax.shard_map(
        partial(on_device, *sizes), mesh=mesh, in_specs=in_specs, out_specs=out_specs, check_vma=False
    )
```

```python
from functools import partial
from types import SimpleNamespace

import jax
import jax.numpy as jnp
from jax import lax
from jax.experimental import pallas as pl
from jax.experimental.pallas import tpu as pltpu
from jax.sharding import PartitionSpec as P

D = 1024
HEADS = 16
HEAD = 64
FF = 4096
VARS = 48
PIX = 4
LEN = 128

highest = lax.Precision.HIGHEST
blocked = -1000000000.0
epsilon = 1e-05
MESH = pl.DeviceIdType.MESH
BF = jnp.bfloat16
F32 = jnp.float32
CHUNK = 256
CP = VARS * PIX
LANES = 128


def nn(a, b):
    return jnp.dot(a, b, preferred_element_type=F32)


def nt(a, b):
    return lax.dot_general(a, b, (((1,), (1,)), ((), ())), preferred_element_type=F32)


def tn(a, b):
    return lax.dot_general(a, b, (((0,), (0,)), ((), ())), preferred_element_type=F32)


def split(x):
    high = x.astype(BF)
    return high, (x - high.astype(F32)).astype(BF)


def iota(shape, dim):
    return lax.broadcasted_iota(jnp.int32, shape, dim)


def colsum(x):
    return jnp.sum(x.astype(F32), axis=0, keepdims=True)


def each(low, high, body):
    if high - low <= 8:
        for k in range(low, high):
            body(k)
    else:

        def step(k, carry):
            body(k)
            return carry

        lax.fori_loop(low, high, step, 0)


class Transfer:
    def __init__(self, make, low, high):
        self.make, self.low, self.high = make, low, high

    def start(self):
        each(self.low, self.high, lambda k: self.make(k).start())
        return self

    def wait_recv(self):
        each(self.low, self.high, lambda k: self.make(k).wait_recv())

    def wait_send(self):
        each(self.low, self.high, lambda k: self.make(k).wait_send())


def kernel(ns, nd, refs_in, refs_out, sc):
    s = lax.axis_index("section")
    r = lax.axis_index("dp")
    nx = 2
    nz = nd // nx
    z, x = lax.div(r, nx), lax.rem(r, nx)
    i, o = refs_in, refs_out
    rows = D // nd
    tokens = i.patches.shape[1]
    shard = tokens // ns
    wl, fl, hl = D // ns, FF // ns, HEADS // ns
    zq = nz // ns
    own_cols = pl.ds(pl.multiple_of(s * wl, LANES), wl)
    own_ff = pl.ds(pl.multiple_of(s * fl, LANES), fl)
    own_rows = pl.ds(pl.multiple_of(s * shard, 16), shard)
    scale = HEAD ** (-0.5)
    send, recv = sc.send, sc.recv
    used = {"n": 0}
    pending = []

    def sems(count):
        base = used["n"]
        used["n"] += count
        return base

    def remote(src, dst, sem, device):
        return pltpu.make_async_remote_copy(
            src_ref=src,
            dst_ref=dst,
            send_sem=send.at[sem],
            recv_sem=recv.at[sem],
            device_id=device,
            device_id_type=MESH,
        )

    def over_section(src, dst):
        base = sems(ns)

        def make(k):
            t = lax.rem(s + k, ns)
            return remote(src(t), dst, base + k, (t, r))

        transfer = Transfer(make, 1, ns).start()
        pending.append(transfer)
        return transfer

    def over_dp(src, dst):
        base = sems(nd)

        def make(k):
            t = lax.rem(r + k, nd)
            return remote(src(t), dst, base + k, (s, t))

        transfer = Transfer(make, 1, nd).start()
        pending.append(transfer)
        return transfer

    def over_z(src, dst):
        base = sems(nz)

        def make(k):
            t = lax.rem(z + k, nz)
            return remote(src(t), dst, base + k, (s, t * nx + x))

        transfer = Transfer(make, 1, nz).start()
        pending.append(transfer)
        return transfer

    def over_x(src, dst):
        base = sems(1)
        transfer = Transfer(lambda k: remote(src, dst, base, (s, z * nx + 1 - x)), 0, 1).start()
        pending.append(transfer)
        return transfer

    local_used = {"n": 0}

    def local(src, dst):
        sem = local_used["n"]
        local_used["n"] += 1
        copy = pltpu.make_async_copy(src, dst, sc.local.at[sem])
        copy.start()
        return copy

    small_loads = [
        local(i.agg_wq.at[:, own_cols], sc.wq),
        local(i.agg_wk.at[:, own_cols], sc.wk),
        local(i.agg_wv.at[:, own_cols], sc.wv),
    ]
    sources = [(i.agg_wo, sc.awo_c, 0, s * wl)]
    sources += [(i.attn_wqkv, sc.qkv_w, j * wl, j * D + s * wl) for j in range(3)]
    sources += [(i.attn_wo, sc.two_c, 0, s * wl)]
    sources += [(i.mlp_up, sc.up_w, j * CHUNK, s * fl + j * CHUNK) for j in range(fl // CHUNK)]
    sources += [(i.mlp_down, sc.down_w, j * CHUNK, s * fl + j * CHUNK) for j in range(fl // CHUNK)]
    pieces = [(dst, pl.ds(at, CHUNK)) for _, dst, at, _ in sources]
    piece_loads = [
        local(src.at[:, pl.ds(pl.multiple_of(col, LANES), CHUNK)], dst.at[z, x, :, pl.ds(at, CHUNK)])
        for src, dst, at, col in sources
    ]
    n_pieces = len(pieces)
    from_z, from_x = {}, {}

    def issue_z(count):
        for c in range(len(from_z), min(len(from_z) + count, n_pieces)):
            dst, cols = pieces[c]
            block = dst.at[z, x, :, cols]
            from_z[c] = over_z(lambda t, block=block: block, block)

    def forward(count):
        for c in range(len(from_x), min(len(from_x) + count, n_pieces)):
            from_z[c].wait_recv()
            dst, cols = pieces[c]
            half = dst.at[:, x, :, cols]
            from_x[c] = over_x(half, half)
            issue_z(1)

    cot_load = local(i.cotangent, sc.g_full.at[:, own_cols])

    barrier = pltpu.get_barrier_semaphore()
    for k in range(1, ns):
        pl.semaphore_signal(barrier, inc=1, device_id=(lax.rem(s + k, ns), r), device_id_type=MESH)
    each(
        1,
        nd,
        lambda k: pl.semaphore_signal(
            barrier, inc=1, device_id=(s, lax.rem(r + k, nd)), device_id_type=MESH
        ),
    )

    chan = (iota((CP, VARS), 0) >> 2 == iota((CP, VARS), 1)).astype(F32).astype(BF)
    ids = jnp.broadcast_to(i.var_ids[...].astype(F32), (CHUNK, VARS)).astype(BF)
    ids = nt(chan, ids)
    lane = iota((CP, CHUNK), 1)
    row = iota((CP, CHUNK), 0)
    hit = ((lane >> 2).astype(F32) == ids) & ((lane & 3) == (row & 3)) & (lane < CP)
    place = hit.astype(F32).astype(BF)
    sc.place[...] = place
    lane = iota((tokens, CHUNK), 1)
    ones = ((lane >= CP) & (lane < CP + VARS)).astype(F32)
    sc.pix[...] = (tn(i.patches[...], place) + ones).astype(BF)
    row = iota((CHUNK, LANES), 0)
    lane = iota((CHUNK, LANES), 1)
    owner = jnp.where(row < CP, row >> 2, row - CP)
    sc.fold[...] = ((owner == lane) & (lane < VARS)).astype(F32).astype(BF)
    chosen = (iota((rows, D), 1) == iota((rows, D), 0) + r * rows).astype(F32).astype(BF)
    lane = iota((CP, CHUNK), 1)
    row = iota((CP, CHUNK), 0)
    widen = (lane == row).astype(F32).astype(BF)
    lane = iota((VARS, CHUNK), 1)
    row = iota((VARS, CHUNK), 0)
    widen_var = (lane == row + CP).astype(F32).astype(BF)
    var_rows = nt(chosen, i.var_embed[...].astype(BF)).astype(BF)
    sc.basis[...] = (tn(i.embed_weight[...], widen) + nn(var_rows, widen_var)).astype(BF)
    query = jnp.broadcast_to(i.agg_query[...].astype(BF).astype(F32), (16, D))
    query = jnp.where(iota((16, D), 0) == 0, query, 0.0).astype(BF)
    query_rows = nt(query, chosen).astype(BF)
    o.query_rows[...] = query_rows
    sc.vecs[...] = jnp.zeros_like(sc.vecs)
    sc.bup[...] = jnp.zeros_like(sc.bup)

    for copy in small_loads:
        copy.wait()
    sc.q_src[...] = nn(query_rows, sc.wq[...])[0:8]
    value_part = tn(sc.basis[...], sc.wv[...])
    blk = CHUNK // nd
    for t in range(nd):
        sc.bv_src[t] = value_part[t * blk : (t + 1) * blk]
    cot_load.wait()
    for copy in piece_loads:
        copy.wait()

    pl.semaphore_wait(barrier, ns - 1 + nd - 1)

    def weight(ref):
        return ref[...].reshape(ref.shape[0] * ref.shape[1] * ref.shape[2], ref.shape[3])

    def scatter(part, landed, value):
        part[...] = value.astype(BF)
        transfer = over_section(lambda t: part.at[pl.ds(pl.multiple_of(t * shard, 16), shard)], landed.at[s])
        landed[s] = part[own_rows, :]
        return transfer

    def gather(full, value):
        full[own_rows, :] = value.astype(BF)
        return over_section(lambda t: full.at[own_rows], full.at[own_rows])

    def landed_sum(landed):
        total = landed[0].astype(F32)
        for k in range(1, ns):
            total = total + landed[k].astype(F32)
        return total

    def normal(value):
        centred = value - jnp.mean(value, axis=-1, keepdims=True)
        rstd = lax.rsqrt(jnp.mean(centred * centred, axis=-1, keepdims=True) + epsilon)
        return centred * rstd, rstd

    def whole_norm(full, gain, bias, dst):
        for t in range(ns):
            at = slice(t * shard, (t + 1) * shard)
            hat, _ = normal(full[at, :].astype(F32))
            dst[at, :] = (hat * gain[...] + bias[...]).astype(BF)

    def kept_norm(full, kept, rstd_kept):
        hat, rstd = normal(full[own_rows, :].astype(F32))
        kept[...] = hat
        rstd_kept[...] = jnp.broadcast_to(rstd, rstd_kept.shape)

    def norm_back(grad, gain, kept, rstd_kept, gain_row, bias_row):
        hat = kept[...]
        sc.vecs[gain_row : gain_row + 1, :] = colsum(grad * hat)
        sc.vecs[bias_row : bias_row + 1, :] = colsum(grad)
        inner = grad * gain[...]
        mean = jnp.mean(inner, axis=-1, keepdims=True)
        dot = jnp.mean(inner * hat, axis=-1, keepdims=True)
        return rstd_kept[:, 0:1] * (inner - mean - hat * dot)

    def transposed(full, dst):
        for j in range(D // CHUNK):
            turned = full[:, j * CHUNK : (j + 1) * CHUNK].astype(F32).T.astype(BF)
            n = dst.shape[0] // (D // CHUNK)
            dst[j * n : (j + 1) * n] = turned.reshape((n,) + dst.shape[1:])

    def by_rows(cols, dst):
        at = pl.ds(s * zq, zq)
        dst[:, :, :, own_cols] = cols[at]
        return over_section(
            lambda t: cols.at[pl.ds(t * zq, zq)], dst.at[:, :, :, own_cols]
        )

    def columns(ref, j):
        return ref[:, :, :, j * CHUNK : (j + 1) * CHUNK].reshape(D, CHUNK)

    def push(src, dst):
        transfer = over_dp(lambda t: src, dst.at[r])
        dst[r] = src[...]
        return transfer

    def summed(dst, count):
        total = dst[0]
        for k in range(1, count):
            total = total + dst[k]
        return total

    q_push = push(sc.q_src, sc.q_recv)
    bv_rs = over_dp(lambda t: sc.bv_src.at[t], sc.bv_recv.at[r])
    sc.bv_recv[r] = sc.bv_src[r]
    g_gather = over_section(lambda t: sc.g_full.at[:, own_cols], sc.g_full.at[:, own_cols])

    issue_z(2)
    q_push.wait_recv()
    query_proj = summed(sc.q_recv, nd)[0:1] + i.agg_bq[:, own_cols]
    sc.query_proj[...] = query_proj
    head_rows = (iota((16, wl), 1) >> 6 == iota((16, wl), 0)).astype(F32)
    high, low = split(head_rows * (query_proj * scale))
    key_query = (nt(high, sc.wk[...]) + nt(low, sc.wk[...])).astype(BF)
    sc.key_query[...] = key_query
    sc.s_src[...] = nn(key_query, sc.basis[...])[0:8]
    s_push = push(sc.s_src, sc.s_recv)
    bv_rs.wait_recv()
    sc.bv_own[...] = summed(sc.bv_recv, nd)
    bv_ag = push(sc.bv_own, sc.bv_all)
    issue_z(1)

    s_push.wait_recv()
    score_rows = summed(sc.s_recv, nd)
    sc.score_rows[...] = score_rows
    fold = sc.fold[...]
    lane_ok = iota((tokens, LANES), 1) < VARS
    for h in range(hl):
        pix = sc.pix[...].astype(F32)
        high, low = split(pix * score_rows[h : h + 1])
        scores = nn(high, fold) + nn(low, fold)
        scores = jnp.where(lane_ok, scores, -1e30)
        scores = jnp.exp(scores - jnp.max(scores, axis=-1, keepdims=True))
        probs = scores / jnp.sum(scores, axis=-1, keepdims=True)
        sc.probs[h] = probs
        wrep = nt(probs.astype(BF), fold)
        sc.wrep[h] = wrep.astype(BF)
        sc.mixed[h] = (wrep * pix).astype(BF)
    issue_z(2)
    forward(1)
    bv_ag.wait_recv()
    for t in range(nd):
        sc.bv[t * blk : (t + 1) * blk] = sc.bv_all[t]
    value_basis = sc.bv[...].astype(BF)
    head_of = iota((1, wl), 1) >> 6
    context = jnp.broadcast_to(i.agg_bv[:, own_cols], (tokens, wl))
    for h in range(hl):
        context = context + jnp.where(head_of == h, nn(sc.mixed[h], value_basis), 0.0)
    sc.context_full[:, own_cols] = context.astype(BF)
    context_gather = over_section(lambda t: sc.context_full.at[:, own_cols], sc.context_full.at[:, own_cols])
    g_gather.wait_recv()
    transposed(sc.g_full, sc.gT)
    forward(1)
    context_gather.wait_recv()
    from_x[0].wait_recv()
    part = nn(sc.context_full[...], weight(sc.awo_c)) + i.agg_bo[:, own_cols]
    sc.agg_full[:, own_cols] = part.astype(BF)
    agg_gather = over_section(lambda t: sc.agg_full.at[:, own_cols], sc.agg_full.at[:, own_cols])
    transposed(sc.context_full, sc.contextT)
    forward(1)
    agg_gather.wait_recv()
    whole_norm(sc.agg_full, i.attn_norm_gain, i.attn_norm_bias, sc.normed)
    kept_norm(sc.agg_full, sc.hat1, sc.rstd1)
    transposed(sc.normed, sc.normedT)
    forward(1)
    normed = sc.normed[...]
    for j in range(3):
        from_x[1 + j].wait_recv()
        part = nn(normed, columns(sc.qkv_w, j))
        if j == 0:
            part = part + i.attn_bq[:, own_cols]
        if j == 2:
            part = part + i.attn_bv[:, own_cols]
        sc.qkv[:, j * wl : (j + 1) * wl] = part.astype(BF)
        if j == 1:
            forward(1)
    lo = (iota((1, LANES), 1) < HEAD).astype(F32)
    first, second = lo.astype(BF), (1.0 - lo).astype(BF)

    def pair(a):
        return jnp.concatenate([a * first, a * second], axis=0)

    def pick(a):
        return jnp.where(iota((LEN, LANES), 1) < HEAD, a[0:LEN], a[LEN:])

    tiles = [(b, p) for b in range(tokens // LEN) for p in range(wl // LANES)]

    def tile(ref, b, p, j=0):
        return ref[b * LEN : (b + 1) * LEN, j * wl + p * LANES : j * wl + (p + 1) * LANES]

    for n, (b, p) in enumerate(tiles):
        q, k, v = [tile(sc.qkv, b, p, j) for j in range(3)]
        ids = jnp.broadcast_to(i.segment_ids[b : b + 1, :].astype(F32), (LEN, LEN))
        same = ids == ids.T
        scores = nt(pair(q), k) * scale
        scores = jnp.where(jnp.concatenate([same, same], axis=0), scores, blocked)
        scores = jnp.exp(scores - jnp.max(scores, axis=-1, keepdims=True))
        probs = scores / jnp.sum(scores, axis=-1, keepdims=True)
        sc.att[n] = probs
        sc.attended[b * LEN : (b + 1) * LEN, p * LANES : (p + 1) * LANES] = pick(
            nn(probs.astype(BF), v)
        ).astype(BF)
    sc.attended_full[:, own_cols] = sc.attended[...]
    attended_gather = over_section(
        lambda t: sc.attended_full.at[:, own_cols], sc.attended_full.at[:, own_cols]
    )
    forward(1)
    attended_gather.wait_recv()
    forward(1)
    from_x[4].wait_recv()
    part = nn(sc.attended_full[...], weight(sc.two_c)) + i.attn_bo[:, own_cols]
    sc.mid_full[:, own_cols] = (part + sc.agg_full[:, own_cols].astype(F32)).astype(BF)
    mid_gather = over_section(lambda t: sc.mid_full.at[:, own_cols], sc.mid_full.at[:, own_cols])
    transposed(sc.attended_full, sc.attendedT)
    forward(1)
    mid_gather.wait_recv()
    awo_rows = by_rows(sc.awo_c, sc.awo)
    two_rows = by_rows(sc.two_c, sc.two)
    whole_norm(sc.mid_full, i.mlp_norm_gain, i.mlp_norm_bias, sc.mnormed)
    kept_norm(sc.mid_full, sc.hat2, sc.rstd2)
    transposed(sc.mnormed, sc.mnormedT)
    forward(1)
    mnormed = sc.mnormed[...]
    for j in range(fl // CHUNK):
        at = slice(j * CHUNK, (j + 1) * CHUNK)
        bias = i.mlp_bup[:, pl.ds(pl.multiple_of(s * fl + j * CHUNK, LANES), CHUNK)]
        from_x[5 + j].wait_recv()
        hidden = nn(mnormed, columns(sc.up_w, j)) + bias
        phi = 0.5 + 0.5 * lax.erf(hidden * 0.7071067811865476)
        density = jnp.exp(hidden * hidden * -0.5) * 0.3989422804014327
        sc.act[:, at] = (hidden * phi).astype(BF)
        sc.slope[:, at] = phi + hidden * density
        if j == 0:
            forward(1)
        if j == 2:
            forward(1)
    forward(2)
    names = (
        [(o.mlp_down, s * fl + j * CHUNK) for j in range(fl // CHUNK)]
        + [(o.mlp_up, s * fl + j * CHUNK) for j in range(fl // CHUNK)]
        + [(o.attn_wo, s * wl)]
        + [(o.attn_wqkv, j * D + s * wl) for j in range(3)]
        + [(o.agg_wo, s * wl)]
    )
    to_x, to_z, made, done = {}, {}, [], []
    out_copies, out_sends = [], []

    def produce(c, left, right):
        def half(side):
            block = left[:, pl.ds(side, 1)].reshape(nz * rows, tokens)
            return nn(block, right).reshape(nz, rows, CHUNK)

        sc.x_send[c] = half(1 - x).astype(BF)
        made.append(c)
        sc.keep[c] = half(x)

    def issue_x(count):
        for c in made[len(to_x) : len(to_x) + count]:
            to_x[c] = over_x(sc.x_send.at[c], sc.x_recv.at[c])

    def middle(c):
        to_x[c].wait_recv()
        if c >= 6:
            issue_x(1)
        sc.z_send[c] = (sc.keep[c] + sc.x_recv[c].astype(F32)).astype(BF)
        to_z[c] = over_z(lambda t: sc.z_send.at[c, t], sc.z_recv.at[c, z])
        sc.z_recv[c, z] = sc.z_send[c, z]

    def publish(c, array, start):
        dst = array.at[:, pl.ds(pl.multiple_of(start, LANES), CHUNK)]
        out_sends.append(over_section(lambda t: sc.final.at[c], dst))
        out_copies.append(local(sc.final.at[c], dst))

    def finish(c):
        to_z[c].wait_recv()
        total = sc.z_recv[c, 0].astype(F32)
        for k in range(1, nz):
            total = total + sc.z_recv[c, k].astype(F32)
        sc.final[c] = total.astype(BF)
        publish(c, *names[c])

    def pump(count):
        for _ in range(count):
            c = len(to_z)
            if c < len(names):
                middle(c)
            if len(done) < len(names) and (c == len(names) or len(done) < c - 1):
                finish(len(done))
                done.append(c)

    for j in range(fl // CHUNK):
        produce(j, sc.gT, sc.act[:, j * CHUNK : (j + 1) * CHUNK])
    issue_x(4)
    g_full = sc.g_full[...]
    nmlp = fl // CHUNK
    for j in range(fl // CHUNK):
        at = slice(j * CHUNK, (j + 1) * CHUNK)
        from_x[5 + nmlp + j].wait_recv()
        d_hidden = nn(g_full, columns(sc.down_w, j)) * sc.slope[:, at]
        sc.d_hidden[:, at] = d_hidden.astype(BF)
    up_w = weight(sc.up_w)
    rs3 = scatter(sc.rs3_part, sc.rs3_recv, nt(sc.d_hidden[...], up_w))
    for j in range(nmlp):
        at = slice(j * CHUNK, (j + 1) * CHUNK)
        produce(nmlp + j, sc.mnormedT, sc.d_hidden[:, at])
    sc.bup[:, own_ff] = colsum(sc.d_hidden[...])
    issue_x(4)
    rs3.wait_recv()
    g_shard = sc.g_full[own_rows, :].astype(F32)
    sc.vecs[0:1, :] = colsum(g_shard)
    d_mid = norm_back(landed_sum(sc.rs3_recv), i.mlp_norm_gain, sc.hat2, sc.rstd2, 1, 2)
    d_mid = (g_shard + d_mid).astype(BF)
    sc.vecs[3:4, :] = colsum(d_mid)
    ag3 = gather(sc.d_mid, d_mid)
    d_mid = d_mid.astype(F32)
    sc.out_part[...] = nt(sc.act[...], weight(sc.down_w))
    sc.out_part[own_rows, :] = sc.out_part[own_rows, :] + sc.mid_full[own_rows, :].astype(F32) + i.mlp_bdown[...]
    sc.out_low[...] = sc.out_part[...].astype(BF)
    out_rs = over_section(
        lambda t: sc.out_low.at[:, pl.ds(pl.multiple_of(t * wl, LANES), wl)], sc.out_recv.at[s]
    )
    sc.out_recv[s] = sc.out_low[:, own_cols]
    pump(2)
    ag3.wait_recv()

    pump(1)
    two_rows.wait_recv()
    d_att = nt(sc.d_mid[...], weight(sc.two)).astype(BF)
    sc.d_att[...] = d_att
    for n, (b, p) in enumerate(tiles):
        q, k, v = [tile(sc.qkv, b, p, j) for j in range(3)]
        q, d_out = pair(q), pair(tile(sc.d_att, b, p))
        probs = sc.att[n]
        d_probs = nt(d_out, v)
        d_scores = probs * (d_probs - jnp.sum(probs * d_probs, axis=-1, keepdims=True))
        d_scores = d_scores.astype(BF)
        parts = (pick(nn(d_scores, k)) * scale, tn(d_scores, q) * scale, tn(probs.astype(BF), d_out))
        for j in range(3):
            lanes = slice(j * wl + p * LANES, j * wl + (p + 1) * LANES)
            sc.d_qkv[b * LEN : (b + 1) * LEN, lanes] = parts[j].astype(BF)
    rs4 = scatter(sc.rs4_part, sc.rs4_recv, nt(sc.d_qkv[...], weight(sc.qkv_w)))
    produce(2 * nmlp, sc.attendedT, sc.d_mid[:, own_cols])
    for j in range(3):
        produce(2 * nmlp + 1 + j, sc.normedT, sc.d_qkv[:, j * wl : (j + 1) * wl])
    sc.vecs[7:8, own_cols] = colsum(sc.d_qkv[:, 0:wl])
    sc.vecs[8:9, own_cols] = colsum(sc.d_qkv[:, 2 * wl : 3 * wl])
    pump(1)
    rs4.wait_recv()
    d_agg = norm_back(landed_sum(sc.rs4_recv), i.attn_norm_gain, sc.hat1, sc.rstd1, 4, 5)
    d_agg = (sc.d_mid[own_rows, :].astype(F32) + d_agg).astype(BF)
    sc.vecs[6:7, :] = colsum(d_agg)
    ag4 = gather(sc.d_agg, d_agg)
    pump(2)
    ag4.wait_recv()

    awo_rows.wait_recv()
    produce(2 * nmlp + 4, sc.contextT, sc.d_agg[:, own_cols])
    d_context = nt(sc.d_agg[...], weight(sc.awo)).astype(BF)
    sc.vecs[9:10, own_cols] = colsum(d_context)
    value_basis = sc.bv[...].astype(BF)
    cross = jnp.zeros((CHUNK, wl), F32)
    grad_pix = jnp.zeros((tokens, CHUNK), F32)
    sc.key_src[...] = jnp.zeros_like(sc.key_src)
    for h in range(hl):
        masked = d_context * (head_of == h).astype(F32).astype(BF)
        pulled = nt(masked, value_basis)
        cross = cross + tn(sc.mixed[h], masked)
        pix = sc.pix[...].astype(F32)
        high, low = split(pulled * pix)
        d_weights = nn(high, fold) + nn(low, fold)
        probs = sc.probs[h]
        d_scores = probs * (d_weights - jnp.sum(probs * d_weights, axis=-1, keepdims=True))
        srep = nt(d_scores.astype(BF), fold)
        sc.key_src[h : h + 1, :] = colsum(srep * pix)
        grad_pix = grad_pix + sc.wrep[h].astype(F32) * pulled
        grad_pix = grad_pix + srep * sc.score_rows[h : h + 1, :]
    key_push = push(sc.key_src, sc.key_recv)
    for t in range(nd):
        sc.m_src[t] = cross[t * blk : (t + 1) * blk]
    m_rs = over_dp(lambda t: sc.m_src.at[t], sc.m_recv.at[r])
    sc.m_recv[r] = sc.m_src[r]
    grad_pix = grad_pix.astype(BF)
    pw = CP // ns
    for t in range(ns):
        sc.pix_src[t] = nt(sc.place[t * pw : (t + 1) * pw, :], grad_pix).astype(BF)
    pix_rs = over_section(lambda t: sc.pix_src.at[t], sc.pix_recv.at[s])
    sc.pix_recv[s] = sc.pix_src[s]
    for t in range(nd):
        sc.small_src[t, 0:10] = sc.vecs[0:10, t * rows : (t + 1) * rows]
        for j in range(FF // D):
            start = (t * (FF // D) + j) * rows
            sc.small_src[t, 10 + j : 11 + j] = sc.bup[:, start : start + rows]
    small_rs = over_dp(lambda t: sc.small_src.at[t], sc.small_recv.at[r])
    sc.small_recv[r] = sc.small_src[r]

    issue_x(1)
    pump(2)
    m_rs.wait_recv()
    sc.m_own[...] = summed(sc.m_recv, nd)
    m_ag = push(sc.m_own, sc.m_all)
    key_push.wait_recv()
    key_terms = summed(sc.key_recv, nd)
    wide = jnp.concatenate([jnp.broadcast_to(key_terms[h : h + 1], (HEAD, CHUNK)) for h in range(hl)], axis=0)
    d_key = nt(sc.basis[...], wide.astype(BF))
    d_query = jnp.sum(sc.wk[...].astype(F32) * d_key, axis=0, keepdims=True) * scale
    sc.dq_src[...] = jnp.broadcast_to(d_query, sc.dq_src.shape)
    dq_push = push(sc.dq_src, sc.dq_recv)
    count = len(names)
    sc.final[count] = (d_key * (sc.query_proj[...] * scale)).astype(BF)
    publish(count, o.agg_wk, s * wl)
    pump(2)
    small_rs.wait_recv()
    sc.sec_small[s] = summed(sc.small_recv, nd)
    small_ag = over_section(lambda t: sc.sec_small.at[s], sc.sec_small.at[s])
    pump(1)
    m_ag.wait_recv()
    for t in range(nd):
        sc.cross[t * blk : (t + 1) * blk] = sc.m_all[t]
    cross = sc.cross[...].astype(BF)
    sc.final[count + 1] = nn(sc.basis[...], cross).astype(BF)
    publish(count + 1, o.agg_wv, s * wl)
    key_low = jnp.concatenate([key_terms, jnp.zeros_like(key_terms)], axis=0).astype(BF)
    grad_basis = nt(cross, sc.wv[...]) + tn(key_low, sc.key_query[...])
    sc.basis_recv[s] = grad_basis.astype(BF)
    basis_sum = over_section(lambda t: sc.basis_recv.at[s], sc.basis_recv.at[s])
    pump(1)
    dq_push.wait_recv()
    o.d_query[s] = summed(sc.dq_recv, nd)
    dq_gather = over_section(lambda t: o.d_query.at[s], o.d_query.at[s])

    def section_total(ref):
        total = ref[0].astype(F32)
        for k in range(1, ns):
            total = total + ref[k].astype(F32)
        return total

    out_rs.wait_recv()
    o.activations[...] = section_total(sc.out_recv).astype(BF)
    pix_rs.wait_recv()
    o.patches[...] = section_total(sc.pix_recv).astype(BF)
    small_ag.wait_recv()
    o.small[...] = summed(sc.sec_small, ns)
    pump(20)
    basis_sum.wait_recv()
    o.basis[...] = section_total(sc.basis_recv)
    dq_gather.wait_recv()
    for transfer in out_sends:
        transfer.wait_recv()
    for copy in out_copies:
        copy.wait()
    for transfer in pending:
        transfer.wait_send()
    assert used["n"] <= send.shape[0], used["n"]
    assert local_used["n"] <= sc.local.shape[0]


def scratch(ns, nd, tokens):
    nz, rows = nd // 2, D // nd
    wl, fl, hl = D // ns, FF // ns, HEADS // ns
    shard, zq, blk = tokens // ns, nz // ns, CHUNK // nd
    chunks = 2 * (fl // CHUNK) + 5
    v = pltpu.VMEM
    shapes = dict(
        wq=v((rows, wl), BF),
        wk=v((rows, wl), BF),
        wv=v((rows, wl), BF),
        qkv_w=v((nz, 2, rows, 3 * wl), BF),
        up_w=v((nz, 2, rows, fl), BF),
        down_w=v((nz, 2, rows, fl), BF),
        awo_c=v((nz, 2, rows, wl), BF),
        two_c=v((nz, 2, rows, wl), BF),
        awo=v((zq, 2, rows, D), BF),
        two=v((zq, 2, rows, D), BF),
        g_full=v((tokens, D), BF),
        place=v((CP, CHUNK), BF),
        pix=v((tokens, CHUNK), BF),
        fold=v((CHUNK, LANES), BF),
        basis=v((rows, CHUNK), BF),
        vecs=v((16, D), F32),
        bup=v((1, FF), F32),
        query_proj=v((1, wl), F32),
        key_query=v((16, rows), BF),
        score_rows=v((8, CHUNK), F32),
        bv_own=v((blk, CHUNK), F32),
        m_own=v((blk, CHUNK), F32),
        bv=v((CHUNK, CHUNK), F32),
        cross=v((CHUNK, CHUNK), F32),
        probs=v((hl, tokens, LANES), F32),
        wrep=v((hl, tokens, CHUNK), BF),
        mixed=v((hl, tokens, CHUNK), BF),
        context_full=v((tokens, D), BF),
        attended_full=v((tokens, D), BF),
        agg_full=v((tokens, D), BF),
        mid_full=v((tokens, D), BF),
        hat1=v((shard, D), F32),
        hat2=v((shard, D), F32),
        rstd1=v((shard, LANES), F32),
        rstd2=v((shard, LANES), F32),
        normed=v((tokens, D), BF),
        mnormed=v((tokens, D), BF),
        qkv=v((tokens, 3 * wl), BF),
        d_qkv=v((tokens, 3 * wl), BF),
        att=v((tokens // LEN * (wl // LANES), 2 * LEN, LEN), F32),
        attended=v((tokens, wl), BF),
        d_att=v((tokens, wl), BF),
        act=v((tokens, fl), BF),
        slope=v((tokens, fl), F32),
        d_hidden=v((tokens, fl), BF),
        d_mid=v((tokens, D), BF),
        d_agg=v((tokens, D), BF),
        out_part=v((tokens, D), F32),
        out_low=v((tokens, D), BF),
        out_recv=v((ns, tokens, wl), BF),
        pix_src=v((ns, CP // ns, tokens), BF),
        pix_recv=v((ns, CP // ns, tokens), BF),
        small_src=v((nd, 16, rows), F32),
        small_recv=v((nd, 16, rows), F32),
        sec_small=v((ns, 16, rows), F32),
        basis_recv=v((ns, CHUNK, rows), BF),
        x_send=v((chunks, nz, rows, CHUNK), BF),
        x_recv=v((chunks, nz, rows, CHUNK), BF),
        keep=v((chunks, nz, rows, CHUNK), F32),
        z_send=v((chunks, nz, rows, CHUNK), BF),
        z_recv=v((chunks, nz, rows, CHUNK), BF),
        final=v((chunks + 2, rows, CHUNK), BF),
    )
    whole = v((nz, 2, rows, tokens), BF)
    shapes.update(gT=whole, contextT=whole, attendedT=whole, normedT=whole, mnormedT=whole)
    part = v((tokens, D), BF)
    shapes.update(rs3_part=part, rs4_part=part)
    part = v((ns, shard, D), BF)
    shapes.update(rs3_recv=part, rs4_recv=part)
    part = v((8, CHUNK), F32)
    shapes.update(q_src=part, s_src=part, key_src=part, dq_src=part)
    part = v((nd, 8, CHUNK), F32)
    shapes.update(q_recv=part, s_recv=part, key_recv=part, dq_recv=part)
    part = v((nd, blk, CHUNK), F32)
    shapes.update(bv_src=part, bv_recv=part, bv_all=part, m_src=part, m_recv=part, m_all=part)
    count = 9 * nd + 24 * ns + 2 * chunks * (1 + nz) + chunks * ns
    dma = pltpu.SemaphoreType.DMA
    shapes.update(send=dma((count,)), recv=dma((count,)), local=dma((8 + 2 * chunks + 4,)))
    return shapes


def fused(ns, nd, near, far):
    tokens = near["patches"].shape[1]
    rows = D // nd
    shapes = scratch(ns, nd, tokens)
    arrays = {**near, **far}
    hbm = pl.BlockSpec(memory_space=pl.ANY)
    vmem = pl.BlockSpec(memory_space=pltpu.VMEM)
    outs = dict(
        activations=((tokens, D // ns), BF, vmem),
        patches=((CP // ns, tokens), BF, vmem),
        basis=((CHUNK, rows), F32, vmem),
        query_rows=((16, rows), BF, vmem),
        d_query=((ns, 8, D // ns), F32, vmem),
        small=((16, rows), F32, vmem),
        mlp_up=((rows, FF), BF, hbm),
        mlp_down=((rows, FF), BF, hbm),
        attn_wqkv=((rows, 3 * D), BF, hbm),
        attn_wo=((rows, D), BF, hbm),
        agg_wo=((rows, D), BF, hbm),
        agg_wv=((rows, D), BF, hbm),
        agg_wk=((rows, D), BF, hbm),
    )

    def body(*refs):
        n_in, n_out = len(arrays), len(outs)
        kernel(
            ns,
            nd,
            SimpleNamespace(**dict(zip(arrays, refs[:n_in]))),
            SimpleNamespace(**dict(zip(outs, refs[n_in : n_in + n_out]))),
            SimpleNamespace(**dict(zip(shapes, refs[n_in + n_out :]))),
        )

    result = pl.pallas_call(
        body,
        out_shape=[jax.ShapeDtypeStruct(shape, kind) for shape, kind, _ in outs.values()],
        in_specs=[vmem] * len(near) + [hbm] * len(far),
        out_specs=[spec for _, _, spec in outs.values()],
        scratch_shapes=list(shapes.values()),
        compiler_params=pltpu.CompilerParams(
            collective_id=0, has_side_effects=True, vmem_limit_bytes=60 * 1024 * 1024
        ),
        name="block",
    )(*arrays.values())
    return SimpleNamespace(**dict(zip(outs, result)))


def widen(nd, got, agg_wq):
    rows = D // nd
    step = min(rows, 32)
    big = dict(
        mlp_up=got.mlp_up,
        mlp_down=got.mlp_down,
        attn_wqkv=got.attn_wqkv,
        attn_wo=got.attn_wo,
        agg_wo=got.agg_wo,
        agg_wv=got.agg_wv,
        agg_wk=got.agg_wk,
    )
    rest = dict(
        activations=got.activations,
        patches=got.patches,
        basis=got.basis,
        query_rows=got.query_rows,
        d_query=got.d_query,
        small=got.small,
        agg_wq=agg_wq,
    )
    line = (1, rows)
    outs = dict(
        activations=(got.activations.shape, BF),
        patches=(got.patches.shape, BF),
        embed=((CP, rows), F32),
        var=((VARS, rows), F32),
        query=(line, F32),
        wq=((rows, D), F32),
        bq=(line, F32),
        bup=((1, rows * (FF // D)), F32),
    )
    lines = tuple(range(10))

    def body(*refs):
        n = len(big)
        for src, dst in zip(refs[:n], refs[n + len(rest) : 2 * n + len(rest)]):
            dst[...] = src[...].astype(F32)
        i = SimpleNamespace(**dict(zip(rest, refs[n : n + len(rest)])))
        left = refs[2 * n + len(rest) :]
        o = SimpleNamespace(**dict(zip(outs, left)))
        left = left[len(outs) :]
        r = lax.axis_index("dp")

        @pl.when(pl.program_id(0) == 0)
        def _():
            o.activations[...] = i.activations[...]
            o.patches[...] = i.patches[...]
            o.embed[...] = i.basis[0:CP]
            o.var[...] = i.basis[CP : CP + VARS]
            d_query = jnp.concatenate([i.d_query[k] for k in range(i.d_query.shape[0])], axis=1)
            d_query = jnp.concatenate([d_query, d_query], axis=0)
            d_query = jnp.where(iota(d_query.shape, 0) == 0, d_query, 0.0)
            high, low = split(d_query)
            low, rest_low = split(d_query - high.astype(F32))
            chosen = (iota((rows, D), 1) == iota((rows, D), 0) + r * rows).astype(F32).astype(BF)
            o.bq[...] = (nt(high, chosen) + nt(low, chosen) + nt(rest_low, chosen))[0:1]
            weight = i.agg_wq[...]
            o.query[...] = (nt(high, weight) + nt(low, weight) + nt(rest_low, weight))[0:1]
            first = i.query_rows[...]
            o.wq[...] = tn(first, high) + tn(first, low) + tn(first, rest_low)
            o.bup[...] = jnp.concatenate([i.small[10 + k : 11 + k] for k in range(FF // D)], axis=1)
            for k in lines:
                left[k][...] = i.small[k : k + 1]

    def by_step(a):
        return pl.BlockSpec((step, a.shape[1]), lambda g: (g, 0))

    def fixed(shape):
        return pl.BlockSpec(shape, lambda g: (0,) * len(shape))

    shaped = [jax.ShapeDtypeStruct(a.shape, F32) for a in big.values()]
    shaped += [jax.ShapeDtypeStruct(*a) for a in outs.values()]
    shaped += [jax.ShapeDtypeStruct(line, F32) for _ in lines]
    result = pl.pallas_call(
        body,
        grid=(rows // step,),
        out_shape=shaped,
        in_specs=[by_step(a) for a in big.values()] + [fixed(a.shape) for a in rest.values()],
        out_specs=[by_step(a) for a in big.values()] + [fixed(a.shape) for a in shaped[len(big) :]],
        compiler_params=pltpu.CompilerParams(vmem_limit_bytes=60 * 1024 * 1024),
        name="widen",
    )(*big.values(), *rest.values())
    names = list(big) + list(outs)
    return SimpleNamespace(**dict(zip(names, result))), [a.reshape(-1) for a in result[len(names) :]]


def on_device(
    ns,
    nd,
    patches,
    var_ids,
    segment_ids,
    embed_weight,
    var_embed,
    agg_query,
    agg_wq,
    agg_bq,
    agg_wk,
    agg_wv,
    agg_bv,
    agg_wo,
    agg_bo,
    attn_norm_gain,
    attn_norm_bias,
    attn_wqkv,
    attn_bq,
    attn_bv,
    attn_wo,
    attn_bo,
    mlp_norm_gain,
    mlp_norm_bias,
    mlp_up,
    mlp_bup,
    mlp_down,
    mlp_bdown,
    cotangent,
):
    near = dict(
        patches=patches,
        var_ids=var_ids,
        segment_ids=segment_ids,
        embed_weight=embed_weight,
        var_embed=var_embed,
        agg_query=agg_query,
        agg_bq=agg_bq,
        agg_bv=agg_bv,
        agg_bo=agg_bo,
        attn_norm_gain=attn_norm_gain,
        attn_norm_bias=attn_norm_bias,
        attn_bq=attn_bq,
        attn_bv=attn_bv,
        attn_bo=attn_bo,
        mlp_norm_gain=mlp_norm_gain,
        mlp_norm_bias=mlp_norm_bias,
        mlp_bup=mlp_bup,
        mlp_bdown=mlp_bdown,
    )
    far = dict(
        agg_wq=agg_wq,
        agg_wk=agg_wk,
        agg_wv=agg_wv,
        agg_wo=agg_wo,
        attn_wqkv=attn_wqkv,
        attn_wo=attn_wo,
        mlp_up=mlp_up,
        mlp_down=mlp_down,
        cotangent=cotangent,
    )
    near = {name: a.reshape(1, -1) if a.ndim == 1 else a for name, a in near.items()}
    near["patches"], near["embed_weight"] = patches.T, embed_weight.T
    got = fused(ns, nd, near, far)
    out, small = widen(nd, got, agg_wq)
    return (
        out.activations,
        out.patches.T,
        out.embed.T,
        out.var,
        out.query.reshape(-1),
        out.wq,
        out.bq.reshape(-1),
        out.agg_wk,
        out.agg_wv,
        small[9],
        out.agg_wo,
        small[6],
        small[4],
        small[5],
        out.attn_wqkv,
        small[7],
        small[8],
        out.attn_wo,
        small[3],
        small[1],
        small[2],
        out.mlp_up,
        out.bup.reshape(-1),
        out.mlp_down,
        small[0],
    )


def solution(mesh):
    in_specs = (
        P("dp", None),
        P(),
        P("dp", None),
        P("dp", None),
        P(),
        P(),
        P("dp", None),
        P(),
        P("dp", None),
        P("dp", None),
        P(),
        P("dp", None),
        P(),
        P(),
        P(),
        P("dp", None),
        P(),
        P(),
        P("dp", None),
        P(),
        P(),
        P(),
        P("dp", None),
        P(),
        P("dp", None),
        P(),
        P("dp", "section"),
    )
    out_specs = (
        P("dp", "section"),
        P("dp", "section"),
        P("dp", None),
        P(None, "dp"),
        P("dp"),
        P("dp", None),
        P("dp"),
        P("dp", None),
        P("dp", None),
        P("dp"),
        P("dp", None),
        P("dp"),
        P("dp"),
        P("dp"),
        P("dp", None),
        P("dp"),
        P("dp"),
        P("dp", None),
        P("dp"),
        P("dp"),
        P("dp"),
        P("dp", None),
        P("dp"),
        P("dp", None),
        P("dp"),
    )
    sizes = (mesh.shape["section"], mesh.shape["dp"])
    return jax.shard_map(
        partial(on_device, *sizes), mesh=mesh, in_specs=in_specs, out_specs=out_specs, check_vma=False
    )
```

```python
from functools import partial
from types import SimpleNamespace

import jax
import jax.numpy as jnp
from jax import lax
from jax.experimental import pallas as pl
from jax.experimental.pallas import tpu as pltpu
from jax.sharding import PartitionSpec as P

D = 1024
HEADS = 16
HEAD = 64
FF = 4096
VARS = 48
PIX = 4
LEN = 128

highest = lax.Precision.HIGHEST
blocked = -1000000000.0
epsilon = 1e-05
MESH = pl.DeviceIdType.MESH
BF = jnp.bfloat16
F32 = jnp.float32
CHUNK = 256
CP = VARS * PIX
LANES = 128


def nn(a, b):
    return jnp.dot(a, b, preferred_element_type=F32)


def nt(a, b):
    return lax.dot_general(a, b, (((1,), (1,)), ((), ())), preferred_element_type=F32)


def tn(a, b):
    return lax.dot_general(a, b, (((0,), (0,)), ((), ())), preferred_element_type=F32)


def split(x):
    high = x.astype(BF)
    return high, (x - high.astype(F32)).astype(BF)


def iota(shape, dim):
    return lax.broadcasted_iota(jnp.int32, shape, dim)


def colsum(x):
    return jnp.sum(x.astype(F32), axis=0, keepdims=True)


def each(low, high, body):
    if high - low <= 8:
        for k in range(low, high):
            body(k)
    else:

        def step(k, carry):
            body(k)
            return carry

        lax.fori_loop(low, high, step, 0)


class Transfer:
    def __init__(self, make, low, high):
        self.make, self.low, self.high = make, low, high

    def start(self):
        each(self.low, self.high, lambda k: self.make(k).start())
        return self

    def wait_recv(self):
        each(self.low, self.high, lambda k: self.make(k).wait_recv())

    def wait_send(self):
        each(self.low, self.high, lambda k: self.make(k).wait_send())


def kernel(ns, nd, refs_in, refs_out, sc):
    s = lax.axis_index("section")
    r = lax.axis_index("dp")
    nx = 2
    nz = nd // nx
    z, x = lax.div(r, nx), lax.rem(r, nx)
    i, o = refs_in, refs_out
    rows = D // nd
    tokens = i.patches.shape[1]
    shard = tokens // ns
    wl, fl, hl = D // ns, FF // ns, HEADS // ns
    zq = nz // ns
    own_cols = pl.ds(pl.multiple_of(s * wl, LANES), wl)
    own_ff = pl.ds(pl.multiple_of(s * fl, LANES), fl)
    own_rows = pl.ds(pl.multiple_of(s * shard, 16), shard)
    scale = HEAD ** (-0.5)
    send, recv = sc.send, sc.recv
    used = {"n": 0}
    pending = []

    def sems(count):
        base = used["n"]
        used["n"] += count
        return base

    def remote(src, dst, sem, device, landing=None):
        return pltpu.make_async_remote_copy(
            src_ref=src,
            dst_ref=dst,
            send_sem=send.at[sem],
            recv_sem=recv.at[sem if landing is None else landing],
            device_id=device,
            device_id_type=MESH,
        )

    def over_section(src, dst):
        base = sems(ns)

        def make(k):
            t = lax.rem(s + k, ns)
            return remote(src(t), dst, base + k, (t, r))

        transfer = Transfer(make, 1, ns).start()
        pending.append(transfer)
        return transfer

    def over_dp(src, dst):
        base = sems(nd)

        def make(k):
            t = lax.rem(r + k, nd)
            return remote(src(t), dst, base + k, (s, t))

        transfer = Transfer(make, 1, nd).start()
        pending.append(transfer)
        return transfer

    def over_z(src, dst):
        base = sems(nz)

        def make(k):
            t = lax.rem(z + k, nz)
            return remote(src(t), dst, base + k, (s, t * nx + x))

        transfer = Transfer(make, 1, nz).start()
        pending.append(transfer)
        return transfer

    line = nz == 4
    partner = z + 1 - 2 * lax.rem(z, 2)
    inner = (z == 1) | (z == 2)
    outer = (z == 0) | (z == 3)
    beyond = [lax.rem(2 * lax.div(z, 2) + 2 + j, 4) for j in range(2)]
    gate = 2 - lax.div(z, 2)

    def at_z(t):
        return (s, t * nx + x)

    def line_spread(block):
        base = sems(8)

        def own(k):
            to = at_z(partner if k == 0 else gate)
            return remote(block(z), block(z), base + 4 + k, to, base + z)

        def passed(j):
            b = beyond[j]
            return remote(block(b), block(b), base + 6 + j, at_z(partner), base + b)

        for k in range(2):
            own(k).start()

        def arrived(k):
            t = [partner, *beyond][k]
            remote(block(t), block(t), base + 4, at_z(partner), base + t).wait_recv()
            if k > 0:

                @pl.when(inner)
                def _():
                    passed(k - 1).start()

            return t

        def wait_send():
            for k in range(2):
                own(k).wait_send()

            @pl.when(inner)
            def _():
                for j in range(2):
                    passed(j).wait_send()

        pending.append(SimpleNamespace(wait_send=wait_send))
        return arrived

    def spread(block):
        if line:
            return line_spread(block)
        return over_z(lambda t: block(z), block(z)).wait_recv

    def line_reduce(parts, landed, merged):
        base = sems(5)

        def near():
            return remote(parts.at[partner], landed.at[0], base, at_z(partner))

        def far(j):
            return remote(parts.at[beyond[j]], landed.at[2 + j], base + 1 + j, at_z(partner))

        def across(j):
            return remote(merged.at[j], landed.at[1], base + 3 + j, at_z(beyond[j]), base + 3)

        near().start()

        @pl.when(outer)
        def _():
            for j in range(2):
                far(j).start()

        def merge():
            @pl.when(inner)
            def _():
                for j in range(2):
                    far(j).wait_recv()
                    both = parts[beyond[j]].astype(F32) + landed[2 + j].astype(F32)
                    merged[j] = both.astype(BF)
                    across(j).start()

        def total():
            near().wait_recv()
            across(0).wait_recv()
            return parts[z].astype(F32) + landed[0].astype(F32) + landed[1].astype(F32)

        def wait_send():
            near().wait_send()

            @pl.when(outer)
            def _():
                for j in range(2):
                    far(j).wait_send()

            @pl.when(inner)
            def _():
                for j in range(2):
                    across(j).wait_send()

        pending.append(SimpleNamespace(wait_send=wait_send))
        return SimpleNamespace(merge=merge, total=total)

    def reduce(parts, landed, merged):
        if line:
            return line_reduce(parts, landed, merged)
        transfer = over_z(lambda t: parts.at[t], landed.at[z])
        landed[z] = parts[z]

        def total():
            transfer.wait_recv()
            value = landed[0].astype(F32)
            for k in range(1, nz):
                value = value + landed[k].astype(F32)
            return value

        return SimpleNamespace(merge=lambda: None, total=total)

    def over_x(src, dst):
        base = sems(1)
        transfer = Transfer(lambda k: remote(src, dst, base, (s, z * nx + 1 - x)), 0, 1).start()
        pending.append(transfer)
        return transfer

    local_used = {"n": 0}

    def local(src, dst):
        sem = local_used["n"]
        local_used["n"] += 1
        copy = pltpu.make_async_copy(src, dst, sc.local.at[sem])
        copy.start()
        return copy

    small_loads = [
        local(i.agg_wq.at[:, own_cols], sc.wq),
        local(i.agg_wk.at[:, own_cols], sc.wk),
        local(i.agg_wv.at[:, own_cols], sc.wv),
    ]
    sources = [(i.agg_wo, sc.awo_c, 0, s * wl)]
    sources += [(i.attn_wqkv, sc.qkv_w, j * wl, j * D + s * wl) for j in range(3)]
    sources += [(i.attn_wo, sc.two_c, 0, s * wl)]
    sources += [(i.mlp_up, sc.up_w, j * CHUNK, s * fl + j * CHUNK) for j in range(fl // CHUNK)]
    sources += [(i.mlp_down, sc.down_w, j * CHUNK, s * fl + j * CHUNK) for j in range(fl // CHUNK)]
    pieces = [(dst, pl.ds(at, CHUNK)) for _, dst, at, _ in sources]
    piece_loads = [
        local(src.at[:, pl.ds(pl.multiple_of(col, LANES), CHUNK)], dst.at[z, x, :, pl.ds(at, CHUNK)])
        for src, dst, at, col in sources
    ]
    n_pieces = len(pieces)
    from_z, from_x, own_x = {}, {}, {}

    def issue_z(count):
        for c in range(len(from_z), min(len(from_z) + count, n_pieces)):
            dst, cols = pieces[c]
            from_z[c] = spread(lambda t, dst=dst, cols=cols: dst.at[t, x, :, cols])

    def issue_own(count):
        for c in range(len(own_x), min(len(own_x) + count, n_pieces if line else 0)):
            dst, cols = pieces[c]
            block = dst.at[z, x, :, cols]
            own_x[c] = over_x(block, block)

    def forward(count):
        for c in range(len(from_x), min(len(from_x) + count, n_pieces)):
            if c >= len(own_x):
                issue_own(1)
            dst, cols = pieces[c]
            if line:
                from_x[c] = []
                for k in range(nz - 1):
                    t = from_z[c](k)
                    block = dst.at[t, x, :, cols]
                    from_x[c].append(over_x(block, block))
            else:
                from_z[c]()
                half = dst.at[:, x, :, cols]
                from_x[c] = [over_x(half, half)]
            issue_z(1)

    def landed_x(c):
        for transfer in from_x[c] + ([own_x[c]] if line else []):
            transfer.wait_recv()

    cot_load = local(i.cotangent, sc.g_full.at[:, own_cols])

    barrier = pltpu.get_barrier_semaphore()
    for k in range(1, ns):
        pl.semaphore_signal(barrier, inc=1, device_id=(lax.rem(s + k, ns), r), device_id_type=MESH)
    each(
        1,
        nd,
        lambda k: pl.semaphore_signal(
            barrier, inc=1, device_id=(s, lax.rem(r + k, nd)), device_id_type=MESH
        ),
    )

    chan = (iota((CP, VARS), 0) >> 2 == iota((CP, VARS), 1)).astype(F32).astype(BF)
    ids = jnp.broadcast_to(i.var_ids[...].astype(F32), (CHUNK, VARS)).astype(BF)
    ids = nt(chan, ids)
    lane = iota((CP, CHUNK), 1)
    row = iota((CP, CHUNK), 0)
    hit = ((lane >> 2).astype(F32) == ids) & ((lane & 3) == (row & 3)) & (lane < CP)
    place = hit.astype(F32).astype(BF)
    sc.place[...] = place
    lane = iota((tokens, CHUNK), 1)
    ones = ((lane >= CP) & (lane < CP + VARS)).astype(F32)
    sc.pix[...] = (tn(i.patches[...], place) + ones).astype(BF)
    row = iota((CHUNK, LANES), 0)
    lane = iota((CHUNK, LANES), 1)
    owner = jnp.where(row < CP, row >> 2, row - CP)
    sc.fold[...] = ((owner == lane) & (lane < VARS)).astype(F32).astype(BF)
    chosen = (iota((rows, D), 1) == iota((rows, D), 0) + r * rows).astype(F32).astype(BF)
    lane = iota((CP, CHUNK), 1)
    row = iota((CP, CHUNK), 0)
    widen = (lane == row).astype(F32).astype(BF)
    lane = iota((VARS, CHUNK), 1)
    row = iota((VARS, CHUNK), 0)
    widen_var = (lane == row + CP).astype(F32).astype(BF)
    var_rows = nt(chosen, i.var_embed[...].astype(BF)).astype(BF)
    sc.basis[...] = (tn(i.embed_weight[...], widen) + nn(var_rows, widen_var)).astype(BF)
    query = jnp.broadcast_to(i.agg_query[...].astype(BF).astype(F32), (16, D))
    query = jnp.where(iota((16, D), 0) == 0, query, 0.0).astype(BF)
    query_rows = nt(query, chosen).astype(BF)
    o.query_rows[...] = query_rows
    sc.vecs[...] = jnp.zeros_like(sc.vecs)
    sc.bup[...] = jnp.zeros_like(sc.bup)

    for copy in small_loads:
        copy.wait()
    sc.q_src[...] = nn(query_rows, sc.wq[...])[0:8]
    value_part = tn(sc.basis[...], sc.wv[...])
    blk = CHUNK // nd
    for t in range(nd):
        sc.bv_src[t] = value_part[t * blk : (t + 1) * blk].astype(sc.bv_src.dtype)
    cot_load.wait()
    for copy in piece_loads:
        copy.wait()

    pl.semaphore_wait(barrier, ns - 1 + nd - 1)

    def weight(ref):
        return ref[...].reshape(ref.shape[0] * ref.shape[1] * ref.shape[2], ref.shape[3])

    def scatter(part, landed, value):
        part[...] = value.astype(BF)
        transfer = over_section(lambda t: part.at[pl.ds(pl.multiple_of(t * shard, 16), shard)], landed.at[s])
        landed[s] = part[own_rows, :]
        return transfer

    def gather(full, value):
        full[own_rows, :] = value.astype(BF)
        return over_section(lambda t: full.at[own_rows], full.at[own_rows])

    def landed_sum(landed):
        total = landed[0].astype(F32)
        for k in range(1, ns):
            total = total + landed[k].astype(F32)
        return total

    def normal(value):
        centred = value - jnp.mean(value, axis=-1, keepdims=True)
        rstd = lax.rsqrt(jnp.mean(centred * centred, axis=-1, keepdims=True) + epsilon)
        return centred * rstd, rstd

    def whole_norm(full, gain, bias, dst):
        for t in range(ns):
            at = slice(t * shard, (t + 1) * shard)
            hat, _ = normal(full[at, :].astype(F32))
            dst[at, :] = (hat * gain[...] + bias[...]).astype(BF)

    def kept_norm(full, kept, rstd_kept):
        hat, rstd = normal(full[own_rows, :].astype(F32))
        kept[...] = hat
        rstd_kept[...] = jnp.broadcast_to(rstd, rstd_kept.shape)

    def norm_back(grad, gain, kept, rstd_kept, gain_row, bias_row):
        hat = kept[...]
        sc.vecs[gain_row : gain_row + 1, :] = colsum(grad * hat)
        sc.vecs[bias_row : bias_row + 1, :] = colsum(grad)
        inner = grad * gain[...]
        mean = jnp.mean(inner, axis=-1, keepdims=True)
        dot = jnp.mean(inner * hat, axis=-1, keepdims=True)
        return rstd_kept[:, 0:1] * (inner - mean - hat * dot)

    def transposed(full, dst):
        for j in range(D // CHUNK):
            turned = full[:, j * CHUNK : (j + 1) * CHUNK].astype(F32).T.astype(BF)
            n = dst.shape[0] // (D // CHUNK)
            dst[j * n : (j + 1) * n] = turned.reshape((n,) + dst.shape[1:])

    def by_rows(cols, dst):
        at = pl.ds(s * zq, zq)
        dst[:, :, :, own_cols] = cols[at]
        return over_section(
            lambda t: cols.at[pl.ds(t * zq, zq)], dst.at[:, :, :, own_cols]
        )

    def columns(ref, j):
        return ref[:, :, :, j * CHUNK : (j + 1) * CHUNK].reshape(D, CHUNK)

    def push(src, dst):
        transfer = over_dp(lambda t: src, dst.at[r])
        dst[r] = src[...]
        return transfer

    def summed(dst, count):
        total = dst[0].astype(F32)
        for k in range(1, count):
            total = total + dst[k].astype(F32)
        return total

    q_push = push(sc.q_src, sc.q_recv)
    bv_rs = over_dp(lambda t: sc.bv_src.at[t], sc.bv_recv.at[r])
    sc.bv_recv[r] = sc.bv_src[r]
    g_gather = over_section(lambda t: sc.g_full.at[:, own_cols], sc.g_full.at[:, own_cols])

    q_push.wait_recv()
    query_proj = summed(sc.q_recv, nd)[0:1] + i.agg_bq[:, own_cols]
    sc.query_proj[...] = query_proj
    head_rows = (iota((16, wl), 1) >> 6 == iota((16, wl), 0)).astype(F32)
    high, low = split(head_rows * (query_proj * scale))
    key_query = (nt(high, sc.wk[...]) + nt(low, sc.wk[...])).astype(BF)
    sc.key_query[...] = key_query
    sc.s_src[...] = nn(key_query, sc.basis[...])[0:8]
    s_push = push(sc.s_src, sc.s_recv)
    bv_rs.wait_recv()
    sc.bv_own[...] = summed(sc.bv_recv, nd).astype(sc.bv_own.dtype)
    bv_ag = push(sc.bv_own, sc.bv_all)
    issue_z(3)
    issue_own(6)

    s_push.wait_recv()
    score_rows = summed(sc.s_recv, nd)
    sc.score_rows[...] = score_rows
    fold = sc.fold[...]
    lane_ok = iota((tokens, LANES), 1) < VARS
    for h in range(hl):
        pix = sc.pix[...].astype(F32)
        high, low = split(pix * score_rows[h : h + 1])
        scores = nn(high, fold) + nn(low, fold)
        scores = jnp.where(lane_ok, scores, -1e30)
        scores = jnp.exp(scores - jnp.max(scores, axis=-1, keepdims=True))
        probs = scores / jnp.sum(scores, axis=-1, keepdims=True)
        sc.probs[h] = probs
        wrep = nt(probs.astype(BF), fold)
        sc.wrep[h] = wrep.astype(BF)
        sc.mixed[h] = (wrep * pix).astype(BF)
    issue_z(2)
    forward(1)
    bv_ag.wait_recv()
    for t in range(nd):
        sc.bv[t * blk : (t + 1) * blk] = sc.bv_all[t].astype(F32)
    value_basis = sc.bv[...].astype(BF)
    head_of = iota((1, wl), 1) >> 6
    context = jnp.broadcast_to(i.agg_bv[:, own_cols], (tokens, wl))
    for h in range(hl):
        context = context + jnp.where(head_of == h, nn(sc.mixed[h], value_basis), 0.0)
    sc.context_full[:, own_cols] = context.astype(BF)
    context_gather = over_section(lambda t: sc.context_full.at[:, own_cols], sc.context_full.at[:, own_cols])
    g_gather.wait_recv()
    transposed(sc.g_full, sc.gT)
    issue_own(2)
    forward(1)
    issue_own(1)
    context_gather.wait_recv()
    landed_x(0)
    part = nn(sc.context_full[...], weight(sc.awo_c)) + i.agg_bo[:, own_cols]
    sc.agg_full[:, own_cols] = part.astype(BF)
    agg_gather = over_section(lambda t: sc.agg_full.at[:, own_cols], sc.agg_full.at[:, own_cols])
    transposed(sc.context_full, sc.contextT)
    forward(1)
    agg_gather.wait_recv()
    whole_norm(sc.agg_full, i.attn_norm_gain, i.attn_norm_bias, sc.normed)
    kept_norm(sc.agg_full, sc.hat1, sc.rstd1)
    transposed(sc.normed, sc.normedT)
    forward(1)
    normed = sc.normed[...]
    for j in range(3):
        landed_x(1 + j)
        part = nn(normed, columns(sc.qkv_w, j))
        if j == 0:
            part = part + i.attn_bq[:, own_cols]
        if j == 2:
            part = part + i.attn_bv[:, own_cols]
        sc.qkv[:, j * wl : (j + 1) * wl] = part.astype(BF)
        if j == 1:
            forward(1)
    lo = (iota((1, LANES), 1) < HEAD).astype(F32)
    first, second = lo.astype(BF), (1.0 - lo).astype(BF)

    def pair(a):
        return jnp.concatenate([a * first, a * second], axis=0)

    def pick(a):
        return jnp.where(iota((LEN, LANES), 1) < HEAD, a[0:LEN], a[LEN:])

    tiles = [(b, p) for b in range(tokens // LEN) for p in range(wl // LANES)]

    def tile(ref, b, p, j=0):
        return ref[b * LEN : (b + 1) * LEN, j * wl + p * LANES : j * wl + (p + 1) * LANES]

    for n, (b, p) in enumerate(tiles):
        q, k, v = [tile(sc.qkv, b, p, j) for j in range(3)]
        ids = jnp.broadcast_to(i.segment_ids[b : b + 1, :].astype(F32), (LEN, LEN))
        same = ids == ids.T
        scores = nt(pair(q), k) * scale
        scores = jnp.where(jnp.concatenate([same, same], axis=0), scores, blocked)
        scores = jnp.exp(scores - jnp.max(scores, axis=-1, keepdims=True))
        probs = scores / jnp.sum(scores, axis=-1, keepdims=True)
        sc.att[n] = probs
        sc.attended[b * LEN : (b + 1) * LEN, p * LANES : (p + 1) * LANES] = pick(
            nn(probs.astype(BF), v)
        ).astype(BF)
    sc.attended_full[:, own_cols] = sc.attended[...]
    attended_gather = over_section(
        lambda t: sc.attended_full.at[:, own_cols], sc.attended_full.at[:, own_cols]
    )
    forward(1)
    attended_gather.wait_recv()
    forward(1)
    landed_x(4)
    part = nn(sc.attended_full[...], weight(sc.two_c)) + i.attn_bo[:, own_cols]
    sc.mid_full[:, own_cols] = (part + sc.agg_full[:, own_cols].astype(F32)).astype(BF)
    mid_gather = over_section(lambda t: sc.mid_full.at[:, own_cols], sc.mid_full.at[:, own_cols])
    transposed(sc.attended_full, sc.attendedT)
    forward(1)
    mid_gather.wait_recv()
    awo_rows = by_rows(sc.awo_c, sc.awo)
    two_rows = by_rows(sc.two_c, sc.two)
    whole_norm(sc.mid_full, i.mlp_norm_gain, i.mlp_norm_bias, sc.mnormed)
    kept_norm(sc.mid_full, sc.hat2, sc.rstd2)
    transposed(sc.mnormed, sc.mnormedT)
    forward(1)
    mnormed = sc.mnormed[...]
    for j in range(fl // CHUNK):
        at = slice(j * CHUNK, (j + 1) * CHUNK)
        bias = i.mlp_bup[:, pl.ds(pl.multiple_of(s * fl + j * CHUNK, LANES), CHUNK)]
        landed_x(5 + j)
        hidden = nn(mnormed, columns(sc.up_w, j)) + bias
        phi = 0.5 + 0.5 * lax.erf(hidden * 0.7071067811865476)
        density = jnp.exp(hidden * hidden * -0.5) * 0.3989422804014327
        sc.act[:, at] = (hidden * phi).astype(BF)
        sc.slope[:, at] = phi + hidden * density
        if j == 0:
            forward(1)
        if j == 2:
            forward(1)
    forward(2)
    names = (
        [(o.mlp_down, s * fl + j * CHUNK) for j in range(fl // CHUNK)]
        + [(o.mlp_up, s * fl + j * CHUNK) for j in range(fl // CHUNK)]
        + [(o.attn_wo, s * wl)]
        + [(o.attn_wqkv, j * D + s * wl) for j in range(3)]
        + [(o.agg_wo, s * wl)]
    )
    to_x, to_z, made, done = {}, {}, [], []
    out_copies, out_sends = [], []

    def produce(c, left, right):
        def half(side):
            block = left[:, pl.ds(side, 1)].reshape(nz * rows, tokens)
            return nn(block, right).reshape(nz, rows, CHUNK)

        sc.x_send[c] = half(1 - x).astype(BF)
        made.append(c)
        sc.keep[c] = half(x)

    def issue_x(count):
        fresh = [c for c in made if c >= early and c not in to_x]
        for c in fresh[:count]:
            to_x[c] = over_x(sc.x_send.at[c], sc.x_recv.at[c])

    early = 2
    merged = [early - 1]

    def produce_early(c, left, right):
        for side in range(nx):
            part = nn(left[:, side].reshape(nz * rows, tokens), right)
            sc.e_send[c, :, side] = part.reshape(nz, rows, CHUNK).astype(BF)
        made.append(c)
        to_z[c] = reduce(sc.e_send.at[c], sc.e_recv.at[c], sc.e_merged.at[c])

    def middle_early(c):
        sc.e_sum[c] = to_z[c].total()
        sc.e_out[c] = sc.e_sum[c, 1 - x].astype(BF)
        to_x[c] = over_x(sc.e_out.at[c], sc.e_in.at[c])

    def finish_early(c):
        to_x[c].wait_recv()
        sc.final[c] = (sc.e_sum[c, x] + sc.e_in[c].astype(F32)).astype(BF)
        publish(c, *names[c])

    def middle(c):
        to_x[c].wait_recv()
        if c >= 6:
            issue_x(1)
        sc.z_send[c] = (sc.keep[c] + sc.x_recv[c].astype(F32)).astype(BF)
        to_z[c] = reduce(sc.z_send.at[c], sc.z_recv.at[c], sc.z_merged.at[c])

    def publish(c, array, start):
        dst = array.at[:, pl.ds(pl.multiple_of(start, LANES), CHUNK)]
        out_sends.append(over_section(lambda t: sc.final.at[c], dst))
        out_copies.append(local(sc.final.at[c], dst))

    def finish(c):
        sc.final[c] = to_z[c].total().astype(BF)
        publish(c, *names[c])

    order = list(range(early, 8)) + list(range(early)) + list(range(8, len(names)))

    def pump(count):
        for _ in range(count):
            c = len(to_z)
            if c < len(names):
                middle(c)
            if early < c <= len(names) and merged[-1] < c - 1:
                merged.append(c - 1)
                to_z[c - 1].merge()
            if c == len(names) and merged[-1] < c - 1:
                merged.append(c - 1)
                to_z[c - 1].merge()
            n = order[len(done)] if len(done) < len(names) else len(names)
            if n < early:
                finish_early(n)
                done.append(n)
            elif n < len(names) and (c == len(names) or n < c - 2):
                finish(n)
                done.append(n)

    for j in range(fl // CHUNK):
        make_part = produce_early if j < early else produce
        make_part(j, sc.gT, sc.act[:, j * CHUNK : (j + 1) * CHUNK])
    issue_x(2)
    g_full = sc.g_full[...]
    nmlp = fl // CHUNK
    for j in range(fl // CHUNK):
        at = slice(j * CHUNK, (j + 1) * CHUNK)
        landed_x(5 + nmlp + j)
        d_hidden = nn(g_full, columns(sc.down_w, j)) * sc.slope[:, at]
        sc.d_hidden[:, at] = d_hidden.astype(BF)
    for c in range(early):
        to_z[c].merge()
    up_w = weight(sc.up_w)
    rs3 = scatter(sc.rs3_part, sc.rs3_recv, nt(sc.d_hidden[...], up_w))
    for j in range(nmlp):
        at = slice(j * CHUNK, (j + 1) * CHUNK)
        produce(nmlp + j, sc.mnormedT, sc.d_hidden[:, at])
    sc.bup[:, own_ff] = colsum(sc.d_hidden[...])
    issue_x(4)
    rs3.wait_recv()
    g_shard = sc.g_full[own_rows, :].astype(F32)
    sc.vecs[0:1, :] = colsum(g_shard)
    d_mid = norm_back(landed_sum(sc.rs3_recv), i.mlp_norm_gain, sc.hat2, sc.rstd2, 1, 2)
    d_mid = (g_shard + d_mid).astype(BF)
    sc.vecs[3:4, :] = colsum(d_mid)
    ag3 = gather(sc.d_mid, d_mid)
    d_mid = d_mid.astype(F32)
    for c in range(early):
        middle_early(c)
    sc.out_part[...] = nt(sc.act[...], weight(sc.down_w))
    sc.out_part[own_rows, :] = sc.out_part[own_rows, :] + sc.mid_full[own_rows, :].astype(F32) + i.mlp_bdown[...]
    sc.out_low[...] = sc.out_part[...].astype(BF)
    out_rs = over_section(
        lambda t: sc.out_low.at[:, pl.ds(pl.multiple_of(t * wl, LANES), wl)], sc.out_recv.at[s]
    )
    sc.out_recv[s] = sc.out_low[:, own_cols]
    pump(2)
    ag3.wait_recv()

    pump(1)
    two_rows.wait_recv()
    d_att = nt(sc.d_mid[...], weight(sc.two)).astype(BF)
    sc.d_att[...] = d_att
    for n, (b, p) in enumerate(tiles):
        q, k, v = [tile(sc.qkv, b, p, j) for j in range(3)]
        q, d_out = pair(q), pair(tile(sc.d_att, b, p))
        probs = sc.att[n]
        d_probs = nt(d_out, v)
        d_scores = probs * (d_probs - jnp.sum(probs * d_probs, axis=-1, keepdims=True))
        d_scores = d_scores.astype(BF)
        parts = (pick(nn(d_scores, k)) * scale, tn(d_scores, q) * scale, tn(probs.astype(BF), d_out))
        for j in range(3):
            lanes = slice(j * wl + p * LANES, j * wl + (p + 1) * LANES)
            sc.d_qkv[b * LEN : (b + 1) * LEN, lanes] = parts[j].astype(BF)
    rs4 = scatter(sc.rs4_part, sc.rs4_recv, nt(sc.d_qkv[...], weight(sc.qkv_w)))
    produce(2 * nmlp, sc.attendedT, sc.d_mid[:, own_cols])
    for j in range(3):
        produce(2 * nmlp + 1 + j, sc.normedT, sc.d_qkv[:, j * wl : (j + 1) * wl])
    sc.vecs[7:8, own_cols] = colsum(sc.d_qkv[:, 0:wl])
    sc.vecs[8:9, own_cols] = colsum(sc.d_qkv[:, 2 * wl : 3 * wl])
    pump(1)
    rs4.wait_recv()
    d_agg = norm_back(landed_sum(sc.rs4_recv), i.attn_norm_gain, sc.hat1, sc.rstd1, 4, 5)
    d_agg = (sc.d_mid[own_rows, :].astype(F32) + d_agg).astype(BF)
    sc.vecs[6:7, :] = colsum(d_agg)
    ag4 = gather(sc.d_agg, d_agg)
    pump(2)
    ag4.wait_recv()

    awo_rows.wait_recv()
    produce(2 * nmlp + 4, sc.contextT, sc.d_agg[:, own_cols])
    d_context = nt(sc.d_agg[...], weight(sc.awo)).astype(BF)
    sc.vecs[9:10, own_cols] = colsum(d_context)
    value_basis = sc.bv[...].astype(BF)
    cross = jnp.zeros((CHUNK, wl), F32)
    grad_pix = jnp.zeros((tokens, CHUNK), F32)
    sc.key_src[...] = jnp.zeros_like(sc.key_src)
    for h in range(hl):
        masked = d_context * (head_of == h).astype(F32).astype(BF)
        pulled = nt(masked, value_basis)
        cross = cross + tn(sc.mixed[h], masked)
        pix = sc.pix[...].astype(F32)
        high, low = split(pulled * pix)
        d_weights = nn(high, fold) + nn(low, fold)
        probs = sc.probs[h]
        d_scores = probs * (d_weights - jnp.sum(probs * d_weights, axis=-1, keepdims=True))
        srep = nt(d_scores.astype(BF), fold)
        sc.key_src[h : h + 1, :] = colsum(srep * pix)
        grad_pix = grad_pix + sc.wrep[h].astype(F32) * pulled
        grad_pix = grad_pix + srep * sc.score_rows[h : h + 1, :]
    key_push = push(sc.key_src, sc.key_recv)
    for t in range(nd):
        sc.m_src[t] = cross[t * blk : (t + 1) * blk].astype(sc.m_src.dtype)
    m_rs = over_dp(lambda t: sc.m_src.at[t], sc.m_recv.at[r])
    sc.m_recv[r] = sc.m_src[r]
    grad_pix = grad_pix.astype(BF)
    pw = CP // ns
    for t in range(ns):
        sc.pix_src[t] = nt(sc.place[t * pw : (t + 1) * pw, :], grad_pix).astype(BF)
    pix_rs = over_section(lambda t: sc.pix_src.at[t], sc.pix_recv.at[s])
    sc.pix_recv[s] = sc.pix_src[s]
    for t in range(nd):
        sc.small_src[t, 0:10] = sc.vecs[0:10, t * rows : (t + 1) * rows]
        for j in range(FF // D):
            start = (t * (FF // D) + j) * rows
            sc.small_src[t, 10 + j : 11 + j] = sc.bup[:, start : start + rows]
    small_rs = over_dp(lambda t: sc.small_src.at[t], sc.small_recv.at[r])
    sc.small_recv[r] = sc.small_src[r]

    issue_x(1)
    pump(2)
    m_rs.wait_recv()
    sc.m_own[...] = summed(sc.m_recv, nd).astype(sc.m_own.dtype)
    m_ag = push(sc.m_own, sc.m_all)
    key_push.wait_recv()
    key_terms = summed(sc.key_recv, nd)
    wide = jnp.concatenate([jnp.broadcast_to(key_terms[h : h + 1], (HEAD, CHUNK)) for h in range(hl)], axis=0)
    d_key = nt(sc.basis[...], wide.astype(BF))
    d_query = jnp.sum(sc.wk[...].astype(F32) * d_key, axis=0, keepdims=True) * scale
    sc.dq_src[...] = jnp.broadcast_to(d_query, sc.dq_src.shape)
    dq_push = push(sc.dq_src, sc.dq_recv)
    count = len(names)
    sc.final[count] = (d_key * (sc.query_proj[...] * scale)).astype(BF)
    publish(count, o.agg_wk, s * wl)
    pump(2)
    small_rs.wait_recv()
    sc.sec_small[s] = summed(sc.small_recv, nd)
    small_ag = over_section(lambda t: sc.sec_small.at[s], sc.sec_small.at[s])
    pump(1)
    m_ag.wait_recv()
    for t in range(nd):
        sc.cross[t * blk : (t + 1) * blk] = sc.m_all[t].astype(F32)
    cross = sc.cross[...].astype(BF)
    sc.final[count + 1] = nn(sc.basis[...], cross).astype(BF)
    publish(count + 1, o.agg_wv, s * wl)
    key_low = jnp.concatenate([key_terms, jnp.zeros_like(key_terms)], axis=0).astype(BF)
    grad_basis = nt(cross, sc.wv[...]) + tn(key_low, sc.key_query[...])
    sc.basis_recv[s] = grad_basis.astype(BF)
    basis_sum = over_section(lambda t: sc.basis_recv.at[s], sc.basis_recv.at[s])
    pump(1)
    dq_push.wait_recv()
    o.d_query[s] = summed(sc.dq_recv, nd)
    dq_gather = over_section(lambda t: o.d_query.at[s], o.d_query.at[s])

    def section_total(ref):
        total = ref[0].astype(F32)
        for k in range(1, ns):
            total = total + ref[k].astype(F32)
        return total

    out_rs.wait_recv()
    o.activations[...] = section_total(sc.out_recv).astype(BF)
    pix_rs.wait_recv()
    o.patches[...] = section_total(sc.pix_recv).astype(BF)
    small_ag.wait_recv()
    o.small[...] = summed(sc.sec_small, ns)
    pump(20)
    basis_sum.wait_recv()
    o.basis[...] = section_total(sc.basis_recv)
    dq_gather.wait_recv()
    for transfer in out_sends:
        transfer.wait_recv()
    for copy in out_copies:
        copy.wait()
    for transfer in pending:
        transfer.wait_send()
    assert used["n"] <= send.shape[0], used["n"]
    assert local_used["n"] <= sc.local.shape[0]


def scratch(ns, nd, tokens):
    nz, rows = nd // 2, D // nd
    wl, fl, hl = D // ns, FF // ns, HEADS // ns
    shard, zq, blk = tokens // ns, nz // ns, CHUNK // nd
    chunks = 2 * (fl // CHUNK) + 5
    v = pltpu.VMEM
    shapes = dict(
        wq=v((rows, wl), BF),
        wk=v((rows, wl), BF),
        wv=v((rows, wl), BF),
        qkv_w=v((nz, 2, rows, 3 * wl), BF),
        up_w=v((nz, 2, rows, fl), BF),
        down_w=v((nz, 2, rows, fl), BF),
        awo_c=v((nz, 2, rows, wl), BF),
        two_c=v((nz, 2, rows, wl), BF),
        awo=v((zq, 2, rows, D), BF),
        two=v((zq, 2, rows, D), BF),
        g_full=v((tokens, D), BF),
        place=v((CP, CHUNK), BF),
        pix=v((tokens, CHUNK), BF),
        fold=v((CHUNK, LANES), BF),
        basis=v((rows, CHUNK), BF),
        vecs=v((16, D), F32),
        bup=v((1, FF), F32),
        query_proj=v((1, wl), F32),
        key_query=v((16, rows), BF),
        score_rows=v((8, CHUNK), F32),
        bv=v((CHUNK, CHUNK), F32),
        cross=v((CHUNK, CHUNK), F32),
        e_send=v((2, nz, 2, rows, CHUNK), BF),
        e_recv=v((2, nz, 2, rows, CHUNK), BF),
        e_merged=v((2, 2, 2, rows, CHUNK), BF),
        z_merged=v((chunks, 2, rows, CHUNK), BF),
        e_sum=v((2, 2, rows, CHUNK), F32),
        e_out=v((2, rows, CHUNK), BF),
        e_in=v((2, rows, CHUNK), BF),
        probs=v((hl, tokens, LANES), F32),
        wrep=v((hl, tokens, CHUNK), BF),
        mixed=v((hl, tokens, CHUNK), BF),
        context_full=v((tokens, D), BF),
        attended_full=v((tokens, D), BF),
        agg_full=v((tokens, D), BF),
        mid_full=v((tokens, D), BF),
        hat1=v((shard, D), F32),
        hat2=v((shard, D), F32),
        rstd1=v((shard, LANES), F32),
        rstd2=v((shard, LANES), F32),
        normed=v((tokens, D), BF),
        mnormed=v((tokens, D), BF),
        qkv=v((tokens, 3 * wl), BF),
        d_qkv=v((tokens, 3 * wl), BF),
        att=v((tokens // LEN * (wl // LANES), 2 * LEN, LEN), F32),
        attended=v((tokens, wl), BF),
        d_att=v((tokens, wl), BF),
        act=v((tokens, fl), BF),
        slope=v((tokens, fl), F32),
        d_hidden=v((tokens, fl), BF),
        d_mid=v((tokens, D), BF),
        d_agg=v((tokens, D), BF),
        out_part=v((tokens, D), F32),
        out_low=v((tokens, D), BF),
        out_recv=v((ns, tokens, wl), BF),
        pix_src=v((ns, CP // ns, tokens), BF),
        pix_recv=v((ns, CP // ns, tokens), BF),
        small_src=v((nd, 16, rows), F32),
        small_recv=v((nd, 16, rows), F32),
        sec_small=v((ns, 16, rows), F32),
        basis_recv=v((ns, CHUNK, rows), BF),
        x_send=v((chunks, nz, rows, CHUNK), BF),
        x_recv=v((chunks, nz, rows, CHUNK), BF),
        keep=v((chunks, nz, rows, CHUNK), F32),
        z_send=v((chunks, nz, rows, CHUNK), BF),
        z_recv=v((chunks, nz, rows, CHUNK), BF),
        final=v((chunks + 2, rows, CHUNK), BF),
    )
    whole = v((nz, 2, rows, tokens), BF)
    shapes.update(gT=whole, contextT=whole, attendedT=whole, normedT=whole, mnormedT=whole)
    part = v((tokens, D), BF)
    shapes.update(rs3_part=part, rs4_part=part)
    part = v((ns, shard, D), BF)
    shapes.update(rs3_recv=part, rs4_recv=part)
    part = v((8, CHUNK), F32)
    shapes.update(q_src=part, s_src=part, key_src=part, dq_src=part)
    part = v((nd, 8, CHUNK), F32)
    shapes.update(q_recv=part, s_recv=part, key_recv=part, dq_recv=part)
    kind = BF if blk % 16 == 0 else F32
    part = v((nd, blk, CHUNK), kind)
    shapes.update(bv_src=part, bv_recv=part, bv_all=part, m_src=part, m_recv=part, m_all=part)
    part = v((blk, CHUNK), kind)
    shapes.update(bv_own=part, m_own=part)
    spread, reduced = (8, 5) if nz == 4 else (nz, nz)
    count = 9 * nd + 32 * ns + chunks * (spread + reduced + 6)
    dma = pltpu.SemaphoreType.DMA
    shapes.update(send=dma((count,)), recv=dma((count,)), local=dma((8 + 2 * chunks + 4,)))
    return shapes


def fused(ns, nd, near, far):
    tokens = near["patches"].shape[1]
    rows = D // nd
    shapes = scratch(ns, nd, tokens)
    arrays = {**near, **far}
    hbm = pl.BlockSpec(memory_space=pl.ANY)
    vmem = pl.BlockSpec(memory_space=pltpu.VMEM)
    outs = dict(
        activations=((tokens, D // ns), BF, vmem),
        patches=((CP // ns, tokens), BF, vmem),
        basis=((CHUNK, rows), F32, vmem),
        query_rows=((16, rows), BF, vmem),
        d_query=((ns, 8, D // ns), F32, vmem),
        small=((16, rows), F32, vmem),
        mlp_up=((rows, FF), BF, hbm),
        mlp_down=((rows, FF), BF, hbm),
        attn_wqkv=((rows, 3 * D), BF, hbm),
        attn_wo=((rows, D), BF, hbm),
        agg_wo=((rows, D), BF, hbm),
        agg_wv=((rows, D), BF, hbm),
        agg_wk=((rows, D), BF, hbm),
    )

    def body(*refs):
        n_in, n_out = len(arrays), len(outs)
        kernel(
            ns,
            nd,
            SimpleNamespace(**dict(zip(arrays, refs[:n_in]))),
            SimpleNamespace(**dict(zip(outs, refs[n_in : n_in + n_out]))),
            SimpleNamespace(**dict(zip(shapes, refs[n_in + n_out :]))),
        )

    result = pl.pallas_call(
        body,
        out_shape=[jax.ShapeDtypeStruct(shape, kind) for shape, kind, _ in outs.values()],
        in_specs=[vmem] * len(near) + [hbm] * len(far),
        out_specs=[spec for _, _, spec in outs.values()],
        scratch_shapes=list(shapes.values()),
        compiler_params=pltpu.CompilerParams(
            collective_id=0, has_side_effects=True, vmem_limit_bytes=60 * 1024 * 1024
        ),
        name="block",
    )(*arrays.values())
    return SimpleNamespace(**dict(zip(outs, result)))


def widen(nd, got, agg_wq):
    rows = D // nd
    step = min(rows, 32)
    big = dict(
        mlp_up=got.mlp_up,
        mlp_down=got.mlp_down,
        attn_wqkv=got.attn_wqkv,
        attn_wo=got.attn_wo,
        agg_wo=got.agg_wo,
        agg_wv=got.agg_wv,
        agg_wk=got.agg_wk,
    )
    rest = dict(
        activations=got.activations,
        patches=got.patches,
        basis=got.basis,
        query_rows=got.query_rows,
        d_query=got.d_query,
        small=got.small,
        agg_wq=agg_wq,
    )
    line = (1, rows)
    outs = dict(
        activations=(got.activations.shape, BF),
        patches=(got.patches.shape, BF),
        embed=((CP, rows), F32),
        var=((VARS, rows), F32),
        query=(line, F32),
        wq=((rows, D), F32),
        bq=(line, F32),
        bup=((1, rows * (FF // D)), F32),
    )
    lines = tuple(range(10))

    def body(*refs):
        n = len(big)
        for src, dst in zip(refs[:n], refs[n + len(rest) : 2 * n + len(rest)]):
            dst[...] = src[...].astype(F32)
        i = SimpleNamespace(**dict(zip(rest, refs[n : n + len(rest)])))
        left = refs[2 * n + len(rest) :]
        o = SimpleNamespace(**dict(zip(outs, left)))
        left = left[len(outs) :]
        r = lax.axis_index("dp")

        @pl.when(pl.program_id(0) == 0)
        def _():
            o.activations[...] = i.activations[...]
            o.patches[...] = i.patches[...]
            o.embed[...] = i.basis[0:CP]
            o.var[...] = i.basis[CP : CP + VARS]
            d_query = jnp.concatenate([i.d_query[k] for k in range(i.d_query.shape[0])], axis=1)
            d_query = jnp.concatenate([d_query, d_query], axis=0)
            d_query = jnp.where(iota(d_query.shape, 0) == 0, d_query, 0.0)
            high, low = split(d_query)
            low, rest_low = split(d_query - high.astype(F32))
            chosen = (iota((rows, D), 1) == iota((rows, D), 0) + r * rows).astype(F32).astype(BF)
            o.bq[...] = (nt(high, chosen) + nt(low, chosen) + nt(rest_low, chosen))[0:1]
            weight = i.agg_wq[...]
            o.query[...] = (nt(high, weight) + nt(low, weight) + nt(rest_low, weight))[0:1]
            first = i.query_rows[...]
            o.wq[...] = tn(first, high) + tn(first, low) + tn(first, rest_low)
            o.bup[...] = jnp.concatenate([i.small[10 + k : 11 + k] for k in range(FF // D)], axis=1)
            for k in lines:
                left[k][...] = i.small[k : k + 1]

    def by_step(a):
        return pl.BlockSpec((step, a.shape[1]), lambda g: (g, 0))

    def fixed(shape):
        return pl.BlockSpec(shape, lambda g: (0,) * len(shape))

    shaped = [jax.ShapeDtypeStruct(a.shape, F32) for a in big.values()]
    shaped += [jax.ShapeDtypeStruct(*a) for a in outs.values()]
    shaped += [jax.ShapeDtypeStruct(line, F32) for _ in lines]
    result = pl.pallas_call(
        body,
        grid=(rows // step,),
        out_shape=shaped,
        in_specs=[by_step(a) for a in big.values()] + [fixed(a.shape) for a in rest.values()],
        out_specs=[by_step(a) for a in big.values()] + [fixed(a.shape) for a in shaped[len(big) :]],
        compiler_params=pltpu.CompilerParams(vmem_limit_bytes=60 * 1024 * 1024),
        name="widen",
    )(*big.values(), *rest.values())
    names = list(big) + list(outs)
    return SimpleNamespace(**dict(zip(names, result))), [a.reshape(-1) for a in result[len(names) :]]


def on_device(
    ns,
    nd,
    patches,
    var_ids,
    segment_ids,
    embed_weight,
    var_embed,
    agg_query,
    agg_wq,
    agg_bq,
    agg_wk,
    agg_wv,
    agg_bv,
    agg_wo,
    agg_bo,
    attn_norm_gain,
    attn_norm_bias,
    attn_wqkv,
    attn_bq,
    attn_bv,
    attn_wo,
    attn_bo,
    mlp_norm_gain,
    mlp_norm_bias,
    mlp_up,
    mlp_bup,
    mlp_down,
    mlp_bdown,
    cotangent,
):
    near = dict(
        patches=patches,
        var_ids=var_ids,
        segment_ids=segment_ids,
        embed_weight=embed_weight,
        var_embed=var_embed,
        agg_query=agg_query,
        agg_bq=agg_bq,
        agg_bv=agg_bv,
        agg_bo=agg_bo,
        attn_norm_gain=attn_norm_gain,
        attn_norm_bias=attn_norm_bias,
        attn_bq=attn_bq,
        attn_bv=attn_bv,
        attn_bo=attn_bo,
        mlp_norm_gain=mlp_norm_gain,
        mlp_norm_bias=mlp_norm_bias,
        mlp_bup=mlp_bup,
        mlp_bdown=mlp_bdown,
    )
    far = dict(
        agg_wq=agg_wq,
        agg_wk=agg_wk,
        agg_wv=agg_wv,
        agg_wo=agg_wo,
        attn_wqkv=attn_wqkv,
        attn_wo=attn_wo,
        mlp_up=mlp_up,
        mlp_down=mlp_down,
        cotangent=cotangent,
    )
    near = {name: a.reshape(1, -1) if a.ndim == 1 else a for name, a in near.items()}
    near["patches"], near["embed_weight"] = patches.T, embed_weight.T
    got = fused(ns, nd, near, far)
    out, small = widen(nd, got, agg_wq)
    return (
        out.activations,
        out.patches.T,
        out.embed.T,
        out.var,
        out.query.reshape(-1),
        out.wq,
        out.bq.reshape(-1),
        out.agg_wk,
        out.agg_wv,
        small[9],
        out.agg_wo,
        small[6],
        small[4],
        small[5],
        out.attn_wqkv,
        small[7],
        small[8],
        out.attn_wo,
        small[3],
        small[1],
        small[2],
        out.mlp_up,
        out.bup.reshape(-1),
        out.mlp_down,
        small[0],
    )


def solution(mesh):
    in_specs = (
        P("dp", None),
        P(),
        P("dp", None),
        P("dp", None),
        P(),
        P(),
        P("dp", None),
        P(),
        P("dp", None),
        P("dp", None),
        P(),
        P("dp", None),
        P(),
        P(),
        P(),
        P("dp", None),
        P(),
        P(),
        P("dp", None),
        P(),
        P(),
        P(),
        P("dp", None),
        P(),
        P("dp", None),
        P(),
        P("dp", "section"),
    )
    out_specs = (
        P("dp", "section"),
        P("dp", "section"),
        P("dp", None),
        P(None, "dp"),
        P("dp"),
        P("dp", None),
        P("dp"),
        P("dp", None),
        P("dp", None),
        P("dp"),
        P("dp", None),
        P("dp"),
        P("dp"),
        P("dp"),
        P("dp", None),
        P("dp"),
        P("dp"),
        P("dp", None),
        P("dp"),
        P("dp"),
        P("dp"),
        P("dp", None),
        P("dp"),
        P("dp", None),
        P("dp"),
    )
    sizes = (mesh.shape["section"], mesh.shape["dp"])
    return jax.shard_map(
        partial(on_device, *sizes), mesh=mesh, in_specs=in_specs, out_specs=out_specs, check_vma=False
    )
```

```python
from functools import partial
from types import SimpleNamespace

import jax
import jax.numpy as jnp
from jax import lax
from jax.experimental import pallas as pl
from jax.experimental.pallas import tpu as pltpu
from jax.sharding import PartitionSpec as P

D = 1024
HEADS = 16
HEAD = 64
FF = 4096
VARS = 48
PIX = 4
LEN = 128

highest = lax.Precision.HIGHEST
blocked = -1000000000.0
epsilon = 1e-05
MESH = pl.DeviceIdType.MESH
BF = jnp.bfloat16
F32 = jnp.float32
CHUNK = 256
CP = VARS * PIX
LANES = 128


def nn(a, b):
    return jnp.dot(a, b, preferred_element_type=F32)


def nt(a, b):
    return lax.dot_general(a, b, (((1,), (1,)), ((), ())), preferred_element_type=F32)


def tn(a, b):
    return lax.dot_general(a, b, (((0,), (0,)), ((), ())), preferred_element_type=F32)


def split(x):
    high = x.astype(BF)
    return high, (x - high.astype(F32)).astype(BF)


def iota(shape, dim):
    return lax.broadcasted_iota(jnp.int32, shape, dim)


def colsum(x):
    return jnp.sum(x.astype(F32), axis=0, keepdims=True)


def each(low, high, body):
    if high - low <= 8:
        for k in range(low, high):
            body(k)
    else:

        def step(k, carry):
            body(k)
            return carry

        lax.fori_loop(low, high, step, 0)


class Transfer:
    def __init__(self, make, low, high, whole):
        self.make, self.low, self.high, self.whole = make, low, high, whole

    def start(self):
        each(self.low, self.high, lambda k: self.make(k).start())
        return self

    def wait_recv(self):
        self.whole().wait_recv()

    def wait_send(self):
        self.whole().wait_send()


def kernel(ns, nd, refs_in, refs_out, sc):
    s = lax.axis_index("section")
    r = lax.axis_index("dp")
    nx = 2
    nz = nd // nx
    z, x = lax.div(r, nx), lax.rem(r, nx)
    i, o = refs_in, refs_out
    rows = D // nd
    tokens = i.patches.shape[1]
    shard = tokens // ns
    wl, fl, hl = D // ns, FF // ns, HEADS // ns
    zq = nz // ns
    own_cols = pl.ds(pl.multiple_of(s * wl, LANES), wl)
    own_ff = pl.ds(pl.multiple_of(s * fl, LANES), fl)
    own_rows = pl.ds(pl.multiple_of(s * shard, 16), shard)
    scale = HEAD ** (-0.5)
    send, recv = sc.send, sc.recv
    used = SimpleNamespace(send=0, recv=0, local=0)
    pending = []

    def send_sem():
        used.send += 1
        return used.send - 1

    def recv_sem(count=1):
        used.recv += count
        return used.recv - count

    def remote(src, dst, out, landing, device):
        return pltpu.make_async_remote_copy(
            src_ref=src,
            dst_ref=dst,
            send_sem=send.at[out],
            recv_sem=recv.at[landing],
            device_id=device,
            device_id_type=MESH,
        )

    beside = (s, z * nx + 1 - x)

    def await_sent(ref, out):
        remote(ref, ref, out, 0, beside).wait_send()

    def await_landed(ref, landing):
        remote(ref, ref, 0, landing, beside).wait_recv()

    def all_sent(ref, out):
        pending.append(lambda: await_sent(ref, out))

    def over(peer, count, src, dst, whole, out=None, landing=None):
        alone = out is None
        out = send_sem() if alone else out
        landing = recv_sem() if landing is None else landing

        def make(k):
            t, device = peer(k)
            return remote(src(t), dst, out, landing, device)

        transfer = Transfer(make, 1, count, lambda: remote(whole, whole, out, landing, beside)).start()
        if alone:
            pending.append(transfer.wait_send)
        return transfer

    def section_peer(k):
        t = lax.rem(s + k, ns)
        return t, (t, r)

    def dp_peer(k):
        t = lax.rem(r + k, nd)
        return t, (s, t)

    def z_peer(k):
        t = lax.rem(z + k, nz)
        return t, (s, t * nx + x)

    def over_section(src, dst, whole):
        return over(section_peer, ns, src, dst, whole)

    def over_dp(src, dst, whole):
        return over(dp_peer, nd, src, dst, whole)

    def over_x(src, dst, out, landing=None, whole=None):
        whole = src if whole is None else whole
        return over(lambda k: (0, beside), 2, lambda t: src, dst, whole, out, landing)

    def local(src, dst, sem):
        copy = pltpu.make_async_copy(src, dst, sc.local.at[sem])
        copy.start()
        return copy

    def await_local(ref, sem):
        pltpu.make_async_copy(ref, ref, sc.local.at[sem]).wait()

    line = nz == 4
    partner = z + 1 - 2 * lax.rem(z, 2)
    inner = (z == 1) | (z == 2)
    outer = (z == 0) | (z == 3)
    beyond = [lax.rem(2 * lax.div(z, 2) + 2 + j, 4) for j in range(2)]
    gate = 2 - lax.div(z, 2)

    def at_z(t):
        return (s, t * nx + x)

    blocks = sc.z_recv
    n_pieces = blocks.shape[0]
    crossing = 2 if line else 0

    def spread_group(count):
        own, passed = send_sem(), send_sem()
        whole = blocks.at[0:count, 0 : min(2, nz)] if line else blocks.at[0:count, 0 : nz - 1]
        all_sent(whole, own)
        if line:

            def sent():
                @pl.when(inner)
                def _():
                    await_sent(whole, passed)

            pending.append(sent)
        return own, passed

    first_spread = spread_group(n_pieces)
    second_spread = spread_group(crossing) if crossing else None

    def line_spread(block, group):
        base = recv_sem(3)
        out, out_passed = group
        mine_beyond = base + 1 + lax.rem(z, 2)
        remote(block(z), block(z), out, base, at_z(partner)).start()
        remote(block(z), block(z), out, mine_beyond, at_z(gate)).start()

        def arrived(k):
            t = [partner, *beyond][k]
            await_landed(block(t), base + k)
            if k > 0:

                @pl.when(inner)
                def _():
                    remote(block(t), block(t), out_passed, base + k, at_z(partner)).start()

            return t

        return arrived

    def spread(block, group=first_spread):
        if line:
            return line_spread(block, group)
        whole = blocks.at[0, 0 : nz - 1]
        return over(z_peer, nz, lambda t: block(z), block(z), whole, group[0]).wait_recv

    def reduce_group(count, landed):
        near, far, across = send_sem(), send_sem(), send_sem()
        if not line:
            all_sent(landed.at[0:count, 0 : nz - 1], near)
            return near, far, across
        all_sent(landed.at[0:count, 0], near)

        def sent():
            @pl.when(outer)
            def _():
                await_sent(landed.at[0:count, 0:2], far)

            @pl.when(inner)
            def _():
                await_sent(landed.at[0:count, 0:2], across)

        pending.append(sent)
        return near, far, across

    def line_reduce(parts, landed, merged, group):
        near, far, across = group
        base = recv_sem(3)
        remote(parts.at[partner], landed.at[0], near, base, at_z(partner)).start()

        @pl.when(outer)
        def _():
            for j in range(2):
                remote(parts.at[beyond[j]], landed.at[2 + j], far, base + 1, at_z(partner)).start()

        def merge():
            @pl.when(inner)
            def _():
                await_landed(landed.at[2:4], base + 1)
                for j in range(2):
                    both = parts[beyond[j]].astype(F32) + landed[2 + j].astype(F32)
                    merged[j] = both.astype(BF)
                    remote(merged.at[j], landed.at[1], across, base + 2, at_z(beyond[j])).start()

        def total():
            await_landed(landed.at[0], base)
            await_landed(landed.at[1], base + 2)
            return parts[z].astype(F32) + landed[0].astype(F32) + landed[1].astype(F32)

        return SimpleNamespace(merge=merge, total=total)

    def reduce(parts, landed, merged, group):
        if line:
            return line_reduce(parts, landed, merged, group)
        transfer = over(
            z_peer, nz, lambda t: parts.at[t], landed.at[z], landed.at[0 : nz - 1], group[0]
        )
        landed[z] = parts[z]

        def total():
            transfer.wait_recv()
            value = landed[0].astype(F32)
            for k in range(1, nz):
                value = value + landed[k].astype(F32)
            return value

        return SimpleNamespace(merge=lambda: None, total=total)

    local(i.agg_wq.at[:, own_cols], sc.wq, 0)
    local(i.agg_wk.at[:, own_cols], sc.wk, 0)
    local(i.agg_wv.at[:, own_cols], sc.wv, 0)
    sources = [(i.agg_wo, sc.awo_c, 0, s * wl)]
    sources += [(i.attn_wqkv, sc.qkv_w, j * wl, j * D + s * wl) for j in range(3)]
    sources += [(i.attn_wo, sc.two_c, 0, s * wl)]
    sources += [(i.mlp_up, sc.up_w, j * CHUNK, s * fl + j * CHUNK) for j in range(fl // CHUNK)]
    sources += [(i.mlp_down, sc.down_w, j * CHUNK, s * fl + j * CHUNK) for j in range(fl // CHUNK)]
    pieces = [(dst, pl.ds(at, CHUNK)) for _, dst, at, _ in sources]
    for src, dst, at, col in sources:
        local(src.at[:, pl.ds(pl.multiple_of(col, LANES), CHUNK)], dst.at[z, x, :, pl.ds(at, CHUNK)], 1)
    from_z, from_x, own_x = {}, {}, {}
    late = range(n_pieces - crossing, n_pieces)
    own_order = [*range(6), *late, *range(6, n_pieces - crossing)] if line else []
    from_own, from_others = send_sem(), send_sem()
    if line:
        all_sent(blocks.at[:, 0], from_own)
        all_sent(blocks.at[0 : n_pieces - crossing, 0 : nz - 1], from_others)
    else:
        all_sent(blocks, from_others)
    x_landed = [recv_sem() for _ in range(n_pieces)]

    def issue_own(count):
        for c in own_order[len(own_x) : len(own_x) + count]:
            dst, cols = pieces[c]
            block = dst.at[z, x, :, cols]
            own_x[c] = over_x(block, block, from_own, x_landed[c])

    def issue_z(count):
        for c in range(len(from_z), min(len(from_z) + count, n_pieces)):
            dst, cols = pieces[c]
            from_z[c] = [spread(lambda t, dst=dst, cols=cols: dst.at[t, x, :, cols])]
            if c in late:
                own_x[c].wait_recv()
                other = lambda t, dst=dst, cols=cols: dst.at[t, 1 - x, :, cols]
                from_z[c].append(spread(other, second_spread))

    def forward(count):
        for c in range(len(from_x), min(len(from_x) + count, n_pieces)):
            while line and c not in own_x:
                issue_own(1)
            dst, cols = pieces[c]
            from_x[c] = True
            if not line:
                from_z[c][0]()
                half = dst.at[:, x, :, cols]
                over_x(half, half, from_others, x_landed[c])
            for k in range(nz - 1 if line else 0):
                for arrived in from_z[c]:
                    block = dst.at[arrived(k), x, :, cols]
                if c not in late:
                    over_x(block, block, from_others, x_landed[c])
            issue_z(1)

    def landed_x(c):
        dst, cols = pieces[c]
        if c not in late:
            await_landed(dst.at[:, 0, :, cols], x_landed[c])

    local(i.cotangent, sc.g_full.at[:, own_cols], 2)

    barrier = pltpu.get_barrier_semaphore()
    for k in range(1, ns):
        pl.semaphore_signal(barrier, inc=1, device_id=(lax.rem(s + k, ns), r), device_id_type=MESH)
    each(
        1,
        nd,
        lambda k: pl.semaphore_signal(
            barrier, inc=1, device_id=(s, lax.rem(r + k, nd)), device_id_type=MESH
        ),
    )

    chan = (iota((CP, VARS), 0) >> 2 == iota((CP, VARS), 1)).astype(F32).astype(BF)
    ids = jnp.broadcast_to(i.var_ids[...].astype(F32), (CHUNK, VARS)).astype(BF)
    ids = nt(chan, ids)
    lane = iota((CP, CHUNK), 1)
    row = iota((CP, CHUNK), 0)
    hit = ((lane >> 2).astype(F32) == ids) & ((lane & 3) == (row & 3)) & (lane < CP)
    place = hit.astype(F32).astype(BF)
    sc.place[...] = place
    lane = iota((tokens, CHUNK), 1)
    ones = ((lane >= CP) & (lane < CP + VARS)).astype(F32)
    sc.pix[...] = (tn(i.patches[...], place) + ones).astype(BF)
    row = iota((CHUNK, LANES), 0)
    lane = iota((CHUNK, LANES), 1)
    owner = jnp.where(row < CP, row >> 2, row - CP)
    sc.fold[...] = ((owner == lane) & (lane < VARS)).astype(F32).astype(BF)
    chosen = (iota((rows, D), 1) == iota((rows, D), 0) + r * rows).astype(F32).astype(BF)
    lane = iota((CP, CHUNK), 1)
    row = iota((CP, CHUNK), 0)
    widen = (lane == row).astype(F32).astype(BF)
    lane = iota((VARS, CHUNK), 1)
    row = iota((VARS, CHUNK), 0)
    widen_var = (lane == row + CP).astype(F32).astype(BF)
    var_rows = nt(chosen, i.var_embed[...].astype(BF)).astype(BF)
    sc.basis[...] = (tn(i.embed_weight[...], widen) + nn(var_rows, widen_var)).astype(BF)
    query = jnp.broadcast_to(i.agg_query[...].astype(BF).astype(F32), (16, D))
    query = jnp.where(iota((16, D), 0) == 0, query, 0.0).astype(BF)
    query_rows = nt(query, chosen).astype(BF)
    o.query_rows[...] = query_rows
    sc.vecs[...] = jnp.zeros_like(sc.vecs)
    sc.bup[...] = jnp.zeros_like(sc.bup)

    await_local(blocks.at[0:3, 0], 0)
    sc.q_src[...] = nn(query_rows, sc.wq[...])[0:8]
    value_part = tn(sc.basis[...], sc.wv[...])
    blk = CHUNK // nd
    for t in range(nd):
        sc.bv_src[t] = value_part[t * blk : (t + 1) * blk].astype(sc.bv_src.dtype)
    await_local(sc.g_full.at[:, own_cols], 2)
    await_local(blocks.at[:, 0], 1)

    pl.semaphore_wait(barrier, ns - 1 + nd - 1)

    def weight(ref):
        return ref[...].reshape(ref.shape[0] * ref.shape[1] * ref.shape[2], ref.shape[3])

    def scatter(part, landed, value):
        part[...] = value.astype(BF)
        transfer = over_section(lambda t: part.at[pl.ds(pl.multiple_of(t * shard, 16), shard)], landed.at[s], landed.at[0 : ns - 1])
        landed[s] = part[own_rows, :]
        return transfer

    def gather(full, value):
        full[own_rows, :] = value.astype(BF)
        return over_section(lambda t: full.at[own_rows], full.at[own_rows], full.at[0 : (ns - 1) * shard])

    def landed_sum(landed):
        total = landed[0].astype(F32)
        for k in range(1, ns):
            total = total + landed[k].astype(F32)
        return total

    def normal(value):
        centred = value - jnp.mean(value, axis=-1, keepdims=True)
        rstd = lax.rsqrt(jnp.mean(centred * centred, axis=-1, keepdims=True) + epsilon)
        return centred * rstd, rstd

    def whole_norm(full, gain, bias, dst):
        for t in range(ns):
            at = slice(t * shard, (t + 1) * shard)
            hat, _ = normal(full[at, :].astype(F32))
            dst[at, :] = (hat * gain[...] + bias[...]).astype(BF)

    def kept_norm(full, kept, rstd_kept):
        hat, rstd = normal(full[own_rows, :].astype(F32))
        kept[...] = hat
        rstd_kept[...] = jnp.broadcast_to(rstd, rstd_kept.shape)

    def norm_back(grad, gain, kept, rstd_kept, gain_row, bias_row):
        hat = kept[...]
        sc.vecs[gain_row : gain_row + 1, :] = colsum(grad * hat)
        sc.vecs[bias_row : bias_row + 1, :] = colsum(grad)
        inner = grad * gain[...]
        mean = jnp.mean(inner, axis=-1, keepdims=True)
        dot = jnp.mean(inner * hat, axis=-1, keepdims=True)
        return rstd_kept[:, 0:1] * (inner - mean - hat * dot)

    def transposed(full, dst):
        for j in range(D // CHUNK):
            turned = full[:, j * CHUNK : (j + 1) * CHUNK].astype(F32).T.astype(BF)
            n = dst.shape[0] // (D // CHUNK)
            dst[j * n : (j + 1) * n] = turned.reshape((n,) + dst.shape[1:])

    def by_rows(cols, dst):
        at = pl.ds(s * zq, zq)
        dst[:, :, :, own_cols] = cols[at]
        return over_section(
            lambda t: cols.at[pl.ds(t * zq, zq)], dst.at[:, :, :, own_cols], dst.at[:, :, :, 0 : (ns - 1) * wl]
        )

    def gather_cols(full):
        block = full.at[:, own_cols]
        return over_section(lambda t: block, block, full.at[:, 0 : (ns - 1) * wl])

    def columns(ref, j):
        return ref[:, :, :, j * CHUNK : (j + 1) * CHUNK].reshape(D, CHUNK)

    def push(src, dst):
        transfer = over_dp(lambda t: src, dst.at[r], dst.at[0 : nd - 1])
        dst[r] = src[...]
        return transfer

    def summed(dst, count):
        total = dst[0].astype(F32)
        for k in range(1, count):
            total = total + dst[k].astype(F32)
        return total

    q_push = push(sc.q_src, sc.q_recv)
    bv_rs = over_dp(lambda t: sc.bv_src.at[t], sc.bv_recv.at[r], sc.bv_recv.at[0 : nd - 1])
    sc.bv_recv[r] = sc.bv_src[r]
    g_gather = gather_cols(sc.g_full)

    issue_own(2)
    q_push.wait_recv()
    query_proj = summed(sc.q_recv, nd)[0:1] + i.agg_bq[:, own_cols]
    sc.query_proj[...] = query_proj
    head_rows = (iota((16, wl), 1) >> 6 == iota((16, wl), 0)).astype(F32)
    high, low = split(head_rows * (query_proj * scale))
    key_query = (nt(high, sc.wk[...]) + nt(low, sc.wk[...])).astype(BF)
    sc.key_query[...] = key_query
    sc.s_src[...] = nn(key_query, sc.basis[...])[0:8]
    s_push = push(sc.s_src, sc.s_recv)
    bv_rs.wait_recv()
    sc.bv_own[...] = summed(sc.bv_recv, nd).astype(sc.bv_own.dtype)
    bv_ag = push(sc.bv_own, sc.bv_all)
    issue_z(3)
    issue_own(4)

    s_push.wait_recv()
    score_rows = summed(sc.s_recv, nd)
    sc.score_rows[...] = score_rows
    fold = sc.fold[...]
    lane_ok = iota((tokens, LANES), 1) < VARS
    for h in range(hl):
        pix = sc.pix[...].astype(F32)
        high, low = split(pix * score_rows[h : h + 1])
        scores = nn(high, fold) + nn(low, fold)
        scores = jnp.where(lane_ok, scores, -1e30)
        scores = jnp.exp(scores - jnp.max(scores, axis=-1, keepdims=True))
        probs = scores / jnp.sum(scores, axis=-1, keepdims=True)
        sc.probs[h] = probs
        wrep = nt(probs.astype(BF), fold)
        sc.wrep[h] = wrep.astype(BF)
        sc.mixed[h] = (wrep * pix).astype(BF)
    issue_z(2)
    forward(1)
    bv_ag.wait_recv()
    for t in range(nd):
        sc.bv[t * blk : (t + 1) * blk] = sc.bv_all[t].astype(F32)
    value_basis = sc.bv[...].astype(BF)
    head_of = iota((1, wl), 1) >> 6
    context = jnp.broadcast_to(i.agg_bv[:, own_cols], (tokens, wl))
    for h in range(hl):
        context = context + jnp.where(head_of == h, nn(sc.mixed[h], value_basis), 0.0)
    sc.context_full[:, own_cols] = context.astype(BF)
    context_gather = gather_cols(sc.context_full)
    g_gather.wait_recv()
    transposed(sc.g_full, sc.gT)
    issue_own(2)
    forward(1)
    issue_own(1)
    context_gather.wait_recv()
    landed_x(0)
    part = nn(sc.context_full[...], weight(sc.awo_c)) + i.agg_bo[:, own_cols]
    sc.agg_full[:, own_cols] = part.astype(BF)
    agg_gather = gather_cols(sc.agg_full)
    transposed(sc.context_full, sc.contextT)
    forward(1)
    agg_gather.wait_recv()
    whole_norm(sc.agg_full, i.attn_norm_gain, i.attn_norm_bias, sc.normed)
    kept_norm(sc.agg_full, sc.hat1, sc.rstd1)
    transposed(sc.normed, sc.normedT)
    forward(1)
    normed = sc.normed[...]
    for j in range(3):
        landed_x(1 + j)
        part = nn(normed, columns(sc.qkv_w, j))
        if j == 0:
            part = part + i.attn_bq[:, own_cols]
        if j == 2:
            part = part + i.attn_bv[:, own_cols]
        sc.qkv[:, j * wl : (j + 1) * wl] = part.astype(BF)
        if j == 1:
            forward(1)
    lo = (iota((1, LANES), 1) < HEAD).astype(F32)
    first, second = lo.astype(BF), (1.0 - lo).astype(BF)

    def pair(a):
        return jnp.concatenate([a * first, a * second], axis=0)

    def pick(a):
        return jnp.where(iota((LEN, LANES), 1) < HEAD, a[0:LEN], a[LEN:])

    tiles = [(b, p) for b in range(tokens // LEN) for p in range(wl // LANES)]

    def tile(ref, b, p, j=0):
        return ref[b * LEN : (b + 1) * LEN, j * wl + p * LANES : j * wl + (p + 1) * LANES]

    for n, (b, p) in enumerate(tiles):
        q, k, v = [tile(sc.qkv, b, p, j) for j in range(3)]
        ids = jnp.broadcast_to(i.segment_ids[b : b + 1, :].astype(F32), (LEN, LEN))
        same = ids == ids.T
        scores = nt(pair(q), k) * scale
        scores = jnp.where(jnp.concatenate([same, same], axis=0), scores, blocked)
        scores = jnp.exp(scores - jnp.max(scores, axis=-1, keepdims=True))
        probs = scores / jnp.sum(scores, axis=-1, keepdims=True)
        sc.att[n] = probs
        sc.attended[b * LEN : (b + 1) * LEN, p * LANES : (p + 1) * LANES] = pick(
            nn(probs.astype(BF), v)
        ).astype(BF)
    sc.attended_full[:, own_cols] = sc.attended[...]
    attended_gather = gather_cols(sc.attended_full)
    forward(1)
    attended_gather.wait_recv()
    forward(1)
    landed_x(4)
    part = nn(sc.attended_full[...], weight(sc.two_c)) + i.attn_bo[:, own_cols]
    sc.mid_full[:, own_cols] = (part + sc.agg_full[:, own_cols].astype(F32)).astype(BF)
    mid_gather = gather_cols(sc.mid_full)
    transposed(sc.attended_full, sc.attendedT)
    forward(1)
    mid_gather.wait_recv()
    awo_rows = by_rows(sc.awo_c, sc.awo)
    two_rows = by_rows(sc.two_c, sc.two)
    whole_norm(sc.mid_full, i.mlp_norm_gain, i.mlp_norm_bias, sc.mnormed)
    kept_norm(sc.mid_full, sc.hat2, sc.rstd2)
    transposed(sc.mnormed, sc.mnormedT)
    forward(1)
    mnormed = sc.mnormed[...]
    for j in range(fl // CHUNK):
        at = slice(j * CHUNK, (j + 1) * CHUNK)
        bias = i.mlp_bup[:, pl.ds(pl.multiple_of(s * fl + j * CHUNK, LANES), CHUNK)]
        landed_x(5 + j)
        hidden = nn(mnormed, columns(sc.up_w, j)) + bias
        phi = 0.5 + 0.5 * lax.erf(hidden * 0.7071067811865476)
        density = jnp.exp(hidden * hidden * -0.5) * 0.3989422804014327
        sc.act[:, at] = (hidden * phi).astype(BF)
        sc.slope[:, at] = phi + hidden * density
        if j == 0:
            forward(1)
        if j == 2:
            forward(1)
    forward(2)
    names = (
        [(o.mlp_down, s * fl + j * CHUNK) for j in range(fl // CHUNK)]
        + [(o.mlp_up, s * fl + j * CHUNK) for j in range(fl // CHUNK)]
        + [(o.attn_wo, s * wl)]
        + [(o.attn_wqkv, j * D + s * wl) for j in range(3)]
        + [(o.agg_wo, s * wl)]
    )
    to_x, to_z, made, done = {}, {}, [], []
    published = [(send_sem(), recv_sem()) for _ in range(ns)]
    early = 2
    chunk_x, early_x = send_sem(), send_sem()
    all_sent(blocks.at[early:], chunk_x)
    all_sent(blocks.at[0:early, 0], early_x)
    chunk_z = reduce_group(n_pieces - early, sc.z_recv)
    early_z = reduce_group(early, sc.e_recv)

    def produce(c, left, right):
        def half(side):
            block = left[:, pl.ds(side, 1)].reshape(nz * rows, tokens)
            return nn(block, right).reshape(nz, rows, CHUNK)

        sc.x_send[c] = half(1 - x).astype(BF)
        made.append(c)
        sc.keep[c] = half(x)

    def issue_x(count):
        fresh = [c for c in made if c >= early and c not in to_x]
        for c in fresh[:count]:
            to_x[c] = over_x(sc.x_send.at[c], sc.x_recv.at[c], chunk_x)

    merged = [early - 1]

    def produce_early(c, left, right):
        for side in range(nx):
            part = nn(left[:, side].reshape(nz * rows, tokens), right)
            sc.e_send[c, :, side] = part.reshape(nz, rows, CHUNK).astype(BF)
        made.append(c)
        to_z[c] = reduce(sc.e_send.at[c], sc.e_recv.at[c], sc.e_merged.at[c], early_z)

    def middle_early(c):
        sc.e_sum[c] = to_z[c].total()
        sc.e_out[c] = sc.e_sum[c, 1 - x].astype(BF)
        to_x[c] = over_x(sc.e_out.at[c], sc.e_in.at[c], early_x)

    def finish_early(c):
        to_x[c].wait_recv()
        sc.final[c] = (sc.e_sum[c, x] + sc.e_in[c].astype(F32)).astype(BF)
        publish(c, *names[c])

    def middle(c):
        to_x[c].wait_recv()
        issue_x(1)
        sc.z_send[c] = (sc.keep[c] + sc.x_recv[c].astype(F32)).astype(BF)
        to_z[c] = reduce(sc.z_send.at[c], sc.z_recv.at[c], sc.z_merged.at[c], chunk_z)

    def publish(c, array, start):
        dst = array.at[:, pl.ds(pl.multiple_of(start, LANES), CHUNK)]
        for k in range(1, ns):
            remote(sc.final.at[c], dst, *published[k], section_peer(k)[1]).start()
        local(sc.final.at[c], dst, 3)

    def finish(c):
        sc.final[c] = to_z[c].total().astype(BF)
        publish(c, *names[c])

    def finish_up_to(last):
        for c in range(early, last + 1):
            if c not in done:
                finish(c)
                done.append(c)

    def pump(count):
        for _ in range(count):
            c = len(to_z)
            middle(c)
            if c > early:
                to_z[c - 1].merge()
            if early + 3 <= c < 2 * early + 3:
                finish_early(c - early - 3)
            finish_up_to(c - 3)

    for j in range(fl // CHUNK):
        make_part = produce_early if j < early else produce
        make_part(j, sc.gT, sc.act[:, j * CHUNK : (j + 1) * CHUNK])
    issue_x(2)
    g_full = sc.g_full[...]
    nmlp = fl // CHUNK
    for j in range(fl // CHUNK):
        at = slice(j * CHUNK, (j + 1) * CHUNK)
        landed_x(5 + nmlp + j)
        d_hidden = nn(g_full, columns(sc.down_w, j)) * sc.slope[:, at]
        sc.d_hidden[:, at] = d_hidden.astype(BF)
    for c in range(early):
        to_z[c].merge()
    up_w = weight(sc.up_w)
    rs3 = scatter(sc.rs3_part, sc.rs3_recv, nt(sc.d_hidden[...], up_w))
    for j in range(nmlp):
        at = slice(j * CHUNK, (j + 1) * CHUNK)
        produce(nmlp + j, sc.mnormedT, sc.d_hidden[:, at])
    sc.bup[:, own_ff] = colsum(sc.d_hidden[...])
    issue_x(1)
    rs3.wait_recv()
    g_shard = sc.g_full[own_rows, :].astype(F32)
    sc.vecs[0:1, :] = colsum(g_shard)
    d_mid = norm_back(landed_sum(sc.rs3_recv), i.mlp_norm_gain, sc.hat2, sc.rstd2, 1, 2)
    d_mid = (g_shard + d_mid).astype(BF)
    sc.vecs[3:4, :] = colsum(d_mid)
    ag3 = gather(sc.d_mid, d_mid)
    d_mid = d_mid.astype(F32)
    for c in range(early):
        middle_early(c)
    sc.out_part[...] = nt(sc.act[...], weight(sc.down_w))
    sc.out_part[own_rows, :] = sc.out_part[own_rows, :] + sc.mid_full[own_rows, :].astype(F32) + i.mlp_bdown[...]
    sc.out_low[...] = sc.out_part[...].astype(BF)
    out_rs = over_section(
        lambda t: sc.out_low.at[:, pl.ds(pl.multiple_of(t * wl, LANES), wl)],
        sc.out_recv.at[s],
        sc.out_recv.at[0 : ns - 1],
    )
    sc.out_recv[s] = sc.out_low[:, own_cols]
    pump(2)
    ag3.wait_recv()

    pump(1)
    two_rows.wait_recv()
    d_att = nt(sc.d_mid[...], weight(sc.two)).astype(BF)
    sc.d_att[...] = d_att
    for n, (b, p) in enumerate(tiles):
        q, k, v = [tile(sc.qkv, b, p, j) for j in range(3)]
        q, d_out = pair(q), pair(tile(sc.d_att, b, p))
        probs = sc.att[n]
        d_probs = nt(d_out, v)
        d_scores = probs * (d_probs - jnp.sum(probs * d_probs, axis=-1, keepdims=True))
        d_scores = d_scores.astype(BF)
        parts = (pick(nn(d_scores, k)) * scale, tn(d_scores, q) * scale, tn(probs.astype(BF), d_out))
        for j in range(3):
            lanes = slice(j * wl + p * LANES, j * wl + (p + 1) * LANES)
            sc.d_qkv[b * LEN : (b + 1) * LEN, lanes] = parts[j].astype(BF)
    rs4 = scatter(sc.rs4_part, sc.rs4_recv, nt(sc.d_qkv[...], weight(sc.qkv_w)))
    produce(2 * nmlp, sc.attendedT, sc.d_mid[:, own_cols])
    for j in range(3):
        produce(2 * nmlp + 1 + j, sc.normedT, sc.d_qkv[:, j * wl : (j + 1) * wl])
    sc.vecs[7:8, own_cols] = colsum(sc.d_qkv[:, 0:wl])
    sc.vecs[8:9, own_cols] = colsum(sc.d_qkv[:, 2 * wl : 3 * wl])
    pump(1)
    rs4.wait_recv()
    d_agg = norm_back(landed_sum(sc.rs4_recv), i.attn_norm_gain, sc.hat1, sc.rstd1, 4, 5)
    d_agg = (sc.d_mid[own_rows, :].astype(F32) + d_agg).astype(BF)
    sc.vecs[6:7, :] = colsum(d_agg)
    ag4 = gather(sc.d_agg, d_agg)
    pump(2)
    ag4.wait_recv()

    awo_rows.wait_recv()
    produce(2 * nmlp + 4, sc.contextT, sc.d_agg[:, own_cols])
    d_context = nt(sc.d_agg[...], weight(sc.awo)).astype(BF)
    sc.vecs[9:10, own_cols] = colsum(d_context)
    value_basis = sc.bv[...].astype(BF)
    cross = jnp.zeros((CHUNK, wl), F32)
    grad_pix = jnp.zeros((tokens, CHUNK), F32)
    sc.key_src[...] = jnp.zeros_like(sc.key_src)
    for h in range(hl):
        masked = d_context * (head_of == h).astype(F32).astype(BF)
        pulled = nt(masked, value_basis)
        cross = cross + tn(sc.mixed[h], masked)
        pix = sc.pix[...].astype(F32)
        high, low = split(pulled * pix)
        d_weights = nn(high, fold) + nn(low, fold)
        probs = sc.probs[h]
        d_scores = probs * (d_weights - jnp.sum(probs * d_weights, axis=-1, keepdims=True))
        srep = nt(d_scores.astype(BF), fold)
        sc.key_src[h : h + 1, :] = colsum(srep * pix)
        grad_pix = grad_pix + sc.wrep[h].astype(F32) * pulled
        grad_pix = grad_pix + srep * sc.score_rows[h : h + 1, :]
    key_push = push(sc.key_src, sc.key_recv)
    for t in range(nd):
        sc.m_src[t] = cross[t * blk : (t + 1) * blk].astype(sc.m_src.dtype)
    m_rs = over_dp(lambda t: sc.m_src.at[t], sc.m_recv.at[r], sc.m_recv.at[0 : nd - 1])
    sc.m_recv[r] = sc.m_src[r]
    grad_pix = grad_pix.astype(BF)
    pw = CP // ns
    for t in range(ns):
        sc.pix_src[t] = nt(sc.place[t * pw : (t + 1) * pw, :], grad_pix).astype(BF)
    pix_rs = over_section(lambda t: sc.pix_src.at[t], sc.pix_recv.at[s], sc.pix_recv.at[0 : ns - 1])
    sc.pix_recv[s] = sc.pix_src[s]
    for t in range(nd):
        sc.small_src[t, 0:10] = sc.vecs[0:10, t * rows : (t + 1) * rows]
        for j in range(FF // D):
            start = (t * (FF // D) + j) * rows
            sc.small_src[t, 10 + j : 11 + j] = sc.bup[:, start : start + rows]
    small_rs = over_dp(lambda t: sc.small_src.at[t], sc.small_recv.at[r], sc.small_recv.at[0 : nd - 1])
    sc.small_recv[r] = sc.small_src[r]

    issue_x(1)
    pump(2)
    m_rs.wait_recv()
    sc.m_own[...] = summed(sc.m_recv, nd).astype(sc.m_own.dtype)
    m_ag = push(sc.m_own, sc.m_all)
    key_push.wait_recv()
    key_terms = summed(sc.key_recv, nd)
    wide = jnp.concatenate([jnp.broadcast_to(key_terms[h : h + 1], (HEAD, CHUNK)) for h in range(hl)], axis=0)
    d_key = nt(sc.basis[...], wide.astype(BF))
    d_query = jnp.sum(sc.wk[...].astype(F32) * d_key, axis=0, keepdims=True) * scale
    sc.dq_src[...] = jnp.broadcast_to(d_query, sc.dq_src.shape)
    dq_push = push(sc.dq_src, sc.dq_recv)
    count = len(names)
    sc.final[count] = (d_key * (sc.query_proj[...] * scale)).astype(BF)
    publish(count, o.agg_wk, s * wl)
    pump(2)
    small_rs.wait_recv()
    sc.sec_small[s] = summed(sc.small_recv, nd)
    small_ag = over_section(lambda t: sc.sec_small.at[s], sc.sec_small.at[s], sc.sec_small.at[0 : ns - 1])
    pump(1)
    m_ag.wait_recv()
    for t in range(nd):
        sc.cross[t * blk : (t + 1) * blk] = sc.m_all[t].astype(F32)
    cross = sc.cross[...].astype(BF)
    sc.final[count + 1] = nn(sc.basis[...], cross).astype(BF)
    publish(count + 1, o.agg_wv, s * wl)
    key_low = jnp.concatenate([key_terms, jnp.zeros_like(key_terms)], axis=0).astype(BF)
    grad_basis = nt(cross, sc.wv[...]) + tn(key_low, sc.key_query[...])
    sc.basis_recv[s] = grad_basis.astype(BF)
    basis_sum = over_section(lambda t: sc.basis_recv.at[s], sc.basis_recv.at[s], sc.basis_recv.at[0 : ns - 1])
    finish_up_to(len(names) - 3)
    to_z[len(names) - 1].merge()
    dq_push.wait_recv()
    o.d_query[s] = summed(sc.dq_recv, nd)
    dq_gather = over_section(lambda t: o.d_query.at[s], o.d_query.at[s], o.d_query.at[0 : ns - 1])

    def section_total(ref):
        total = ref[0].astype(F32)
        for k in range(1, ns):
            total = total + ref[k].astype(F32)
        return total

    out_rs.wait_recv()
    o.activations[...] = section_total(sc.out_recv).astype(BF)
    pix_rs.wait_recv()
    o.patches[...] = section_total(sc.pix_recv).astype(BF)
    small_ag.wait_recv()
    o.small[...] = summed(sc.sec_small, ns)
    finish_up_to(len(names) - 1)
    basis_sum.wait_recv()
    o.basis[...] = section_total(sc.basis_recv)
    dq_gather.wait_recv()
    for k in range(1, ns):
        await_landed(sc.final, published[k][1])
        await_sent(sc.final, published[k][0])
    await_local(sc.final, 3)
    for wait in pending:
        wait()
    assert used.send <= send.shape[0] and used.recv <= recv.shape[0], used


def scratch(ns, nd, tokens):
    nz, rows = nd // 2, D // nd
    wl, fl, hl = D // ns, FF // ns, HEADS // ns
    shard, zq, blk = tokens // ns, nz // ns, CHUNK // nd
    chunks = 2 * (fl // CHUNK) + 5
    v = pltpu.VMEM
    shapes = dict(
        wq=v((rows, wl), BF),
        wk=v((rows, wl), BF),
        wv=v((rows, wl), BF),
        qkv_w=v((nz, 2, rows, 3 * wl), BF),
        up_w=v((nz, 2, rows, fl), BF),
        down_w=v((nz, 2, rows, fl), BF),
        awo_c=v((nz, 2, rows, wl), BF),
        two_c=v((nz, 2, rows, wl), BF),
        awo=v((zq, 2, rows, D), BF),
        two=v((zq, 2, rows, D), BF),
        g_full=v((tokens, D), BF),
        place=v((CP, CHUNK), BF),
        pix=v((tokens, CHUNK), BF),
        fold=v((CHUNK, LANES), BF),
        basis=v((rows, CHUNK), BF),
        vecs=v((16, D), F32),
        bup=v((1, FF), F32),
        query_proj=v((1, wl), F32),
        key_query=v((16, rows), BF),
        score_rows=v((8, CHUNK), F32),
        bv=v((CHUNK, CHUNK), F32),
        cross=v((CHUNK, CHUNK), F32),
        e_send=v((2, nz, 2, rows, CHUNK), BF),
        e_recv=v((2, nz, 2, rows, CHUNK), BF),
        e_merged=v((2, 2, 2, rows, CHUNK), BF),
        z_merged=v((chunks, 2, rows, CHUNK), BF),
        e_sum=v((2, 2, rows, CHUNK), F32),
        e_out=v((2, rows, CHUNK), BF),
        e_in=v((2, rows, CHUNK), BF),
        probs=v((hl, tokens, LANES), F32),
        wrep=v((hl, tokens, CHUNK), BF),
        mixed=v((hl, tokens, CHUNK), BF),
        context_full=v((tokens, D), BF),
        attended_full=v((tokens, D), BF),
        agg_full=v((tokens, D), BF),
        mid_full=v((tokens, D), BF),
        hat1=v((shard, D), F32),
        hat2=v((shard, D), F32),
        rstd1=v((shard, LANES), F32),
        rstd2=v((shard, LANES), F32),
        normed=v((tokens, D), BF),
        mnormed=v((tokens, D), BF),
        qkv=v((tokens, 3 * wl), BF),
        d_qkv=v((tokens, 3 * wl), BF),
        att=v((tokens // LEN * (wl // LANES), 2 * LEN, LEN), F32),
        attended=v((tokens, wl), BF),
        d_att=v((tokens, wl), BF),
        act=v((tokens, fl), BF),
        slope=v((tokens, fl), F32),
        d_hidden=v((tokens, fl), BF),
        d_mid=v((tokens, D), BF),
        d_agg=v((tokens, D), BF),
        out_part=v((tokens, D), F32),
        out_low=v((tokens, D), BF),
        out_recv=v((ns, tokens, wl), BF),
        pix_src=v((ns, CP // ns, tokens), BF),
        pix_recv=v((ns, CP // ns, tokens), BF),
        small_src=v((nd, 16, rows), F32),
        small_recv=v((nd, 16, rows), F32),
        sec_small=v((ns, 16, rows), F32),
        basis_recv=v((ns, CHUNK, rows), BF),
        x_send=v((chunks, nz, rows, CHUNK), BF),
        x_recv=v((chunks, nz, rows, CHUNK), BF),
        keep=v((chunks, nz, rows, CHUNK), F32),
        z_send=v((chunks, nz, rows, CHUNK), BF),
        z_recv=v((chunks, nz, rows, CHUNK), BF),
        final=v((chunks + 2, rows, CHUNK), BF),
    )
    whole = v((nz, 2, rows, tokens), BF)
    shapes.update(gT=whole, contextT=whole, attendedT=whole, normedT=whole, mnormedT=whole)
    part = v((tokens, D), BF)
    shapes.update(rs3_part=part, rs4_part=part)
    part = v((ns, shard, D), BF)
    shapes.update(rs3_recv=part, rs4_recv=part)
    part = v((8, CHUNK), F32)
    shapes.update(q_src=part, s_src=part, key_src=part, dq_src=part)
    part = v((nd, 8, CHUNK), F32)
    shapes.update(q_recv=part, s_recv=part, key_recv=part, dq_recv=part)
    kind = BF if blk % 16 == 0 else F32
    part = v((nd, blk, CHUNK), kind)
    shapes.update(bv_src=part, bv_recv=part, bv_all=part, m_src=part, m_recv=part, m_all=part)
    part = v((blk, CHUNK), kind)
    shapes.update(bv_own=part, m_own=part)
    dma = pltpu.SemaphoreType.DMA
    shapes.update(send=dma((48,)), recv=dma((160,)), local=dma((4,)))
    return shapes


def fused(ns, nd, near, far):
    tokens = near["patches"].shape[1]
    rows = D // nd
    shapes = scratch(ns, nd, tokens)
    arrays = {**near, **far}
    hbm = pl.BlockSpec(memory_space=pl.ANY)
    vmem = pl.BlockSpec(memory_space=pltpu.VMEM)
    outs = dict(
        activations=((tokens, D // ns), BF, vmem),
        patches=((CP // ns, tokens), BF, vmem),
        basis=((CHUNK, rows), F32, vmem),
        query_rows=((16, rows), BF, vmem),
        d_query=((ns, 8, D // ns), F32, vmem),
        small=((16, rows), F32, vmem),
        mlp_up=((rows, FF), BF, hbm),
        mlp_down=((rows, FF), BF, hbm),
        attn_wqkv=((rows, 3 * D), BF, hbm),
        attn_wo=((rows, D), BF, hbm),
        agg_wo=((rows, D), BF, hbm),
        agg_wv=((rows, D), BF, hbm),
        agg_wk=((rows, D), BF, hbm),
    )

    def body(*refs):
        n_in, n_out = len(arrays), len(outs)
        kernel(
            ns,
            nd,
            SimpleNamespace(**dict(zip(arrays, refs[:n_in]))),
            SimpleNamespace(**dict(zip(outs, refs[n_in : n_in + n_out]))),
            SimpleNamespace(**dict(zip(shapes, refs[n_in + n_out :]))),
        )

    result = pl.pallas_call(
        body,
        out_shape=[jax.ShapeDtypeStruct(shape, kind) for shape, kind, _ in outs.values()],
        in_specs=[vmem] * len(near) + [hbm] * len(far),
        out_specs=[spec for _, _, spec in outs.values()],
        scratch_shapes=list(shapes.values()),
        compiler_params=pltpu.CompilerParams(
            collective_id=0, has_side_effects=True, vmem_limit_bytes=60 * 1024 * 1024
        ),
        name="block",
    )(*arrays.values())
    return SimpleNamespace(**dict(zip(outs, result)))


def widen(nd, got, agg_wq):
    rows = D // nd
    step = min(rows, 32)
    big = dict(
        mlp_up=got.mlp_up,
        mlp_down=got.mlp_down,
        attn_wqkv=got.attn_wqkv,
        attn_wo=got.attn_wo,
        agg_wo=got.agg_wo,
        agg_wv=got.agg_wv,
        agg_wk=got.agg_wk,
    )
    rest = dict(
        activations=got.activations,
        patches=got.patches,
        basis=got.basis,
        query_rows=got.query_rows,
        d_query=got.d_query,
        small=got.small,
        agg_wq=agg_wq,
    )
    line = (1, rows)
    outs = dict(
        activations=(got.activations.shape, BF),
        patches=(got.patches.shape, BF),
        embed=((CP, rows), F32),
        var=((VARS, rows), F32),
        query=(line, F32),
        wq=((rows, D), F32),
        bq=(line, F32),
        bup=((1, rows * (FF // D)), F32),
    )
    lines = tuple(range(10))

    def body(*refs):
        n = len(big)
        for src, dst in zip(refs[:n], refs[n + len(rest) : 2 * n + len(rest)]):
            dst[...] = src[...].astype(F32)
        i = SimpleNamespace(**dict(zip(rest, refs[n : n + len(rest)])))
        left = refs[2 * n + len(rest) :]
        o = SimpleNamespace(**dict(zip(outs, left)))
        left = left[len(outs) :]
        r = lax.axis_index("dp")

        @pl.when(pl.program_id(0) == 0)
        def _():
            o.activations[...] = i.activations[...]
            o.patches[...] = i.patches[...]
            o.embed[...] = i.basis[0:CP]
            o.var[...] = i.basis[CP : CP + VARS]
            d_query = jnp.concatenate([i.d_query[k] for k in range(i.d_query.shape[0])], axis=1)
            d_query = jnp.concatenate([d_query, d_query], axis=0)
            d_query = jnp.where(iota(d_query.shape, 0) == 0, d_query, 0.0)
            high, low = split(d_query)
            low, rest_low = split(d_query - high.astype(F32))
            chosen = (iota((rows, D), 1) == iota((rows, D), 0) + r * rows).astype(F32).astype(BF)
            o.bq[...] = (nt(high, chosen) + nt(low, chosen) + nt(rest_low, chosen))[0:1]
            weight = i.agg_wq[...]
            o.query[...] = (nt(high, weight) + nt(low, weight) + nt(rest_low, weight))[0:1]
            first = i.query_rows[...]
            o.wq[...] = tn(first, high) + tn(first, low) + tn(first, rest_low)
            o.bup[...] = jnp.concatenate([i.small[10 + k : 11 + k] for k in range(FF // D)], axis=1)
            for k in lines:
                left[k][...] = i.small[k : k + 1]

    def by_step(a):
        return pl.BlockSpec((step, a.shape[1]), lambda g: (g, 0))

    def fixed(shape):
        return pl.BlockSpec(shape, lambda g: (0,) * len(shape))

    shaped = [jax.ShapeDtypeStruct(a.shape, F32) for a in big.values()]
    shaped += [jax.ShapeDtypeStruct(*a) for a in outs.values()]
    shaped += [jax.ShapeDtypeStruct(line, F32) for _ in lines]
    result = pl.pallas_call(
        body,
        grid=(rows // step,),
        out_shape=shaped,
        in_specs=[by_step(a) for a in big.values()] + [fixed(a.shape) for a in rest.values()],
        out_specs=[by_step(a) for a in big.values()] + [fixed(a.shape) for a in shaped[len(big) :]],
        compiler_params=pltpu.CompilerParams(vmem_limit_bytes=60 * 1024 * 1024),
        name="widen",
    )(*big.values(), *rest.values())
    names = list(big) + list(outs)
    return SimpleNamespace(**dict(zip(names, result))), [a.reshape(-1) for a in result[len(names) :]]


def on_device(
    ns,
    nd,
    patches,
    var_ids,
    segment_ids,
    embed_weight,
    var_embed,
    agg_query,
    agg_wq,
    agg_bq,
    agg_wk,
    agg_wv,
    agg_bv,
    agg_wo,
    agg_bo,
    attn_norm_gain,
    attn_norm_bias,
    attn_wqkv,
    attn_bq,
    attn_bv,
    attn_wo,
    attn_bo,
    mlp_norm_gain,
    mlp_norm_bias,
    mlp_up,
    mlp_bup,
    mlp_down,
    mlp_bdown,
    cotangent,
):
    near = dict(
        patches=patches,
        var_ids=var_ids,
        segment_ids=segment_ids,
        embed_weight=embed_weight,
        var_embed=var_embed,
        agg_query=agg_query,
        agg_bq=agg_bq,
        agg_bv=agg_bv,
        agg_bo=agg_bo,
        attn_norm_gain=attn_norm_gain,
        attn_norm_bias=attn_norm_bias,
        attn_bq=attn_bq,
        attn_bv=attn_bv,
        attn_bo=attn_bo,
        mlp_norm_gain=mlp_norm_gain,
        mlp_norm_bias=mlp_norm_bias,
        mlp_bup=mlp_bup,
        mlp_bdown=mlp_bdown,
    )
    far = dict(
        agg_wq=agg_wq,
        agg_wk=agg_wk,
        agg_wv=agg_wv,
        agg_wo=agg_wo,
        attn_wqkv=attn_wqkv,
        attn_wo=attn_wo,
        mlp_up=mlp_up,
        mlp_down=mlp_down,
        cotangent=cotangent,
    )
    near = {name: a.reshape(1, -1) if a.ndim == 1 else a for name, a in near.items()}
    near["patches"], near["embed_weight"] = patches.T, embed_weight.T
    got = fused(ns, nd, near, far)
    out, small = widen(nd, got, agg_wq)
    return (
        out.activations,
        out.patches.T,
        out.embed.T,
        out.var,
        out.query.reshape(-1),
        out.wq,
        out.bq.reshape(-1),
        out.agg_wk,
        out.agg_wv,
        small[9],
        out.agg_wo,
        small[6],
        small[4],
        small[5],
        out.attn_wqkv,
        small[7],
        small[8],
        out.attn_wo,
        small[3],
        small[1],
        small[2],
        out.mlp_up,
        out.bup.reshape(-1),
        out.mlp_down,
        small[0],
    )


def solution(mesh):
    in_specs = (
        P("dp", None),
        P(),
        P("dp", None),
        P("dp", None),
        P(),
        P(),
        P("dp", None),
        P(),
        P("dp", None),
        P("dp", None),
        P(),
        P("dp", None),
        P(),
        P(),
        P(),
        P("dp", None),
        P(),
        P(),
        P("dp", None),
        P(),
        P(),
        P(),
        P("dp", None),
        P(),
        P("dp", None),
        P(),
        P("dp", "section"),
    )
    out_specs = (
        P("dp", "section"),
        P("dp", "section"),
        P("dp", None),
        P(None, "dp"),
        P("dp"),
        P("dp", None),
        P("dp"),
        P("dp", None),
        P("dp", None),
        P("dp"),
        P("dp", None),
        P("dp"),
        P("dp"),
        P("dp"),
        P("dp", None),
        P("dp"),
        P("dp"),
        P("dp", None),
        P("dp"),
        P("dp"),
        P("dp"),
        P("dp", None),
        P("dp"),
        P("dp", None),
        P("dp"),
    )
    sizes = (mesh.shape["section"], mesh.shape["dp"])
    return jax.shard_map(
        partial(on_device, *sizes), mesh=mesh, in_specs=in_specs, out_specs=out_specs, check_vma=False
    )
```

```python
from functools import partial
from types import SimpleNamespace

import jax
import jax.numpy as jnp
from jax import lax
from jax.experimental import pallas as pl
from jax.experimental.pallas import tpu as pltpu
from jax.sharding import PartitionSpec as P

D = 1024
HEADS = 16
HEAD = 64
FF = 4096
VARS = 48
PIX = 4
LEN = 128

highest = lax.Precision.HIGHEST
blocked = -1000000000.0
epsilon = 1e-05
MESH = pl.DeviceIdType.MESH
BF = jnp.bfloat16
F32 = jnp.float32
CHUNK = 256
CP = VARS * PIX
LANES = 128


def nn(a, b):
    return jnp.dot(a, b, preferred_element_type=F32)


def nt(a, b):
    return lax.dot_general(a, b, (((1,), (1,)), ((), ())), preferred_element_type=F32)


def tn(a, b):
    return lax.dot_general(a, b, (((0,), (0,)), ((), ())), preferred_element_type=F32)


def split(x):
    high = x.astype(BF)
    return high, (x - high.astype(F32)).astype(BF)


def iota(shape, dim):
    return lax.broadcasted_iota(jnp.int32, shape, dim)


def colsum(x):
    return jnp.sum(x.astype(F32), axis=0, keepdims=True)


def each(low, high, body):
    if high - low <= 8:
        for k in range(low, high):
            body(k)
    else:

        def step(k, carry):
            body(k)
            return carry

        lax.fori_loop(low, high, step, 0)


class Transfer:
    def __init__(self, make, low, high, whole):
        self.make, self.low, self.high, self.whole = make, low, high, whole

    def start(self):
        each(self.low, self.high, lambda k: self.make(k).start())
        return self

    def wait_recv(self):
        self.whole().wait_recv()

    def wait_send(self):
        self.whole().wait_send()


def kernel(ns, nd, refs_in, refs_out, sc):
    s = lax.axis_index("section")
    r = lax.axis_index("dp")
    nx = 2
    nz = nd // nx
    z, x = lax.div(r, nx), lax.rem(r, nx)
    i, o = refs_in, refs_out
    rows = D // nd
    tokens = i.patches.shape[1]
    shard = tokens // ns
    wl, fl, hl = D // ns, FF // ns, HEADS // ns
    zq = nz // ns
    own_cols = pl.ds(pl.multiple_of(s * wl, LANES), wl)
    own_ff = pl.ds(pl.multiple_of(s * fl, LANES), fl)
    own_rows = pl.ds(pl.multiple_of(s * shard, 16), shard)
    scale = HEAD ** (-0.5)
    send, recv = sc.send, sc.recv
    used = SimpleNamespace(send=0, recv=0, local=0)
    pending = []

    def send_sem():
        used.send += 1
        return used.send - 1

    def recv_sem(count=1):
        used.recv += count
        return used.recv - count

    def remote(src, dst, out, landing, device):
        return pltpu.make_async_remote_copy(
            src_ref=src,
            dst_ref=dst,
            send_sem=send.at[out],
            recv_sem=recv.at[landing],
            device_id=device,
            device_id_type=MESH,
        )

    beside = (s, z * nx + 1 - x)

    def await_sent(ref, out):
        remote(ref, ref, out, 0, beside).wait_send()

    def await_landed(ref, landing):
        remote(ref, ref, 0, landing, beside).wait_recv()

    def all_sent(ref, out):
        pending.append(lambda: await_sent(ref, out))

    def over(peer, count, src, dst, whole, out=None, landing=None):
        alone = out is None
        out = send_sem() if alone else out
        landing = recv_sem() if landing is None else landing

        def make(k):
            t, device = peer(k)
            return remote(src(t), dst, out, landing, device)

        transfer = Transfer(make, 1, count, lambda: remote(whole, whole, out, landing, beside)).start()
        if alone:
            pending.append(transfer.wait_send)
        return transfer

    def section_peer(k):
        t = lax.rem(s + k, ns)
        return t, (t, r)

    def dp_peer(k):
        t = lax.rem(r + k, nd)
        return t, (s, t)

    def z_peer(k):
        t = lax.rem(z + k, nz)
        return t, (s, t * nx + x)

    def over_section(src, dst, whole):
        return over(section_peer, ns, src, dst, whole)

    def over_dp(src, dst, whole):
        return over(dp_peer, nd, src, dst, whole)

    def over_x(src, dst, out, landing=None, whole=None):
        whole = src if whole is None else whole
        return over(lambda k: (0, beside), 2, lambda t: src, dst, whole, out, landing)

    def local(src, dst, sem):
        copy = pltpu.make_async_copy(src, dst, sc.local.at[sem])
        copy.start()
        return copy

    def await_local(ref, sem):
        pltpu.make_async_copy(ref, ref, sc.local.at[sem]).wait()

    line = nz == 4
    partner = z + 1 - 2 * lax.rem(z, 2)
    inner = (z == 1) | (z == 2)
    outer = (z == 0) | (z == 3)
    beyond = [lax.rem(2 * lax.div(z, 2) + 2 + j, 4) for j in range(2)]
    gate = 2 - lax.div(z, 2)

    def at_z(t):
        return (s, t * nx + x)

    blocks = sc.z_recv
    n_pieces = blocks.shape[0]
    crossing = 2 if line else 0

    def spread_group(count):
        own, passed = send_sem(), send_sem()
        whole = blocks.at[0:count, 0 : min(2, nz)] if line else blocks.at[0:count, 0 : nz - 1]
        all_sent(whole, own)
        if line:

            def sent():
                @pl.when(inner)
                def _():
                    await_sent(whole, passed)

            pending.append(sent)
        return own, passed

    first_spread = spread_group(n_pieces)
    second_spread = spread_group(crossing) if crossing else None

    def line_spread(block, group):
        base = recv_sem(3)
        out, out_passed = group
        mine_beyond = base + 1 + lax.rem(z, 2)
        remote(block(z), block(z), out, base, at_z(partner)).start()
        remote(block(z), block(z), out, mine_beyond, at_z(gate)).start()

        def arrived(k):
            t = [partner, *beyond][k]
            await_landed(block(t), base + k)
            if k > 0:

                @pl.when(inner)
                def _():
                    remote(block(t), block(t), out_passed, base + k, at_z(partner)).start()

            return t

        return arrived

    def spread(block, group=first_spread):
        if line:
            return line_spread(block, group)
        whole = blocks.at[0, 0 : nz - 1]
        return over(z_peer, nz, lambda t: block(z), block(z), whole, group[0]).wait_recv

    def reduce_group(count, landed):
        near, far, across = send_sem(), send_sem(), send_sem()
        if not line:
            all_sent(landed.at[0:count, 0 : nz - 1], near)
            return near, far, across
        all_sent(landed.at[0:count, 0], near)

        def sent():
            @pl.when(outer)
            def _():
                await_sent(landed.at[0:count, 0:2], far)

            @pl.when(inner)
            def _():
                await_sent(landed.at[0:count, 0:2], across)

        pending.append(sent)
        return near, far, across

    def line_reduce(parts, landed, merged, group, hold):
        near, far, across = group
        base = recv_sem(3)

        def first():
            remote(parts.at[partner], landed.at[0], near, base, at_z(partner)).start()

        def begin():
            pl.when(inner)(first)

        @pl.when(outer)
        def _():
            first()
            for j in range(2):
                remote(parts.at[beyond[j]], landed.at[2 + j], far, base + 1, at_z(partner)).start()

        if not hold:
            begin()

        def merge():
            @pl.when(inner)
            def _():
                await_landed(landed.at[2:4], base + 1)
                for j in range(2):
                    both = parts[beyond[j]].astype(F32) + landed[2 + j].astype(F32)
                    merged[j] = both.astype(BF)
                    remote(merged.at[j], landed.at[1], across, base + 2, at_z(beyond[j])).start()

        def total():
            await_landed(landed.at[0], base)
            await_landed(landed.at[1], base + 2)
            return parts[z].astype(F32) + landed[0].astype(F32) + landed[1].astype(F32)

        return SimpleNamespace(begin=begin, merge=merge, total=total)

    def reduce(parts, landed, merged, group, hold=False):
        if line:
            return line_reduce(parts, landed, merged, group, hold)
        transfer = over(
            z_peer, nz, lambda t: parts.at[t], landed.at[z], landed.at[0 : nz - 1], group[0]
        )
        landed[z] = parts[z]

        def total():
            transfer.wait_recv()
            value = landed[0].astype(F32)
            for k in range(1, nz):
                value = value + landed[k].astype(F32)
            return value

        return SimpleNamespace(begin=lambda: None, merge=lambda: None, total=total)

    local(i.agg_wq.at[:, own_cols], sc.wq, 0)
    local(i.agg_wk.at[:, own_cols], sc.wk, 0)
    local(i.agg_wv.at[:, own_cols], sc.wv, 0)
    sources = [(i.agg_wo, sc.awo_c, 0, s * wl)]
    sources += [(i.attn_wqkv, sc.qkv_w, j * wl, j * D + s * wl) for j in range(3)]
    sources += [(i.attn_wo, sc.two_c, 0, s * wl)]
    sources += [(i.mlp_up, sc.up_w, j * CHUNK, s * fl + j * CHUNK) for j in range(fl // CHUNK)]
    sources += [(i.mlp_down, sc.down_w, j * CHUNK, s * fl + j * CHUNK) for j in range(fl // CHUNK)]
    pieces = [(dst, pl.ds(at, CHUNK)) for _, dst, at, _ in sources]
    for src, dst, at, col in sources:
        local(src.at[:, pl.ds(pl.multiple_of(col, LANES), CHUNK)], dst.at[z, x, :, pl.ds(at, CHUNK)], 1)
    from_z, from_x, own_x = {}, {}, {}
    late = range(n_pieces - crossing, n_pieces)
    own_order = [*range(6), *late, *range(6, n_pieces - crossing)] if line else []
    from_own, from_others = send_sem(), send_sem()
    if line:
        all_sent(blocks.at[:, 0], from_own)
        all_sent(blocks.at[0 : n_pieces - crossing, 0 : nz - 1], from_others)
    else:
        all_sent(blocks, from_others)
    x_landed = [recv_sem() for _ in range(n_pieces)]

    def issue_own(count):
        for c in own_order[len(own_x) : len(own_x) + count]:
            dst, cols = pieces[c]
            block = dst.at[z, x, :, cols]
            own_x[c] = over_x(block, block, from_own, x_landed[c])

    def issue_z(count):
        for c in range(len(from_z), min(len(from_z) + count, n_pieces)):
            dst, cols = pieces[c]
            from_z[c] = [spread(lambda t, dst=dst, cols=cols: dst.at[t, x, :, cols])]
            if c in late:
                own_x[c].wait_recv()
                other = lambda t, dst=dst, cols=cols: dst.at[t, 1 - x, :, cols]
                from_z[c].append(spread(other, second_spread))

    def forward(count):
        for c in range(len(from_x), min(len(from_x) + count, n_pieces)):
            while line and c not in own_x:
                issue_own(1)
            dst, cols = pieces[c]
            from_x[c] = True
            if not line:
                from_z[c][0]()
                half = dst.at[:, x, :, cols]
                over_x(half, half, from_others, x_landed[c])
            for k in range(nz - 1 if line else 0):
                for arrived in from_z[c]:
                    block = dst.at[arrived(k), x, :, cols]
                if c not in late:
                    over_x(block, block, from_others, x_landed[c])
            issue_z(1)

    def landed_x(c):
        dst, cols = pieces[c]
        if c not in late:
            await_landed(dst.at[:, 0, :, cols], x_landed[c])

    local(i.cotangent, sc.g_full.at[:, own_cols], 2)

    barrier = pltpu.get_barrier_semaphore()
    for k in range(1, ns):
        pl.semaphore_signal(barrier, inc=1, device_id=(lax.rem(s + k, ns), r), device_id_type=MESH)
    each(
        1,
        nd,
        lambda k: pl.semaphore_signal(
            barrier, inc=1, device_id=(s, lax.rem(r + k, nd)), device_id_type=MESH
        ),
    )

    chan = (iota((CP, VARS), 0) >> 2 == iota((CP, VARS), 1)).astype(F32).astype(BF)
    ids = jnp.broadcast_to(i.var_ids[...].astype(F32), (CHUNK, VARS)).astype(BF)
    ids = nt(chan, ids)
    lane = iota((CP, CHUNK), 1)
    row = iota((CP, CHUNK), 0)
    hit = ((lane >> 2).astype(F32) == ids) & ((lane & 3) == (row & 3)) & (lane < CP)
    place = hit.astype(F32).astype(BF)
    sc.place[...] = place
    lane = iota((tokens, CHUNK), 1)
    ones = ((lane >= CP) & (lane < CP + VARS)).astype(F32)
    sc.pix[...] = (tn(i.patches[...], place) + ones).astype(BF)
    row = iota((CHUNK, LANES), 0)
    lane = iota((CHUNK, LANES), 1)
    owner = jnp.where(row < CP, row >> 2, row - CP)
    sc.fold[...] = ((owner == lane) & (lane < VARS)).astype(F32).astype(BF)
    chosen = (iota((rows, D), 1) == iota((rows, D), 0) + r * rows).astype(F32).astype(BF)
    lane = iota((CP, CHUNK), 1)
    row = iota((CP, CHUNK), 0)
    widen = (lane == row).astype(F32).astype(BF)
    lane = iota((VARS, CHUNK), 1)
    row = iota((VARS, CHUNK), 0)
    widen_var = (lane == row + CP).astype(F32).astype(BF)
    var_rows = nt(chosen, i.var_embed[...].astype(BF)).astype(BF)
    sc.basis[...] = (tn(i.embed_weight[...], widen) + nn(var_rows, widen_var)).astype(BF)
    query = jnp.broadcast_to(i.agg_query[...].astype(BF).astype(F32), (16, D))
    query = jnp.where(iota((16, D), 0) == 0, query, 0.0).astype(BF)
    query_rows = nt(query, chosen).astype(BF)
    o.query_rows[...] = query_rows
    sc.vecs[...] = jnp.zeros_like(sc.vecs)
    sc.bup[...] = jnp.zeros_like(sc.bup)

    await_local(blocks.at[0:3, 0], 0)
    sc.q_src[...] = nn(query_rows, sc.wq[...])[0:8]
    value_part = tn(sc.basis[...], sc.wv[...])
    blk = CHUNK // nd
    for t in range(nd):
        sc.bv_src[t] = value_part[t * blk : (t + 1) * blk].astype(sc.bv_src.dtype)
    await_local(sc.g_full.at[:, own_cols], 2)
    await_local(blocks.at[:, 0], 1)

    pl.semaphore_wait(barrier, ns - 1 + nd - 1)

    def weight(ref):
        return ref[...].reshape(ref.shape[0] * ref.shape[1] * ref.shape[2], ref.shape[3])

    def scatter(part, landed, value):
        part[...] = value.astype(BF)
        transfer = over_section(lambda t: part.at[pl.ds(pl.multiple_of(t * shard, 16), shard)], landed.at[s], landed.at[0 : ns - 1])
        landed[s] = part[own_rows, :]
        return transfer

    def gather(full, value):
        full[own_rows, :] = value.astype(BF)
        return over_section(lambda t: full.at[own_rows], full.at[own_rows], full.at[0 : (ns - 1) * shard])

    def landed_sum(landed):
        total = landed[0].astype(F32)
        for k in range(1, ns):
            total = total + landed[k].astype(F32)
        return total

    def normal(value):
        centred = value - jnp.mean(value, axis=-1, keepdims=True)
        rstd = lax.rsqrt(jnp.mean(centred * centred, axis=-1, keepdims=True) + epsilon)
        return centred * rstd, rstd

    def whole_norm(full, gain, bias, dst):
        for t in range(ns):
            at = slice(t * shard, (t + 1) * shard)
            hat, _ = normal(full[at, :].astype(F32))
            dst[at, :] = (hat * gain[...] + bias[...]).astype(BF)

    def kept_norm(full, kept, rstd_kept):
        hat, rstd = normal(full[own_rows, :].astype(F32))
        kept[...] = hat
        rstd_kept[...] = jnp.broadcast_to(rstd, rstd_kept.shape)

    def norm_back(grad, gain, kept, rstd_kept, gain_row, bias_row):
        hat = kept[...]
        sc.vecs[gain_row : gain_row + 1, :] = colsum(grad * hat)
        sc.vecs[bias_row : bias_row + 1, :] = colsum(grad)
        inner = grad * gain[...]
        mean = jnp.mean(inner, axis=-1, keepdims=True)
        dot = jnp.mean(inner * hat, axis=-1, keepdims=True)
        return rstd_kept[:, 0:1] * (inner - mean - hat * dot)

    def transposed(full, dst):
        for j in range(D // CHUNK):
            turned = full[:, j * CHUNK : (j + 1) * CHUNK].astype(F32).T.astype(BF)
            n = dst.shape[0] // (D // CHUNK)
            dst[j * n : (j + 1) * n] = turned.reshape((n,) + dst.shape[1:])

    def by_rows(cols, dst):
        at = pl.ds(s * zq, zq)
        dst[:, :, :, own_cols] = cols[at]
        return over_section(
            lambda t: cols.at[pl.ds(t * zq, zq)], dst.at[:, :, :, own_cols], dst.at[:, :, :, 0 : (ns - 1) * wl]
        )

    def gather_cols(full):
        block = full.at[:, own_cols]
        return over_section(lambda t: block, block, full.at[:, 0 : (ns - 1) * wl])

    def columns(ref, j):
        return ref[:, :, :, j * CHUNK : (j + 1) * CHUNK].reshape(D, CHUNK)

    def push(src, dst):
        transfer = over_dp(lambda t: src, dst.at[r], dst.at[0 : nd - 1])
        dst[r] = src[...]
        return transfer

    def summed(dst, count):
        total = dst[0].astype(F32)
        for k in range(1, count):
            total = total + dst[k].astype(F32)
        return total

    q_push = push(sc.q_src, sc.q_recv)
    bv_rs = over_dp(lambda t: sc.bv_src.at[t], sc.bv_recv.at[r], sc.bv_recv.at[0 : nd - 1])
    sc.bv_recv[r] = sc.bv_src[r]
    g_gather = gather_cols(sc.g_full)

    issue_own(2)
    issue_z(1)
    q_push.wait_recv()
    query_proj = summed(sc.q_recv, nd)[0:1] + i.agg_bq[:, own_cols]
    sc.query_proj[...] = query_proj
    head_rows = (iota((16, wl), 1) >> 6 == iota((16, wl), 0)).astype(F32)
    high, low = split(head_rows * (query_proj * scale))
    key_query = (nt(high, sc.wk[...]) + nt(low, sc.wk[...])).astype(BF)
    sc.key_query[...] = key_query
    sc.s_src[...] = nn(key_query, sc.basis[...])[0:8]
    s_push = push(sc.s_src, sc.s_recv)
    bv_rs.wait_recv()
    sc.bv_own[...] = summed(sc.bv_recv, nd).astype(sc.bv_own.dtype)
    bv_ag = push(sc.bv_own, sc.bv_all)
    issue_z(2)
    issue_own(4)

    s_push.wait_recv()
    score_rows = summed(sc.s_recv, nd)
    sc.score_rows[...] = score_rows
    fold = sc.fold[...]
    lane_ok = iota((tokens, LANES), 1) < VARS
    for h in range(hl):
        pix = sc.pix[...].astype(F32)
        high, low = split(pix * score_rows[h : h + 1])
        scores = nn(high, fold) + nn(low, fold)
        scores = jnp.where(lane_ok, scores, -1e30)
        scores = jnp.exp(scores - jnp.max(scores, axis=-1, keepdims=True))
        probs = scores / jnp.sum(scores, axis=-1, keepdims=True)
        sc.probs[h] = probs
        wrep = nt(probs.astype(BF), fold)
        sc.wrep[h] = wrep.astype(BF)
        sc.mixed[h] = (wrep * pix).astype(BF)
    issue_z(2)
    forward(1)
    bv_ag.wait_recv()
    for t in range(nd):
        sc.bv[t * blk : (t + 1) * blk] = sc.bv_all[t].astype(F32)
    value_basis = sc.bv[...].astype(BF)
    head_of = iota((1, wl), 1) >> 6
    context = jnp.broadcast_to(i.agg_bv[:, own_cols], (tokens, wl))
    for h in range(hl):
        context = context + jnp.where(head_of == h, nn(sc.mixed[h], value_basis), 0.0)
    sc.context_full[:, own_cols] = context.astype(BF)
    context_gather = gather_cols(sc.context_full)
    g_gather.wait_recv()
    transposed(sc.g_full, sc.gT)
    issue_own(2)
    forward(1)
    issue_own(1)
    context_gather.wait_recv()
    landed_x(0)
    part = nn(sc.context_full[...], weight(sc.awo_c)) + i.agg_bo[:, own_cols]
    sc.agg_full[:, own_cols] = part.astype(BF)
    agg_gather = gather_cols(sc.agg_full)
    transposed(sc.context_full, sc.contextT)
    forward(1)
    agg_gather.wait_recv()
    whole_norm(sc.agg_full, i.attn_norm_gain, i.attn_norm_bias, sc.normed)
    kept_norm(sc.agg_full, sc.hat1, sc.rstd1)
    transposed(sc.normed, sc.normedT)
    forward(1)
    normed = sc.normed[...]
    for j in range(3):
        landed_x(1 + j)
        part = nn(normed, columns(sc.qkv_w, j))
        if j == 0:
            part = part + i.attn_bq[:, own_cols]
        if j == 2:
            part = part + i.attn_bv[:, own_cols]
        sc.qkv[:, j * wl : (j + 1) * wl] = part.astype(BF)
        if j == 1:
            forward(1)
    lo = (iota((1, LANES), 1) < HEAD).astype(F32)
    first, second = lo.astype(BF), (1.0 - lo).astype(BF)

    def pair(a):
        return jnp.concatenate([a * first, a * second], axis=0)

    def pick(a):
        return jnp.where(iota((LEN, LANES), 1) < HEAD, a[0:LEN], a[LEN:])

    tiles = [(b, p) for b in range(tokens // LEN) for p in range(wl // LANES)]

    def tile(ref, b, p, j=0):
        return ref[b * LEN : (b + 1) * LEN, j * wl + p * LANES : j * wl + (p + 1) * LANES]

    for n, (b, p) in enumerate(tiles):
        q, k, v = [tile(sc.qkv, b, p, j) for j in range(3)]
        ids = jnp.broadcast_to(i.segment_ids[b : b + 1, :].astype(F32), (LEN, LEN))
        same = ids == ids.T
        scores = nt(pair(q), k) * scale
        scores = jnp.where(jnp.concatenate([same, same], axis=0), scores, blocked)
        scores = jnp.exp(scores - jnp.max(scores, axis=-1, keepdims=True))
        probs = scores / jnp.sum(scores, axis=-1, keepdims=True)
        sc.att[n] = probs
        sc.attended[b * LEN : (b + 1) * LEN, p * LANES : (p + 1) * LANES] = pick(
            nn(probs.astype(BF), v)
        ).astype(BF)
    sc.attended_full[:, own_cols] = sc.attended[...]
    attended_gather = gather_cols(sc.attended_full)
    forward(1)
    attended_gather.wait_recv()
    forward(1)
    landed_x(4)
    part = nn(sc.attended_full[...], weight(sc.two_c)) + i.attn_bo[:, own_cols]
    sc.mid_full[:, own_cols] = (part + sc.agg_full[:, own_cols].astype(F32)).astype(BF)
    mid_gather = gather_cols(sc.mid_full)
    transposed(sc.attended_full, sc.attendedT)
    forward(1)
    mid_gather.wait_recv()
    awo_rows = by_rows(sc.awo_c, sc.awo)
    two_rows = by_rows(sc.two_c, sc.two)
    whole_norm(sc.mid_full, i.mlp_norm_gain, i.mlp_norm_bias, sc.mnormed)
    kept_norm(sc.mid_full, sc.hat2, sc.rstd2)
    transposed(sc.mnormed, sc.mnormedT)
    forward(1)
    mnormed = sc.mnormed[...]
    for j in range(fl // CHUNK):
        at = slice(j * CHUNK, (j + 1) * CHUNK)
        bias = i.mlp_bup[:, pl.ds(pl.multiple_of(s * fl + j * CHUNK, LANES), CHUNK)]
        landed_x(5 + j)
        hidden = nn(mnormed, columns(sc.up_w, j)) + bias
        phi = 0.5 + 0.5 * lax.erf(hidden * 0.7071067811865476)
        density = jnp.exp(hidden * hidden * -0.5) * 0.3989422804014327
        sc.act[:, at] = (hidden * phi).astype(BF)
        sc.slope[:, at] = phi + hidden * density
        if j == 0:
            forward(1)
        if j == 2:
            forward(1)
    names = [(o.mlp_down, lambda q, j=j: q * fl + j * CHUNK) for j in range(fl // CHUNK)]
    names += [(o.mlp_up, lambda q, j=j: q * fl + j * CHUNK) for j in range(fl // CHUNK)]
    names += [(o.attn_wo, lambda q: q * wl)]
    names += [(o.attn_wqkv, lambda q, j=j: j * D + q * wl) for j in range(3)]
    names += [(o.agg_wo, lambda q: q * wl)]
    steps = [(c, 0, CHUNK) for c in range(n_pieces - 1)]
    steps += [(n_pieces - 1, 0, CHUNK // 2), (n_pieces - 1, CHUNK // 2, CHUNK // 2)]
    last = len(steps)

    def view(ref, n):
        c, at, width = steps[n]
        return ref.at[c] if width == CHUNK else ref.at[c, :, :, pl.ds(at, width)]

    to_x, to_z, made, done = {}, {}, [], []
    published = [(send_sem(), recv_sem()) for _ in range(ns)]
    early = 2
    chunk_x, early_x = send_sem(), send_sem()
    all_sent(blocks.at[early:], chunk_x)
    all_sent(blocks.at[0:early, 0], early_x)
    chunk_z = reduce_group(n_pieces - early, sc.z_recv)
    early_z = reduce_group(early, sc.e_recv)

    def produce(c, left, right):
        def half(side):
            block = left[:, pl.ds(side, 1)].reshape(nz * rows, tokens)
            return nn(block, right).reshape(nz, rows, CHUNK)

        sc.x_send[c] = half(1 - x).astype(BF)
        made.extend(n for n in range(last) if steps[n][0] == c)
        sc.keep[c] = half(x)

    def issue_x(count):
        fresh = [c for c in made if c >= early and c not in to_x]
        for c in fresh[:count]:
            to_x[c] = over_x(view(sc.x_send, c), view(sc.x_recv, c), chunk_x)

    merged = [early - 1]

    def produce_early(c, left, right):
        for side in range(nx):
            part = nn(left[:, side].reshape(nz * rows, tokens), right)
            sc.e_send[c, :, side] = part.reshape(nz, rows, CHUNK).astype(BF)
        made.append(c)
        to_z[c] = reduce(sc.e_send.at[c], sc.e_recv.at[c], sc.e_merged.at[c], early_z, True)

    def middle_early(c):
        sc.e_sum[c] = to_z[c].total()
        sc.e_out[c] = sc.e_sum[c, 1 - x].astype(BF)
        to_x[c] = over_x(sc.e_out.at[c], sc.e_in.at[c], early_x)

    def finish_early(c):
        to_x[c].wait_recv()
        sc.final[c] = (sc.e_sum[c, x] + sc.e_in[c].astype(F32)).astype(BF)
        publish(sc.final.at[c], *names[c])

    def middle(n):
        to_x[n].wait_recv()
        issue_x({2: 2, 5: 0, 6: 0, 8: 2}.get(n, 1))
        merged_x = view(sc.keep, n)[...] + view(sc.x_recv, n)[...].astype(F32)
        view(sc.z_send, n)[...] = merged_x.astype(BF)
        to_z[n] = reduce(view(sc.z_send, n), view(sc.z_recv, n), view(sc.z_merged, n), chunk_z)

    mate = s + 1 - 2 * lax.rem(s, 2)
    other = lax.rem(s + ns // 2, ns)
    relayed = []

    def publish(block, array, col, at=0, width=CHUNK):
        def cols(q):
            return array.at[:, pl.ds(pl.multiple_of(col(q) + at, LANES), width)]

        (near, landed), (across, _), (passed, landed_passed) = published[0:3]
        arrival = recv_sem()
        remote(block, cols(s), near, landed, (mate, r)).start()
        remote(block, cols(s), across, arrival, (other, r)).start()
        local(block, cols(s), 3)

        def relay():
            await_landed(cols(other), arrival)
            remote(cols(other), cols(other), passed, landed_passed, (mate, r)).start()

        relayed.append(relay)

    def relay_until(left):
        while len(relayed) > left:
            relayed.pop(0)()

    def finish(n):
        c, at, width = steps[n]
        block = sc.final.at[c] if width == CHUNK else sc.final.at[c, :, pl.ds(at, width)]
        block[...] = to_z[n].total().astype(BF)
        publish(block, *names[c], at, width)

    def finish_up_to(to):
        for c in range(early, to + 1):
            if c not in done:
                finish(c)
                done.append(c)

    def pump(count):
        for _ in range(count):
            c = len(to_z)
            middle(c)
            if c > early + 1:
                to_z[c - 2].merge()
            if early + 6 <= c < 2 * early + 6:
                finish_early(c - early - 6)
            relay_until(1)
            finish_up_to(c - 4)

    for j in range(fl // CHUNK):
        make_part = produce_early if j < early else produce
        make_part(j, sc.gT, sc.act[:, j * CHUNK : (j + 1) * CHUNK])
    issue_x(2)
    forward(2)
    for c in range(early):
        to_z[c].begin()
    g_full = sc.g_full[...]
    nmlp = fl // CHUNK
    for j in range(fl // CHUNK):
        at = slice(j * CHUNK, (j + 1) * CHUNK)
        landed_x(5 + nmlp + j)
        d_hidden = nn(g_full, columns(sc.down_w, j)) * sc.slope[:, at]
        sc.d_hidden[:, at] = d_hidden.astype(BF)
    up_w = weight(sc.up_w)
    rs3 = scatter(sc.rs3_part, sc.rs3_recv, nt(sc.d_hidden[...], up_w))
    for j in range(nmlp):
        at = slice(j * CHUNK, (j + 1) * CHUNK)
        produce(nmlp + j, sc.mnormedT, sc.d_hidden[:, at])
    sc.bup[:, own_ff] = colsum(sc.d_hidden[...])
    issue_x(2)
    rs3.wait_recv()
    g_shard = sc.g_full[own_rows, :].astype(F32)
    sc.vecs[0:1, :] = colsum(g_shard)
    d_mid = norm_back(landed_sum(sc.rs3_recv), i.mlp_norm_gain, sc.hat2, sc.rstd2, 1, 2)
    d_mid = (g_shard + d_mid).astype(BF)
    sc.vecs[3:4, :] = colsum(d_mid)
    ag3 = gather(sc.d_mid, d_mid)
    d_mid = d_mid.astype(F32)
    sc.out_part[...] = nt(sc.act[...], weight(sc.down_w))
    sc.out_part[own_rows, :] = sc.out_part[own_rows, :] + sc.mid_full[own_rows, :].astype(F32) + i.mlp_bdown[...]
    sc.out_low[...] = sc.out_part[...].astype(BF)
    out_rs = over_section(
        lambda t: sc.out_low.at[:, pl.ds(pl.multiple_of(t * wl, LANES), wl)],
        sc.out_recv.at[s],
        sc.out_recv.at[0 : ns - 1],
    )
    sc.out_recv[s] = sc.out_low[:, own_cols]
    to_z[0].merge()
    pump(1)
    to_z[1].merge()
    ag3.wait_recv()

    pump(2)
    two_rows.wait_recv()
    d_att = nt(sc.d_mid[...], weight(sc.two)).astype(BF)
    sc.d_att[...] = d_att
    for n, (b, p) in enumerate(tiles):
        q, k, v = [tile(sc.qkv, b, p, j) for j in range(3)]
        q, d_out = pair(q), pair(tile(sc.d_att, b, p))
        probs = sc.att[n]
        d_probs = nt(d_out, v)
        d_scores = probs * (d_probs - jnp.sum(probs * d_probs, axis=-1, keepdims=True))
        d_scores = d_scores.astype(BF)
        parts = (pick(nn(d_scores, k)) * scale, tn(d_scores, q) * scale, tn(probs.astype(BF), d_out))
        for j in range(3):
            lanes = slice(j * wl + p * LANES, j * wl + (p + 1) * LANES)
            sc.d_qkv[b * LEN : (b + 1) * LEN, lanes] = parts[j].astype(BF)
    rs4 = scatter(sc.rs4_part, sc.rs4_recv, nt(sc.d_qkv[...], weight(sc.qkv_w)))
    produce(2 * nmlp, sc.attendedT, sc.d_mid[:, own_cols])
    for j in range(3):
        produce(2 * nmlp + 1 + j, sc.normedT, sc.d_qkv[:, j * wl : (j + 1) * wl])
    sc.vecs[7:8, own_cols] = colsum(sc.d_qkv[:, 0:wl])
    sc.vecs[8:9, own_cols] = colsum(sc.d_qkv[:, 2 * wl : 3 * wl])
    middle_early(0)
    pump(1)
    rs4.wait_recv()
    d_agg = norm_back(landed_sum(sc.rs4_recv), i.attn_norm_gain, sc.hat1, sc.rstd1, 4, 5)
    d_agg = (sc.d_mid[own_rows, :].astype(F32) + d_agg).astype(BF)
    sc.vecs[6:7, :] = colsum(d_agg)
    ag4 = gather(sc.d_agg, d_agg)
    middle_early(1)
    pump(2)
    ag4.wait_recv()

    awo_rows.wait_recv()
    produce(2 * nmlp + 4, sc.contextT, sc.d_agg[:, own_cols])
    d_context = nt(sc.d_agg[...], weight(sc.awo)).astype(BF)
    sc.vecs[9:10, own_cols] = colsum(d_context)
    value_basis = sc.bv[...].astype(BF)
    cross = jnp.zeros((CHUNK, wl), F32)
    grad_pix = jnp.zeros((tokens, CHUNK), F32)
    sc.key_src[...] = jnp.zeros_like(sc.key_src)
    for h in range(hl):
        masked = d_context * (head_of == h).astype(F32).astype(BF)
        pulled = nt(masked, value_basis)
        cross = cross + tn(sc.mixed[h], masked)
        pix = sc.pix[...].astype(F32)
        high, low = split(pulled * pix)
        d_weights = nn(high, fold) + nn(low, fold)
        probs = sc.probs[h]
        d_scores = probs * (d_weights - jnp.sum(probs * d_weights, axis=-1, keepdims=True))
        srep = nt(d_scores.astype(BF), fold)
        sc.key_src[h : h + 1, :] = colsum(srep * pix)
        grad_pix = grad_pix + sc.wrep[h].astype(F32) * pulled
        grad_pix = grad_pix + srep * sc.score_rows[h : h + 1, :]
    key_push = push(sc.key_src, sc.key_recv)
    for t in range(nd):
        sc.m_src[t] = cross[t * blk : (t + 1) * blk].astype(sc.m_src.dtype)
    m_rs = over_dp(lambda t: sc.m_src.at[t], sc.m_recv.at[r], sc.m_recv.at[0 : nd - 1])
    sc.m_recv[r] = sc.m_src[r]
    grad_pix = grad_pix.astype(BF)
    pw = CP // ns
    for t in range(ns):
        sc.pix_src[t] = nt(sc.place[t * pw : (t + 1) * pw, :], grad_pix).astype(BF)
    pix_rs = over_section(lambda t: sc.pix_src.at[t], sc.pix_recv.at[s], sc.pix_recv.at[0 : ns - 1])
    sc.pix_recv[s] = sc.pix_src[s]
    for t in range(nd):
        sc.small_src[t, 0:10] = sc.vecs[0:10, t * rows : (t + 1) * rows]
        for j in range(FF // D):
            start = (t * (FF // D) + j) * rows
            sc.small_src[t, 10 + j : 11 + j] = sc.bup[:, start : start + rows]
    small_rs = over_dp(lambda t: sc.small_src.at[t], sc.small_recv.at[r], sc.small_recv.at[0 : nd - 1])
    sc.small_recv[r] = sc.small_src[r]

    issue_x(1)
    pump(2)
    m_rs.wait_recv()
    sc.m_own[...] = summed(sc.m_recv, nd).astype(sc.m_own.dtype)
    m_ag = push(sc.m_own, sc.m_all)
    key_push.wait_recv()
    key_terms = summed(sc.key_recv, nd)
    wide = jnp.concatenate([jnp.broadcast_to(key_terms[h : h + 1], (HEAD, CHUNK)) for h in range(hl)], axis=0)
    d_key = nt(sc.basis[...], wide.astype(BF))
    d_query = jnp.sum(sc.wk[...].astype(F32) * d_key, axis=0, keepdims=True) * scale
    sc.dq_src[...] = jnp.broadcast_to(d_query, sc.dq_src.shape)
    dq_push = push(sc.dq_src, sc.dq_recv)
    count = len(names)
    sc.final[count] = (d_key * (sc.query_proj[...] * scale)).astype(BF)
    publish(sc.final.at[count], o.agg_wk, lambda q: q * wl)
    pump(2)
    small_rs.wait_recv()
    sc.sec_small[s] = summed(sc.small_recv, nd)
    small_ag = over_section(lambda t: sc.sec_small.at[s], sc.sec_small.at[s], sc.sec_small.at[0 : ns - 1])
    pump(2)
    m_ag.wait_recv()
    for t in range(nd):
        sc.cross[t * blk : (t + 1) * blk] = sc.m_all[t].astype(F32)
    cross = sc.cross[...].astype(BF)
    sc.final[count + 1] = nn(sc.basis[...], cross).astype(BF)
    publish(sc.final.at[count + 1], o.agg_wv, lambda q: q * wl)
    key_low = jnp.concatenate([key_terms, jnp.zeros_like(key_terms)], axis=0).astype(BF)
    grad_basis = nt(cross, sc.wv[...]) + tn(key_low, sc.key_query[...])
    sc.basis_recv[s] = grad_basis.astype(BF)
    basis_sum = over_section(lambda t: sc.basis_recv.at[s], sc.basis_recv.at[s], sc.basis_recv.at[0 : ns - 1])
    to_z[last - 2].merge()
    finish_up_to(last - 4)
    relay_until(2)
    to_z[last - 1].merge()
    finish_up_to(last - 3)
    dq_push.wait_recv()
    o.d_query[s] = summed(sc.dq_recv, nd)
    dq_gather = over_section(lambda t: o.d_query.at[s], o.d_query.at[s], o.d_query.at[0 : ns - 1])

    def section_total(ref):
        total = ref[0].astype(F32)
        for k in range(1, ns):
            total = total + ref[k].astype(F32)
        return total

    out_rs.wait_recv()
    o.activations[...] = section_total(sc.out_recv).astype(BF)
    pix_rs.wait_recv()
    o.patches[...] = section_total(sc.pix_recv).astype(BF)
    small_ag.wait_recv()
    o.small[...] = summed(sc.sec_small, ns)
    finish_up_to(last - 1)
    relay_until(2)
    basis_sum.wait_recv()
    o.basis[...] = section_total(sc.basis_recv)
    dq_gather.wait_recv()
    relay_until(0)
    await_landed(sc.final, published[0][1])
    await_landed(sc.final, published[2][1])
    for out, _ in published[0:3]:
        await_sent(sc.final, out)
    await_local(sc.final, 3)
    for wait in pending:
        wait()
    assert used.send <= send.shape[0] and used.recv <= recv.shape[0], used


def scratch(ns, nd, tokens):
    nz, rows = nd // 2, D // nd
    wl, fl, hl = D // ns, FF // ns, HEADS // ns
    shard, zq, blk = tokens // ns, nz // ns, CHUNK // nd
    chunks = 2 * (fl // CHUNK) + 5
    v = pltpu.VMEM
    shapes = dict(
        wq=v((rows, wl), BF),
        wk=v((rows, wl), BF),
        wv=v((rows, wl), BF),
        qkv_w=v((nz, 2, rows, 3 * wl), BF),
        up_w=v((nz, 2, rows, fl), BF),
        down_w=v((nz, 2, rows, fl), BF),
        awo_c=v((nz, 2, rows, wl), BF),
        two_c=v((nz, 2, rows, wl), BF),
        awo=v((zq, 2, rows, D), BF),
        two=v((zq, 2, rows, D), BF),
        g_full=v((tokens, D), BF),
        place=v((CP, CHUNK), BF),
        pix=v((tokens, CHUNK), BF),
        fold=v((CHUNK, LANES), BF),
        basis=v((rows, CHUNK), BF),
        vecs=v((16, D), F32),
        bup=v((1, FF), F32),
        query_proj=v((1, wl), F32),
        key_query=v((16, rows), BF),
        score_rows=v((8, CHUNK), F32),
        bv=v((CHUNK, CHUNK), F32),
        cross=v((CHUNK, CHUNK), F32),
        e_send=v((2, nz, 2, rows, CHUNK), BF),
        e_recv=v((2, nz, 2, rows, CHUNK), BF),
        e_merged=v((2, 2, 2, rows, CHUNK), BF),
        z_merged=v((chunks, 2, rows, CHUNK), BF),
        e_sum=v((2, 2, rows, CHUNK), F32),
        e_out=v((2, rows, CHUNK), BF),
        e_in=v((2, rows, CHUNK), BF),
        probs=v((hl, tokens, LANES), F32),
        wrep=v((hl, tokens, CHUNK), BF),
        mixed=v((hl, tokens, CHUNK), BF),
        context_full=v((tokens, D), BF),
        attended_full=v((tokens, D), BF),
        agg_full=v((tokens, D), BF),
        mid_full=v((tokens, D), BF),
        hat1=v((shard, D), F32),
        hat2=v((shard, D), F32),
        rstd1=v((shard, LANES), F32),
        rstd2=v((shard, LANES), F32),
        normed=v((tokens, D), BF),
        mnormed=v((tokens, D), BF),
        qkv=v((tokens, 3 * wl), BF),
        d_qkv=v((tokens, 3 * wl), BF),
        att=v((tokens // LEN * (wl // LANES), 2 * LEN, LEN), F32),
        attended=v((tokens, wl), BF),
        d_att=v((tokens, wl), BF),
        act=v((tokens, fl), BF),
        slope=v((tokens, fl), F32),
        d_hidden=v((tokens, fl), BF),
        d_mid=v((tokens, D), BF),
        d_agg=v((tokens, D), BF),
        out_part=v((tokens, D), F32),
        out_low=v((tokens, D), BF),
        out_recv=v((ns, tokens, wl), BF),
        pix_src=v((ns, CP // ns, tokens), BF),
        pix_recv=v((ns, CP // ns, tokens), BF),
        small_src=v((nd, 16, rows), F32),
        small_recv=v((nd, 16, rows), F32),
        sec_small=v((ns, 16, rows), F32),
        basis_recv=v((ns, CHUNK, rows), BF),
        x_send=v((chunks, nz, rows, CHUNK), BF),
        x_recv=v((chunks, nz, rows, CHUNK), BF),
        keep=v((chunks, nz, rows, CHUNK), F32),
        z_send=v((chunks, nz, rows, CHUNK), BF),
        z_recv=v((chunks, nz, rows, CHUNK), BF),
        final=v((chunks + 2, rows, CHUNK), BF),
    )
    whole = v((nz, 2, rows, tokens), BF)
    shapes.update(gT=whole, contextT=whole, attendedT=whole, normedT=whole, mnormedT=whole)
    part = v((tokens, D), BF)
    shapes.update(rs3_part=part, rs4_part=part)
    part = v((ns, shard, D), BF)
    shapes.update(rs3_recv=part, rs4_recv=part)
    part = v((8, CHUNK), F32)
    shapes.update(q_src=part, s_src=part, key_src=part, dq_src=part)
    part = v((nd, 8, CHUNK), F32)
    shapes.update(q_recv=part, s_recv=part, key_recv=part, dq_recv=part)
    kind = BF if blk % 16 == 0 else F32
    part = v((nd, blk, CHUNK), kind)
    shapes.update(bv_src=part, bv_recv=part, bv_all=part, m_src=part, m_recv=part, m_all=part)
    part = v((blk, CHUNK), kind)
    shapes.update(bv_own=part, m_own=part)
    dma = pltpu.SemaphoreType.DMA
    shapes.update(send=dma((48,)), recv=dma((180,)), local=dma((4,)))
    return shapes


def fused(ns, nd, near, far):
    tokens = near["patches"].shape[1]
    rows = D // nd
    shapes = scratch(ns, nd, tokens)
    arrays = {**near, **far}
    hbm = pl.BlockSpec(memory_space=pl.ANY)
    vmem = pl.BlockSpec(memory_space=pltpu.VMEM)
    outs = dict(
        activations=((tokens, D // ns), BF, vmem),
        patches=((CP // ns, tokens), BF, vmem),
        basis=((CHUNK, rows), F32, vmem),
        query_rows=((16, rows), BF, vmem),
        d_query=((ns, 8, D // ns), F32, vmem),
        small=((16, rows), F32, vmem),
        mlp_up=((rows, FF), BF, hbm),
        mlp_down=((rows, FF), BF, hbm),
        attn_wqkv=((rows, 3 * D), BF, hbm),
        attn_wo=((rows, D), BF, hbm),
        agg_wo=((rows, D), BF, hbm),
        agg_wv=((rows, D), BF, hbm),
        agg_wk=((rows, D), BF, hbm),
    )

    def body(*refs):
        n_in, n_out = len(arrays), len(outs)
        kernel(
            ns,
            nd,
            SimpleNamespace(**dict(zip(arrays, refs[:n_in]))),
            SimpleNamespace(**dict(zip(outs, refs[n_in : n_in + n_out]))),
            SimpleNamespace(**dict(zip(shapes, refs[n_in + n_out :]))),
        )

    result = pl.pallas_call(
        body,
        out_shape=[jax.ShapeDtypeStruct(shape, kind) for shape, kind, _ in outs.values()],
        in_specs=[vmem] * len(near) + [hbm] * len(far),
        out_specs=[spec for _, _, spec in outs.values()],
        scratch_shapes=list(shapes.values()),
        compiler_params=pltpu.CompilerParams(
            collective_id=0, has_side_effects=True, vmem_limit_bytes=60 * 1024 * 1024
        ),
        name="block",
    )(*arrays.values())
    return SimpleNamespace(**dict(zip(outs, result)))


def widen(nd, got, agg_wq):
    rows = D // nd
    step = min(rows, 64)
    big = dict(
        mlp_up=got.mlp_up,
        mlp_down=got.mlp_down,
        attn_wqkv=got.attn_wqkv,
        attn_wo=got.attn_wo,
        agg_wo=got.agg_wo,
        agg_wv=got.agg_wv,
        agg_wk=got.agg_wk,
    )
    rest = dict(
        activations=got.activations,
        patches=got.patches,
        basis=got.basis,
        query_rows=got.query_rows,
        d_query=got.d_query,
        small=got.small,
        agg_wq=agg_wq,
    )
    line = (1, rows)
    outs = dict(
        activations=(got.activations.shape, BF),
        patches=(got.patches.shape, BF),
        embed=((CP, rows), F32),
        var=((VARS, rows), F32),
        query=(line, F32),
        wq=((rows, D), F32),
        bq=(line, F32),
        bup=((1, rows * (FF // D)), F32),
    )
    lines = tuple(range(10))

    def body(*refs):
        n = len(big)
        for src, dst in zip(refs[:n], refs[n + len(rest) : 2 * n + len(rest)]):
            dst[...] = src[...].astype(F32)
        i = SimpleNamespace(**dict(zip(rest, refs[n : n + len(rest)])))
        left = refs[2 * n + len(rest) :]
        o = SimpleNamespace(**dict(zip(outs, left)))
        left = left[len(outs) :]
        r = lax.axis_index("dp")

        @pl.when(pl.program_id(0) == 0)
        def _():
            o.activations[...] = i.activations[...]
            o.patches[...] = i.patches[...]
            o.embed[...] = i.basis[0:CP]
            o.var[...] = i.basis[CP : CP + VARS]
            d_query = jnp.concatenate([i.d_query[k] for k in range(i.d_query.shape[0])], axis=1)
            d_query = jnp.concatenate([d_query, d_query], axis=0)
            d_query = jnp.where(iota(d_query.shape, 0) == 0, d_query, 0.0)
            high, low = split(d_query)
            low, rest_low = split(d_query - high.astype(F32))
            chosen = (iota((rows, D), 1) == iota((rows, D), 0) + r * rows).astype(F32).astype(BF)
            o.bq[...] = (nt(high, chosen) + nt(low, chosen) + nt(rest_low, chosen))[0:1]
            weight = i.agg_wq[...]
            o.query[...] = (nt(high, weight) + nt(low, weight) + nt(rest_low, weight))[0:1]
            first = i.query_rows[...]
            o.wq[...] = tn(first, high) + tn(first, low) + tn(first, rest_low)
            o.bup[...] = jnp.concatenate([i.small[10 + k : 11 + k] for k in range(FF // D)], axis=1)
            for k in lines:
                left[k][...] = i.small[k : k + 1]

    def by_step(a):
        return pl.BlockSpec((step, a.shape[1]), lambda g: (g, 0))

    def fixed(shape):
        return pl.BlockSpec(shape, lambda g: (0,) * len(shape))

    shaped = [jax.ShapeDtypeStruct(a.shape, F32) for a in big.values()]
    shaped += [jax.ShapeDtypeStruct(*a) for a in outs.values()]
    shaped += [jax.ShapeDtypeStruct(line, F32) for _ in lines]
    result = pl.pallas_call(
        body,
        grid=(rows // step,),
        out_shape=shaped,
        in_specs=[by_step(a) for a in big.values()] + [fixed(a.shape) for a in rest.values()],
        out_specs=[by_step(a) for a in big.values()] + [fixed(a.shape) for a in shaped[len(big) :]],
        compiler_params=pltpu.CompilerParams(vmem_limit_bytes=60 * 1024 * 1024),
        name="widen",
    )(*big.values(), *rest.values())
    names = list(big) + list(outs)
    return SimpleNamespace(**dict(zip(names, result))), [a.reshape(-1) for a in result[len(names) :]]


def on_device(
    ns,
    nd,
    patches,
    var_ids,
    segment_ids,
    embed_weight,
    var_embed,
    agg_query,
    agg_wq,
    agg_bq,
    agg_wk,
    agg_wv,
    agg_bv,
    agg_wo,
    agg_bo,
    attn_norm_gain,
    attn_norm_bias,
    attn_wqkv,
    attn_bq,
    attn_bv,
    attn_wo,
    attn_bo,
    mlp_norm_gain,
    mlp_norm_bias,
    mlp_up,
    mlp_bup,
    mlp_down,
    mlp_bdown,
    cotangent,
):
    near = dict(
        patches=patches,
        var_ids=var_ids,
        segment_ids=segment_ids,
        embed_weight=embed_weight,
        var_embed=var_embed,
        agg_query=agg_query,
        agg_bq=agg_bq,
        agg_bv=agg_bv,
        agg_bo=agg_bo,
        attn_norm_gain=attn_norm_gain,
        attn_norm_bias=attn_norm_bias,
        attn_bq=attn_bq,
        attn_bv=attn_bv,
        attn_bo=attn_bo,
        mlp_norm_gain=mlp_norm_gain,
        mlp_norm_bias=mlp_norm_bias,
        mlp_bup=mlp_bup,
        mlp_bdown=mlp_bdown,
    )
    far = dict(
        agg_wq=agg_wq,
        agg_wk=agg_wk,
        agg_wv=agg_wv,
        agg_wo=agg_wo,
        attn_wqkv=attn_wqkv,
        attn_wo=attn_wo,
        mlp_up=mlp_up,
        mlp_down=mlp_down,
        cotangent=cotangent,
    )
    near = {name: a.reshape(1, -1) if a.ndim == 1 else a for name, a in near.items()}
    near["patches"], near["embed_weight"] = patches.T, embed_weight.T
    got = fused(ns, nd, near, far)
    out, small = widen(nd, got, agg_wq)
    return (
        out.activations,
        out.patches.T,
        out.embed.T,
        out.var,
        out.query.reshape(-1),
        out.wq,
        out.bq.reshape(-1),
        out.agg_wk,
        out.agg_wv,
        small[9],
        out.agg_wo,
        small[6],
        small[4],
        small[5],
        out.attn_wqkv,
        small[7],
        small[8],
        out.attn_wo,
        small[3],
        small[1],
        small[2],
        out.mlp_up,
        out.bup.reshape(-1),
        out.mlp_down,
        small[0],
    )


def solution(mesh):
    in_specs = (
        P("dp", None),
        P(),
        P("dp", None),
        P("dp", None),
        P(),
        P(),
        P("dp", None),
        P(),
        P("dp", None),
        P("dp", None),
        P(),
        P("dp", None),
        P(),
        P(),
        P(),
        P("dp", None),
        P(),
        P(),
        P("dp", None),
        P(),
        P(),
        P(),
        P("dp", None),
        P(),
        P("dp", None),
        P(),
        P("dp", "section"),
    )
    out_specs = (
        P("dp", "section"),
        P("dp", "section"),
        P("dp", None),
        P(None, "dp"),
        P("dp"),
        P("dp", None),
        P("dp"),
        P("dp", None),
        P("dp", None),
        P("dp"),
        P("dp", None),
        P("dp"),
        P("dp"),
        P("dp"),
        P("dp", None),
        P("dp"),
        P("dp"),
        P("dp", None),
        P("dp"),
        P("dp"),
        P("dp"),
        P("dp", None),
        P("dp"),
        P("dp", None),
        P("dp"),
    )
    sizes = (mesh.shape["section"], mesh.shape["dp"])
    return jax.shard_map(
        partial(on_device, *sizes), mesh=mesh, in_specs=in_specs, out_specs=out_specs, check_vma=False
    )
```

```python
from functools import partial
from types import SimpleNamespace

import jax
import jax.numpy as jnp
from jax import lax
from jax.experimental import pallas as pl
from jax.experimental.pallas import tpu as pltpu
from jax.sharding import PartitionSpec as P

D = 1024
HEADS = 16
HEAD = 64
FF = 4096
VARS = 48
PIX = 4
LEN = 128

highest = lax.Precision.HIGHEST
blocked = -1000000000.0
epsilon = 1e-05
MESH = pl.DeviceIdType.MESH
BF = jnp.bfloat16
F32 = jnp.float32
CHUNK = 256
CP = VARS * PIX
LANES = 128


def nn(a, b):
    return jnp.dot(a, b, preferred_element_type=F32)


def nt(a, b):
    return lax.dot_general(a, b, (((1,), (1,)), ((), ())), preferred_element_type=F32)


def tn(a, b):
    return lax.dot_general(a, b, (((0,), (0,)), ((), ())), preferred_element_type=F32)


def split(x):
    high = x.astype(BF)
    return high, (x - high.astype(F32)).astype(BF)


def iota(shape, dim):
    return lax.broadcasted_iota(jnp.int32, shape, dim)


def colsum(x):
    return jnp.sum(x.astype(F32), axis=0, keepdims=True)


def each(low, high, body):
    if high - low <= 8:
        for k in range(low, high):
            body(k)
    else:

        def step(k, carry):
            body(k)
            return carry

        lax.fori_loop(low, high, step, 0)


class Transfer:
    def __init__(self, make, low, high, whole):
        self.make, self.low, self.high, self.whole = make, low, high, whole

    def start(self):
        each(self.low, self.high, lambda k: self.make(k).start())
        return self

    def wait_recv(self):
        self.whole().wait_recv()

    def wait_send(self):
        self.whole().wait_send()


def kernel(ns, nd, refs_in, refs_out, sc, near_names, near):
    s = lax.axis_index("section")
    r = lax.axis_index("dp")
    nx = 2
    nz = nd // nx
    z, x = lax.div(r, nx), lax.rem(r, nx)
    o = refs_out
    i = SimpleNamespace(**{**vars(refs_in), **dict(zip(near_names, near))})
    rows = D // nd
    tokens = i.patches.shape[1]
    shard = tokens // ns
    wl, fl, hl = D // ns, FF // ns, HEADS // ns
    zq = nz // ns
    own_cols = pl.ds(pl.multiple_of(s * wl, LANES), wl)
    own_ff = pl.ds(pl.multiple_of(s * fl, LANES), fl)
    own_rows = pl.ds(pl.multiple_of(s * shard, 16), shard)
    scale = HEAD ** (-0.5)
    send, recv = sc.send, sc.recv
    used = SimpleNamespace(send=0, recv=0, local=0)
    pending = []

    def send_sem():
        used.send += 1
        return used.send - 1

    def recv_sem(count=1):
        used.recv += count
        return used.recv - count

    def remote(src, dst, out, landing, device):
        return pltpu.make_async_remote_copy(
            src_ref=src,
            dst_ref=dst,
            send_sem=send.at[out],
            recv_sem=recv.at[landing],
            device_id=device,
            device_id_type=MESH,
        )

    beside = (s, z * nx + 1 - x)

    def await_sent(ref, out):
        remote(ref, ref, out, 0, beside).wait_send()

    def await_landed(ref, landing):
        remote(ref, ref, 0, landing, beside).wait_recv()

    def all_sent(ref, out):
        pending.append(lambda: await_sent(ref, out))

    def over(peer, count, src, dst, whole, out=None, landing=None):
        alone = out is None
        out = send_sem() if alone else out
        landing = recv_sem() if landing is None else landing

        def make(k):
            t, device = peer(k)
            return remote(src(t), dst, out, landing, device)

        transfer = Transfer(make, 1, count, lambda: remote(whole, whole, out, landing, beside)).start()
        if alone:
            pending.append(transfer.wait_send)
        return transfer

    def section_peer(k):
        t = lax.rem(s + k, ns)
        return t, (t, r)

    def dp_peer(k):
        t = lax.rem(r + k, nd)
        return t, (s, t)

    def z_peer(k):
        t = lax.rem(z + k, nz)
        return t, (s, t * nx + x)

    def over_section(src, dst, whole):
        return over(section_peer, ns, src, dst, whole)

    def over_dp(src, dst, whole):
        return over(dp_peer, nd, src, dst, whole)

    def over_x(src, dst, out, landing=None, whole=None):
        whole = src if whole is None else whole
        return over(lambda k: (0, beside), 2, lambda t: src, dst, whole, out, landing)

    def local(src, dst, sem):
        copy = pltpu.make_async_copy(src, dst, sc.local.at[sem])
        copy.start()
        return copy

    def await_local(ref, sem):
        pltpu.make_async_copy(ref, ref, sc.local.at[sem]).wait()

    line = nz == 4
    partner = z + 1 - 2 * lax.rem(z, 2)
    inner = (z == 1) | (z == 2)
    outer = (z == 0) | (z == 3)
    beyond = [lax.rem(2 * lax.div(z, 2) + 2 + j, 4) for j in range(2)]
    gate = 2 - lax.div(z, 2)

    def at_z(t):
        return (s, t * nx + x)

    blocks = sc.z_recv
    n_pieces = blocks.shape[0]
    crossing = 2 if line else 0

    def spread_group(count):
        own, passed = send_sem(), send_sem()
        whole = blocks.at[0:count, 0 : min(2, nz)] if line else blocks.at[0:count, 0 : nz - 1]
        all_sent(whole, own)
        if line:

            def sent():
                @pl.when(inner)
                def _():
                    await_sent(whole, passed)

            pending.append(sent)
        return own, passed

    first_spread = spread_group(n_pieces)
    second_spread = spread_group(crossing) if crossing else None

    def line_spread(block, group):
        base = recv_sem(3)
        out, out_passed = group
        mine_beyond = base + 1 + lax.rem(z, 2)
        remote(block(z), block(z), out, base, at_z(partner)).start()
        remote(block(z), block(z), out, mine_beyond, at_z(gate)).start()

        def pass_on(k):
            t = beyond[k - 1]

            @pl.when(inner)
            def _():
                await_landed(block(t), base + k)
                remote(block(t), block(t), out_passed, base + k, at_z(partner)).start()

        def arrived(k, passed=False):
            t = [partner, *beyond][k]
            if k == 0:
                await_landed(block(t), base)
                return t
            if not passed:
                pass_on(k)

            @pl.when(outer)
            def _():
                await_landed(block(t), base + k)

            return t

        arrived.pass_on = pass_on
        return arrived

    def spread(block, group=first_spread):
        if line:
            return line_spread(block, group)
        whole = blocks.at[0, 0 : nz - 1]
        return over(z_peer, nz, lambda t: block(z), block(z), whole, group[0]).wait_recv

    def reduce_group(count, landed):
        near, far, across = send_sem(), send_sem(), send_sem()
        if not line:
            all_sent(landed.at[0:count, 0 : nz - 1], near)
            return near, far, across
        all_sent(landed.at[0:count, 0], near)

        def sent():
            @pl.when(outer)
            def _():
                await_sent(landed.at[0:count, 0:2], far)

            @pl.when(inner)
            def _():
                await_sent(landed.at[0:count, 0:2], across)

        pending.append(sent)
        return near, far, across

    def line_reduce(parts, landed, merged, group, hold):
        near, far, across = group
        base = recv_sem(3)

        def first():
            remote(parts.at[partner], landed.at[0], near, base, at_z(partner)).start()

        def begin():
            pl.when(inner)(first)

        @pl.when(outer)
        def _():
            first()
            for j in range(2):
                remote(parts.at[beyond[j]], landed.at[2 + j], far, base + 1, at_z(partner)).start()

        if not hold:
            begin()

        def merge():
            @pl.when(inner)
            def _():
                await_landed(landed.at[2:4], base + 1)
                for j in range(2):
                    both = parts[beyond[j]].astype(F32) + landed[2 + j].astype(F32)
                    merged[j] = both.astype(BF)
                    remote(merged.at[j], landed.at[1], across, base + 2, at_z(beyond[j])).start()

        def total():
            await_landed(landed.at[0], base)
            await_landed(landed.at[1], base + 2)
            return parts[z].astype(F32) + landed[0].astype(F32) + landed[1].astype(F32)

        return SimpleNamespace(begin=begin, merge=merge, total=total)

    def reduce(parts, landed, merged, group, hold=False):
        if line and group is not None:
            return line_reduce(parts, landed, merged, group, hold)
        out = None if group is None else group[0]
        transfer = over(z_peer, nz, lambda t: parts.at[t], landed.at[z], landed.at[0 : nz - 1], out)
        landed[z] = parts[z]

        def total():
            transfer.wait_recv()
            value = landed[0].astype(F32)
            for k in range(1, nz):
                value = value + landed[k].astype(F32)
            return value

        return SimpleNamespace(begin=lambda: None, merge=lambda: None, total=total)

    barrier = pltpu.get_barrier_semaphore()
    for k in range(1, ns):
        pl.semaphore_signal(barrier, inc=1, device_id=(lax.rem(s + k, ns), r), device_id_type=MESH)
    each(
        1,
        nd,
        lambda k: pl.semaphore_signal(
            barrier, inc=1, device_id=(s, lax.rem(r + k, nd)), device_id_type=MESH
        ),
    )

    local(i.agg_wq.at[:, own_cols], sc.wq, 0)
    local(i.agg_wk.at[:, own_cols], sc.wk, 0)
    local(i.agg_wv.at[:, own_cols], sc.wv, 0)
    sources = [(i.agg_wo, sc.awo_c, 0, s * wl)]
    sources += [(i.attn_wqkv, sc.qkv_w, j * wl, j * D + s * wl) for j in range(3)]
    sources += [(i.attn_wo, sc.two_c, 0, s * wl)]
    sources += [(i.mlp_up, sc.up_w, j * CHUNK, s * fl + j * CHUNK) for j in range(fl // CHUNK)]
    sources += [(i.mlp_down, sc.down_w, j * CHUNK, s * fl + j * CHUNK) for j in range(fl // CHUNK)]
    pieces = [(dst, pl.ds(at, CHUNK)) for _, dst, at, _ in sources]
    for src, dst, at, col in sources:
        local(src.at[:, pl.ds(pl.multiple_of(col, LANES), CHUNK)], dst.at[z, x, :, pl.ds(at, CHUNK)], 1)
    from_z, from_x, own_x, early_passed = {}, {}, {}, set()

    def pass_next():
        c = max([-1, *early_passed, *from_x]) + 1
        if line:
            early_passed.add(c)
            for k in range(1, nz - 1):
                for arrived in from_z[c]:
                    arrived.pass_on(k)

    late = range(n_pieces - crossing, n_pieces)
    own_order = [*range(6), *late, *range(6, n_pieces - crossing)] if line else []
    from_own, from_others = send_sem(), send_sem()
    if line:
        all_sent(blocks.at[:, 0], from_own)
        all_sent(blocks.at[0 : n_pieces - crossing, 0 : nz - 1], from_others)
    else:
        all_sent(blocks, from_others)
    x_landed = [recv_sem() for _ in range(n_pieces)]

    def issue_own(count):
        for c in own_order[len(own_x) : len(own_x) + count]:
            dst, cols = pieces[c]
            block = dst.at[z, x, :, cols]
            own_x[c] = over_x(block, block, from_own, x_landed[c])

    def issue_z(count):
        for c in range(len(from_z), min(len(from_z) + count, n_pieces)):
            dst, cols = pieces[c]
            from_z[c] = [spread(lambda t, dst=dst, cols=cols: dst.at[t, x, :, cols])]
            if c in late:
                own_x[c].wait_recv()
                other = lambda t, dst=dst, cols=cols: dst.at[t, 1 - x, :, cols]
                from_z[c].append(spread(other, second_spread))

    def forward(count):
        for c in range(len(from_x), min(len(from_x) + count, n_pieces)):
            while line and c not in own_x:
                issue_own(1)
            dst, cols = pieces[c]
            from_x[c] = True
            if not line:
                from_z[c][0]()
                half = dst.at[:, x, :, cols]
                over_x(half, half, from_others, x_landed[c])
            for k in range(nz - 1 if line else 0):
                for arrived in from_z[c]:
                    t = arrived(k, c in early_passed)
                    block = dst.at[t, x, :, cols]
                if c not in late:
                    over_x(block, block, from_others, x_landed[c])
            issue_z(1)

    def landed_x(c):
        dst, cols = pieces[c]
        if c not in late:
            await_landed(dst.at[:, 0, :, cols], x_landed[c])

    local(i.cotangent, sc.g_full.at[:, own_cols], 2)

    for n, name in enumerate(near_names):
        local(getattr(refs_in, name), near[n], 10 + n)
    for n, ref in enumerate(near):
        await_local(ref, 10 + n)

    chan = (iota((CP, VARS), 0) >> 2 == iota((CP, VARS), 1)).astype(F32).astype(BF)
    ids = jnp.broadcast_to(i.var_ids[...].astype(F32), (CHUNK, VARS)).astype(BF)
    ids = nt(chan, ids)
    lane = iota((CP, CHUNK), 1)
    row = iota((CP, CHUNK), 0)
    hit = ((lane >> 2).astype(F32) == ids) & ((lane & 3) == (row & 3)) & (lane < CP)
    place = hit.astype(F32).astype(BF)
    sc.place[...] = place
    lane = iota((tokens, CHUNK), 1)
    ones = ((lane >= CP) & (lane < CP + VARS)).astype(F32)
    sc.pix[...] = (tn(i.patches[...], place) + ones).astype(BF)
    row = iota((CHUNK, LANES), 0)
    lane = iota((CHUNK, LANES), 1)
    owner = jnp.where(row < CP, row >> 2, row - CP)
    sc.fold[...] = ((owner == lane) & (lane < VARS)).astype(F32).astype(BF)
    chosen = (iota((rows, D), 1) == iota((rows, D), 0) + r * rows).astype(F32).astype(BF)
    lane = iota((CP, CHUNK), 1)
    row = iota((CP, CHUNK), 0)
    widen = (lane == row).astype(F32).astype(BF)
    lane = iota((VARS, CHUNK), 1)
    row = iota((VARS, CHUNK), 0)
    widen_var = (lane == row + CP).astype(F32).astype(BF)
    var_rows = nt(chosen, i.var_embed[...].astype(BF)).astype(BF)
    sc.basis[...] = (tn(i.embed_weight[...], widen) + nn(var_rows, widen_var)).astype(BF)
    query = jnp.broadcast_to(i.agg_query[...].astype(BF).astype(F32), (16, D))
    query = jnp.where(iota((16, D), 0) == 0, query, 0.0).astype(BF)
    query_rows = nt(query, chosen).astype(BF)
    sc.query_rows[...] = query_rows
    local(sc.query_rows, o.query_rows, 4)
    sc.vecs[...] = jnp.zeros_like(sc.vecs)
    sc.bup[...] = jnp.zeros_like(sc.bup)

    await_local(blocks.at[0:3, 0], 0)
    sc.q_src[...] = nn(query_rows, sc.wq[...])[0:1]
    value_part = tn(sc.basis[...], sc.wv[...])
    blk = CHUNK // nd
    for t in range(nd):
        sc.bv_src[t] = value_part[t * blk : (t + 1) * blk].astype(sc.bv_src.dtype)
    await_local(sc.g_full.at[:, own_cols], 2)
    await_local(blocks.at[:, 0], 1)

    pl.semaphore_wait(barrier, ns - 1 + nd - 1)

    def weight(ref):
        return ref[...].reshape(ref.shape[0] * ref.shape[1] * ref.shape[2], ref.shape[3])

    def scatter(part, landed, value):
        part[...] = value.astype(BF)
        transfer = over_section(lambda t: part.at[pl.ds(pl.multiple_of(t * shard, 16), shard)], landed.at[s], landed.at[0 : ns - 1])
        landed[s] = part[own_rows, :]
        return transfer

    def gather(full, value):
        full[own_rows, :] = value.astype(BF)
        return over_section(lambda t: full.at[own_rows], full.at[own_rows], full.at[0 : (ns - 1) * shard])

    def landed_sum(landed):
        total = landed[0].astype(F32)
        for k in range(1, ns):
            total = total + landed[k].astype(F32)
        return total

    def normal(value):
        centred = value - jnp.mean(value, axis=-1, keepdims=True)
        rstd = lax.rsqrt(jnp.mean(centred * centred, axis=-1, keepdims=True) + epsilon)
        return centred * rstd, rstd

    def whole_norm(full, gain, bias, dst):
        for t in range(ns):
            at = slice(t * shard, (t + 1) * shard)
            hat, _ = normal(full[at, :].astype(F32))
            dst[at, :] = (hat * gain[...] + bias[...]).astype(BF)

    def kept_norm(full, kept, rstd_kept):
        hat, rstd = normal(full[own_rows, :].astype(F32))
        kept[...] = hat
        rstd_kept[...] = jnp.broadcast_to(rstd, rstd_kept.shape)

    def norm_back(grad, gain, kept, rstd_kept, gain_row, bias_row):
        hat = kept[...]
        sc.vecs[gain_row : gain_row + 1, :] = colsum(grad * hat)
        sc.vecs[bias_row : bias_row + 1, :] = colsum(grad)
        inner = grad * gain[...]
        mean = jnp.mean(inner, axis=-1, keepdims=True)
        dot = jnp.mean(inner * hat, axis=-1, keepdims=True)
        return rstd_kept[:, 0:1] * (inner - mean - hat * dot)

    def transposed(full, dst):
        for j in range(D // CHUNK):
            turned = full[:, j * CHUNK : (j + 1) * CHUNK].astype(F32).T.astype(BF)
            n = dst.shape[0] // (D // CHUNK)
            dst[j * n : (j + 1) * n] = turned.reshape((n,) + dst.shape[1:])

    def by_rows(cols, dst):
        at = pl.ds(s * zq, zq)
        dst[:, :, :, own_cols] = cols[at]
        return over_section(
            lambda t: cols.at[pl.ds(t * zq, zq)], dst.at[:, :, :, own_cols], dst.at[:, :, :, 0 : (ns - 1) * wl]
        )

    def gather_cols(full):
        block = full.at[:, own_cols]
        return over_section(lambda t: block, block, full.at[:, 0 : (ns - 1) * wl])

    def columns(ref, j):
        return ref[:, :, :, j * CHUNK : (j + 1) * CHUNK].reshape(D, CHUNK)

    def push(src, dst):
        transfer = over_dp(lambda t: src, dst.at[r], dst.at[0 : nd - 1])
        dst[r] = src[...]
        return transfer

    def summed(dst, count):
        total = dst[0].astype(F32)
        for k in range(1, count):
            total = total + dst[k].astype(F32)
        return total

    q_push = push(sc.q_src, sc.q_recv)
    bv_rs = over_dp(lambda t: sc.bv_src.at[t], sc.bv_recv.at[r], sc.bv_recv.at[0 : nd - 1])
    sc.bv_recv[r] = sc.bv_src[r]
    g_gather = gather_cols(sc.g_full)

    issue_own(4)
    issue_z(1)
    q_push.wait_recv()
    query_proj = summed(sc.q_recv, nd) + i.agg_bq[:, own_cols]
    sc.query_proj[...] = query_proj
    head_rows = (iota((16, wl), 1) >> 6 == iota((16, wl), 0)).astype(F32)
    high, low = split(head_rows * (query_proj * scale))
    key_query = (nt(high, sc.wk[...]) + nt(low, sc.wk[...])).astype(BF)
    sc.key_query[...] = key_query
    sc.s_src[...] = nn(key_query, sc.basis[...])[0:8]
    s_push = push(sc.s_src, sc.s_recv)
    bv_rs.wait_recv()
    sc.bv_own[...] = summed(sc.bv_recv, nd).astype(sc.bv_own.dtype)
    bv_ag = push(sc.bv_own, sc.bv_all)
    issue_z(4)
    issue_own(2)

    s_push.wait_recv()
    score_rows = summed(sc.s_recv, nd)
    sc.score_rows[...] = score_rows
    fold = sc.fold[...]
    lane_ok = iota((tokens, LANES), 1) < VARS
    for h in range(hl):
        pix = sc.pix[...].astype(F32)
        high, low = split(pix * score_rows[h : h + 1])
        scores = nn(high, fold) + nn(low, fold)
        scores = jnp.where(lane_ok, scores, -1e30)
        scores = jnp.exp(scores - jnp.max(scores, axis=-1, keepdims=True))
        probs = scores / jnp.sum(scores, axis=-1, keepdims=True)
        sc.probs[h] = probs
        wrep = nt(probs.astype(BF), fold)
        sc.wrep[h] = wrep.astype(BF)
        sc.mixed[h] = (wrep * pix).astype(BF)
    issue_z(1)
    forward(1)
    issue_own(2)
    bv_ag.wait_recv()
    for t in range(nd):
        sc.bv[t * blk : (t + 1) * blk] = sc.bv_all[t].astype(F32)
    value_basis = sc.bv[...].astype(BF)
    head_of = iota((1, wl), 1) >> 6
    context = jnp.broadcast_to(i.agg_bv[:, own_cols], (tokens, wl))
    for h in range(hl):
        context = context + jnp.where(head_of == h, nn(sc.mixed[h], value_basis), 0.0)
    sc.context_full[:, own_cols] = context.astype(BF)
    context_gather = gather_cols(sc.context_full)
    g_gather.wait_recv()
    transposed(sc.g_full, sc.gT)
    issue_own(2)
    forward(1)
    issue_own(1)
    context_gather.wait_recv()
    pass_next()
    landed_x(0)
    part = nn(sc.context_full[...], weight(sc.awo_c)) + i.agg_bo[:, own_cols]
    sc.agg_full[:, own_cols] = part.astype(BF)
    agg_gather = gather_cols(sc.agg_full)
    transposed(sc.context_full, sc.contextT)
    forward(1)
    pass_next()
    agg_gather.wait_recv()
    whole_norm(sc.agg_full, i.attn_norm_gain, i.attn_norm_bias, sc.normed)
    kept_norm(sc.agg_full, sc.hat1, sc.rstd1)
    transposed(sc.normed, sc.normedT)
    pass_next()
    forward(1)
    normed = sc.normed[...]
    for j in range(3):
        landed_x(1 + j)
        part = nn(normed, columns(sc.qkv_w, j))
        if j == 0:
            part = part + i.attn_bq[:, own_cols]
        if j == 2:
            part = part + i.attn_bv[:, own_cols]
        sc.qkv[:, j * wl : (j + 1) * wl] = part.astype(BF)
        if j < 2:
            pass_next()
        if j == 1:
            forward(1)
    lo = (iota((1, LANES), 1) < HEAD).astype(F32)
    first, second = lo.astype(BF), (1.0 - lo).astype(BF)

    def pair(a):
        return jnp.concatenate([a * first, a * second], axis=0)

    def pick(a):
        return jnp.where(iota((LEN, LANES), 1) < HEAD, a[0:LEN], a[LEN:])

    tiles = [(b, p) for b in range(tokens // LEN) for p in range(wl // LANES)]

    def tile(ref, b, p, j=0):
        return ref[b * LEN : (b + 1) * LEN, j * wl + p * LANES : j * wl + (p + 1) * LANES]

    for n, (b, p) in enumerate(tiles):
        q, k, v = [tile(sc.qkv, b, p, j) for j in range(3)]
        ids = jnp.broadcast_to(i.segment_ids[b : b + 1, :].astype(F32), (LEN, LEN))
        same = ids == ids.T
        scores = nt(pair(q), k) * scale
        scores = jnp.where(jnp.concatenate([same, same], axis=0), scores, blocked)
        scores = jnp.exp(scores - jnp.max(scores, axis=-1, keepdims=True))
        probs = scores / jnp.sum(scores, axis=-1, keepdims=True)
        sc.att[n] = probs
        sc.attended[b * LEN : (b + 1) * LEN, p * LANES : (p + 1) * LANES] = pick(
            nn(probs.astype(BF), v)
        ).astype(BF)
    sc.attended_full[:, own_cols] = sc.attended[...]
    attended_gather = gather_cols(sc.attended_full)
    forward(1)
    pass_next()
    attended_gather.wait_recv()
    forward(1)
    pass_next()
    landed_x(4)
    part = nn(sc.attended_full[...], weight(sc.two_c)) + i.attn_bo[:, own_cols]
    sc.mid_full[:, own_cols] = (part + sc.agg_full[:, own_cols].astype(F32)).astype(BF)
    mid_gather = gather_cols(sc.mid_full)
    transposed(sc.attended_full, sc.attendedT)
    forward(1)
    pass_next()
    mid_gather.wait_recv()
    awo_rows = by_rows(sc.awo_c, sc.awo)
    two_rows = by_rows(sc.two_c, sc.two)
    whole_norm(sc.mid_full, i.mlp_norm_gain, i.mlp_norm_bias, sc.mnormed)
    kept_norm(sc.mid_full, sc.hat2, sc.rstd2)
    transposed(sc.mnormed, sc.mnormedT)
    pass_next()
    forward(3)
    mnormed = sc.mnormed[...]
    for j in range(fl // CHUNK):
        at = slice(j * CHUNK, (j + 1) * CHUNK)
        bias = i.mlp_bup[:, pl.ds(pl.multiple_of(s * fl + j * CHUNK, LANES), CHUNK)]
        landed_x(5 + j)
        hidden = nn(mnormed, columns(sc.up_w, j)) + bias
        phi = 0.5 + 0.5 * lax.erf(hidden * 0.7071067811865476)
        density = jnp.exp(hidden * hidden * -0.5) * 0.3989422804014327
        sc.act[:, at] = (hidden * phi).astype(BF)
        sc.slope[:, at] = phi + hidden * density
        if 0 < j <= crossing:
            pass_next()
    names = [(o.mlp_down, lambda q, j=j: q * fl + j * CHUNK) for j in range(fl // CHUNK)]
    names += [(o.mlp_up, lambda q, j=j: q * fl + j * CHUNK) for j in range(fl // CHUNK)]
    names += [(o.singles, lambda q: 3 * D + q * wl)]
    names += [(o.attn_wqkv, lambda q, j=j: j * D + q * wl) for j in range(3)]
    names += [(o.singles, lambda q: 2 * D + q * wl)]
    steps = [(c, 0, CHUNK) for c in range(n_pieces - 1)]
    steps += [(n_pieces - 1, 0, CHUNK // 2), (n_pieces - 1, CHUNK // 2, CHUNK // 2)]
    last = len(steps)

    def view(ref, n):
        c, at, width = steps[n]
        return ref.at[c] if width == CHUNK else ref.at[c, :, :, pl.ds(at, width)]

    to_x, to_z, made, done = {}, {}, [], []
    published = [(send_sem(), recv_sem()) for _ in range(ns)]
    early = 2
    chunk_x, early_x = send_sem(), send_sem()
    all_sent(blocks.at[early:], chunk_x)
    all_sent(blocks.at[0:early, 0], early_x)
    chunk_z = reduce_group(n_pieces - early - 1, sc.z_recv)
    early_z = reduce_group(early, sc.e_recv)

    def produce(c, left, right):
        def half(side):
            block = left[:, pl.ds(side, 1)].reshape(nz * rows, tokens)
            return nn(block, right).reshape(nz, rows, CHUNK)

        sc.x_send[c] = half(1 - x).astype(BF)
        made.extend(n for n in range(last) if steps[n][0] == c)
        sc.keep[c] = half(x)

    def issue_x(until):
        for c in [c for c in made if early <= c <= until and c not in to_x]:
            to_x[c] = over_x(view(sc.x_send, c), view(sc.x_recv, c), chunk_x)

    unmerged = list(range(early, last))

    def produce_early(c, left, right):
        for side in range(nx):
            part = nn(left[:, side].reshape(nz * rows, tokens), right)
            sc.e_send[c, :, side] = part.reshape(nz, rows, CHUNK).astype(BF)
        made.append(c)
        to_z[c] = reduce(sc.e_send.at[c], sc.e_recv.at[c], sc.e_merged.at[c], early_z, True)

    def middle_early(c):
        sc.e_sum[c] = to_z[c].total()
        sc.e_out[c] = sc.e_sum[c, 1 - x].astype(BF)
        to_x[c] = over_x(sc.e_out.at[c], sc.e_in.at[c], early_x)

    def finish_early(c):
        to_x[c].wait_recv()
        sc.final[c] = (sc.e_sum[c, x] + sc.e_in[c].astype(F32)).astype(BF)
        publish(sc.final.at[c], *names[c])

    def middle(n):
        to_x[n].wait_recv()
        issue_x({2: 7, 5: 9, 8: 11}.get(n, 0))
        merged_x = view(sc.keep, n)[...] + view(sc.x_recv, n)[...].astype(F32)
        view(sc.z_send, n)[...] = merged_x.astype(BF)
        group = chunk_z if steps[n][2] == CHUNK else None
        to_z[n] = reduce(view(sc.z_send, n), view(sc.z_recv, n), view(sc.z_merged, n), group)

    mate = s + 1 - 2 * lax.rem(s, 2)
    other = lax.rem(s + ns // 2, ns)
    relayed = []

    def publish(block, array, col, at=0, width=CHUNK):
        def cols(q):
            return array.at[:, pl.ds(pl.multiple_of(col(q) + at, LANES), width)]

        (near, landed), (across, _), (passed, landed_passed) = published[0:3]
        arrival = recv_sem()
        remote(block, cols(s), near, landed, (mate, r)).start()
        remote(block, cols(s), across, arrival, (other, r)).start()
        local(block, cols(s), 3)

        def relay():
            await_landed(cols(other), arrival)
            remote(cols(other), cols(other), passed, landed_passed, (mate, r)).start()

        relayed.append(relay)

    def relay_until(left):
        while len(relayed) > left:
            relayed.pop(0)()

    def finish(n):
        c, at, width = steps[n]
        block = sc.final.at[c] if width == CHUNK else sc.final.at[c, :, pl.ds(at, width)]
        block[...] = to_z[n].total().astype(BF)
        publish(block, *names[c], at, width)

    def finish_up_to(to):
        for c in range(early, to + 1):
            if c not in done:
                finish(c)
                done.append(c)

    def pump(count):
        for _ in range(count):
            c = len(to_z)
            middle(c)
            if c - 2 in unmerged:
                unmerged.remove(c - 2)
                to_z[c - 2].merge()
            if 8 <= c < last - 2 and c - 1 in unmerged:
                unmerged.remove(c - 1)
                to_z[c - 1].merge()
            relay_until(1)
            finish_up_to(c - (3 if c > 9 else 4))

    for j in range(fl // CHUNK):
        make_part = produce_early if j < early else produce
        make_part(j, sc.gT, sc.act[:, j * CHUNK : (j + 1) * CHUNK])
    issue_x(3)
    forward(2)
    for c in range(early):
        to_z[c].begin()
    g_full = sc.g_full[...]
    nmlp = fl // CHUNK
    for j in range(fl // CHUNK):
        at = slice(j * CHUNK, (j + 1) * CHUNK)
        landed_x(5 + nmlp + j)
        d_hidden = nn(g_full, columns(sc.down_w, j)) * sc.slope[:, at]
        sc.d_hidden[:, at] = d_hidden.astype(BF)
    up_w = weight(sc.up_w)
    rs3 = scatter(sc.rs3_part, sc.rs3_recv, nt(sc.d_hidden[...], up_w))
    for j in range(nmlp):
        at = slice(j * CHUNK, (j + 1) * CHUNK)
        produce(nmlp + j, sc.mnormedT, sc.d_hidden[:, at])
    sc.bup[:, own_ff] = colsum(sc.d_hidden[...])
    issue_x(5)
    rs3.wait_recv()
    g_shard = sc.g_full[own_rows, :].astype(F32)
    sc.vecs[0:1, :] = colsum(g_shard)
    d_mid = norm_back(landed_sum(sc.rs3_recv), i.mlp_norm_gain, sc.hat2, sc.rstd2, 1, 2)
    d_mid = (g_shard + d_mid).astype(BF)
    sc.vecs[3:4, :] = colsum(d_mid)
    ag3 = gather(sc.d_mid, d_mid)
    d_mid = d_mid.astype(F32)
    sc.out_part[...] = nt(sc.act[...], weight(sc.down_w))
    sc.out_part[own_rows, :] = sc.out_part[own_rows, :] + sc.mid_full[own_rows, :].astype(F32) + i.mlp_bdown[...]
    sc.out_low[...] = sc.out_part[...].astype(BF)
    out_rs = over_section(
        lambda t: sc.out_low.at[:, pl.ds(pl.multiple_of(t * wl, LANES), wl)],
        sc.out_recv.at[s],
        sc.out_recv.at[0 : ns - 1],
    )
    sc.out_recv[s] = sc.out_low[:, own_cols]
    to_z[0].merge()
    pump(1)
    to_z[1].merge()
    ag3.wait_recv()

    pump(2)
    two_rows.wait_recv()
    d_att = nt(sc.d_mid[...], weight(sc.two)).astype(BF)
    sc.d_att[...] = d_att
    for n, (b, p) in enumerate(tiles):
        q, k, v = [tile(sc.qkv, b, p, j) for j in range(3)]
        q, d_out = pair(q), pair(tile(sc.d_att, b, p))
        probs = sc.att[n]
        d_probs = nt(d_out, v)
        d_scores = probs * (d_probs - jnp.sum(probs * d_probs, axis=-1, keepdims=True))
        d_scores = d_scores.astype(BF)
        parts = (pick(nn(d_scores, k)) * scale, tn(d_scores, q) * scale, tn(probs.astype(BF), d_out))
        for j in range(3):
            lanes = slice(j * wl + p * LANES, j * wl + (p + 1) * LANES)
            sc.d_qkv[b * LEN : (b + 1) * LEN, lanes] = parts[j].astype(BF)
    rs4 = scatter(sc.rs4_part, sc.rs4_recv, nt(sc.d_qkv[...], weight(sc.qkv_w)))
    produce(2 * nmlp, sc.attendedT, sc.d_mid[:, own_cols])
    for j in range(3):
        produce(2 * nmlp + 1 + j, sc.normedT, sc.d_qkv[:, j * wl : (j + 1) * wl])
    sc.vecs[7:8, own_cols] = colsum(sc.d_qkv[:, 0:wl])
    sc.vecs[8:9, own_cols] = colsum(sc.d_qkv[:, 2 * wl : 3 * wl])
    issue_x(8)
    pump(1)
    rs4.wait_recv()
    d_agg = norm_back(landed_sum(sc.rs4_recv), i.attn_norm_gain, sc.hat1, sc.rstd1, 4, 5)
    d_agg = (sc.d_mid[own_rows, :].astype(F32) + d_agg).astype(BF)
    sc.vecs[6:7, :] = colsum(d_agg)
    ag4 = gather(sc.d_agg, d_agg)
    pump(2)
    ag4.wait_recv()

    awo_rows.wait_recv()
    produce(2 * nmlp + 4, sc.contextT, sc.d_agg[:, own_cols])
    d_context = nt(sc.d_agg[...], weight(sc.awo)).astype(BF)
    sc.vecs[9:10, own_cols] = colsum(d_context)
    value_basis = sc.bv[...].astype(BF)
    cross = jnp.zeros((CHUNK, wl), F32)
    grad_pix = jnp.zeros((tokens, CHUNK), F32)
    sc.key_src[...] = jnp.zeros_like(sc.key_src)
    for h in range(hl):
        masked = d_context * (head_of == h).astype(F32).astype(BF)
        pulled = nt(masked, value_basis)
        cross = cross + tn(sc.mixed[h], masked)
        pix = sc.pix[...].astype(F32)
        high, low = split(pulled * pix)
        d_weights = nn(high, fold) + nn(low, fold)
        probs = sc.probs[h]
        d_scores = probs * (d_weights - jnp.sum(probs * d_weights, axis=-1, keepdims=True))
        srep = nt(d_scores.astype(BF), fold)
        sc.key_src[h : h + 1, :] = colsum(srep * pix)
        grad_pix = grad_pix + sc.wrep[h].astype(F32) * pulled
        grad_pix = grad_pix + srep * sc.score_rows[h : h + 1, :]
    key_push = push(sc.key_src, sc.key_recv)
    for t in range(nd):
        sc.m_src[t] = cross[t * blk : (t + 1) * blk].astype(sc.m_src.dtype)
    m_rs = over_dp(lambda t: sc.m_src.at[t], sc.m_recv.at[r], sc.m_recv.at[0 : nd - 1])
    sc.m_recv[r] = sc.m_src[r]
    grad_pix = grad_pix.astype(BF)
    pw = CP // ns
    for t in range(ns):
        sc.pix_src[t] = nt(sc.place[t * pw : (t + 1) * pw, :], grad_pix).astype(BF)
    pix_rs = over_section(lambda t: sc.pix_src.at[t], sc.pix_recv.at[s], sc.pix_recv.at[0 : ns - 1])
    sc.pix_recv[s] = sc.pix_src[s]
    for t in range(nd):
        sc.small_src[t, 0:10] = sc.vecs[0:10, t * rows : (t + 1) * rows]
        for j in range(FF // D):
            start = (t * (FF // D) + j) * rows
            sc.small_src[t, 10 + j : 11 + j] = sc.bup[:, start : start + rows]
    small_rs = over_dp(lambda t: sc.small_src.at[t], sc.small_recv.at[r], sc.small_recv.at[0 : nd - 1])
    sc.small_recv[r] = sc.small_src[r]

    issue_x(10)
    pump(2)
    m_rs.wait_recv()
    sc.m_own[...] = summed(sc.m_recv, nd).astype(sc.m_own.dtype)
    m_ag = push(sc.m_own, sc.m_all)
    key_push.wait_recv()
    key_terms = summed(sc.key_recv, nd)
    wide = jnp.concatenate([jnp.broadcast_to(key_terms[h : h + 1], (HEAD, CHUNK)) for h in range(hl)], axis=0)
    d_key = nt(sc.basis[...], wide.astype(BF))
    d_query = jnp.sum(sc.wk[...].astype(F32) * d_key, axis=0, keepdims=True) * scale
    sc.dq_src[...] = d_query
    dq_push = push(sc.dq_src, sc.dq_recv)
    count = len(names)
    sc.final[count] = (d_key * (sc.query_proj[...] * scale)).astype(BF)
    publish(sc.final.at[count], o.singles, lambda q: q * wl)
    issue_x(last)
    for c in range(early):
        middle_early(c)
    pump(2)
    small_rs.wait_recv()
    sc.sec_small[s] = summed(sc.small_recv, nd)
    small_ag = over_section(lambda t: sc.sec_small.at[s], sc.sec_small.at[s], sc.sec_small.at[0 : ns - 1])
    m_ag.wait_recv()
    for t in range(nd):
        sc.cross[t * blk : (t + 1) * blk] = sc.m_all[t].astype(F32)
    cross = sc.cross[...].astype(BF)
    sc.final[count + 1] = nn(sc.basis[...], cross).astype(BF)
    publish(sc.final.at[count + 1], o.singles, lambda q: 1 * D + q * wl)
    key_low = jnp.concatenate([key_terms, jnp.zeros_like(key_terms)], axis=0).astype(BF)
    grad_basis = nt(cross, sc.wv[...]) + tn(key_low, sc.key_query[...])
    sc.basis_recv[s] = grad_basis.astype(BF)
    basis_sum = over_section(lambda t: sc.basis_recv.at[s], sc.basis_recv.at[s], sc.basis_recv.at[0 : ns - 1])
    dq_push.wait_recv()
    sc.d_query[...] = jnp.broadcast_to(summed(sc.dq_recv, nd), sc.d_query.shape)
    dq_gather = over_section(lambda t: sc.d_query, o.d_query.at[s], o.d_query.at[0 : ns - 1])
    local(sc.d_query, o.d_query.at[s], 5)

    def section_total(ref):
        total = ref[0].astype(F32)
        for k in range(1, ns):
            total = total + ref[k].astype(F32)
        return total

    pump(2)
    finish_up_to(last - 4)
    to_z[last - 2].merge()
    to_z[last - 1].merge()
    for c in range(early):
        finish_early(c)
    finish_up_to(last - 3)
    finish_up_to(last - 2)
    finish_up_to(last - 1)
    out_rs.wait_recv()
    sc.activations[...] = section_total(sc.out_recv).astype(BF)
    local(sc.activations, o.activations, 6)
    pix_rs.wait_recv()
    sc.patches_out[...] = section_total(sc.pix_recv).astype(BF)
    local(sc.patches_out, o.patches, 7)
    small_ag.wait_recv()
    sc.small_out[...] = summed(sc.sec_small, ns)
    local(sc.small_out, o.small, 8)
    relay_until(2)
    basis_sum.wait_recv()
    sc.basis_out[...] = section_total(sc.basis_recv)
    local(sc.basis_out, o.basis, 9)
    dq_gather.wait_recv()
    relay_until(0)
    await_landed(sc.final, published[0][1])
    await_landed(sc.final, published[2][1])
    for out, _ in published[0:3]:
        await_sent(sc.final, out)
    await_local(sc.final, 3)
    await_local(sc.query_rows, 4)
    await_local(sc.d_query, 5)
    await_local(sc.activations, 6)
    await_local(sc.patches_out, 7)
    await_local(sc.small_out, 8)
    await_local(sc.basis_out, 9)
    for wait in pending:
        wait()
    assert used.send <= send.shape[0] and used.recv <= recv.shape[0], used


def scratch(ns, nd, tokens):
    nz, rows = nd // 2, D // nd
    wl, fl, hl = D // ns, FF // ns, HEADS // ns
    shard, zq, blk = tokens // ns, nz // ns, CHUNK // nd
    chunks = 2 * (fl // CHUNK) + 5
    v = pltpu.VMEM
    shapes = dict(
        wq=v((rows, wl), BF),
        wk=v((rows, wl), BF),
        wv=v((rows, wl), BF),
        qkv_w=v((nz, 2, rows, 3 * wl), BF),
        up_w=v((nz, 2, rows, fl), BF),
        down_w=v((nz, 2, rows, fl), BF),
        awo_c=v((nz, 2, rows, wl), BF),
        two_c=v((nz, 2, rows, wl), BF),
        awo=v((zq, 2, rows, D), BF),
        two=v((zq, 2, rows, D), BF),
        g_full=v((tokens, D), BF),
        place=v((CP, CHUNK), BF),
        pix=v((tokens, CHUNK), BF),
        fold=v((CHUNK, LANES), BF),
        basis=v((rows, CHUNK), BF),
        vecs=v((16, D), F32),
        bup=v((1, FF), F32),
        query_proj=v((1, wl), F32),
        key_query=v((16, rows), BF),
        score_rows=v((8, CHUNK), F32),
        bv=v((CHUNK, CHUNK), F32),
        cross=v((CHUNK, CHUNK), F32),
        e_send=v((2, nz, 2, rows, CHUNK), BF),
        e_recv=v((2, nz, 2, rows, CHUNK), BF),
        e_merged=v((2, 2, 2, rows, CHUNK), BF),
        z_merged=v((chunks, 2, rows, CHUNK), BF),
        e_sum=v((2, 2, rows, CHUNK), F32),
        e_out=v((2, rows, CHUNK), BF),
        e_in=v((2, rows, CHUNK), BF),
        probs=v((hl, tokens, LANES), F32),
        wrep=v((hl, tokens, CHUNK), BF),
        mixed=v((hl, tokens, CHUNK), BF),
        context_full=v((tokens, D), BF),
        attended_full=v((tokens, D), BF),
        agg_full=v((tokens, D), BF),
        mid_full=v((tokens, D), BF),
        hat1=v((shard, D), F32),
        hat2=v((shard, D), F32),
        rstd1=v((shard, LANES), F32),
        rstd2=v((shard, LANES), F32),
        normed=v((tokens, D), BF),
        mnormed=v((tokens, D), BF),
        qkv=v((tokens, 3 * wl), BF),
        d_qkv=v((tokens, 3 * wl), BF),
        att=v((tokens // LEN * (wl // LANES), 2 * LEN, LEN), F32),
        attended=v((tokens, wl), BF),
        d_att=v((tokens, wl), BF),
        act=v((tokens, fl), BF),
        slope=v((tokens, fl), F32),
        d_hidden=v((tokens, fl), BF),
        d_mid=v((tokens, D), BF),
        d_agg=v((tokens, D), BF),
        out_part=v((tokens, D), F32),
        out_low=v((tokens, D), BF),
        out_recv=v((ns, tokens, wl), BF),
        pix_src=v((ns, CP // ns, tokens), BF),
        pix_recv=v((ns, CP // ns, tokens), BF),
        small_src=v((nd, 16, rows), F32),
        small_recv=v((nd, 16, rows), F32),
        sec_small=v((ns, 16, rows), F32),
        basis_recv=v((ns, CHUNK, rows), BF),
        x_send=v((chunks, nz, rows, CHUNK), BF),
        x_recv=v((chunks, nz, rows, CHUNK), BF),
        keep=v((chunks, nz, rows, CHUNK), F32),
        z_send=v((chunks, nz, rows, CHUNK), BF),
        z_recv=v((chunks, nz, rows, CHUNK), BF),
        final=v((chunks + 2, rows, CHUNK), BF),
    )
    whole = v((nz, 2, rows, tokens), BF)
    shapes.update(gT=whole, contextT=whole, attendedT=whole, normedT=whole, mnormedT=whole)
    part = v((tokens, D), BF)
    shapes.update(rs3_part=part, rs4_part=part)
    part = v((ns, shard, D), BF)
    shapes.update(rs3_recv=part, rs4_recv=part)
    part = v((8, CHUNK), F32)
    shapes.update(s_src=part, key_src=part)
    part = v((nd, 8, CHUNK), F32)
    shapes.update(s_recv=part, key_recv=part)
    shapes.update(q_src=v((1, CHUNK), F32), dq_src=v((1, CHUNK), F32))
    part = v((nd, 1, CHUNK), F32)
    shapes.update(q_recv=part, dq_recv=part)
    kind = BF if blk % 16 == 0 else F32
    part = v((nd, blk, CHUNK), kind)
    shapes.update(bv_src=part, bv_recv=part, bv_all=part, m_src=part, m_recv=part, m_all=part)
    part = v((blk, CHUNK), kind)
    shapes.update(bv_own=part, m_own=part)
    shapes.update(
        query_rows=v((16, rows), BF),
        d_query=v((8, wl), F32),
        activations=v((tokens, wl), BF),
        patches_out=v((CP // ns, tokens), BF),
        small_out=v((16, rows), F32),
        basis_out=v((CHUNK, rows), F32),
    )
    dma = pltpu.SemaphoreType.DMA
    shapes.update(send=dma((48,)), recv=dma((180,)), local=dma((40,)))
    return shapes


def fused(ns, nd, near, far):
    tokens = near["patches"].shape[1]
    rows = D // nd
    shapes = scratch(ns, nd, tokens)
    arrays = {**near, **far}
    hbm = pl.BlockSpec(memory_space=pl.ANY)
    outs = dict(
        activations=((tokens, D // ns), BF),
        patches=((CP // ns, tokens), BF),
        basis=((CHUNK, rows), F32),
        query_rows=((16, rows), BF),
        d_query=((ns, 8, D // ns), F32),
        small=((16, rows), F32),
        mlp_up=((rows, FF), BF),
        mlp_down=((rows, FF), BF),
        attn_wqkv=((rows, 3 * D), BF),
        singles=((rows, 4 * D), BF),
    )

    def body(*refs):
        n_in, n_out = len(arrays), len(outs)
        kernel(
            ns,
            nd,
            SimpleNamespace(**dict(zip(arrays, refs[:n_in]))),
            SimpleNamespace(**dict(zip(outs, refs[n_in : n_in + n_out]))),
            SimpleNamespace(**dict(zip(shapes, refs[n_in + n_out :]))),
            list(near),
            refs[n_in + n_out + len(shapes) :],
        )

    result = pl.pallas_call(
        body,
        out_shape=[jax.ShapeDtypeStruct(*a) for a in outs.values()],
        in_specs=[hbm] * len(arrays),
        out_specs=[hbm] * len(outs),
        scratch_shapes=list(shapes.values()) + [pltpu.VMEM(a.shape, a.dtype) for a in near.values()],
        compiler_params=pltpu.CompilerParams(
            collective_id=0, has_side_effects=True, vmem_limit_bytes=60 * 1024 * 1024
        ),
        name="block",
    )(*arrays.values())
    return SimpleNamespace(**dict(zip(outs, result)))


def widen(nd, got, agg_wq):
    rows = D // nd
    arrays = [got.mlp_up, got.mlp_down, got.attn_wqkv, got.singles]
    rest = dict(
        activations=got.activations,
        patches=got.patches,
        basis=got.basis,
        query_rows=got.query_rows,
        d_query=got.d_query,
        small=got.small,
        agg_wq=agg_wq,
    )
    line = (1, rows)
    outs = dict(
        activations=(got.activations.shape, BF),
        patches=(got.patches.shape, BF),
        embed=((CP, rows), F32),
        var=((VARS, rows), F32),
        query=(line, F32),
        wq=((rows, D), F32),
        bq=(line, F32),
        bup=((1, rows * (FF // D)), F32),
    )
    lines = tuple(range(10))
    wide = dict(
        mlp_up=((rows, FF), F32),
        mlp_down=((rows, FF), F32),
        attn_wqkv=((rows, 3 * D), F32),
        agg_wk=((rows, D), F32),
        agg_wv=((rows, D), F32),
        agg_wo=((rows, D), F32),
        attn_wo=((rows, D), F32),
    )
    half, third = FF // 2, 3 * D // 2
    tiles = [(0, at, half, 0, at) for at in (0, half)]
    tiles += [(1, at, half, 1, at) for at in (0, half)]
    tiles += [(2, at, third, 2, at) for at in (0, third)]
    tiles += [(3, n * D, D, 3 + n, 0) for n in range(4)]
    everything = {**wide, **outs}
    shaped = [jax.ShapeDtypeStruct(*a) for a in everything.values()]
    shaped += [jax.ShapeDtypeStruct(line, F32) for _ in lines]
    slim = shaped[len(wide) :]

    def body(*refs):
        sources, refs = refs[: len(arrays)], refs[len(arrays) :]
        rest_in, refs = refs[: len(rest)], refs[len(rest) :]
        targets, refs = refs[: len(wide)], refs[len(wide) :]
        slim_out, refs = refs[: len(slim)], refs[len(slim) :]
        near, refs = refs[: len(arrays)], refs[len(arrays) :]
        far, refs = refs[: len(wide)], refs[len(wide) :]
        rest_near, refs = refs[: len(rest)], refs[len(rest) :]
        slim_near, (ins, outgoing) = refs[: len(slim)], refs[len(slim) :]

        def load(t):
            m, at, width, _, _ = tiles[t]
            cols = pl.ds(at, width)
            return pltpu.make_async_copy(sources[m].at[:, cols], near[m].at[:, cols], ins.at[t])

        def store(t):
            _, _, width, m, at = tiles[t]
            cols = pl.ds(at, width)
            return pltpu.make_async_copy(far[m].at[:, cols], targets[m].at[:, cols], outgoing.at[t])

        def load_rest(n):
            return pltpu.make_async_copy(rest_in[n], rest_near[n], ins.at[len(tiles) + n])

        def store_slim(n):
            return pltpu.make_async_copy(slim_near[n], slim_out[n], outgoing.at[len(tiles) + n])

        def widen_tile(t):
            load(t).wait()
            m, at, width, to, start = tiles[t]
            far[to][:, start : start + width] = near[m][:, at : at + width].astype(F32)
            store(t).start()

        for t in range(len(tiles)):
            load(t).start()
        for n in range(len(rest)):
            load_rest(n).start()
        for t in range(len(tiles) // 2):
            widen_tile(t)
        for n in range(len(rest)):
            load_rest(n).wait()
        i = SimpleNamespace(**dict(zip(rest, rest_near)))
        o = SimpleNamespace(**dict(zip(outs, slim_near)))
        left = slim_near[len(outs) :]
        r = lax.axis_index("dp")
        o.activations[...] = i.activations[...]
        o.patches[...] = i.patches[...]
        o.embed[...] = i.basis[0:CP]
        o.var[...] = i.basis[CP : CP + VARS]
        d_query = jnp.concatenate([i.d_query[k] for k in range(i.d_query.shape[0])], axis=1)
        d_query = jnp.concatenate([d_query, d_query], axis=0)
        d_query = jnp.where(iota(d_query.shape, 0) == 0, d_query, 0.0)
        high, low = split(d_query)
        low, rest_low = split(d_query - high.astype(F32))
        chosen = (iota((rows, D), 1) == iota((rows, D), 0) + r * rows).astype(F32).astype(BF)
        o.bq[...] = (nt(high, chosen) + nt(low, chosen) + nt(rest_low, chosen))[0:1]
        weight = i.agg_wq[...]
        o.query[...] = (nt(high, weight) + nt(low, weight) + nt(rest_low, weight))[0:1]
        first = i.query_rows[...]
        o.wq[...] = tn(first, high) + tn(first, low) + tn(first, rest_low)
        o.bup[...] = jnp.concatenate([i.small[10 + k : 11 + k] for k in range(FF // D)], axis=1)
        for k in lines:
            left[k][...] = i.small[k : k + 1]
        for n in range(len(slim)):
            store_slim(n).start()
        for t in range(len(tiles) // 2, len(tiles)):
            widen_tile(t)
        for t in range(len(tiles)):
            store(t).wait()
        for n in range(len(slim)):
            store_slim(n).wait()

    hbm = pl.BlockSpec(memory_space=pl.ANY)
    dma = pltpu.SemaphoreType.DMA
    result = pl.pallas_call(
        body,
        out_shape=shaped,
        in_specs=[hbm] * (len(arrays) + len(rest)),
        out_specs=[hbm] * len(shaped),
        scratch_shapes=[pltpu.VMEM(a.shape, a.dtype) for a in [*arrays, *shaped[: len(wide)], *rest.values(), *slim]]
        + [dma((len(tiles) + len(rest),)), dma((len(tiles) + len(slim),))],
        compiler_params=pltpu.CompilerParams(vmem_limit_bytes=60 * 1024 * 1024),
        name="widen",
    )(*arrays, *rest.values())
    names = list(everything)
    return SimpleNamespace(**dict(zip(names, result))), [a.reshape(-1) for a in result[len(names) :]]


def on_device(
    ns,
    nd,
    patches,
    var_ids,
    segment_ids,
    embed_weight,
    var_embed,
    agg_query,
    agg_wq,
    agg_bq,
    agg_wk,
    agg_wv,
    agg_bv,
    agg_wo,
    agg_bo,
    attn_norm_gain,
    attn_norm_bias,
    attn_wqkv,
    attn_bq,
    attn_bv,
    attn_wo,
    attn_bo,
    mlp_norm_gain,
    mlp_norm_bias,
    mlp_up,
    mlp_bup,
    mlp_down,
    mlp_bdown,
    cotangent,
):
    near = dict(
        patches=patches,
        var_ids=var_ids,
        segment_ids=segment_ids,
        embed_weight=embed_weight,
        var_embed=var_embed,
        agg_query=agg_query,
        agg_bq=agg_bq,
        agg_bv=agg_bv,
        agg_bo=agg_bo,
        attn_norm_gain=attn_norm_gain,
        attn_norm_bias=attn_norm_bias,
        attn_bq=attn_bq,
        attn_bv=attn_bv,
        attn_bo=attn_bo,
        mlp_norm_gain=mlp_norm_gain,
        mlp_norm_bias=mlp_norm_bias,
        mlp_bup=mlp_bup,
        mlp_bdown=mlp_bdown,
    )
    far = dict(
        agg_wq=agg_wq,
        agg_wk=agg_wk,
        agg_wv=agg_wv,
        agg_wo=agg_wo,
        attn_wqkv=attn_wqkv,
        attn_wo=attn_wo,
        mlp_up=mlp_up,
        mlp_down=mlp_down,
        cotangent=cotangent,
    )
    near = {name: a.reshape(1, -1) if a.ndim == 1 else a for name, a in near.items()}
    near["patches"], near["embed_weight"] = patches.T, embed_weight.T
    got = fused(ns, nd, near, far)
    out, small = widen(nd, got, agg_wq)
    return (
        out.activations,
        out.patches.T,
        out.embed.T,
        out.var,
        out.query.reshape(-1),
        out.wq,
        out.bq.reshape(-1),
        out.agg_wk,
        out.agg_wv,
        small[9],
        out.agg_wo,
        small[6],
        small[4],
        small[5],
        out.attn_wqkv,
        small[7],
        small[8],
        out.attn_wo,
        small[3],
        small[1],
        small[2],
        out.mlp_up,
        out.bup.reshape(-1),
        out.mlp_down,
        small[0],
    )


def solution(mesh):
    in_specs = (
        P("dp", None),
        P(),
        P("dp", None),
        P("dp", None),
        P(),
        P(),
        P("dp", None),
        P(),
        P("dp", None),
        P("dp", None),
        P(),
        P("dp", None),
        P(),
        P(),
        P(),
        P("dp", None),
        P(),
        P(),
        P("dp", None),
        P(),
        P(),
        P(),
        P("dp", None),
        P(),
        P("dp", None),
        P(),
        P("dp", "section"),
    )
    out_specs = (
        P("dp", "section"),
        P("dp", "section"),
        P("dp", None),
        P(None, "dp"),
        P("dp"),
        P("dp", None),
        P("dp"),
        P("dp", None),
        P("dp", None),
        P("dp"),
        P("dp", None),
        P("dp"),
        P("dp"),
        P("dp"),
        P("dp", None),
        P("dp"),
        P("dp"),
        P("dp", None),
        P("dp"),
        P("dp"),
        P("dp"),
        P("dp", None),
        P("dp"),
        P("dp", None),
        P("dp"),
    )
    sizes = (mesh.shape["section"], mesh.shape["dp"])
    return jax.shard_map(
        partial(on_device, *sizes), mesh=mesh, in_specs=in_specs, out_specs=out_specs, check_vma=False
    )
```

```python
from functools import partial
from types import SimpleNamespace

import jax
import jax.numpy as jnp
from jax import lax
from jax.experimental import pallas as pl
from jax.experimental.pallas import tpu as pltpu
from jax.sharding import PartitionSpec as P

D = 1024
HEADS = 16
HEAD = 64
FF = 4096
VARS = 48
PIX = 4
LEN = 128

highest = lax.Precision.HIGHEST
blocked = -1000000000.0
epsilon = 1e-05
MESH = pl.DeviceIdType.MESH
BF = jnp.bfloat16
F32 = jnp.float32
CHUNK = 256
CP = VARS * PIX
LANES = 128


def nn(a, b):
    return jnp.dot(a, b, preferred_element_type=F32)


def nt(a, b):
    return lax.dot_general(a, b, (((1,), (1,)), ((), ())), preferred_element_type=F32)


def tn(a, b):
    return lax.dot_general(a, b, (((0,), (0,)), ((), ())), preferred_element_type=F32)


def split(x):
    high = x.astype(BF)
    return high, (x - high.astype(F32)).astype(BF)


def iota(shape, dim):
    return lax.broadcasted_iota(jnp.int32, shape, dim)


def colsum(x):
    return jnp.sum(x.astype(F32), axis=0, keepdims=True)


def each(low, high, body):
    if high - low <= 8:
        for k in range(low, high):
            body(k)
    else:

        def step(k, carry):
            body(k)
            return carry

        lax.fori_loop(low, high, step, 0)


class Transfer:
    def __init__(self, make, low, high, whole):
        self.make, self.low, self.high, self.whole = make, low, high, whole

    def start(self):
        each(self.low, self.high, lambda k: self.make(k).start())
        return self

    def wait_recv(self):
        self.whole().wait_recv()

    def wait_send(self):
        self.whole().wait_send()


def kernel(ns, nd, refs_in, refs_out, sc, near_names, near):
    s = lax.axis_index("section")
    r = lax.axis_index("dp")
    nx = 2
    nz = nd // nx
    z, x = lax.div(r, nx), lax.rem(r, nx)
    o = refs_out
    i = SimpleNamespace(**{**vars(refs_in), **dict(zip(near_names, near))})
    rows = D // nd
    tokens = i.patches.shape[1]
    shard = tokens // ns
    wl, fl, hl = D // ns, FF // ns, HEADS // ns
    zq = nz // ns
    own_cols = pl.ds(pl.multiple_of(s * wl, LANES), wl)
    own_ff = pl.ds(pl.multiple_of(s * fl, LANES), fl)
    own_rows = pl.ds(pl.multiple_of(s * shard, 16), shard)
    scale = HEAD ** (-0.5)
    send, recv = sc.send, sc.recv
    used = SimpleNamespace(send=0, recv=0, local=0)
    pending = []

    def send_sem():
        used.send += 1
        return used.send - 1

    def recv_sem(count=1):
        used.recv += count
        return used.recv - count

    def remote(src, dst, out, landing, device):
        return pltpu.make_async_remote_copy(
            src_ref=src,
            dst_ref=dst,
            send_sem=send.at[out],
            recv_sem=recv.at[landing],
            device_id=device,
            device_id_type=MESH,
        )

    beside = (s, z * nx + 1 - x)

    def await_sent(ref, out):
        remote(ref, ref, out, 0, beside).wait_send()

    def await_landed(ref, landing):
        remote(ref, ref, 0, landing, beside).wait_recv()

    def all_sent(ref, out):
        pending.append(lambda: await_sent(ref, out))

    def over(peer, count, src, dst, whole, out=None, landing=None):
        alone = out is None
        out = send_sem() if alone else out
        landing = recv_sem() if landing is None else landing

        def make(k):
            t, device = peer(k)
            return remote(src(t), dst, out, landing, device)

        transfer = Transfer(make, 1, count, lambda: remote(whole, whole, out, landing, beside)).start()
        if alone:
            pending.append(transfer.wait_send)
        return transfer

    def section_peer(k):
        t = lax.rem(s + k, ns)
        return t, (t, r)

    def dp_peer(k):
        t = lax.rem(r + k, nd)
        return t, (s, t)

    def z_peer(k):
        t = lax.rem(z + k, nz)
        return t, (s, t * nx + x)

    def over_section(src, dst, whole):
        return over(section_peer, ns, src, dst, whole)

    def over_dp(src, dst, whole):
        return over(dp_peer, nd, src, dst, whole)

    def over_x(src, dst, out, landing=None, whole=None):
        whole = src if whole is None else whole
        return over(lambda k: (0, beside), 2, lambda t: src, dst, whole, out, landing)

    def local(src, dst, sem):
        copy = pltpu.make_async_copy(src, dst, sc.local.at[sem])
        copy.start()
        return copy

    def await_local(ref, sem):
        pltpu.make_async_copy(ref, ref, sc.local.at[sem]).wait()

    line = nz == 4
    partner = z + 1 - 2 * lax.rem(z, 2)
    inner = (z == 1) | (z == 2)
    outer = (z == 0) | (z == 3)
    beyond = [lax.rem(2 * lax.div(z, 2) + 2 + j, 4) for j in range(2)]
    gate = 2 - lax.div(z, 2)

    def at_z(t):
        return (s, t * nx + x)

    blocks = sc.z_recv
    n_pieces = blocks.shape[0]
    crossing = 2 if line else 0

    def spread_group(count):
        own, passed = send_sem(), send_sem()
        whole = blocks.at[0:count, 0 : min(2, nz)] if line else blocks.at[0:count, 0 : nz - 1]
        all_sent(whole, own)
        if line:

            def sent():
                @pl.when(inner)
                def _():
                    await_sent(whole, passed)

            pending.append(sent)
        return own, passed

    first_spread = spread_group(n_pieces)
    second_spread = spread_group(crossing) if crossing else None

    def line_spread(block, group):
        base = recv_sem(3)
        out, out_passed = group
        mine_beyond = base + 1 + lax.rem(z, 2)
        remote(block(z), block(z), out, base, at_z(partner)).start()
        remote(block(z), block(z), out, mine_beyond, at_z(gate)).start()

        def pass_on(k):
            t = beyond[k - 1]

            @pl.when(inner)
            def _():
                await_landed(block(t), base + k)
                remote(block(t), block(t), out_passed, base + k, at_z(partner)).start()

        def arrived(k, passed=False):
            t = [partner, *beyond][k]
            if k == 0:
                await_landed(block(t), base)
                return t
            if not passed:
                pass_on(k)

            @pl.when(outer)
            def _():
                await_landed(block(t), base + k)

            return t

        arrived.pass_on = pass_on
        return arrived

    def spread(block, group=first_spread):
        if line:
            return line_spread(block, group)
        whole = blocks.at[0, 0 : nz - 1]
        return over(z_peer, nz, lambda t: block(z), block(z), whole, group[0]).wait_recv

    def reduce_group(count, landed):
        near, far, across = send_sem(), send_sem(), send_sem()
        if not line:
            all_sent(landed.at[0:count, 0 : nz - 1], near)
            return near, far, across
        all_sent(landed.at[0:count, 0], near)

        def sent():
            @pl.when(outer)
            def _():
                await_sent(landed.at[0:count, 0:2], far)

            @pl.when(inner)
            def _():
                await_sent(landed.at[0:count, 0:2], across)

        pending.append(sent)
        return near, far, across

    def line_reduce(parts, landed, merged, group, hold):
        near, far, across = group
        base = recv_sem(3)

        def first():
            remote(parts.at[partner], landed.at[0], near, base, at_z(partner)).start()

        def begin():
            pl.when(inner)(first)

        @pl.when(outer)
        def _():
            first()
            for j in range(2):
                remote(parts.at[beyond[j]], landed.at[2 + j], far, base + 1, at_z(partner)).start()

        if not hold:
            begin()

        def merge():
            @pl.when(inner)
            def _():
                await_landed(landed.at[2:4], base + 1)
                for j in range(2):
                    both = parts[beyond[j]].astype(F32) + landed[2 + j].astype(F32)
                    merged[j] = both.astype(BF)
                    remote(merged.at[j], landed.at[1], across, base + 2, at_z(beyond[j])).start()

        def total():
            await_landed(landed.at[0], base)
            await_landed(landed.at[1], base + 2)
            return parts[z].astype(F32) + landed[0].astype(F32) + landed[1].astype(F32)

        return SimpleNamespace(begin=begin, merge=merge, total=total)

    def reduce(parts, landed, merged, group, hold=False):
        if line and group is not None:
            return line_reduce(parts, landed, merged, group, hold)
        out = None if group is None else group[0]
        transfer = over(z_peer, nz, lambda t: parts.at[t], landed.at[z], landed.at[0 : nz - 1], out)
        landed[z] = parts[z]

        def total():
            transfer.wait_recv()
            value = landed[0].astype(F32)
            for k in range(1, nz):
                value = value + landed[k].astype(F32)
            return value

        return SimpleNamespace(begin=lambda: None, merge=lambda: None, total=total)

    barrier = pltpu.get_barrier_semaphore()
    for k in range(1, ns):
        pl.semaphore_signal(barrier, inc=1, device_id=(lax.rem(s + k, ns), r), device_id_type=MESH)
    each(
        1,
        nd,
        lambda k: pl.semaphore_signal(
            barrier, inc=1, device_id=(s, lax.rem(r + k, nd)), device_id_type=MESH
        ),
    )

    local(i.agg_wq.at[:, own_cols], sc.wq, 0)
    local(i.agg_wk.at[:, own_cols], sc.wk, 0)
    local(i.agg_wv.at[:, own_cols], sc.wv, 0)
    sources = [(i.agg_wo, sc.awo_c, 0, s * wl)]
    sources += [(i.attn_wqkv, sc.qkv_w, j * wl, j * D + s * wl) for j in range(3)]
    sources += [(i.attn_wo, sc.two_c, 0, s * wl)]
    sources += [(i.mlp_up, sc.up_w, j * CHUNK, s * fl + j * CHUNK) for j in range(fl // CHUNK)]
    sources += [(i.mlp_down, sc.down_w, j * CHUNK, s * fl + j * CHUNK) for j in range(fl // CHUNK)]
    pieces = [(dst, pl.ds(at, CHUNK)) for _, dst, at, _ in sources]
    for src, dst, at, col in sources:
        local(src.at[:, pl.ds(pl.multiple_of(col, LANES), CHUNK)], dst.at[z, x, :, pl.ds(at, CHUNK)], 1)
    from_z, from_x, own_x, early_passed = {}, {}, {}, set()

    def pass_next():
        c = max([-1, *early_passed, *from_x]) + 1
        if line:
            early_passed.add(c)
            for k in range(1, nz - 1):
                for arrived in from_z[c]:
                    arrived.pass_on(k)

    late = range(n_pieces - crossing, n_pieces)
    own_order = [*range(6), *late, *range(6, n_pieces - crossing)] if line else []
    from_own, from_others = send_sem(), send_sem()
    if line:
        all_sent(blocks.at[:, 0], from_own)
        all_sent(blocks.at[0 : n_pieces - crossing, 0 : nz - 1], from_others)
    else:
        all_sent(blocks, from_others)
    x_landed = [recv_sem() for _ in range(n_pieces)]

    def issue_own(count):
        for c in own_order[len(own_x) : len(own_x) + count]:
            dst, cols = pieces[c]
            block = dst.at[z, x, :, cols]
            own_x[c] = over_x(block, block, from_own, x_landed[c])

    def issue_z(count):
        for c in range(len(from_z), min(len(from_z) + count, n_pieces)):
            dst, cols = pieces[c]
            from_z[c] = [spread(lambda t, dst=dst, cols=cols: dst.at[t, x, :, cols])]
            if c in late:
                own_x[c].wait_recv()
                other = lambda t, dst=dst, cols=cols: dst.at[t, 1 - x, :, cols]
                from_z[c].append(spread(other, second_spread))

    def forward(count):
        for c in range(len(from_x), min(len(from_x) + count, n_pieces)):
            while line and c not in own_x:
                issue_own(1)
            dst, cols = pieces[c]
            from_x[c] = True
            if not line:
                from_z[c][0]()
                half = dst.at[:, x, :, cols]
                over_x(half, half, from_others, x_landed[c])
            for k in range(nz - 1 if line else 0):
                for arrived in from_z[c]:
                    t = arrived(k, c in early_passed)
                    block = dst.at[t, x, :, cols]
                if c not in late:
                    over_x(block, block, from_others, x_landed[c])
            issue_z(1)

    def landed_x(c):
        dst, cols = pieces[c]
        if c not in late:
            await_landed(dst.at[:, 0, :, cols], x_landed[c])

    local(i.cotangent, sc.g_full.at[:, own_cols], 2)

    for n, name in enumerate(near_names):
        local(getattr(refs_in, name), near[n], 10 + n)
    for n, ref in enumerate(near):
        await_local(ref, 10 + n)

    chan = (iota((CP, VARS), 0) >> 2 == iota((CP, VARS), 1)).astype(F32).astype(BF)
    ids = jnp.broadcast_to(i.var_ids[...].astype(F32), (CHUNK, VARS)).astype(BF)
    ids = nt(chan, ids)
    lane = iota((CP, CHUNK), 1)
    row = iota((CP, CHUNK), 0)
    hit = ((lane >> 2).astype(F32) == ids) & ((lane & 3) == (row & 3)) & (lane < CP)
    place = hit.astype(F32).astype(BF)
    sc.place[...] = place
    lane = iota((tokens, CHUNK), 1)
    ones = ((lane >= CP) & (lane < CP + VARS)).astype(F32)
    sc.pix[...] = (tn(i.patches[...], place) + ones).astype(BF)
    row = iota((CHUNK, LANES), 0)
    lane = iota((CHUNK, LANES), 1)
    owner = jnp.where(row < CP, row >> 2, row - CP)
    sc.fold[...] = ((owner == lane) & (lane < VARS)).astype(F32).astype(BF)
    chosen = (iota((rows, D), 1) == iota((rows, D), 0) + r * rows).astype(F32).astype(BF)
    lane = iota((CP, CHUNK), 1)
    row = iota((CP, CHUNK), 0)
    widen = (lane == row).astype(F32).astype(BF)
    lane = iota((VARS, CHUNK), 1)
    row = iota((VARS, CHUNK), 0)
    widen_var = (lane == row + CP).astype(F32).astype(BF)
    var_rows = nt(chosen, i.var_embed[...].astype(BF)).astype(BF)
    sc.basis[...] = (tn(i.embed_weight[...], widen) + nn(var_rows, widen_var)).astype(BF)
    query = jnp.broadcast_to(i.agg_query[...].astype(BF).astype(F32), (16, D))
    query = jnp.where(iota((16, D), 0) == 0, query, 0.0).astype(BF)
    query_rows = nt(query, chosen).astype(BF)
    sc.query_rows[...] = query_rows
    local(sc.query_rows, o.query_rows, 4)
    sc.vecs[...] = jnp.zeros_like(sc.vecs)
    sc.bup[...] = jnp.zeros_like(sc.bup)

    await_local(blocks.at[0:3, 0], 0)
    sc.q_src[...] = nn(query_rows, sc.wq[...])[0:1]
    value_part = tn(sc.basis[...], sc.wv[...])
    blk = CHUNK // nd
    for t in range(nd):
        sc.bv_src[t] = value_part[t * blk : (t + 1) * blk].astype(sc.bv_src.dtype)
    await_local(sc.g_full.at[:, own_cols], 2)
    await_local(blocks.at[:, 0], 1)

    pl.semaphore_wait(barrier, ns - 1 + nd - 1)

    def weight(ref):
        return ref[...].reshape(ref.shape[0] * ref.shape[1] * ref.shape[2], ref.shape[3])

    def scatter(part, landed, value):
        part[...] = value.astype(BF)
        transfer = over_section(lambda t: part.at[pl.ds(pl.multiple_of(t * shard, 16), shard)], landed.at[s], landed.at[0 : ns - 1])
        landed[s] = part[own_rows, :]
        return transfer

    def gather(full, value):
        full[own_rows, :] = value.astype(BF)
        return over_section(lambda t: full.at[own_rows], full.at[own_rows], full.at[0 : (ns - 1) * shard])

    def landed_sum(landed):
        total = landed[0].astype(F32)
        for k in range(1, ns):
            total = total + landed[k].astype(F32)
        return total

    def normal(value):
        centred = value - jnp.mean(value, axis=-1, keepdims=True)
        rstd = lax.rsqrt(jnp.mean(centred * centred, axis=-1, keepdims=True) + epsilon)
        return centred * rstd, rstd

    def whole_norm(full, gain, bias, dst):
        for t in range(ns):
            at = slice(t * shard, (t + 1) * shard)
            hat, _ = normal(full[at, :].astype(F32))
            dst[at, :] = (hat * gain[...] + bias[...]).astype(BF)

    def kept_norm(full, kept, rstd_kept):
        hat, rstd = normal(full[own_rows, :].astype(F32))
        kept[...] = hat
        rstd_kept[...] = jnp.broadcast_to(rstd, rstd_kept.shape)

    def norm_back(grad, gain, kept, rstd_kept, gain_row, bias_row):
        hat = kept[...]
        sc.vecs[gain_row : gain_row + 1, :] = colsum(grad * hat)
        sc.vecs[bias_row : bias_row + 1, :] = colsum(grad)
        inner = grad * gain[...]
        mean = jnp.mean(inner, axis=-1, keepdims=True)
        dot = jnp.mean(inner * hat, axis=-1, keepdims=True)
        return rstd_kept[:, 0:1] * (inner - mean - hat * dot)

    def transposed(full, dst):
        for j in range(D // CHUNK):
            turned = full[:, j * CHUNK : (j + 1) * CHUNK].astype(F32).T.astype(BF)
            n = dst.shape[0] // (D // CHUNK)
            dst[j * n : (j + 1) * n] = turned.reshape((n,) + dst.shape[1:])

    def by_rows(cols, dst):
        at = pl.ds(s * zq, zq)
        dst[:, :, :, own_cols] = cols[at]
        return over_section(
            lambda t: cols.at[pl.ds(t * zq, zq)], dst.at[:, :, :, own_cols], dst.at[:, :, :, 0 : (ns - 1) * wl]
        )

    def gather_cols(full):
        block = full.at[:, own_cols]
        return over_section(lambda t: block, block, full.at[:, 0 : (ns - 1) * wl])

    def columns(ref, j):
        return ref[:, :, :, j * CHUNK : (j + 1) * CHUNK].reshape(D, CHUNK)

    def push(src, dst):
        transfer = over_dp(lambda t: src, dst.at[r], dst.at[0 : nd - 1])
        dst[r] = src[...]
        return transfer

    def summed(dst, count):
        total = dst[0].astype(F32)
        for k in range(1, count):
            total = total + dst[k].astype(F32)
        return total

    q_push = push(sc.q_src, sc.q_recv)
    bv_rs = over_dp(lambda t: sc.bv_src.at[t], sc.bv_recv.at[r], sc.bv_recv.at[0 : nd - 1])
    sc.bv_recv[r] = sc.bv_src[r]
    g_gather = gather_cols(sc.g_full)

    issue_own(4)
    issue_z(1)
    q_push.wait_recv()
    query_proj = summed(sc.q_recv, nd) + i.agg_bq[:, own_cols]
    sc.query_proj[...] = query_proj
    head_rows = (iota((16, wl), 1) >> 6 == iota((16, wl), 0)).astype(F32)
    high, low = split(head_rows * (query_proj * scale))
    key_query = (nt(high, sc.wk[...]) + nt(low, sc.wk[...])).astype(BF)
    sc.key_query[...] = key_query
    sc.s_src[...] = nn(key_query, sc.basis[...])[0:hl]
    s_push = push(sc.s_src, sc.s_recv)
    bv_rs.wait_recv()
    sc.bv_own[...] = summed(sc.bv_recv, nd).astype(sc.bv_own.dtype)
    bv_ag = push(sc.bv_own, sc.bv_all)
    issue_z(4)
    issue_own(4)
    pass_next()

    s_push.wait_recv()
    score_rows = summed(sc.s_recv, nd)
    sc.score_rows[...] = score_rows
    fold = sc.fold[...]
    lane_ok = iota((tokens, LANES), 1) < VARS
    for h in range(hl):
        pix = sc.pix[...].astype(F32)
        high, low = split(pix * score_rows[h : h + 1])
        scores = nn(high, fold) + nn(low, fold)
        scores = jnp.where(lane_ok, scores, -1e30)
        scores = jnp.exp(scores - jnp.max(scores, axis=-1, keepdims=True))
        probs = scores / jnp.sum(scores, axis=-1, keepdims=True)
        sc.probs[h] = probs
        wrep = nt(probs.astype(BF), fold)
        sc.wrep[h] = wrep.astype(BF)
        sc.mixed[h] = (wrep * pix).astype(BF)
    issue_z(1)
    forward(1)
    issue_own(2)
    pass_next()
    bv_ag.wait_recv()
    for t in range(nd):
        sc.bv[t * blk : (t + 1) * blk] = sc.bv_all[t].astype(F32)
    value_basis = sc.bv[...].astype(BF)
    head_of = iota((1, wl), 1) >> 6
    context = jnp.broadcast_to(i.agg_bv[:, own_cols], (tokens, wl))
    for h in range(hl):
        context = context + jnp.where(head_of == h, nn(sc.mixed[h], value_basis), 0.0)
    sc.context_full[:, own_cols] = context.astype(BF)
    context_gather = gather_cols(sc.context_full)
    g_gather.wait_recv()
    transposed(sc.g_full, sc.gT)
    issue_own(2)
    forward(1)
    issue_own(1)
    context_gather.wait_recv()
    pass_next()
    landed_x(0)
    part = nn(sc.context_full[...], weight(sc.awo_c)) + i.agg_bo[:, own_cols]
    sc.agg_full[:, own_cols] = part.astype(BF)
    agg_gather = gather_cols(sc.agg_full)
    transposed(sc.context_full, sc.contextT)
    forward(1)
    pass_next()
    agg_gather.wait_recv()
    whole_norm(sc.agg_full, i.attn_norm_gain, i.attn_norm_bias, sc.normed)
    kept_norm(sc.agg_full, sc.hat1, sc.rstd1)
    transposed(sc.normed, sc.normedT)
    pass_next()
    forward(1)
    normed = sc.normed[...]
    for j in range(3):
        landed_x(1 + j)
        part = nn(normed, columns(sc.qkv_w, j))
        if j == 0:
            part = part + i.attn_bq[:, own_cols]
        if j == 2:
            part = part + i.attn_bv[:, own_cols]
        sc.qkv[:, j * wl : (j + 1) * wl] = part.astype(BF)
        if j < 2:
            pass_next()
        if j == 1:
            forward(1)
    lo = (iota((1, LANES), 1) < HEAD).astype(F32)
    first, second = lo.astype(BF), (1.0 - lo).astype(BF)

    def pair(a):
        return jnp.concatenate([a * first, a * second], axis=0)

    def pick(a):
        return jnp.where(iota((LEN, LANES), 1) < HEAD, a[0:LEN], a[LEN:])

    tiles = [(b, p) for b in range(tokens // LEN) for p in range(wl // LANES)]

    def tile(ref, b, p, j=0):
        return ref[b * LEN : (b + 1) * LEN, j * wl + p * LANES : j * wl + (p + 1) * LANES]

    for n, (b, p) in enumerate(tiles):
        q, k, v = [tile(sc.qkv, b, p, j) for j in range(3)]
        ids = jnp.broadcast_to(i.segment_ids[b : b + 1, :].astype(F32), (LEN, LEN))
        same = ids == ids.T
        scores = nt(pair(q), k) * scale
        scores = jnp.where(jnp.concatenate([same, same], axis=0), scores, blocked)
        scores = jnp.exp(scores - jnp.max(scores, axis=-1, keepdims=True))
        probs = scores / jnp.sum(scores, axis=-1, keepdims=True)
        sc.att[n] = probs
        sc.attended[b * LEN : (b + 1) * LEN, p * LANES : (p + 1) * LANES] = pick(
            nn(probs.astype(BF), v)
        ).astype(BF)
    sc.attended_full[:, own_cols] = sc.attended[...]
    attended_gather = gather_cols(sc.attended_full)
    forward(1)
    pass_next()
    attended_gather.wait_recv()
    forward(1)
    pass_next()
    landed_x(4)
    part = nn(sc.attended_full[...], weight(sc.two_c)) + i.attn_bo[:, own_cols]
    sc.mid_full[:, own_cols] = (part + sc.agg_full[:, own_cols].astype(F32)).astype(BF)
    mid_gather = gather_cols(sc.mid_full)
    transposed(sc.attended_full, sc.attendedT)
    forward(1)
    pass_next()
    mid_gather.wait_recv()
    awo_rows = by_rows(sc.awo_c, sc.awo)
    two_rows = by_rows(sc.two_c, sc.two)
    whole_norm(sc.mid_full, i.mlp_norm_gain, i.mlp_norm_bias, sc.mnormed)
    kept_norm(sc.mid_full, sc.hat2, sc.rstd2)
    transposed(sc.mnormed, sc.mnormedT)
    pass_next()
    forward(3)
    mnormed = sc.mnormed[...]
    for j in range(fl // CHUNK):
        at = slice(j * CHUNK, (j + 1) * CHUNK)
        bias = i.mlp_bup[:, pl.ds(pl.multiple_of(s * fl + j * CHUNK, LANES), CHUNK)]
        landed_x(5 + j)
        hidden = nn(mnormed, columns(sc.up_w, j)) + bias
        phi = 0.5 + 0.5 * lax.erf(hidden * 0.7071067811865476)
        density = jnp.exp(hidden * hidden * -0.5) * 0.3989422804014327
        sc.act[:, at] = (hidden * phi).astype(BF)
        sc.slope[:, at] = phi + hidden * density
        if 0 < j <= crossing:
            pass_next()
    names = [(o.mlp_down, lambda q, j=j: q * fl + j * CHUNK) for j in range(fl // CHUNK)]
    names += [(o.mlp_up, lambda q, j=j: q * fl + j * CHUNK) for j in range(fl // CHUNK)]
    names += [(o.singles, lambda q: 3 * D + q * wl)]
    names += [(o.attn_wqkv, lambda q, j=j: j * D + q * wl) for j in range(3)]
    names += [(o.singles, lambda q: 2 * D + q * wl)]
    halved = 2
    steps = [(c, 0, CHUNK) for c in range(n_pieces - halved)]
    steps += [(c, at, CHUNK // 2) for c in range(n_pieces - halved, n_pieces) for at in (0, CHUNK // 2)]
    last = len(steps)

    def view(ref, n):
        c, at, width = steps[n]
        return ref.at[c] if width == CHUNK else ref.at[c, :, :, pl.ds(at, width)]

    to_x, to_z, made, done = {}, {}, [], []
    published = [(send_sem(), recv_sem()) for _ in range(ns)]
    early = 2
    chunk_x, early_x = send_sem(), send_sem()
    all_sent(blocks.at[early:], chunk_x)
    all_sent(blocks.at[0:early, 0], early_x)
    chunk_z = reduce_group(n_pieces - early - halved, sc.z_recv)
    early_z = reduce_group(early, sc.e_recv)

    def produce(c, left, right):
        def half(side):
            block = left[:, pl.ds(side, 1)].reshape(nz * rows, tokens)
            return nn(block, right).reshape(nz, rows, CHUNK)

        sc.x_send[c] = half(1 - x).astype(BF)
        made.extend(n for n in range(last) if steps[n][0] == c)
        sc.keep[c] = half(x)

    def issue_x(until):
        for c in [c for c in made if early <= c <= until and c not in to_x]:
            to_x[c] = over_x(view(sc.x_send, c), view(sc.x_recv, c), chunk_x)

    unmerged = list(range(early, last))

    def produce_early(c, left, right):
        for side in range(nx):
            part = nn(left[:, side].reshape(nz * rows, tokens), right)
            sc.e_send[c, :, side] = part.reshape(nz, rows, CHUNK).astype(BF)
        made.append(c)
        to_z[c] = reduce(sc.e_send.at[c], sc.e_recv.at[c], sc.e_merged.at[c], early_z, True)

    def middle_early(c):
        sc.e_sum[c] = to_z[c].total()
        sc.e_out[c] = sc.e_sum[c, 1 - x].astype(BF)
        to_x[c] = over_x(sc.e_out.at[c], sc.e_in.at[c], early_x)

    def finish_early(c):
        to_x[c].wait_recv()
        sc.final[c] = (sc.e_sum[c, x] + sc.e_in[c].astype(F32)).astype(BF)
        publish(sc.final.at[c], *names[c])

    def middle(n):
        to_x[n].wait_recv()
        issue_x({2: 7, 5: 9, 8: 12}.get(n, 0))
        merged_x = view(sc.keep, n)[...] + view(sc.x_recv, n)[...].astype(F32)
        view(sc.z_send, n)[...] = merged_x.astype(BF)
        group = chunk_z if steps[n][2] == CHUNK else None
        to_z[n] = reduce(view(sc.z_send, n), view(sc.z_recv, n), view(sc.z_merged, n), group)

    mate = s + 1 - 2 * lax.rem(s, 2)
    other = lax.rem(s + ns // 2, ns)
    relayed = []

    def publish(block, array, col, at=0, width=CHUNK):
        def cols(q):
            return array.at[:, pl.ds(pl.multiple_of(col(q) + at, LANES), width)]

        (near, landed), (across, _), (passed, landed_passed) = published[0:3]
        arrival = recv_sem()
        remote(block, cols(s), near, landed, (mate, r)).start()
        remote(block, cols(s), across, arrival, (other, r)).start()
        local(block, cols(s), 3)

        def relay():
            await_landed(cols(other), arrival)
            remote(cols(other), cols(other), passed, landed_passed, (mate, r)).start()

        relayed.append(relay)

    def relay_until(left):
        while len(relayed) > left:
            relayed.pop(0)()

    def finish(n):
        c, at, width = steps[n]
        block = sc.final.at[c] if width == CHUNK else sc.final.at[c, :, pl.ds(at, width)]
        block[...] = to_z[n].total().astype(BF)
        publish(block, *names[c], at, width)

    def finish_up_to(to):
        for c in range(early, to + 1):
            if c not in done:
                finish(c)
                done.append(c)

    def pump(count):
        for _ in range(count):
            c = len(to_z)
            middle(c)
            if c - 2 in unmerged:
                unmerged.remove(c - 2)
                to_z[c - 2].merge()
            if c >= 8 and c - 1 in unmerged:
                unmerged.remove(c - 1)
                to_z[c - 1].merge()
            relay_until(1)
            finish_up_to(min(c - (3 if c > 9 else 4), last - 2 * halved - 1))

    for j in range(fl // CHUNK):
        make_part = produce_early if j < early else produce
        make_part(j, sc.gT, sc.act[:, j * CHUNK : (j + 1) * CHUNK])
    issue_x(3)
    forward(2)
    for c in range(early):
        to_z[c].begin()
    g_full = sc.g_full[...]
    nmlp = fl // CHUNK
    for j in range(fl // CHUNK):
        at = slice(j * CHUNK, (j + 1) * CHUNK)
        landed_x(5 + nmlp + j)
        d_hidden = nn(g_full, columns(sc.down_w, j)) * sc.slope[:, at]
        sc.d_hidden[:, at] = d_hidden.astype(BF)
    up_w = weight(sc.up_w)
    rs3 = scatter(sc.rs3_part, sc.rs3_recv, nt(sc.d_hidden[...], up_w))
    for j in range(nmlp):
        at = slice(j * CHUNK, (j + 1) * CHUNK)
        produce(nmlp + j, sc.mnormedT, sc.d_hidden[:, at])
    sc.bup[:, own_ff] = colsum(sc.d_hidden[...])
    issue_x(5)
    rs3.wait_recv()
    g_shard = sc.g_full[own_rows, :].astype(F32)
    sc.vecs[0:1, :] = colsum(g_shard)
    d_mid = norm_back(landed_sum(sc.rs3_recv), i.mlp_norm_gain, sc.hat2, sc.rstd2, 1, 2)
    d_mid = (g_shard + d_mid).astype(BF)
    sc.vecs[3:4, :] = colsum(d_mid)
    ag3 = gather(sc.d_mid, d_mid)
    d_mid = d_mid.astype(F32)
    sc.out_part[...] = nt(sc.act[...], weight(sc.down_w))
    sc.out_part[own_rows, :] = sc.out_part[own_rows, :] + sc.mid_full[own_rows, :].astype(F32) + i.mlp_bdown[...]
    sc.out_low[...] = sc.out_part[...].astype(BF)
    out_rs = over_section(
        lambda t: sc.out_low.at[:, pl.ds(pl.multiple_of(t * wl, LANES), wl)],
        sc.out_recv.at[s],
        sc.out_recv.at[0 : ns - 1],
    )
    sc.out_recv[s] = sc.out_low[:, own_cols]
    to_z[0].merge()
    pump(1)
    to_z[1].merge()
    ag3.wait_recv()

    pump(2)
    two_rows.wait_recv()
    d_att = nt(sc.d_mid[...], weight(sc.two)).astype(BF)
    sc.d_att[...] = d_att
    for n, (b, p) in enumerate(tiles):
        q, k, v = [tile(sc.qkv, b, p, j) for j in range(3)]
        q, d_out = pair(q), pair(tile(sc.d_att, b, p))
        probs = sc.att[n]
        d_probs = nt(d_out, v)
        d_scores = probs * (d_probs - jnp.sum(probs * d_probs, axis=-1, keepdims=True))
        d_scores = d_scores.astype(BF)
        parts = (pick(nn(d_scores, k)) * scale, tn(d_scores, q) * scale, tn(probs.astype(BF), d_out))
        for j in range(3):
            lanes = slice(j * wl + p * LANES, j * wl + (p + 1) * LANES)
            sc.d_qkv[b * LEN : (b + 1) * LEN, lanes] = parts[j].astype(BF)
    rs4 = scatter(sc.rs4_part, sc.rs4_recv, nt(sc.d_qkv[...], weight(sc.qkv_w)))
    produce(2 * nmlp, sc.attendedT, sc.d_mid[:, own_cols])
    for j in range(3):
        produce(2 * nmlp + 1 + j, sc.normedT, sc.d_qkv[:, j * wl : (j + 1) * wl])
    sc.vecs[7:8, own_cols] = colsum(sc.d_qkv[:, 0:wl])
    sc.vecs[8:9, own_cols] = colsum(sc.d_qkv[:, 2 * wl : 3 * wl])
    issue_x(8)
    pump(1)
    rs4.wait_recv()
    d_agg = norm_back(landed_sum(sc.rs4_recv), i.attn_norm_gain, sc.hat1, sc.rstd1, 4, 5)
    d_agg = (sc.d_mid[own_rows, :].astype(F32) + d_agg).astype(BF)
    sc.vecs[6:7, :] = colsum(d_agg)
    ag4 = gather(sc.d_agg, d_agg)
    pump(2)
    ag4.wait_recv()

    awo_rows.wait_recv()
    produce(2 * nmlp + 4, sc.contextT, sc.d_agg[:, own_cols])
    d_context = nt(sc.d_agg[...], weight(sc.awo)).astype(BF)
    sc.vecs[9:10, own_cols] = colsum(d_context)
    value_basis = sc.bv[...].astype(BF)
    cross = jnp.zeros((CHUNK, wl), F32)
    grad_pix = jnp.zeros((tokens, CHUNK), F32)
    for h in range(hl):
        masked = d_context * (head_of == h).astype(F32).astype(BF)
        pulled = nt(masked, value_basis)
        cross = cross + tn(sc.mixed[h], masked)
        pix = sc.pix[...].astype(F32)
        high, low = split(pulled * pix)
        d_weights = nn(high, fold) + nn(low, fold)
        probs = sc.probs[h]
        d_scores = probs * (d_weights - jnp.sum(probs * d_weights, axis=-1, keepdims=True))
        srep = nt(d_scores.astype(BF), fold)
        sc.key_src[h : h + 1, :] = colsum(srep * pix)
        grad_pix = grad_pix + sc.wrep[h].astype(F32) * pulled
        grad_pix = grad_pix + srep * sc.score_rows[h : h + 1, :]
    key_push = push(sc.key_src, sc.key_recv)
    for t in range(nd):
        sc.m_src[t] = cross[t * blk : (t + 1) * blk].astype(sc.m_src.dtype)
    m_rs = over_dp(lambda t: sc.m_src.at[t], sc.m_recv.at[r], sc.m_recv.at[0 : nd - 1])
    sc.m_recv[r] = sc.m_src[r]
    grad_pix = grad_pix.astype(BF)
    pw = CP // ns
    for t in range(ns):
        sc.pix_src[t] = nt(sc.place[t * pw : (t + 1) * pw, :], grad_pix).astype(BF)
    pix_rs = over_section(lambda t: sc.pix_src.at[t], sc.pix_recv.at[s], sc.pix_recv.at[0 : ns - 1])
    sc.pix_recv[s] = sc.pix_src[s]
    for t in range(nd):
        sc.small_src[t, 0:10] = sc.vecs[0:10, t * rows : (t + 1) * rows]
        for j in range(FF // D):
            start = (t * (FF // D) + j) * rows
            sc.small_src[t, 10 + j : 11 + j] = sc.bup[:, start : start + rows]
    small_rs = over_dp(lambda t: sc.small_src.at[t], sc.small_recv.at[r], sc.small_recv.at[0 : nd - 1])
    sc.small_recv[r] = sc.small_src[r]

    issue_x(10)
    pump(2)
    m_rs.wait_recv()
    sc.m_own[...] = summed(sc.m_recv, nd).astype(sc.m_own.dtype)
    m_ag = push(sc.m_own, sc.m_all)
    key_push.wait_recv()
    key_terms = summed(sc.key_recv, nd)
    wide = jnp.concatenate([jnp.broadcast_to(key_terms[h : h + 1], (HEAD, CHUNK)) for h in range(hl)], axis=0)
    d_key = nt(sc.basis[...], wide.astype(BF))
    d_query = jnp.sum(sc.wk[...].astype(F32) * d_key, axis=0, keepdims=True) * scale
    sc.dq_src[...] = d_query
    dq_push = push(sc.dq_src, sc.dq_recv)
    count = len(names)
    sc.final[count] = (d_key * (sc.query_proj[...] * scale)).astype(BF)
    publish(sc.final.at[count], o.singles, lambda q: q * wl)
    issue_x(last)
    for c in range(early):
        middle_early(c)
    pump(2)
    small_rs.wait_recv()
    sc.sec_small[s] = summed(sc.small_recv, nd)
    small_ag = over_section(lambda t: sc.sec_small.at[s], sc.sec_small.at[s], sc.sec_small.at[0 : ns - 1])
    m_ag.wait_recv()
    for t in range(nd):
        sc.cross[t * blk : (t + 1) * blk] = sc.m_all[t].astype(F32)
    cross = sc.cross[...].astype(BF)
    sc.final[count + 1] = nn(sc.basis[...], cross).astype(BF)
    publish(sc.final.at[count + 1], o.singles, lambda q: 1 * D + q * wl)
    key_low = jnp.concatenate([key_terms, jnp.zeros((16 - hl, CHUNK), F32)], axis=0).astype(BF)
    grad_basis = nt(cross, sc.wv[...]) + tn(key_low, sc.key_query[...])
    sc.basis_recv[s] = grad_basis.astype(BF)
    basis_sum = over_section(lambda t: sc.basis_recv.at[s], sc.basis_recv.at[s], sc.basis_recv.at[0 : ns - 1])
    dq_push.wait_recv()
    sc.d_query[...] = jnp.broadcast_to(summed(sc.dq_recv, nd), sc.d_query.shape)
    dq_gather = over_section(lambda t: sc.d_query, o.d_query.at[s], o.d_query.at[0 : ns - 1])
    local(sc.d_query, o.d_query.at[s], 5)

    def section_total(ref):
        total = ref[0].astype(F32)
        for k in range(1, ns):
            total = total + ref[k].astype(F32)
        return total

    pump(3)
    finish_up_to(last - 2 * halved)
    for c in range(early):
        finish_early(c)
    finish_up_to(last - 3)
    finish_up_to(last - 2)
    finish_up_to(last - 1)
    out_rs.wait_recv()
    sc.activations[...] = section_total(sc.out_recv).astype(BF)
    local(sc.activations, o.activations, 6)
    pix_rs.wait_recv()
    sc.patches_out[...] = section_total(sc.pix_recv).astype(BF)
    local(sc.patches_out, o.patches, 7)
    small_ag.wait_recv()
    sc.small_out[...] = summed(sc.sec_small, ns)
    local(sc.small_out, o.small, 8)
    relay_until(2)
    basis_sum.wait_recv()
    sc.basis_out[...] = section_total(sc.basis_recv)
    local(sc.basis_out, o.basis, 9)
    dq_gather.wait_recv()
    relay_until(0)
    await_landed(sc.final, published[0][1])
    await_landed(sc.final, published[2][1])
    for out, _ in published[0:3]:
        await_sent(sc.final, out)
    await_local(sc.final, 3)
    await_local(sc.query_rows, 4)
    await_local(sc.d_query, 5)
    await_local(sc.activations, 6)
    await_local(sc.patches_out, 7)
    await_local(sc.small_out, 8)
    await_local(sc.basis_out, 9)
    for wait in pending:
        wait()
    assert used.send <= send.shape[0] and used.recv <= recv.shape[0], used


def scratch(ns, nd, tokens):
    nz, rows = nd // 2, D // nd
    wl, fl, hl = D // ns, FF // ns, HEADS // ns
    shard, zq, blk = tokens // ns, nz // ns, CHUNK // nd
    chunks = 2 * (fl // CHUNK) + 5
    v = pltpu.VMEM
    shapes = dict(
        wq=v((rows, wl), BF),
        wk=v((rows, wl), BF),
        wv=v((rows, wl), BF),
        qkv_w=v((nz, 2, rows, 3 * wl), BF),
        up_w=v((nz, 2, rows, fl), BF),
        down_w=v((nz, 2, rows, fl), BF),
        awo_c=v((nz, 2, rows, wl), BF),
        two_c=v((nz, 2, rows, wl), BF),
        awo=v((zq, 2, rows, D), BF),
        two=v((zq, 2, rows, D), BF),
        g_full=v((tokens, D), BF),
        place=v((CP, CHUNK), BF),
        pix=v((tokens, CHUNK), BF),
        fold=v((CHUNK, LANES), BF),
        basis=v((rows, CHUNK), BF),
        vecs=v((16, D), F32),
        bup=v((1, FF), F32),
        query_proj=v((1, wl), F32),
        key_query=v((16, rows), BF),
        score_rows=v((hl, CHUNK), F32),
        bv=v((CHUNK, CHUNK), F32),
        cross=v((CHUNK, CHUNK), F32),
        e_send=v((2, nz, 2, rows, CHUNK), BF),
        e_recv=v((2, nz, 2, rows, CHUNK), BF),
        e_merged=v((2, 2, 2, rows, CHUNK), BF),
        z_merged=v((chunks, 2, rows, CHUNK), BF),
        e_sum=v((2, 2, rows, CHUNK), F32),
        e_out=v((2, rows, CHUNK), BF),
        e_in=v((2, rows, CHUNK), BF),
        probs=v((hl, tokens, LANES), F32),
        wrep=v((hl, tokens, CHUNK), BF),
        mixed=v((hl, tokens, CHUNK), BF),
        context_full=v((tokens, D), BF),
        attended_full=v((tokens, D), BF),
        agg_full=v((tokens, D), BF),
        mid_full=v((tokens, D), BF),
        hat1=v((shard, D), F32),
        hat2=v((shard, D), F32),
        rstd1=v((shard, LANES), F32),
        rstd2=v((shard, LANES), F32),
        normed=v((tokens, D), BF),
        mnormed=v((tokens, D), BF),
        qkv=v((tokens, 3 * wl), BF),
        d_qkv=v((tokens, 3 * wl), BF),
        att=v((tokens // LEN * (wl // LANES), 2 * LEN, LEN), F32),
        attended=v((tokens, wl), BF),
        d_att=v((tokens, wl), BF),
        act=v((tokens, fl), BF),
        slope=v((tokens, fl), F32),
        d_hidden=v((tokens, fl), BF),
        d_mid=v((tokens, D), BF),
        d_agg=v((tokens, D), BF),
        out_part=v((tokens, D), F32),
        out_low=v((tokens, D), BF),
        out_recv=v((ns, tokens, wl), BF),
        pix_src=v((ns, CP // ns, tokens), BF),
        pix_recv=v((ns, CP // ns, tokens), BF),
        small_src=v((nd, 16, rows), F32),
        small_recv=v((nd, 16, rows), F32),
        sec_small=v((ns, 16, rows), F32),
        basis_recv=v((ns, CHUNK, rows), BF),
        x_send=v((chunks, nz, rows, CHUNK), BF),
        x_recv=v((chunks, nz, rows, CHUNK), BF),
        keep=v((chunks, nz, rows, CHUNK), F32),
        z_send=v((chunks, nz, rows, CHUNK), BF),
        z_recv=v((chunks, nz, rows, CHUNK), BF),
        final=v((chunks + 2, rows, CHUNK), BF),
    )
    whole = v((nz, 2, rows, tokens), BF)
    shapes.update(gT=whole, contextT=whole, attendedT=whole, normedT=whole, mnormedT=whole)
    part = v((tokens, D), BF)
    shapes.update(rs3_part=part, rs4_part=part)
    part = v((ns, shard, D), BF)
    shapes.update(rs3_recv=part, rs4_recv=part)
    part = v((hl, CHUNK), F32)
    shapes.update(s_src=part, key_src=part)
    part = v((nd, hl, CHUNK), F32)
    shapes.update(s_recv=part, key_recv=part)
    shapes.update(q_src=v((1, CHUNK), F32), dq_src=v((1, CHUNK), F32))
    part = v((nd, 1, CHUNK), F32)
    shapes.update(q_recv=part, dq_recv=part)
    kind = BF if blk % 16 == 0 else F32
    part = v((nd, blk, CHUNK), kind)
    shapes.update(bv_src=part, bv_recv=part, bv_all=part, m_src=part, m_recv=part, m_all=part)
    part = v((blk, CHUNK), kind)
    shapes.update(bv_own=part, m_own=part)
    shapes.update(
        query_rows=v((16, rows), BF),
        d_query=v((8, wl), F32),
        activations=v((tokens, wl), BF),
        patches_out=v((CP // ns, tokens), BF),
        small_out=v((16, rows), F32),
        basis_out=v((CHUNK, rows), F32),
    )
    dma = pltpu.SemaphoreType.DMA
    shapes.update(send=dma((52,)), recv=dma((160,)), local=dma((28,)))
    return shapes


def fused(ns, nd, near, far):
    tokens = near["patches"].shape[1]
    rows = D // nd
    shapes = scratch(ns, nd, tokens)
    arrays = {**near, **far}
    hbm = pl.BlockSpec(memory_space=pl.ANY)
    outs = dict(
        activations=((tokens, D // ns), BF),
        patches=((CP // ns, tokens), BF),
        basis=((CHUNK, rows), F32),
        query_rows=((16, rows), BF),
        d_query=((ns, 8, D // ns), F32),
        small=((16, rows), F32),
        mlp_up=((rows, FF), BF),
        mlp_down=((rows, FF), BF),
        attn_wqkv=((rows, 3 * D), BF),
        singles=((rows, 4 * D), BF),
    )

    def body(*refs):
        n_in, n_out = len(arrays), len(outs)
        kernel(
            ns,
            nd,
            SimpleNamespace(**dict(zip(arrays, refs[:n_in]))),
            SimpleNamespace(**dict(zip(outs, refs[n_in : n_in + n_out]))),
            SimpleNamespace(**dict(zip(shapes, refs[n_in + n_out :]))),
            list(near),
            refs[n_in + n_out + len(shapes) :],
        )

    result = pl.pallas_call(
        body,
        out_shape=[jax.ShapeDtypeStruct(*a) for a in outs.values()],
        in_specs=[hbm] * len(arrays),
        out_specs=[hbm] * len(outs),
        scratch_shapes=list(shapes.values()) + [pltpu.VMEM(a.shape, a.dtype) for a in near.values()],
        compiler_params=pltpu.CompilerParams(
            collective_id=0, has_side_effects=True, vmem_limit_bytes=60 * 1024 * 1024
        ),
        name="block",
    )(*arrays.values())
    return SimpleNamespace(**dict(zip(outs, result)))


def widen(nd, got, agg_wq):
    rows = D // nd
    arrays = [got.mlp_up, got.mlp_down, got.attn_wqkv, got.singles]
    rest = dict(
        activations=got.activations,
        patches=got.patches,
        basis=got.basis,
        query_rows=got.query_rows,
        d_query=got.d_query,
        small=got.small,
        agg_wq=agg_wq,
    )
    line = (1, rows)
    outs = dict(
        activations=(got.activations.shape, BF),
        patches=(got.patches.shape, BF),
        embed=((CP, rows), F32),
        var=((VARS, rows), F32),
        query=(line, F32),
        wq=((rows, D), F32),
        bq=(line, F32),
        bup=((1, rows * (FF // D)), F32),
    )
    lines = tuple(range(10))
    wide = dict(
        mlp_up=((rows, FF), F32),
        mlp_down=((rows, FF), F32),
        attn_wqkv=((rows, 3 * D), F32),
        agg_wk=((rows, D), F32),
        agg_wv=((rows, D), F32),
        agg_wo=((rows, D), F32),
        attn_wo=((rows, D), F32),
    )
    half, third = FF // 2, 3 * D // 2
    tiles = [(0, at, half, 0, at) for at in (0, half)]
    tiles += [(1, at, half, 1, at) for at in (0, half)]
    tiles += [(2, at, third, 2, at) for at in (0, third)]
    tiles += [(3, n * D, D, 3 + n, 0) for n in range(4)]
    everything = {**wide, **outs}
    shaped = [jax.ShapeDtypeStruct(*a) for a in everything.values()]
    shaped += [jax.ShapeDtypeStruct(line, F32) for _ in lines]
    slim = shaped[len(wide) :]

    def body(*refs):
        sources, refs = refs[: len(arrays)], refs[len(arrays) :]
        rest_in, refs = refs[: len(rest)], refs[len(rest) :]
        targets, refs = refs[: len(wide)], refs[len(wide) :]
        slim_out, refs = refs[: len(slim)], refs[len(slim) :]
        near, refs = refs[: len(arrays)], refs[len(arrays) :]
        far, refs = refs[: len(wide)], refs[len(wide) :]
        rest_near, refs = refs[: len(rest)], refs[len(rest) :]
        slim_near, (ins, outgoing) = refs[: len(slim)], refs[len(slim) :]

        def load(t):
            m, at, width, _, _ = tiles[t]
            cols = pl.ds(at, width)
            return pltpu.make_async_copy(sources[m].at[:, cols], near[m].at[:, cols], ins.at[t])

        def store(t):
            _, _, width, m, at = tiles[t]
            cols = pl.ds(at, width)
            return pltpu.make_async_copy(far[m].at[:, cols], targets[m].at[:, cols], outgoing.at[t])

        def load_rest(n):
            return pltpu.make_async_copy(rest_in[n], rest_near[n], ins.at[len(tiles) + n])

        def store_slim(n):
            return pltpu.make_async_copy(slim_near[n], slim_out[n], outgoing.at[len(tiles) + n])

        def widen_tile(t):
            load(t).wait()
            m, at, width, to, start = tiles[t]
            far[to][:, start : start + width] = near[m][:, at : at + width].astype(F32)
            store(t).start()

        for n in range(len(rest)):
            load_rest(n).start()
        for t in range(len(tiles)):
            load(t).start()
        for n in range(len(rest)):
            load_rest(n).wait()
        i = SimpleNamespace(**dict(zip(rest, rest_near)))
        o = SimpleNamespace(**dict(zip(outs, slim_near)))
        left = slim_near[len(outs) :]
        r = lax.axis_index("dp")
        o.activations[...] = i.activations[...]
        o.patches[...] = i.patches[...]
        o.embed[...] = i.basis[0:CP]
        o.var[...] = i.basis[CP : CP + VARS]
        d_query = jnp.concatenate([i.d_query[k] for k in range(i.d_query.shape[0])], axis=1)
        d_query = jnp.concatenate([d_query, d_query], axis=0)
        d_query = jnp.where(iota(d_query.shape, 0) == 0, d_query, 0.0)
        high, low = split(d_query)
        low, rest_low = split(d_query - high.astype(F32))
        chosen = (iota((rows, D), 1) == iota((rows, D), 0) + r * rows).astype(F32).astype(BF)
        o.bq[...] = (nt(high, chosen) + nt(low, chosen) + nt(rest_low, chosen))[0:1]
        weight = i.agg_wq[...]
        o.query[...] = (nt(high, weight) + nt(low, weight) + nt(rest_low, weight))[0:1]
        first = i.query_rows[...]
        o.wq[...] = tn(first, high) + tn(first, low) + tn(first, rest_low)
        o.bup[...] = jnp.concatenate([i.small[10 + k : 11 + k] for k in range(FF // D)], axis=1)
        for k in lines:
            left[k][...] = i.small[k : k + 1]
        for n in range(len(slim)):
            store_slim(n).start()
        for t in range(len(tiles)):
            widen_tile(t)
        for t in range(len(tiles)):
            store(t).wait()
        for n in range(len(slim)):
            store_slim(n).wait()

    hbm = pl.BlockSpec(memory_space=pl.ANY)
    dma = pltpu.SemaphoreType.DMA
    result = pl.pallas_call(
        body,
        out_shape=shaped,
        in_specs=[hbm] * (len(arrays) + len(rest)),
        out_specs=[hbm] * len(shaped),
        scratch_shapes=[pltpu.VMEM(a.shape, a.dtype) for a in [*arrays, *shaped[: len(wide)], *rest.values(), *slim]]
        + [dma((len(tiles) + len(rest),)), dma((len(tiles) + len(slim),))],
        compiler_params=pltpu.CompilerParams(vmem_limit_bytes=60 * 1024 * 1024),
        name="widen",
    )(*arrays, *rest.values())
    names = list(everything)
    return SimpleNamespace(**dict(zip(names, result))), [a.reshape(-1) for a in result[len(names) :]]


def on_device(
    ns,
    nd,
    patches,
    var_ids,
    segment_ids,
    embed_weight,
    var_embed,
    agg_query,
    agg_wq,
    agg_bq,
    agg_wk,
    agg_wv,
    agg_bv,
    agg_wo,
    agg_bo,
    attn_norm_gain,
    attn_norm_bias,
    attn_wqkv,
    attn_bq,
    attn_bv,
    attn_wo,
    attn_bo,
    mlp_norm_gain,
    mlp_norm_bias,
    mlp_up,
    mlp_bup,
    mlp_down,
    mlp_bdown,
    cotangent,
):
    near = dict(
        patches=patches,
        var_ids=var_ids,
        segment_ids=segment_ids,
        embed_weight=embed_weight,
        var_embed=var_embed,
        agg_query=agg_query,
        agg_bq=agg_bq,
        agg_bv=agg_bv,
        agg_bo=agg_bo,
        attn_norm_gain=attn_norm_gain,
        attn_norm_bias=attn_norm_bias,
        attn_bq=attn_bq,
        attn_bv=attn_bv,
        attn_bo=attn_bo,
        mlp_norm_gain=mlp_norm_gain,
        mlp_norm_bias=mlp_norm_bias,
        mlp_bup=mlp_bup,
        mlp_bdown=mlp_bdown,
    )
    far = dict(
        agg_wq=agg_wq,
        agg_wk=agg_wk,
        agg_wv=agg_wv,
        agg_wo=agg_wo,
        attn_wqkv=attn_wqkv,
        attn_wo=attn_wo,
        mlp_up=mlp_up,
        mlp_down=mlp_down,
        cotangent=cotangent,
    )
    near = {name: a.reshape(1, -1) if a.ndim == 1 else a for name, a in near.items()}
    near["patches"], near["embed_weight"] = patches.T, embed_weight.T
    got = fused(ns, nd, near, far)
    out, small = widen(nd, got, agg_wq)
    return (
        out.activations,
        out.patches.T,
        out.embed.T,
        out.var,
        out.query.reshape(-1),
        out.wq,
        out.bq.reshape(-1),
        out.agg_wk,
        out.agg_wv,
        small[9],
        out.agg_wo,
        small[6],
        small[4],
        small[5],
        out.attn_wqkv,
        small[7],
        small[8],
        out.attn_wo,
        small[3],
        small[1],
        small[2],
        out.mlp_up,
        out.bup.reshape(-1),
        out.mlp_down,
        small[0],
    )


def solution(mesh):
    in_specs = (
        P("dp", None),
        P(),
        P("dp", None),
        P("dp", None),
        P(),
        P(),
        P("dp", None),
        P(),
        P("dp", None),
        P("dp", None),
        P(),
        P("dp", None),
        P(),
        P(),
        P(),
        P("dp", None),
        P(),
        P(),
        P("dp", None),
        P(),
        P(),
        P(),
        P("dp", None),
        P(),
        P("dp", None),
        P(),
        P("dp", "section"),
    )
    out_specs = (
        P("dp", "section"),
        P("dp", "section"),
        P("dp", None),
        P(None, "dp"),
        P("dp"),
        P("dp", None),
        P("dp"),
        P("dp", None),
        P("dp", None),
        P("dp"),
        P("dp", None),
        P("dp"),
        P("dp"),
        P("dp"),
        P("dp", None),
        P("dp"),
        P("dp"),
        P("dp", None),
        P("dp"),
        P("dp"),
        P("dp"),
        P("dp", None),
        P("dp"),
        P("dp", None),
        P("dp"),
    )
    sizes = (mesh.shape["section"], mesh.shape["dp"])
    return jax.shard_map(
        partial(on_device, *sizes), mesh=mesh, in_specs=in_specs, out_specs=out_specs, check_vma=False
    )
```

```python
from functools import partial
from types import SimpleNamespace

import jax
import jax.numpy as jnp
from jax import lax
from jax.experimental import pallas as pl
from jax.experimental.pallas import tpu as pltpu
from jax.sharding import PartitionSpec as P

D = 1024
HEADS = 16
HEAD = 64
FF = 4096
VARS = 48
PIX = 4
LEN = 128

highest = lax.Precision.HIGHEST
blocked = -1000000000.0
epsilon = 1e-05
MESH = pl.DeviceIdType.MESH
BF = jnp.bfloat16
F32 = jnp.float32
CHUNK = 256
CP = VARS * PIX
LANES = 128


def nn(a, b):
    return jnp.dot(a, b, preferred_element_type=F32)


def nt(a, b):
    return lax.dot_general(a, b, (((1,), (1,)), ((), ())), preferred_element_type=F32)


def tn(a, b):
    return lax.dot_general(a, b, (((0,), (0,)), ((), ())), preferred_element_type=F32)


def split(x):
    high = x.astype(BF)
    return high, (x - high.astype(F32)).astype(BF)


def iota(shape, dim):
    return lax.broadcasted_iota(jnp.int32, shape, dim)


def colsum(x):
    return jnp.sum(x.astype(F32), axis=0, keepdims=True)


def each(low, high, body):
    if high - low <= 8:
        for k in range(low, high):
            body(k)
    else:

        def step(k, carry):
            body(k)
            return carry

        lax.fori_loop(low, high, step, 0)


class Transfer:
    def __init__(self, make, low, high, whole):
        self.make, self.low, self.high, self.whole = make, low, high, whole

    def start(self):
        each(self.low, self.high, lambda k: self.make(k).start())
        return self

    def wait_recv(self):
        self.whole().wait_recv()

    def wait_send(self):
        self.whole().wait_send()


def kernel(ns, nd, refs_in, refs_out, sc, near_names, near):
    s = lax.axis_index("section")
    r = lax.axis_index("dp")
    nx = 2
    nz = nd // nx
    z, x = lax.div(r, nx), lax.rem(r, nx)
    o = refs_out
    i = SimpleNamespace(**{**vars(refs_in), **dict(zip(near_names, near))})
    rows = D // nd
    tokens = i.patches.shape[1]
    shard = tokens // ns
    wl, fl, hl = D // ns, FF // ns, HEADS // ns
    zq = nz // ns
    own_cols = pl.ds(pl.multiple_of(s * wl, LANES), wl)
    own_ff = pl.ds(pl.multiple_of(s * fl, LANES), fl)
    own_rows = pl.ds(pl.multiple_of(s * shard, 16), shard)
    scale = HEAD ** (-0.5)
    send, recv = sc.send, sc.recv
    used = SimpleNamespace(send=0, recv=0, local=0)
    pending = []

    def send_sem():
        used.send += 1
        return used.send - 1

    def recv_sem(count=1):
        used.recv += count
        return used.recv - count

    def remote(src, dst, out, landing, device):
        return pltpu.make_async_remote_copy(
            src_ref=src,
            dst_ref=dst,
            send_sem=send.at[out],
            recv_sem=recv.at[landing],
            device_id=device,
            device_id_type=MESH,
        )

    beside = (s, z * nx + 1 - x)

    def await_sent(ref, out):
        remote(ref, ref, out, 0, beside).wait_send()

    def await_landed(ref, landing):
        remote(ref, ref, 0, landing, beside).wait_recv()

    def all_sent(ref, out):
        pending.append(lambda: await_sent(ref, out))

    def over(peer, count, src, dst, whole, out=None, landing=None):
        alone = out is None
        out = send_sem() if alone else out
        landing = recv_sem() if landing is None else landing

        def make(k):
            t, device = peer(k)
            return remote(src(t), dst, out, landing, device)

        transfer = Transfer(make, 1, count, lambda: remote(whole, whole, out, landing, beside)).start()
        if alone:
            pending.append(transfer.wait_send)
        return transfer

    def section_peer(k):
        t = lax.rem(s + k, ns)
        return t, (t, r)

    def dp_peer(k):
        t = lax.rem(r + k, nd)
        return t, (s, t)

    def z_peer(k):
        t = lax.rem(z + k, nz)
        return t, (s, t * nx + x)

    def over_section(src, dst, whole):
        return over(section_peer, ns, src, dst, whole)

    def over_dp(src, dst, whole):
        return over(dp_peer, nd, src, dst, whole)

    def over_x(src, dst, out, landing=None, whole=None):
        whole = src if whole is None else whole
        return over(lambda k: (0, beside), 2, lambda t: src, dst, whole, out, landing)

    def local(src, dst, sem):
        copy = pltpu.make_async_copy(src, dst, sc.local.at[sem])
        copy.start()
        return copy

    def await_local(ref, sem):
        pltpu.make_async_copy(ref, ref, sc.local.at[sem]).wait()

    line = nz == 4
    partner = z + 1 - 2 * lax.rem(z, 2)
    inner = (z == 1) | (z == 2)
    outer = (z == 0) | (z == 3)
    beyond = [lax.rem(2 * lax.div(z, 2) + 2 + j, 4) for j in range(2)]
    gate = 2 - lax.div(z, 2)

    def at_z(t):
        return (s, t * nx + x)

    blocks = sc.z_recv
    n_pieces = blocks.shape[0]
    crossing = 2 if line else 0

    def spread_group(count):
        own, passed = send_sem(), send_sem()
        whole = blocks.at[0:count, 0 : min(2, nz)] if line else blocks.at[0:count, 0 : nz - 1]
        all_sent(whole, own)
        if line:

            def sent():
                @pl.when(inner)
                def _():
                    await_sent(whole, passed)

            pending.append(sent)
        return own, passed

    first_spread = spread_group(n_pieces)
    second_spread = spread_group(crossing) if crossing else None

    def line_spread(block, group):
        base = recv_sem(3)
        out, out_passed = group
        mine_beyond = base + 1 + lax.rem(z, 2)
        remote(block(z), block(z), out, base, at_z(partner)).start()
        remote(block(z), block(z), out, mine_beyond, at_z(gate)).start()

        def pass_on(k):
            t = beyond[k - 1]

            @pl.when(inner)
            def _():
                await_landed(block(t), base + k)
                remote(block(t), block(t), out_passed, base + k, at_z(partner)).start()

        def arrived(k, passed=False):
            t = [partner, *beyond][k]
            if k == 0:
                await_landed(block(t), base)
                return t
            if not passed:
                pass_on(k)

            @pl.when(outer)
            def _():
                await_landed(block(t), base + k)

            return t

        arrived.pass_on = pass_on
        return arrived

    def spread(block, group=first_spread):
        if line:
            return line_spread(block, group)
        whole = blocks.at[0, 0 : nz - 1]
        return over(z_peer, nz, lambda t: block(z), block(z), whole, group[0]).wait_recv

    def reduce_group(count, landed):
        near, far, across = send_sem(), send_sem(), send_sem()
        if not line:
            all_sent(landed.at[0:count, 0 : nz - 1], near)
            return near, far, across
        all_sent(landed.at[0:count, 0], near)

        def sent():
            @pl.when(outer)
            def _():
                await_sent(landed.at[0:count, 0:2], far)

            @pl.when(inner)
            def _():
                await_sent(landed.at[0:count, 0:2], across)

        pending.append(sent)
        return near, far, across

    def line_reduce(parts, landed, merged, group, hold):
        near, far, across = group
        base = recv_sem(3)

        def first():
            remote(parts.at[partner], landed.at[0], near, base, at_z(partner)).start()

        def begin():
            pl.when(inner)(first)

        @pl.when(outer)
        def _():
            first()
            for j in range(2):
                remote(parts.at[beyond[j]], landed.at[2 + j], far, base + 1, at_z(partner)).start()

        if not hold:
            begin()

        def merge():
            @pl.when(inner)
            def _():
                await_landed(landed.at[2:4], base + 1)
                for j in range(2):
                    both = parts[beyond[j]].astype(F32) + landed[2 + j].astype(F32)
                    merged[j] = both.astype(BF)
                    remote(merged.at[j], landed.at[1], across, base + 2, at_z(beyond[j])).start()

        def total():
            await_landed(landed.at[0], base)
            await_landed(landed.at[1], base + 2)
            return parts[z].astype(F32) + landed[0].astype(F32) + landed[1].astype(F32)

        return SimpleNamespace(begin=begin, merge=merge, total=total)

    def reduce(parts, landed, merged, group, hold=False):
        if line and group is not None:
            return line_reduce(parts, landed, merged, group, hold)
        out = None if group is None else group[0]
        transfer = over(z_peer, nz, lambda t: parts.at[t], landed.at[z], landed.at[0 : nz - 1], out)
        landed[z] = parts[z]

        def total():
            transfer.wait_recv()
            value = landed[0].astype(F32)
            for k in range(1, nz):
                value = value + landed[k].astype(F32)
            return value

        return SimpleNamespace(begin=lambda: None, merge=lambda: None, total=total)

    barrier = pltpu.get_barrier_semaphore()
    for k in range(1, ns):
        pl.semaphore_signal(barrier, inc=1, device_id=(lax.rem(s + k, ns), r), device_id_type=MESH)
    each(
        1,
        nd,
        lambda k: pl.semaphore_signal(
            barrier, inc=1, device_id=(s, lax.rem(r + k, nd)), device_id_type=MESH
        ),
    )

    local(i.agg_wq.at[:, own_cols], sc.wq, 0)
    local(i.agg_wk.at[:, own_cols], sc.wk, 0)
    local(i.agg_wv.at[:, own_cols], sc.wv, 0)
    sources = [(i.agg_wo, sc.awo_c, 0, s * wl)]
    sources += [(i.attn_wqkv, sc.qkv_w, j * wl, j * D + s * wl) for j in range(3)]
    sources += [(i.attn_wo, sc.two_c, 0, s * wl)]
    sources += [(i.mlp_up, sc.up_w, j * CHUNK, s * fl + j * CHUNK) for j in range(fl // CHUNK)]
    sources += [(i.mlp_down, sc.down_w, j * CHUNK, s * fl + j * CHUNK) for j in range(fl // CHUNK)]
    pieces = [(dst, pl.ds(at, CHUNK)) for _, dst, at, _ in sources]
    for src, dst, at, col in sources:
        local(src.at[:, pl.ds(pl.multiple_of(col, LANES), CHUNK)], dst.at[z, x, :, pl.ds(at, CHUNK)], 1)
    from_z, from_x, own_x, early_passed = {}, {}, {}, set()

    def pass_next():
        c = max([-1, *early_passed, *from_x]) + 1
        if line:
            early_passed.add(c)
            for k in range(1, nz - 1):
                for arrived in from_z[c]:
                    arrived.pass_on(k)

    late = range(n_pieces - crossing, n_pieces)
    own_order = [*range(6), *late, *range(6, n_pieces - crossing)] if line else []
    from_own, from_others = send_sem(), send_sem()
    if line:
        all_sent(blocks.at[:, 0], from_own)
        all_sent(blocks.at[0 : n_pieces - crossing, 0 : nz - 1], from_others)
    else:
        all_sent(blocks, from_others)
    x_landed = [recv_sem() for _ in range(n_pieces)]

    def issue_own(count):
        for c in own_order[len(own_x) : len(own_x) + count]:
            dst, cols = pieces[c]
            block = dst.at[z, x, :, cols]
            own_x[c] = over_x(block, block, from_own, x_landed[c])

    def issue_z(count):
        for c in range(len(from_z), min(len(from_z) + count, n_pieces)):
            dst, cols = pieces[c]
            from_z[c] = [spread(lambda t, dst=dst, cols=cols: dst.at[t, x, :, cols])]
            if c in late:
                own_x[c].wait_recv()
                other = lambda t, dst=dst, cols=cols: dst.at[t, 1 - x, :, cols]
                from_z[c].append(spread(other, second_spread))

    def forward(count):
        for c in range(len(from_x), min(len(from_x) + count, n_pieces)):
            while line and c not in own_x:
                issue_own(1)
            dst, cols = pieces[c]
            from_x[c] = True
            if not line:
                from_z[c][0]()
                half = dst.at[:, x, :, cols]
                over_x(half, half, from_others, x_landed[c])
            for k in range(nz - 1 if line else 0):
                for arrived in from_z[c]:
                    t = arrived(k, c in early_passed)
                    block = dst.at[t, x, :, cols]
                if c not in late:
                    over_x(block, block, from_others, x_landed[c])
            issue_z(1)

    def landed_x(c):
        dst, cols = pieces[c]
        if c not in late:
            await_landed(dst.at[:, 0, :, cols], x_landed[c])

    local(i.cotangent, sc.g_full.at[:, own_cols], 2)

    for n, name in enumerate(near_names):
        local(getattr(refs_in, name), near[n], 10 + n)
    for n, ref in enumerate(near):
        await_local(ref, 10 + n)

    chan = (iota((CP, VARS), 0) >> 2 == iota((CP, VARS), 1)).astype(F32).astype(BF)
    ids = jnp.broadcast_to(i.var_ids[...].astype(F32), (CHUNK, VARS)).astype(BF)
    ids = nt(chan, ids)
    lane = iota((CP, CHUNK), 1)
    row = iota((CP, CHUNK), 0)
    hit = ((lane >> 2).astype(F32) == ids) & ((lane & 3) == (row & 3)) & (lane < CP)
    place = hit.astype(F32).astype(BF)
    sc.place[...] = place
    lane = iota((tokens, CHUNK), 1)
    ones = ((lane >= CP) & (lane < CP + VARS)).astype(F32)
    sc.pix[...] = (tn(i.patches[...], place) + ones).astype(BF)
    row = iota((CHUNK, LANES), 0)
    lane = iota((CHUNK, LANES), 1)
    owner = jnp.where(row < CP, row >> 2, row - CP)
    sc.fold[...] = ((owner == lane) & (lane < VARS)).astype(F32).astype(BF)
    chosen = (iota((rows, D), 1) == iota((rows, D), 0) + r * rows).astype(F32).astype(BF)
    lane = iota((CP, CHUNK), 1)
    row = iota((CP, CHUNK), 0)
    widen = (lane == row).astype(F32).astype(BF)
    lane = iota((VARS, CHUNK), 1)
    row = iota((VARS, CHUNK), 0)
    widen_var = (lane == row + CP).astype(F32).astype(BF)
    var_rows = nt(chosen, i.var_embed[...].astype(BF)).astype(BF)
    sc.basis[...] = (tn(i.embed_weight[...], widen) + nn(var_rows, widen_var)).astype(BF)
    query = jnp.broadcast_to(i.agg_query[...].astype(BF).astype(F32), (16, D))
    query = jnp.where(iota((16, D), 0) == 0, query, 0.0).astype(BF)
    query_rows = nt(query, chosen).astype(BF)
    sc.query_rows[...] = query_rows
    local(sc.query_rows, o.query_rows, 4)
    sc.vecs[...] = jnp.zeros_like(sc.vecs)
    sc.bup[...] = jnp.zeros_like(sc.bup)

    await_local(blocks.at[0:3, 0], 0)
    sc.q_src[...] = nn(query_rows, sc.wq[...])[0:1]
    value_part = tn(sc.basis[...], sc.wv[...])
    blk = CHUNK // nd
    for t in range(nd):
        sc.bv_src[t] = value_part[t * blk : (t + 1) * blk].astype(sc.bv_src.dtype)
    await_local(sc.g_full.at[:, own_cols], 2)
    await_local(blocks.at[:, 0], 1)

    pl.semaphore_wait(barrier, ns - 1 + nd - 1)

    def weight(ref):
        return ref[...].reshape(ref.shape[0] * ref.shape[1] * ref.shape[2], ref.shape[3])

    def scatter(part, landed, value):
        part[...] = value.astype(BF)
        transfer = over_section(lambda t: part.at[pl.ds(pl.multiple_of(t * shard, 16), shard)], landed.at[s], landed.at[0 : ns - 1])
        landed[s] = part[own_rows, :]
        return transfer

    def gather(full, value):
        full[own_rows, :] = value.astype(BF)
        return over_section(lambda t: full.at[own_rows], full.at[own_rows], full.at[0 : (ns - 1) * shard])

    def landed_sum(landed):
        total = landed[0].astype(F32)
        for k in range(1, ns):
            total = total + landed[k].astype(F32)
        return total

    def normal(value):
        centred = value - jnp.mean(value, axis=-1, keepdims=True)
        rstd = lax.rsqrt(jnp.mean(centred * centred, axis=-1, keepdims=True) + epsilon)
        return centred * rstd, rstd

    def whole_norm(full, gain, bias, dst):
        for t in range(ns):
            at = slice(t * shard, (t + 1) * shard)
            hat, _ = normal(full[at, :].astype(F32))
            dst[at, :] = (hat * gain[...] + bias[...]).astype(BF)

    def kept_norm(full, kept, rstd_kept):
        hat, rstd = normal(full[own_rows, :].astype(F32))
        kept[...] = hat
        rstd_kept[...] = jnp.broadcast_to(rstd, rstd_kept.shape)

    def norm_back(grad, gain, kept, rstd_kept, gain_row, bias_row):
        hat = kept[...]
        sc.vecs[gain_row : gain_row + 1, :] = colsum(grad * hat)
        sc.vecs[bias_row : bias_row + 1, :] = colsum(grad)
        inner = grad * gain[...]
        mean = jnp.mean(inner, axis=-1, keepdims=True)
        dot = jnp.mean(inner * hat, axis=-1, keepdims=True)
        return rstd_kept[:, 0:1] * (inner - mean - hat * dot)

    def transposed(full, dst):
        for j in range(D // CHUNK):
            turned = full[:, j * CHUNK : (j + 1) * CHUNK].astype(F32).T.astype(BF)
            n = dst.shape[0] // (D // CHUNK)
            dst[j * n : (j + 1) * n] = turned.reshape((n,) + dst.shape[1:])

    def by_rows(cols, dst):
        at = pl.ds(s * zq, zq)
        dst[:, :, :, own_cols] = cols[at]
        return over_section(
            lambda t: cols.at[pl.ds(t * zq, zq)], dst.at[:, :, :, own_cols], dst.at[:, :, :, 0 : (ns - 1) * wl]
        )

    def gather_cols(full):
        block = full.at[:, own_cols]
        return over_section(lambda t: block, block, full.at[:, 0 : (ns - 1) * wl])

    def columns(ref, j):
        return ref[:, :, :, j * CHUNK : (j + 1) * CHUNK].reshape(D, CHUNK)

    def push(src, dst):
        transfer = over_dp(lambda t: src, dst.at[r], dst.at[0 : nd - 1])
        dst[r] = src[...]
        return transfer

    def summed(dst, count):
        total = dst[0].astype(F32)
        for k in range(1, count):
            total = total + dst[k].astype(F32)
        return total

    q_push = push(sc.q_src, sc.q_recv)
    bv_rs = over_dp(lambda t: sc.bv_src.at[t], sc.bv_recv.at[r], sc.bv_recv.at[0 : nd - 1])
    sc.bv_recv[r] = sc.bv_src[r]
    g_gather = gather_cols(sc.g_full)

    issue_own(4)
    issue_z(1)
    q_push.wait_recv()
    query_proj = summed(sc.q_recv, nd) + i.agg_bq[:, own_cols]
    sc.query_proj[...] = query_proj
    head_rows = (iota((16, wl), 1) >> 6 == iota((16, wl), 0)).astype(F32)
    high, low = split(head_rows * (query_proj * scale))
    key_query = (nt(high, sc.wk[...]) + nt(low, sc.wk[...])).astype(BF)
    sc.key_query[...] = key_query
    sc.s_src[...] = nn(key_query, sc.basis[...])[0:hl]
    s_push = push(sc.s_src, sc.s_recv)
    bv_rs.wait_recv()
    sc.bv_own[...] = summed(sc.bv_recv, nd).astype(sc.bv_own.dtype)
    bv_ag = push(sc.bv_own, sc.bv_all)
    issue_z(4)
    issue_own(4)
    pass_next()

    s_push.wait_recv()
    score_rows = summed(sc.s_recv, nd)
    sc.score_rows[...] = score_rows
    fold = sc.fold[...]
    lane_ok = iota((tokens, LANES), 1) < VARS
    for h in range(hl):
        pix = sc.pix[...].astype(F32)
        high, low = split(pix * score_rows[h : h + 1])
        scores = nn(high, fold) + nn(low, fold)
        scores = jnp.where(lane_ok, scores, -1e30)
        scores = jnp.exp(scores - jnp.max(scores, axis=-1, keepdims=True))
        probs = scores / jnp.sum(scores, axis=-1, keepdims=True)
        sc.probs[h] = probs
        wrep = nt(probs.astype(BF), fold)
        sc.wrep[h] = wrep.astype(BF)
        sc.mixed[h] = (wrep * pix).astype(BF)
    issue_z(1)
    forward(1)
    issue_own(2)
    pass_next()
    bv_ag.wait_recv()
    for t in range(nd):
        sc.bv[t * blk : (t + 1) * blk] = sc.bv_all[t].astype(F32)
    value_basis = sc.bv[...].astype(BF)
    head_of = iota((1, wl), 1) >> 6
    context = jnp.broadcast_to(i.agg_bv[:, own_cols], (tokens, wl))
    for h in range(hl):
        context = context + jnp.where(head_of == h, nn(sc.mixed[h], value_basis), 0.0)
    sc.context_full[:, own_cols] = context.astype(BF)
    context_gather = gather_cols(sc.context_full)
    g_gather.wait_recv()
    transposed(sc.g_full, sc.gT)
    issue_own(2)
    forward(1)
    issue_own(1)
    context_gather.wait_recv()
    pass_next()
    landed_x(0)
    part = nn(sc.context_full[...], weight(sc.awo_c)) + i.agg_bo[:, own_cols]
    sc.agg_full[:, own_cols] = part.astype(BF)
    agg_gather = gather_cols(sc.agg_full)
    transposed(sc.context_full, sc.contextT)
    forward(1)
    pass_next()
    agg_gather.wait_recv()
    whole_norm(sc.agg_full, i.attn_norm_gain, i.attn_norm_bias, sc.normed)
    kept_norm(sc.agg_full, sc.hat1, sc.rstd1)
    transposed(sc.normed, sc.normedT)
    pass_next()
    forward(1)
    normed = sc.normed[...]
    for j in range(3):
        landed_x(1 + j)
        part = nn(normed, columns(sc.qkv_w, j))
        if j == 0:
            part = part + i.attn_bq[:, own_cols]
        if j == 2:
            part = part + i.attn_bv[:, own_cols]
        sc.qkv[:, j * wl : (j + 1) * wl] = part.astype(BF)
        if j < 2:
            pass_next()
        if j == 1:
            forward(1)
    lo = (iota((1, LANES), 1) < HEAD).astype(F32)
    first, second = lo.astype(BF), (1.0 - lo).astype(BF)

    def pair(a):
        return jnp.concatenate([a * first, a * second], axis=0)

    def pick(a):
        return jnp.where(iota((LEN, LANES), 1) < HEAD, a[0:LEN], a[LEN:])

    tiles = [(b, p) for b in range(tokens // LEN) for p in range(wl // LANES)]

    def tile(ref, b, p, j=0):
        return ref[b * LEN : (b + 1) * LEN, j * wl + p * LANES : j * wl + (p + 1) * LANES]

    for n, (b, p) in enumerate(tiles):
        q, k, v = [tile(sc.qkv, b, p, j) for j in range(3)]
        ids = jnp.broadcast_to(i.segment_ids[b : b + 1, :].astype(F32), (LEN, LEN))
        same = ids == ids.T
        scores = nt(pair(q), k) * scale
        scores = jnp.where(jnp.concatenate([same, same], axis=0), scores, blocked)
        scores = jnp.exp(scores - jnp.max(scores, axis=-1, keepdims=True))
        probs = scores / jnp.sum(scores, axis=-1, keepdims=True)
        sc.att[n] = probs
        sc.attended[b * LEN : (b + 1) * LEN, p * LANES : (p + 1) * LANES] = pick(
            nn(probs.astype(BF), v)
        ).astype(BF)
    sc.attended_full[:, own_cols] = sc.attended[...]
    attended_gather = gather_cols(sc.attended_full)
    forward(1)
    pass_next()
    attended_gather.wait_recv()
    forward(1)
    pass_next()
    landed_x(4)
    part = nn(sc.attended_full[...], weight(sc.two_c)) + i.attn_bo[:, own_cols]
    sc.mid_full[:, own_cols] = (part + sc.agg_full[:, own_cols].astype(F32)).astype(BF)
    mid_gather = gather_cols(sc.mid_full)
    transposed(sc.attended_full, sc.attendedT)
    forward(1)
    pass_next()
    mid_gather.wait_recv()
    awo_rows = by_rows(sc.awo_c, sc.awo)
    two_rows = by_rows(sc.two_c, sc.two)
    whole_norm(sc.mid_full, i.mlp_norm_gain, i.mlp_norm_bias, sc.mnormed)
    kept_norm(sc.mid_full, sc.hat2, sc.rstd2)
    transposed(sc.mnormed, sc.mnormedT)
    pass_next()
    forward(3)
    mnormed = sc.mnormed[...]
    for j in range(fl // CHUNK):
        at = slice(j * CHUNK, (j + 1) * CHUNK)
        bias = i.mlp_bup[:, pl.ds(pl.multiple_of(s * fl + j * CHUNK, LANES), CHUNK)]
        landed_x(5 + j)
        hidden = nn(mnormed, columns(sc.up_w, j)) + bias
        phi = 0.5 + 0.5 * lax.erf(hidden * 0.7071067811865476)
        density = jnp.exp(hidden * hidden * -0.5) * 0.3989422804014327
        sc.act[:, at] = (hidden * phi).astype(BF)
        sc.slope[:, at] = phi + hidden * density
        if 0 < j <= crossing:
            pass_next()
    names = [(o.mlp_down, lambda q, j=j: q * fl + j * CHUNK) for j in range(fl // CHUNK)]
    names += [(o.mlp_up, lambda q, j=j: q * fl + j * CHUNK) for j in range(fl // CHUNK)]
    names += [(o.singles, lambda q: 3 * D + q * wl)]
    names += [(o.attn_wqkv, lambda q, j=j: j * D + q * wl) for j in range(3)]
    names += [(o.singles, lambda q: 2 * D + q * wl)]
    halved = 2
    steps = [(c, 0, CHUNK) for c in range(n_pieces - halved)]
    steps += [(c, at, CHUNK // 2) for c in range(n_pieces - halved, n_pieces) for at in (0, CHUNK // 2)]
    last = len(steps)

    def view(ref, n):
        c, at, width = steps[n]
        return ref.at[c] if width == CHUNK else ref.at[c, :, :, pl.ds(at, width)]

    to_x, to_z, made, done = {}, {}, [], []
    published = [(send_sem(), recv_sem()) for _ in range(ns)]
    early = 2
    chunk_x, early_x = send_sem(), send_sem()
    all_sent(blocks.at[early:], chunk_x)
    all_sent(blocks.at[0:early, 0], early_x)
    chunk_z = reduce_group(n_pieces - early - halved, sc.z_recv)
    early_z = reduce_group(early, sc.e_recv)

    def produce(c, left, right):
        def half(side):
            block = left[:, pl.ds(side, 1)].reshape(nz * rows, tokens)
            return nn(block, right).reshape(nz, rows, CHUNK)

        sc.x_send[c] = half(1 - x).astype(BF)
        made.extend(n for n in range(last) if steps[n][0] == c)
        sc.keep[c] = half(x)

    def issue_x(until):
        for c in [c for c in made if early <= c <= until and c not in to_x]:
            to_x[c] = over_x(view(sc.x_send, c), view(sc.x_recv, c), chunk_x)

    unmerged = list(range(early, last))

    def produce_early(c, left, right):
        for side in range(nx):
            part = nn(left[:, side].reshape(nz * rows, tokens), right)
            sc.e_send[c, :, side] = part.reshape(nz, rows, CHUNK).astype(BF)
        made.append(c)
        to_z[c] = reduce(sc.e_send.at[c], sc.e_recv.at[c], sc.e_merged.at[c], early_z, True)

    def middle_early(c):
        sc.e_sum[c] = to_z[c].total()
        sc.e_out[c] = sc.e_sum[c, 1 - x].astype(BF)
        to_x[c] = over_x(sc.e_out.at[c], sc.e_in.at[c], early_x)

    def finish_early(c):
        to_x[c].wait_recv()
        sc.final[c] = (sc.e_sum[c, x] + sc.e_in[c].astype(F32)).astype(BF)
        publish(sc.final.at[c], *names[c])

    def middle(n):
        to_x[n].wait_recv()
        issue_x({2: 7, 5: 9, 8: 12}.get(n, 0))
        merged_x = view(sc.keep, n)[...] + view(sc.x_recv, n)[...].astype(F32)
        view(sc.z_send, n)[...] = merged_x.astype(BF)
        group = chunk_z if steps[n][2] == CHUNK else None
        to_z[n] = reduce(view(sc.z_send, n), view(sc.z_recv, n), view(sc.z_merged, n), group)

    mate = s + 1 - 2 * lax.rem(s, 2)
    other = lax.rem(s + ns // 2, ns)
    relayed = []

    def publish(block, array, col, at=0, width=CHUNK):
        def cols(q):
            return array.at[:, pl.ds(pl.multiple_of(col(q) + at, LANES), width)]

        (near, landed), (across, _), (passed, landed_passed) = published[0:3]
        arrival = recv_sem()
        remote(block, cols(s), near, landed, (mate, r)).start()
        remote(block, cols(s), across, arrival, (other, r)).start()
        local(block, cols(s), 3)

        def relay():
            await_landed(cols(other), arrival)
            remote(cols(other), cols(other), passed, landed_passed, (mate, r)).start()

        relayed.append(relay)

    def relay_until(left):
        while len(relayed) > left:
            relayed.pop(0)()

    def finish(n):
        c, at, width = steps[n]
        block = sc.final.at[c] if width == CHUNK else sc.final.at[c, :, pl.ds(at, width)]
        block[...] = to_z[n].total().astype(BF)
        publish(block, *names[c], at, width)

    def finish_up_to(to):
        for c in range(early, to + 1):
            if c not in done:
                finish(c)
                done.append(c)

    def pump(count):
        for _ in range(count):
            c = len(to_z)
            middle(c)
            if c - 2 in unmerged:
                unmerged.remove(c - 2)
                to_z[c - 2].merge()
            if c >= 8 and c - 1 in unmerged:
                unmerged.remove(c - 1)
                to_z[c - 1].merge()
            relay_until(1)
            finish_up_to(min(c - (3 if c > 9 else 4), last - 2 * halved - 1))

    for j in range(fl // CHUNK):
        make_part = produce_early if j < early else produce
        make_part(j, sc.gT, sc.act[:, j * CHUNK : (j + 1) * CHUNK])
    issue_x(3)
    forward(2)
    for c in range(early):
        to_z[c].begin()
    g_full = sc.g_full[...]
    nmlp = fl // CHUNK
    for j in range(fl // CHUNK):
        at = slice(j * CHUNK, (j + 1) * CHUNK)
        landed_x(5 + nmlp + j)
        d_hidden = nn(g_full, columns(sc.down_w, j)) * sc.slope[:, at]
        sc.d_hidden[:, at] = d_hidden.astype(BF)
    up_w = weight(sc.up_w)
    rs3 = scatter(sc.rs3_part, sc.rs3_recv, nt(sc.d_hidden[...], up_w))
    for j in range(nmlp):
        at = slice(j * CHUNK, (j + 1) * CHUNK)
        produce(nmlp + j, sc.mnormedT, sc.d_hidden[:, at])
    sc.bup[:, own_ff] = colsum(sc.d_hidden[...])
    issue_x(5)
    rs3.wait_recv()
    g_shard = sc.g_full[own_rows, :].astype(F32)
    sc.vecs[0:1, :] = colsum(g_shard)
    d_mid = norm_back(landed_sum(sc.rs3_recv), i.mlp_norm_gain, sc.hat2, sc.rstd2, 1, 2)
    d_mid = (g_shard + d_mid).astype(BF)
    sc.vecs[3:4, :] = colsum(d_mid)
    ag3 = gather(sc.d_mid, d_mid)
    d_mid = d_mid.astype(F32)
    sc.out_part[...] = nt(sc.act[...], weight(sc.down_w))
    sc.out_part[own_rows, :] = sc.out_part[own_rows, :] + sc.mid_full[own_rows, :].astype(F32) + i.mlp_bdown[...]
    sc.out_low[...] = sc.out_part[...].astype(BF)
    out_rs = over_section(
        lambda t: sc.out_low.at[:, pl.ds(pl.multiple_of(t * wl, LANES), wl)],
        sc.out_recv.at[s],
        sc.out_recv.at[0 : ns - 1],
    )
    sc.out_recv[s] = sc.out_low[:, own_cols]
    to_z[0].merge()
    pump(1)
    to_z[1].merge()
    ag3.wait_recv()

    pump(2)
    two_rows.wait_recv()
    d_att = nt(sc.d_mid[...], weight(sc.two)).astype(BF)
    sc.d_att[...] = d_att
    for n, (b, p) in enumerate(tiles):
        q, k, v = [tile(sc.qkv, b, p, j) for j in range(3)]
        q, d_out = pair(q), pair(tile(sc.d_att, b, p))
        probs = sc.att[n]
        d_probs = nt(d_out, v)
        d_scores = probs * (d_probs - jnp.sum(probs * d_probs, axis=-1, keepdims=True))
        d_scores = d_scores.astype(BF)
        parts = (pick(nn(d_scores, k)) * scale, tn(d_scores, q) * scale, tn(probs.astype(BF), d_out))
        for j in range(3):
            lanes = slice(j * wl + p * LANES, j * wl + (p + 1) * LANES)
            sc.d_qkv[b * LEN : (b + 1) * LEN, lanes] = parts[j].astype(BF)
    rs4 = scatter(sc.rs4_part, sc.rs4_recv, nt(sc.d_qkv[...], weight(sc.qkv_w)))
    produce(2 * nmlp, sc.attendedT, sc.d_mid[:, own_cols])
    for j in range(3):
        produce(2 * nmlp + 1 + j, sc.normedT, sc.d_qkv[:, j * wl : (j + 1) * wl])
    sc.vecs[7:8, own_cols] = colsum(sc.d_qkv[:, 0:wl])
    sc.vecs[8:9, own_cols] = colsum(sc.d_qkv[:, 2 * wl : 3 * wl])
    issue_x(8)
    pump(1)
    rs4.wait_recv()
    d_agg = norm_back(landed_sum(sc.rs4_recv), i.attn_norm_gain, sc.hat1, sc.rstd1, 4, 5)
    d_agg = (sc.d_mid[own_rows, :].astype(F32) + d_agg).astype(BF)
    sc.vecs[6:7, :] = colsum(d_agg)
    ag4 = gather(sc.d_agg, d_agg)
    pump(2)
    ag4.wait_recv()

    awo_rows.wait_recv()
    produce(2 * nmlp + 4, sc.contextT, sc.d_agg[:, own_cols])
    d_context = nt(sc.d_agg[...], weight(sc.awo)).astype(BF)
    sc.vecs[9:10, own_cols] = colsum(d_context)
    value_basis = sc.bv[...].astype(BF)
    cross = jnp.zeros((CHUNK, wl), F32)
    grad_pix = jnp.zeros((tokens, CHUNK), F32)
    for h in range(hl):
        masked = d_context * (head_of == h).astype(F32).astype(BF)
        pulled = nt(masked, value_basis)
        cross = cross + tn(sc.mixed[h], masked)
        pix = sc.pix[...].astype(F32)
        high, low = split(pulled * pix)
        d_weights = nn(high, fold) + nn(low, fold)
        probs = sc.probs[h]
        d_scores = probs * (d_weights - jnp.sum(probs * d_weights, axis=-1, keepdims=True))
        srep = nt(d_scores.astype(BF), fold)
        sc.key_src[h : h + 1, :] = colsum(srep * pix)
        grad_pix = grad_pix + sc.wrep[h].astype(F32) * pulled
        grad_pix = grad_pix + srep * sc.score_rows[h : h + 1, :]
    key_push = push(sc.key_src, sc.key_recv)
    for t in range(nd):
        sc.m_src[t] = cross[t * blk : (t + 1) * blk].astype(sc.m_src.dtype)
    m_rs = over_dp(lambda t: sc.m_src.at[t], sc.m_recv.at[r], sc.m_recv.at[0 : nd - 1])
    sc.m_recv[r] = sc.m_src[r]
    grad_pix = grad_pix.astype(BF)
    pw = CP // ns
    for t in range(ns):
        sc.pix_src[t] = nt(sc.place[t * pw : (t + 1) * pw, :], grad_pix).astype(BF)
    pix_rs = over_section(lambda t: sc.pix_src.at[t], sc.pix_recv.at[s], sc.pix_recv.at[0 : ns - 1])
    sc.pix_recv[s] = sc.pix_src[s]
    for t in range(nd):
        sc.small_src[t, 0:10] = sc.vecs[0:10, t * rows : (t + 1) * rows]
        for j in range(FF // D):
            start = (t * (FF // D) + j) * rows
            sc.small_src[t, 10 + j : 11 + j] = sc.bup[:, start : start + rows]
    small_rs = over_dp(lambda t: sc.small_src.at[t], sc.small_recv.at[r], sc.small_recv.at[0 : nd - 1])
    sc.small_recv[r] = sc.small_src[r]

    issue_x(10)
    pump(2)
    m_rs.wait_recv()
    sc.m_own[...] = summed(sc.m_recv, nd).astype(sc.m_own.dtype)
    m_ag = push(sc.m_own, sc.m_all)
    key_push.wait_recv()
    key_terms = summed(sc.key_recv, nd)
    wide = jnp.concatenate([jnp.broadcast_to(key_terms[h : h + 1], (HEAD, CHUNK)) for h in range(hl)], axis=0)
    d_key = nt(sc.basis[...], wide.astype(BF))
    d_query = jnp.sum(sc.wk[...].astype(F32) * d_key, axis=0, keepdims=True) * scale
    sc.dq_src[...] = d_query
    dq_push = push(sc.dq_src, sc.dq_recv)
    count = len(names)
    sc.final[count] = (d_key * (sc.query_proj[...] * scale)).astype(BF)
    publish(sc.final.at[count], o.singles, lambda q: q * wl)
    issue_x(last)
    for c in range(early):
        middle_early(c)
    pump(2)
    small_rs.wait_recv()
    sc.sec_small[s] = summed(sc.small_recv, nd)
    small_ag = over_section(lambda t: sc.sec_small.at[s], sc.sec_small.at[s], sc.sec_small.at[0 : ns - 1])
    def section_total(ref):
        total = ref[0].astype(F32)
        for k in range(1, ns):
            total = total + ref[k].astype(F32)
        return total

    pump(1)
    m_ag.wait_recv()
    for t in range(nd):
        sc.cross[t * blk : (t + 1) * blk] = sc.m_all[t].astype(F32)
    cross = sc.cross[...].astype(BF)
    sc.final[count + 1] = nn(sc.basis[...], cross).astype(BF)
    publish(sc.final.at[count + 1], o.singles, lambda q: 1 * D + q * wl)
    key_low = jnp.concatenate([key_terms, jnp.zeros((16 - hl, CHUNK), F32)], axis=0).astype(BF)
    grad_basis = nt(cross, sc.wv[...]) + tn(key_low, sc.key_query[...])
    sc.basis_recv[s] = grad_basis.astype(BF)
    basis_sum = over_section(lambda t: sc.basis_recv.at[s], sc.basis_recv.at[s], sc.basis_recv.at[0 : ns - 1])
    dq_push.wait_recv()
    sc.d_query[...] = jnp.broadcast_to(summed(sc.dq_recv, nd), sc.d_query.shape)
    dq_gather = over_section(lambda t: sc.d_query, o.d_query.at[s], o.d_query.at[0 : ns - 1])
    local(sc.d_query, o.d_query.at[s], 5)

    pump(2)
    finish_up_to(last - 2 * halved)
    for c in range(early):
        finish_early(c)
    finish_up_to(last - 3)
    finish_up_to(last - 2)
    finish_up_to(last - 1)
    out_rs.wait_recv()
    sc.activations[...] = section_total(sc.out_recv).astype(BF)
    local(sc.activations, o.activations, 6)
    pix_rs.wait_recv()
    sc.patches_out[...] = section_total(sc.pix_recv).astype(BF)
    local(sc.patches_out, o.patches, 7)
    small_ag.wait_recv()
    sc.small_out[...] = summed(sc.sec_small, ns)
    local(sc.small_out, o.small, 8)
    relay_until(2)
    basis_sum.wait_recv()
    sc.basis_out[...] = section_total(sc.basis_recv)
    local(sc.basis_out, o.basis, 9)
    dq_gather.wait_recv()
    relay_until(0)
    await_landed(sc.final, published[0][1])
    await_landed(sc.final, published[2][1])
    for out, _ in published[0:3]:
        await_sent(sc.final, out)
    await_local(sc.final, 3)
    await_local(sc.query_rows, 4)
    await_local(sc.d_query, 5)
    await_local(sc.activations, 6)
    await_local(sc.patches_out, 7)
    await_local(sc.small_out, 8)
    await_local(sc.basis_out, 9)
    for wait in pending:
        wait()
    assert used.send <= send.shape[0] and used.recv <= recv.shape[0], used


def scratch(ns, nd, tokens):
    nz, rows = nd // 2, D // nd
    wl, fl, hl = D // ns, FF // ns, HEADS // ns
    shard, zq, blk = tokens // ns, nz // ns, CHUNK // nd
    chunks = 2 * (fl // CHUNK) + 5
    v = pltpu.VMEM
    shapes = dict(
        wq=v((rows, wl), BF),
        wk=v((rows, wl), BF),
        wv=v((rows, wl), BF),
        qkv_w=v((nz, 2, rows, 3 * wl), BF),
        up_w=v((nz, 2, rows, fl), BF),
        down_w=v((nz, 2, rows, fl), BF),
        awo_c=v((nz, 2, rows, wl), BF),
        two_c=v((nz, 2, rows, wl), BF),
        awo=v((zq, 2, rows, D), BF),
        two=v((zq, 2, rows, D), BF),
        g_full=v((tokens, D), BF),
        place=v((CP, CHUNK), BF),
        pix=v((tokens, CHUNK), BF),
        fold=v((CHUNK, LANES), BF),
        basis=v((rows, CHUNK), BF),
        vecs=v((16, D), F32),
        bup=v((1, FF), F32),
        query_proj=v((1, wl), F32),
        key_query=v((16, rows), BF),
        score_rows=v((hl, CHUNK), F32),
        bv=v((CHUNK, CHUNK), F32),
        cross=v((CHUNK, CHUNK), F32),
        e_send=v((2, nz, 2, rows, CHUNK), BF),
        e_recv=v((2, nz, 2, rows, CHUNK), BF),
        e_merged=v((2, 2, 2, rows, CHUNK), BF),
        z_merged=v((chunks, 2, rows, CHUNK), BF),
        e_sum=v((2, 2, rows, CHUNK), F32),
        e_out=v((2, rows, CHUNK), BF),
        e_in=v((2, rows, CHUNK), BF),
        probs=v((hl, tokens, LANES), F32),
        wrep=v((hl, tokens, CHUNK), BF),
        mixed=v((hl, tokens, CHUNK), BF),
        context_full=v((tokens, D), BF),
        attended_full=v((tokens, D), BF),
        agg_full=v((tokens, D), BF),
        mid_full=v((tokens, D), BF),
        hat1=v((shard, D), F32),
        hat2=v((shard, D), F32),
        rstd1=v((shard, LANES), F32),
        rstd2=v((shard, LANES), F32),
        normed=v((tokens, D), BF),
        mnormed=v((tokens, D), BF),
        qkv=v((tokens, 3 * wl), BF),
        d_qkv=v((tokens, 3 * wl), BF),
        att=v((tokens // LEN * (wl // LANES), 2 * LEN, LEN), F32),
        attended=v((tokens, wl), BF),
        d_att=v((tokens, wl), BF),
        act=v((tokens, fl), BF),
        slope=v((tokens, fl), F32),
        d_hidden=v((tokens, fl), BF),
        d_mid=v((tokens, D), BF),
        d_agg=v((tokens, D), BF),
        out_part=v((tokens, D), F32),
        out_low=v((tokens, D), BF),
        out_recv=v((ns, tokens, wl), BF),
        pix_src=v((ns, CP // ns, tokens), BF),
        pix_recv=v((ns, CP // ns, tokens), BF),
        small_src=v((nd, 16, rows), F32),
        small_recv=v((nd, 16, rows), F32),
        sec_small=v((ns, 16, rows), F32),
        basis_recv=v((ns, CHUNK, rows), BF),
        x_send=v((chunks, nz, rows, CHUNK), BF),
        x_recv=v((chunks, nz, rows, CHUNK), BF),
        keep=v((chunks, nz, rows, CHUNK), F32),
        z_send=v((chunks, nz, rows, CHUNK), BF),
        z_recv=v((chunks, nz, rows, CHUNK), BF),
        final=v((chunks + 2, rows, CHUNK), BF),
    )
    whole = v((nz, 2, rows, tokens), BF)
    shapes.update(gT=whole, contextT=whole, attendedT=whole, normedT=whole, mnormedT=whole)
    part = v((tokens, D), BF)
    shapes.update(rs3_part=part, rs4_part=part)
    part = v((ns, shard, D), BF)
    shapes.update(rs3_recv=part, rs4_recv=part)
    part = v((hl, CHUNK), F32)
    shapes.update(s_src=part, key_src=part)
    part = v((nd, hl, CHUNK), F32)
    shapes.update(s_recv=part, key_recv=part)
    shapes.update(q_src=v((1, CHUNK), F32), dq_src=v((1, CHUNK), F32))
    part = v((nd, 1, CHUNK), F32)
    shapes.update(q_recv=part, dq_recv=part)
    kind = BF if blk % 16 == 0 else F32
    part = v((nd, blk, CHUNK), kind)
    shapes.update(bv_src=part, bv_recv=part, bv_all=part, m_src=part, m_recv=part, m_all=part)
    part = v((blk, CHUNK), kind)
    shapes.update(bv_own=part, m_own=part)
    shapes.update(
        query_rows=v((16, rows), BF),
        d_query=v((8, wl), F32),
        activations=v((tokens, wl), BF),
        patches_out=v((CP // ns, tokens), BF),
        small_out=v((16, rows), F32),
        basis_out=v((CHUNK, rows), F32),
    )
    dma = pltpu.SemaphoreType.DMA
    shapes.update(send=dma((52,)), recv=dma((160,)), local=dma((28,)))
    return shapes


def fused(ns, nd, near, far):
    tokens = near["patches"].shape[1]
    rows = D // nd
    shapes = scratch(ns, nd, tokens)
    arrays = {**near, **far}
    hbm = pl.BlockSpec(memory_space=pl.ANY)
    outs = dict(
        activations=((tokens, D // ns), BF),
        patches=((CP // ns, tokens), BF),
        basis=((CHUNK, rows), F32),
        query_rows=((16, rows), BF),
        d_query=((ns, 8, D // ns), F32),
        small=((16, rows), F32),
        mlp_up=((rows, FF), BF),
        mlp_down=((rows, FF), BF),
        attn_wqkv=((rows, 3 * D), BF),
        singles=((rows, 4 * D), BF),
    )

    def body(*refs):
        n_in, n_out = len(arrays), len(outs)
        kernel(
            ns,
            nd,
            SimpleNamespace(**dict(zip(arrays, refs[:n_in]))),
            SimpleNamespace(**dict(zip(outs, refs[n_in : n_in + n_out]))),
            SimpleNamespace(**dict(zip(shapes, refs[n_in + n_out :]))),
            list(near),
            refs[n_in + n_out + len(shapes) :],
        )

    result = pl.pallas_call(
        body,
        out_shape=[jax.ShapeDtypeStruct(*a) for a in outs.values()],
        in_specs=[hbm] * len(arrays),
        out_specs=[hbm] * len(outs),
        scratch_shapes=list(shapes.values()) + [pltpu.VMEM(a.shape, a.dtype) for a in near.values()],
        compiler_params=pltpu.CompilerParams(
            collective_id=0, has_side_effects=True, vmem_limit_bytes=60 * 1024 * 1024
        ),
        name="block",
    )(*arrays.values())
    return SimpleNamespace(**dict(zip(outs, result)))


def widen(nd, got, agg_wq):
    rows = D // nd
    arrays = [got.mlp_up, got.mlp_down, got.attn_wqkv, got.singles]
    rest = dict(
        activations=got.activations,
        patches=got.patches,
        basis=got.basis,
        query_rows=got.query_rows,
        d_query=got.d_query,
        small=got.small,
        agg_wq=agg_wq,
    )
    line = (1, rows)
    outs = dict(
        activations=(got.activations.shape, BF),
        patches=(got.patches.shape, BF),
        embed=((CP, rows), F32),
        var=((VARS, rows), F32),
        query=(line, F32),
        wq=((rows, D), F32),
        bq=(line, F32),
        bup=((1, rows * (FF // D)), F32),
    )
    lines = tuple(range(10))
    wide = dict(
        mlp_up=((rows, FF), F32),
        mlp_down=((rows, FF), F32),
        attn_wqkv=((rows, 3 * D), F32),
        agg_wk=((rows, D), F32),
        agg_wv=((rows, D), F32),
        agg_wo=((rows, D), F32),
        attn_wo=((rows, D), F32),
    )
    half, third = FF // 2, 3 * D // 2
    tiles = [(0, at, half, 0, at) for at in (0, half)]
    tiles += [(1, at, half, 1, at) for at in (0, half)]
    tiles += [(2, at, third, 2, at) for at in (0, third)]
    tiles += [(3, n * D, D, 3 + n, 0) for n in range(4)]
    everything = {**wide, **outs}
    shaped = [jax.ShapeDtypeStruct(*a) for a in everything.values()]
    shaped += [jax.ShapeDtypeStruct(line, F32) for _ in lines]
    slim = shaped[len(wide) :]

    def body(*refs):
        sources, refs = refs[: len(arrays)], refs[len(arrays) :]
        rest_in, refs = refs[: len(rest)], refs[len(rest) :]
        targets, refs = refs[: len(wide)], refs[len(wide) :]
        slim_out, refs = refs[: len(slim)], refs[len(slim) :]
        near, refs = refs[: len(arrays)], refs[len(arrays) :]
        far, refs = refs[: len(wide)], refs[len(wide) :]
        rest_near, refs = refs[: len(rest)], refs[len(rest) :]
        slim_near, (ins, outgoing) = refs[: len(slim)], refs[len(slim) :]

        def load(t):
            m, at, width, _, _ = tiles[t]
            cols = pl.ds(at, width)
            return pltpu.make_async_copy(sources[m].at[:, cols], near[m].at[:, cols], ins.at[t])

        def store(t):
            _, _, width, m, at = tiles[t]
            cols = pl.ds(at, width)
            return pltpu.make_async_copy(far[m].at[:, cols], targets[m].at[:, cols], outgoing.at[t])

        def load_rest(n):
            return pltpu.make_async_copy(rest_in[n], rest_near[n], ins.at[len(tiles) + n])

        def store_slim(n):
            return pltpu.make_async_copy(slim_near[n], slim_out[n], outgoing.at[len(tiles) + n])

        def widen_tile(t):
            load(t).wait()
            m, at, width, to, start = tiles[t]
            far[to][:, start : start + width] = near[m][:, at : at + width].astype(F32)
            store(t).start()

        for n in range(len(rest)):
            load_rest(n).start()
        for t in range(len(tiles)):
            load(t).start()
        for t in range(len(tiles) // 2):
            widen_tile(t)
        for n in range(len(rest)):
            load_rest(n).wait()
        i = SimpleNamespace(**dict(zip(rest, rest_near)))
        o = SimpleNamespace(**dict(zip(outs, slim_near)))
        left = slim_near[len(outs) :]
        r = lax.axis_index("dp")
        o.activations[...] = i.activations[...]
        o.patches[...] = i.patches[...]
        o.embed[...] = i.basis[0:CP]
        o.var[...] = i.basis[CP : CP + VARS]
        d_query = jnp.concatenate([i.d_query[k] for k in range(i.d_query.shape[0])], axis=1)
        d_query = jnp.concatenate([d_query, d_query], axis=0)
        d_query = jnp.where(iota(d_query.shape, 0) == 0, d_query, 0.0)
        high, low = split(d_query)
        low, rest_low = split(d_query - high.astype(F32))
        chosen = (iota((rows, D), 1) == iota((rows, D), 0) + r * rows).astype(F32).astype(BF)
        o.bq[...] = (nt(high, chosen) + nt(low, chosen) + nt(rest_low, chosen))[0:1]
        weight = i.agg_wq[...]
        o.query[...] = (nt(high, weight) + nt(low, weight) + nt(rest_low, weight))[0:1]
        first = i.query_rows[...]
        o.wq[...] = tn(first, high) + tn(first, low) + tn(first, rest_low)
        o.bup[...] = jnp.concatenate([i.small[10 + k : 11 + k] for k in range(FF // D)], axis=1)
        for k in lines:
            left[k][...] = i.small[k : k + 1]
        for n in range(len(slim)):
            store_slim(n).start()
        for t in range(len(tiles) // 2, len(tiles)):
            widen_tile(t)
        for t in range(len(tiles)):
            store(t).wait()
        for n in range(len(slim)):
            store_slim(n).wait()

    hbm = pl.BlockSpec(memory_space=pl.ANY)
    dma = pltpu.SemaphoreType.DMA
    result = pl.pallas_call(
        body,
        out_shape=shaped,
        in_specs=[hbm] * (len(arrays) + len(rest)),
        out_specs=[hbm] * len(shaped),
        scratch_shapes=[pltpu.VMEM(a.shape, a.dtype) for a in [*arrays, *shaped[: len(wide)], *rest.values(), *slim]]
        + [dma((len(tiles) + len(rest),)), dma((len(tiles) + len(slim),))],
        compiler_params=pltpu.CompilerParams(vmem_limit_bytes=60 * 1024 * 1024),
        name="widen",
    )(*arrays, *rest.values())
    names = list(everything)
    return SimpleNamespace(**dict(zip(names, result))), [a.reshape(-1) for a in result[len(names) :]]


def on_device(
    ns,
    nd,
    patches,
    var_ids,
    segment_ids,
    embed_weight,
    var_embed,
    agg_query,
    agg_wq,
    agg_bq,
    agg_wk,
    agg_wv,
    agg_bv,
    agg_wo,
    agg_bo,
    attn_norm_gain,
    attn_norm_bias,
    attn_wqkv,
    attn_bq,
    attn_bv,
    attn_wo,
    attn_bo,
    mlp_norm_gain,
    mlp_norm_bias,
    mlp_up,
    mlp_bup,
    mlp_down,
    mlp_bdown,
    cotangent,
):
    near = dict(
        patches=patches,
        var_ids=var_ids,
        segment_ids=segment_ids,
        embed_weight=embed_weight,
        var_embed=var_embed,
        agg_query=agg_query,
        agg_bq=agg_bq,
        agg_bv=agg_bv,
        agg_bo=agg_bo,
        attn_norm_gain=attn_norm_gain,
        attn_norm_bias=attn_norm_bias,
        attn_bq=attn_bq,
        attn_bv=attn_bv,
        attn_bo=attn_bo,
        mlp_norm_gain=mlp_norm_gain,
        mlp_norm_bias=mlp_norm_bias,
        mlp_bup=mlp_bup,
        mlp_bdown=mlp_bdown,
    )
    far = dict(
        agg_wq=agg_wq,
        agg_wk=agg_wk,
        agg_wv=agg_wv,
        agg_wo=agg_wo,
        attn_wqkv=attn_wqkv,
        attn_wo=attn_wo,
        mlp_up=mlp_up,
        mlp_down=mlp_down,
        cotangent=cotangent,
    )
    near = {name: a.reshape(1, -1) if a.ndim == 1 else a for name, a in near.items()}
    near["patches"], near["embed_weight"] = patches.T, embed_weight.T
    got = fused(ns, nd, near, far)
    out, small = widen(nd, got, agg_wq)
    return (
        out.activations,
        out.patches.T,
        out.embed.T,
        out.var,
        out.query.reshape(-1),
        out.wq,
        out.bq.reshape(-1),
        out.agg_wk,
        out.agg_wv,
        small[9],
        out.agg_wo,
        small[6],
        small[4],
        small[5],
        out.attn_wqkv,
        small[7],
        small[8],
        out.attn_wo,
        small[3],
        small[1],
        small[2],
        out.mlp_up,
        out.bup.reshape(-1),
        out.mlp_down,
        small[0],
    )


def solution(mesh):
    in_specs = (
        P("dp", None),
        P(),
        P("dp", None),
        P("dp", None),
        P(),
        P(),
        P("dp", None),
        P(),
        P("dp", None),
        P("dp", None),
        P(),
        P("dp", None),
        P(),
        P(),
        P(),
        P("dp", None),
        P(),
        P(),
        P("dp", None),
        P(),
        P(),
        P(),
        P("dp", None),
        P(),
        P("dp", None),
        P(),
        P("dp", "section"),
    )
    out_specs = (
        P("dp", "section"),
        P("dp", "section"),
        P("dp", None),
        P(None, "dp"),
        P("dp"),
        P("dp", None),
        P("dp"),
        P("dp", None),
        P("dp", None),
        P("dp"),
        P("dp", None),
        P("dp"),
        P("dp"),
        P("dp"),
        P("dp", None),
        P("dp"),
        P("dp"),
        P("dp", None),
        P("dp"),
        P("dp"),
        P("dp"),
        P("dp", None),
        P("dp"),
        P("dp", None),
        P("dp"),
    )
    sizes = (mesh.shape["section"], mesh.shape["dp"])
    return jax.shard_map(
        partial(on_device, *sizes), mesh=mesh, in_specs=in_specs, out_specs=out_specs, check_vma=False
    )
```

```python
from functools import partial
from types import SimpleNamespace

import jax
import jax.numpy as jnp
from jax import lax
from jax.experimental import pallas as pl
from jax.experimental.pallas import tpu as pltpu
from jax.sharding import PartitionSpec as P

D = 1024
HEADS = 16
HEAD = 64
FF = 4096
VARS = 48
PIX = 4
LEN = 128

highest = lax.Precision.HIGHEST
blocked = -1000000000.0
epsilon = 1e-05
MESH = pl.DeviceIdType.MESH
BF = jnp.bfloat16
F32 = jnp.float32
CHUNK = 256
CP = VARS * PIX
LANES = 128


def nn(a, b):
    return jnp.dot(a, b, preferred_element_type=F32)


def nt(a, b):
    return lax.dot_general(a, b, (((1,), (1,)), ((), ())), preferred_element_type=F32)


def tn(a, b):
    return lax.dot_general(a, b, (((0,), (0,)), ((), ())), preferred_element_type=F32)


def split(x):
    high = x.astype(BF)
    return high, (x - high.astype(F32)).astype(BF)


def iota(shape, dim):
    return lax.broadcasted_iota(jnp.int32, shape, dim)


def colsum(x):
    return jnp.sum(x.astype(F32), axis=0, keepdims=True)


def each(low, high, body):
    if high - low <= 8:
        for k in range(low, high):
            body(k)
    else:

        def step(k, carry):
            body(k)
            return carry

        lax.fori_loop(low, high, step, 0)


class Transfer:
    def __init__(self, make, low, high, whole):
        self.make, self.low, self.high, self.whole = make, low, high, whole

    def start(self):
        each(self.low, self.high, lambda k: self.make(k).start())
        return self

    def wait_recv(self):
        self.whole().wait_recv()

    def wait_send(self):
        self.whole().wait_send()


def kernel(ns, nd, refs_in, refs_out, sc, near_names, near):
    s = lax.axis_index("section")
    r = lax.axis_index("dp")
    nx = 2
    nz = nd // nx
    z, x = lax.div(r, nx), lax.rem(r, nx)
    o = refs_out
    i = SimpleNamespace(**{**vars(refs_in), **dict(zip(near_names, near))})
    rows = D // nd
    tokens = i.patches.shape[1]
    shard = tokens // ns
    wl, fl, hl = D // ns, FF // ns, HEADS // ns
    zq = nz // ns
    own_cols = pl.ds(pl.multiple_of(s * wl, LANES), wl)
    own_ff = pl.ds(pl.multiple_of(s * fl, LANES), fl)
    own_rows = pl.ds(pl.multiple_of(s * shard, 16), shard)
    scale = HEAD ** (-0.5)
    send, recv = sc.send, sc.recv
    used = SimpleNamespace(send=0, recv=0, local=0)
    pending = []

    def send_sem():
        used.send += 1
        return used.send - 1

    def recv_sem(count=1):
        used.recv += count
        return used.recv - count

    def remote(src, dst, out, landing, device):
        return pltpu.make_async_remote_copy(
            src_ref=src,
            dst_ref=dst,
            send_sem=send.at[out],
            recv_sem=recv.at[landing],
            device_id=device,
            device_id_type=MESH,
        )

    beside = (s, z * nx + 1 - x)

    def await_sent(ref, out):
        remote(ref, ref, out, 0, beside).wait_send()

    def await_landed(ref, landing):
        remote(ref, ref, 0, landing, beside).wait_recv()

    def all_sent(ref, out):
        pending.append(lambda: await_sent(ref, out))

    def over(peer, count, src, dst, whole, out=None, landing=None):
        alone = out is None
        out = send_sem() if alone else out
        landing = recv_sem() if landing is None else landing

        def make(k):
            t, device = peer(k)
            return remote(src(t), dst, out, landing, device)

        transfer = Transfer(make, 1, count, lambda: remote(whole, whole, out, landing, beside)).start()
        if alone:
            pending.append(transfer.wait_send)
        return transfer

    def section_peer(k):
        t = lax.rem(s + k, ns)
        return t, (t, r)

    def dp_peer(k):
        t = lax.rem(r + k, nd)
        return t, (s, t)

    def z_peer(k):
        t = lax.rem(z + k, nz)
        return t, (s, t * nx + x)

    def over_section(src, dst, whole):
        return over(section_peer, ns, src, dst, whole)

    def over_dp(src, dst, whole):
        return over(dp_peer, nd, src, dst, whole)

    def over_x(src, dst, out, landing=None, whole=None):
        whole = src if whole is None else whole
        return over(lambda k: (0, beside), 2, lambda t: src, dst, whole, out, landing)

    def local(src, dst, sem):
        copy = pltpu.make_async_copy(src, dst, sc.local.at[sem])
        copy.start()
        return copy

    def await_local(ref, sem):
        pltpu.make_async_copy(ref, ref, sc.local.at[sem]).wait()

    line = nz == 4
    partner = z + 1 - 2 * lax.rem(z, 2)
    inner = (z == 1) | (z == 2)
    outer = (z == 0) | (z == 3)
    beyond = [lax.rem(2 * lax.div(z, 2) + 2 + j, 4) for j in range(2)]
    gate = 2 - lax.div(z, 2)

    def at_z(t):
        return (s, t * nx + x)

    blocks = sc.z_recv
    n_pieces = blocks.shape[0]
    crossing = 2 if line else 0

    def spread_group(count):
        own, passed = send_sem(), send_sem()
        whole = blocks.at[0:count, 0 : min(2, nz)] if line else blocks.at[0:count, 0 : nz - 1]
        all_sent(whole, own)
        if line:

            def sent():
                @pl.when(inner)
                def _():
                    await_sent(whole, passed)

            pending.append(sent)
        return own, passed

    first_spread = spread_group(n_pieces)
    second_spread = spread_group(crossing) if crossing else None

    def line_spread(block, group):
        base = recv_sem(3)
        out, out_passed = group
        mine_beyond = base + 1 + lax.rem(z, 2)
        remote(block(z), block(z), out, base, at_z(partner)).start()
        remote(block(z), block(z), out, mine_beyond, at_z(gate)).start()

        def pass_on(k):
            t = beyond[k - 1]

            @pl.when(inner)
            def _():
                await_landed(block(t), base + k)
                remote(block(t), block(t), out_passed, base + k, at_z(partner)).start()

        def arrived(k, passed=False):
            t = [partner, *beyond][k]
            if k == 0:
                await_landed(block(t), base)
                return t
            if not passed:
                pass_on(k)

            @pl.when(outer)
            def _():
                await_landed(block(t), base + k)

            return t

        arrived.pass_on = pass_on
        return arrived

    def spread(block, group=first_spread):
        if line:
            return line_spread(block, group)
        whole = blocks.at[0, 0 : nz - 1]
        return over(z_peer, nz, lambda t: block(z), block(z), whole, group[0]).wait_recv

    def reduce_group(count, landed):
        near, far, across = send_sem(), send_sem(), send_sem()
        if not line:
            all_sent(landed.at[0:count, 0 : nz - 1], near)
            return near, far, across
        all_sent(landed.at[0:count, 0], near)

        def sent():
            @pl.when(outer)
            def _():
                await_sent(landed.at[0:count, 0:2], far)

            @pl.when(inner)
            def _():
                await_sent(landed.at[0:count, 0:2], across)

        pending.append(sent)
        return near, far, across

    def line_reduce(parts, landed, merged, group, hold):
        near, far, across = group
        base = recv_sem(3)

        def first():
            remote(parts.at[partner], landed.at[0], near, base, at_z(partner)).start()

        def begin():
            pl.when(inner)(first)

        @pl.when(outer)
        def _():
            first()
            for j in range(2):
                remote(parts.at[beyond[j]], landed.at[2 + j], far, base + 1, at_z(partner)).start()

        if not hold:
            begin()

        def merge():
            @pl.when(inner)
            def _():
                await_landed(landed.at[2:4], base + 1)
                for j in range(2):
                    both = parts[beyond[j]].astype(F32) + landed[2 + j].astype(F32)
                    merged[j] = both.astype(BF)
                    remote(merged.at[j], landed.at[1], across, base + 2, at_z(beyond[j])).start()

        def total():
            await_landed(landed.at[0], base)
            await_landed(landed.at[1], base + 2)
            return parts[z].astype(F32) + landed[0].astype(F32) + landed[1].astype(F32)

        return SimpleNamespace(begin=begin, merge=merge, total=total)

    def reduce(parts, landed, merged, group, hold=False):
        if line and group is not None:
            return line_reduce(parts, landed, merged, group, hold)
        out = None if group is None else group[0]
        transfer = over(z_peer, nz, lambda t: parts.at[t], landed.at[z], landed.at[0 : nz - 1], out)
        landed[z] = parts[z]

        def total():
            transfer.wait_recv()
            value = landed[0].astype(F32)
            for k in range(1, nz):
                value = value + landed[k].astype(F32)
            return value

        return SimpleNamespace(begin=lambda: None, merge=lambda: None, total=total)

    barrier = pltpu.get_barrier_semaphore()
    for k in range(1, ns):
        pl.semaphore_signal(barrier, inc=1, device_id=(lax.rem(s + k, ns), r), device_id_type=MESH)
    each(
        1,
        nd,
        lambda k: pl.semaphore_signal(
            barrier, inc=1, device_id=(s, lax.rem(r + k, nd)), device_id_type=MESH
        ),
    )

    local(i.agg_wq.at[:, own_cols], sc.wq, 0)
    local(i.agg_wk.at[:, own_cols], sc.wk, 0)
    local(i.agg_wv.at[:, own_cols], sc.wv, 0)
    sources = [(i.agg_wo, sc.awo_c, 0, s * wl)]
    sources += [(i.attn_wqkv, sc.qkv_w, j * wl, j * D + s * wl) for j in range(3)]
    sources += [(i.attn_wo, sc.two_c, 0, s * wl)]
    sources += [(i.mlp_up, sc.up_w, j * CHUNK, s * fl + j * CHUNK) for j in range(fl // CHUNK)]
    sources += [(i.mlp_down, sc.down_w, j * CHUNK, s * fl + j * CHUNK) for j in range(fl // CHUNK)]
    pieces = [(dst, pl.ds(at, CHUNK)) for _, dst, at, _ in sources]
    for src, dst, at, col in sources:
        local(src.at[:, pl.ds(pl.multiple_of(col, LANES), CHUNK)], dst.at[z, x, :, pl.ds(at, CHUNK)], 1)
    from_z, from_x, own_x, early_passed = {}, {}, {}, set()

    def pass_next():
        c = max([-1, *early_passed, *from_x]) + 1
        if line:
            early_passed.add(c)
            for k in range(1, nz - 1):
                for arrived in from_z[c]:
                    arrived.pass_on(k)

    late = range(n_pieces - crossing, n_pieces)
    own_order = [*range(6), *late, *range(6, n_pieces - crossing)] if line else []
    from_own, from_others = send_sem(), send_sem()
    if line:
        all_sent(blocks.at[:, 0], from_own)
        all_sent(blocks.at[0 : n_pieces - crossing, 0 : nz - 1], from_others)
    else:
        all_sent(blocks, from_others)
    x_landed = [recv_sem() for _ in range(n_pieces)]

    def issue_own(count):
        for c in own_order[len(own_x) : len(own_x) + count]:
            dst, cols = pieces[c]
            block = dst.at[z, x, :, cols]
            own_x[c] = over_x(block, block, from_own, x_landed[c])

    def issue_z(count):
        for c in range(len(from_z), min(len(from_z) + count, n_pieces)):
            dst, cols = pieces[c]
            from_z[c] = [spread(lambda t, dst=dst, cols=cols: dst.at[t, x, :, cols])]
            if c in late:
                own_x[c].wait_recv()
                other = lambda t, dst=dst, cols=cols: dst.at[t, 1 - x, :, cols]
                from_z[c].append(spread(other, second_spread))

    def forward(count):
        for c in range(len(from_x), min(len(from_x) + count, n_pieces)):
            while line and c not in own_x:
                issue_own(1)
            dst, cols = pieces[c]
            from_x[c] = True
            if not line:
                from_z[c][0]()
                half = dst.at[:, x, :, cols]
                over_x(half, half, from_others, x_landed[c])
            for k in range(nz - 1 if line else 0):
                for arrived in from_z[c]:
                    t = arrived(k, c in early_passed)
                    block = dst.at[t, x, :, cols]
                if c not in late:
                    over_x(block, block, from_others, x_landed[c])
            issue_z(1)

    def landed_x(c):
        dst, cols = pieces[c]
        if c not in late:
            await_landed(dst.at[:, 0, :, cols], x_landed[c])

    local(i.cotangent, sc.g_full.at[:, own_cols], 2)

    for n, name in enumerate(near_names):
        local(getattr(refs_in, name), near[n], 10 + n)
    for n, ref in enumerate(near):
        await_local(ref, 10 + n)

    chan = (iota((CP, VARS), 0) >> 2 == iota((CP, VARS), 1)).astype(F32).astype(BF)
    ids = jnp.broadcast_to(i.var_ids[...].astype(F32), (CHUNK, VARS)).astype(BF)
    ids = nt(chan, ids)
    lane = iota((CP, CHUNK), 1)
    row = iota((CP, CHUNK), 0)
    hit = ((lane >> 2).astype(F32) == ids) & ((lane & 3) == (row & 3)) & (lane < CP)
    place = hit.astype(F32).astype(BF)
    sc.place[...] = place
    lane = iota((tokens, CHUNK), 1)
    ones = ((lane >= CP) & (lane < CP + VARS)).astype(F32)
    sc.pix[...] = (tn(i.patches[...], place) + ones).astype(BF)
    row = iota((CHUNK, LANES), 0)
    lane = iota((CHUNK, LANES), 1)
    owner = jnp.where(row < CP, row >> 2, row - CP)
    sc.fold[...] = ((owner == lane) & (lane < VARS)).astype(F32).astype(BF)
    chosen = (iota((rows, D), 1) == iota((rows, D), 0) + r * rows).astype(F32).astype(BF)
    lane = iota((CP, CHUNK), 1)
    row = iota((CP, CHUNK), 0)
    widen = (lane == row).astype(F32).astype(BF)
    lane = iota((VARS, CHUNK), 1)
    row = iota((VARS, CHUNK), 0)
    widen_var = (lane == row + CP).astype(F32).astype(BF)
    var_rows = nt(chosen, i.var_embed[...].astype(BF)).astype(BF)
    sc.basis[...] = (tn(i.embed_weight[...], widen) + nn(var_rows, widen_var)).astype(BF)
    query = jnp.broadcast_to(i.agg_query[...].astype(BF).astype(F32), (16, D))
    query = jnp.where(iota((16, D), 0) == 0, query, 0.0).astype(BF)
    query_rows = nt(query, chosen).astype(BF)
    sc.query_rows[...] = query_rows
    local(sc.query_rows, o.query_rows, 4)
    sc.vecs[...] = jnp.zeros_like(sc.vecs)
    sc.bup[...] = jnp.zeros_like(sc.bup)

    await_local(blocks.at[0:3, 0], 0)
    sc.q_src[...] = nn(query_rows, sc.wq[...])[0:1]
    value_part = tn(sc.basis[...], sc.wv[...])
    blk = CHUNK // nd
    for t in range(nd):
        sc.bv_src[t] = value_part[t * blk : (t + 1) * blk].astype(sc.bv_src.dtype)
    await_local(sc.g_full.at[:, own_cols], 2)
    await_local(blocks.at[:, 0], 1)

    pl.semaphore_wait(barrier, ns - 1 + nd - 1)

    def weight(ref):
        return ref[...].reshape(ref.shape[0] * ref.shape[1] * ref.shape[2], ref.shape[3])

    def scatter(part, landed, value):
        part[...] = value.astype(BF)
        transfer = over_section(lambda t: part.at[pl.ds(pl.multiple_of(t * shard, 16), shard)], landed.at[s], landed.at[0 : ns - 1])
        landed[s] = part[own_rows, :]
        return transfer

    def gather(full, value):
        full[own_rows, :] = value.astype(BF)
        return over_section(lambda t: full.at[own_rows], full.at[own_rows], full.at[0 : (ns - 1) * shard])

    def landed_sum(landed):
        total = landed[0].astype(F32)
        for k in range(1, ns):
            total = total + landed[k].astype(F32)
        return total

    def normal(value):
        centred = value - jnp.mean(value, axis=-1, keepdims=True)
        rstd = lax.rsqrt(jnp.mean(centred * centred, axis=-1, keepdims=True) + epsilon)
        return centred * rstd, rstd

    def whole_norm(full, gain, bias, dst):
        for t in range(ns):
            at = slice(t * shard, (t + 1) * shard)
            hat, _ = normal(full[at, :].astype(F32))
            dst[at, :] = (hat * gain[...] + bias[...]).astype(BF)

    def kept_norm(full, kept, rstd_kept):
        hat, rstd = normal(full[own_rows, :].astype(F32))
        kept[...] = hat
        rstd_kept[...] = jnp.broadcast_to(rstd, rstd_kept.shape)

    def norm_back(grad, gain, kept, rstd_kept, gain_row, bias_row):
        hat = kept[...]
        sc.vecs[gain_row : gain_row + 1, :] = colsum(grad * hat)
        sc.vecs[bias_row : bias_row + 1, :] = colsum(grad)
        inner = grad * gain[...]
        mean = jnp.mean(inner, axis=-1, keepdims=True)
        dot = jnp.mean(inner * hat, axis=-1, keepdims=True)
        return rstd_kept[:, 0:1] * (inner - mean - hat * dot)

    def transposed(full, dst):
        for j in range(D // CHUNK):
            turned = full[:, j * CHUNK : (j + 1) * CHUNK].astype(F32).T.astype(BF)
            n = dst.shape[0] // (D // CHUNK)
            dst[j * n : (j + 1) * n] = turned.reshape((n,) + dst.shape[1:])

    def by_rows(cols, dst):
        at = pl.ds(s * zq, zq)
        dst[:, :, :, own_cols] = cols[at]
        return over_section(
            lambda t: cols.at[pl.ds(t * zq, zq)], dst.at[:, :, :, own_cols], dst.at[:, :, :, 0 : (ns - 1) * wl]
        )

    def gather_cols(full):
        block = full.at[:, own_cols]
        return over_section(lambda t: block, block, full.at[:, 0 : (ns - 1) * wl])

    def columns(ref, j):
        return ref[:, :, :, j * CHUNK : (j + 1) * CHUNK].reshape(D, CHUNK)

    def push(src, dst):
        transfer = over_dp(lambda t: src, dst.at[r], dst.at[0 : nd - 1])
        dst[r] = src[...]
        return transfer

    def summed(dst, count):
        total = dst[0].astype(F32)
        for k in range(1, count):
            total = total + dst[k].astype(F32)
        return total

    q_push = push(sc.q_src, sc.q_recv)
    bv_rs = over_dp(lambda t: sc.bv_src.at[t], sc.bv_recv.at[r], sc.bv_recv.at[0 : nd - 1])
    sc.bv_recv[r] = sc.bv_src[r]
    g_gather = gather_cols(sc.g_full)

    issue_own(4)
    issue_z(1)
    q_push.wait_recv()
    query_proj = summed(sc.q_recv, nd) + i.agg_bq[:, own_cols]
    sc.query_proj[...] = query_proj
    head_rows = (iota((16, wl), 1) >> 6 == iota((16, wl), 0)).astype(F32)
    high, low = split(head_rows * (query_proj * scale))
    key_query = (nt(high, sc.wk[...]) + nt(low, sc.wk[...])).astype(BF)
    sc.key_query[...] = key_query
    sc.s_src[...] = nn(key_query, sc.basis[...])[0:hl]
    s_push = push(sc.s_src, sc.s_recv)
    bv_rs.wait_recv()
    sc.bv_own[...] = summed(sc.bv_recv, nd).astype(sc.bv_own.dtype)
    bv_ag = push(sc.bv_own, sc.bv_all)
    issue_z(5)
    issue_own(4)
    pass_next()

    s_push.wait_recv()
    score_rows = summed(sc.s_recv, nd)
    sc.score_rows[...] = score_rows
    fold = sc.fold[...]
    lane_ok = iota((tokens, LANES), 1) < VARS
    for h in range(hl):
        pix = sc.pix[...].astype(F32)
        high, low = split(pix * score_rows[h : h + 1])
        scores = nn(high, fold) + nn(low, fold)
        scores = jnp.where(lane_ok, scores, -1e30)
        scores = jnp.exp(scores - jnp.max(scores, axis=-1, keepdims=True))
        probs = scores / jnp.sum(scores, axis=-1, keepdims=True)
        sc.probs[h] = probs
        wrep = nt(probs.astype(BF), fold)
        sc.wrep[h] = wrep.astype(BF)
        sc.mixed[h] = (wrep * pix).astype(BF)
    issue_z(1)
    forward(1)
    issue_own(2)
    pass_next()
    bv_ag.wait_recv()
    for t in range(nd):
        sc.bv[t * blk : (t + 1) * blk] = sc.bv_all[t].astype(F32)
    value_basis = sc.bv[...].astype(BF)
    head_of = iota((1, wl), 1) >> 6
    context = jnp.broadcast_to(i.agg_bv[:, own_cols], (tokens, wl))
    for h in range(hl):
        context = context + jnp.where(head_of == h, nn(sc.mixed[h], value_basis), 0.0)
    sc.context_full[:, own_cols] = context.astype(BF)
    context_gather = gather_cols(sc.context_full)
    g_gather.wait_recv()
    transposed(sc.g_full, sc.gT)
    issue_own(2)
    forward(1)
    issue_own(1)
    context_gather.wait_recv()
    pass_next()
    landed_x(0)
    part = nn(sc.context_full[...], weight(sc.awo_c)) + i.agg_bo[:, own_cols]
    sc.agg_full[:, own_cols] = part.astype(BF)
    agg_gather = gather_cols(sc.agg_full)
    transposed(sc.context_full, sc.contextT)
    forward(1)
    pass_next()
    agg_gather.wait_recv()
    whole_norm(sc.agg_full, i.attn_norm_gain, i.attn_norm_bias, sc.normed)
    kept_norm(sc.agg_full, sc.hat1, sc.rstd1)
    transposed(sc.normed, sc.normedT)
    pass_next()
    forward(1)
    normed = sc.normed[...]
    for j in range(3):
        landed_x(1 + j)
        part = nn(normed, columns(sc.qkv_w, j))
        if j == 0:
            part = part + i.attn_bq[:, own_cols]
        if j == 2:
            part = part + i.attn_bv[:, own_cols]
        sc.qkv[:, j * wl : (j + 1) * wl] = part.astype(BF)
        if j < 2:
            pass_next()
        if j == 1:
            forward(1)
    lo = (iota((1, LANES), 1) < HEAD).astype(F32)
    first, second = lo.astype(BF), (1.0 - lo).astype(BF)

    def pair(a):
        return jnp.concatenate([a * first, a * second], axis=0)

    def pick(a):
        return jnp.where(iota((LEN, LANES), 1) < HEAD, a[0:LEN], a[LEN:])

    tiles = [(b, p) for b in range(tokens // LEN) for p in range(wl // LANES)]

    def tile(ref, b, p, j=0):
        return ref[b * LEN : (b + 1) * LEN, j * wl + p * LANES : j * wl + (p + 1) * LANES]

    for n, (b, p) in enumerate(tiles):
        q, k, v = [tile(sc.qkv, b, p, j) for j in range(3)]
        ids = jnp.broadcast_to(i.segment_ids[b : b + 1, :].astype(F32), (LEN, LEN))
        same = ids == ids.T
        scores = nt(pair(q), k) * scale
        scores = jnp.where(jnp.concatenate([same, same], axis=0), scores, blocked)
        scores = jnp.exp(scores - jnp.max(scores, axis=-1, keepdims=True))
        probs = scores / jnp.sum(scores, axis=-1, keepdims=True)
        sc.att[n] = probs
        sc.attended[b * LEN : (b + 1) * LEN, p * LANES : (p + 1) * LANES] = pick(
            nn(probs.astype(BF), v)
        ).astype(BF)
    sc.attended_full[:, own_cols] = sc.attended[...]
    attended_gather = gather_cols(sc.attended_full)
    forward(1)
    pass_next()
    attended_gather.wait_recv()
    forward(1)
    pass_next()
    landed_x(4)
    part = nn(sc.attended_full[...], weight(sc.two_c)) + i.attn_bo[:, own_cols]
    sc.mid_full[:, own_cols] = (part + sc.agg_full[:, own_cols].astype(F32)).astype(BF)
    mid_gather = gather_cols(sc.mid_full)
    transposed(sc.attended_full, sc.attendedT)
    forward(1)
    pass_next()
    mid_gather.wait_recv()
    awo_rows = by_rows(sc.awo_c, sc.awo)
    two_rows = by_rows(sc.two_c, sc.two)
    whole_norm(sc.mid_full, i.mlp_norm_gain, i.mlp_norm_bias, sc.mnormed)
    kept_norm(sc.mid_full, sc.hat2, sc.rstd2)
    transposed(sc.mnormed, sc.mnormedT)
    pass_next()
    forward(3)
    mnormed = sc.mnormed[...]
    for j in range(fl // CHUNK):
        at = slice(j * CHUNK, (j + 1) * CHUNK)
        bias = i.mlp_bup[:, pl.ds(pl.multiple_of(s * fl + j * CHUNK, LANES), CHUNK)]
        landed_x(5 + j)
        hidden = nn(mnormed, columns(sc.up_w, j)) + bias
        phi = 0.5 + 0.5 * lax.erf(hidden * 0.7071067811865476)
        density = jnp.exp(hidden * hidden * -0.5) * 0.3989422804014327
        sc.act[:, at] = (hidden * phi).astype(BF)
        sc.slope[:, at] = phi + hidden * density
        if 0 < j <= crossing:
            pass_next()
    names = [(o.mlp_down, lambda q, j=j: q * fl + j * CHUNK) for j in range(fl // CHUNK)]
    names += [(o.mlp_up, lambda q, j=j: q * fl + j * CHUNK) for j in range(fl // CHUNK)]
    names += [(o.singles, lambda q: 3 * D + q * wl)]
    names += [(o.attn_wqkv, lambda q, j=j: j * D + q * wl) for j in range(3)]
    names += [(o.singles, lambda q: 2 * D + q * wl)]
    halved = 2
    steps = [(c, 0, CHUNK) for c in range(n_pieces - halved)]
    steps += [(c, at, CHUNK // 2) for c in range(n_pieces - halved, n_pieces) for at in (0, CHUNK // 2)]
    last = len(steps)

    def view(ref, n):
        c, at, width = steps[n]
        return ref.at[c] if width == CHUNK else ref.at[c, :, :, pl.ds(at, width)]

    to_x, to_z, made, done = {}, {}, [], []
    published = [(send_sem(), recv_sem()) for _ in range(ns)]
    early = 2
    chunk_x, early_x = send_sem(), send_sem()
    all_sent(blocks.at[early:], chunk_x)
    all_sent(blocks.at[0:early, 0], early_x)
    chunk_z = reduce_group(n_pieces - early - halved, sc.z_recv)
    early_z = reduce_group(early, sc.e_recv)

    def produce(c, left, right):
        def half(side):
            block = left[:, pl.ds(side, 1)].reshape(nz * rows, tokens)
            return nn(block, right).reshape(nz, rows, CHUNK)

        sc.x_send[c] = half(1 - x).astype(BF)
        made.extend(n for n in range(last) if steps[n][0] == c)
        sc.keep[c] = half(x)

    def issue_x(until):
        for c in [c for c in made if early <= c <= until and c not in to_x]:
            to_x[c] = over_x(view(sc.x_send, c), view(sc.x_recv, c), chunk_x)

    unmerged = list(range(early, last))

    def produce_early(c, left, right):
        for side in range(nx):
            part = nn(left[:, side].reshape(nz * rows, tokens), right)
            sc.e_send[c, :, side] = part.reshape(nz, rows, CHUNK).astype(BF)
        made.append(c)
        to_z[c] = reduce(sc.e_send.at[c], sc.e_recv.at[c], sc.e_merged.at[c], early_z, True)

    def middle_early(c):
        sc.e_sum[c] = to_z[c].total()
        sc.e_out[c] = sc.e_sum[c, 1 - x].astype(BF)
        to_x[c] = over_x(sc.e_out.at[c], sc.e_in.at[c], early_x)

    def finish_early(c):
        to_x[c].wait_recv()
        sc.final[c] = (sc.e_sum[c, x] + sc.e_in[c].astype(F32)).astype(BF)
        publish(sc.final.at[c], *names[c])

    def middle(n):
        to_x[n].wait_recv()
        issue_x({2: 7, 5: 9, 8: 12}.get(n, 0))
        merged_x = view(sc.keep, n)[...] + view(sc.x_recv, n)[...].astype(F32)
        view(sc.z_send, n)[...] = merged_x.astype(BF)
        group = chunk_z if steps[n][2] == CHUNK else None
        to_z[n] = reduce(view(sc.z_send, n), view(sc.z_recv, n), view(sc.z_merged, n), group)

    mate = s + 1 - 2 * lax.rem(s, 2)
    other = lax.rem(s + ns // 2, ns)
    relayed = []

    def publish(block, array, col, at=0, width=CHUNK):
        def cols(q):
            return array.at[:, pl.ds(pl.multiple_of(col(q) + at, LANES), width)]

        (near, landed), (across, _), (passed, landed_passed) = published[0:3]
        arrival = recv_sem()
        remote(block, cols(s), near, landed, (mate, r)).start()
        remote(block, cols(s), across, arrival, (other, r)).start()
        local(block, cols(s), 3)

        def relay():
            await_landed(cols(other), arrival)
            remote(cols(other), cols(other), passed, landed_passed, (mate, r)).start()

        relayed.append(relay)

    def relay_until(left):
        while len(relayed) > left:
            relayed.pop(0)()

    def finish(n):
        c, at, width = steps[n]
        block = sc.final.at[c] if width == CHUNK else sc.final.at[c, :, pl.ds(at, width)]
        block[...] = to_z[n].total().astype(BF)
        publish(block, *names[c], at, width)

    def finish_up_to(to):
        for c in range(early, to + 1):
            if c not in done:
                finish(c)
                done.append(c)

    def pump(count):
        for _ in range(count):
            c = len(to_z)
            middle(c)
            if c - 2 in unmerged:
                unmerged.remove(c - 2)
                to_z[c - 2].merge()
            if c >= 8 and c - 1 in unmerged:
                unmerged.remove(c - 1)
                to_z[c - 1].merge()
            relay_until(1)
            finish_up_to(min(c - (3 if c > 9 else 4), last - 2 * halved - 1))

    for j in range(fl // CHUNK):
        make_part = produce_early if j < early else produce
        make_part(j, sc.gT, sc.act[:, j * CHUNK : (j + 1) * CHUNK])
    issue_x(3)
    forward(2)
    for c in range(early):
        to_z[c].begin()
    g_full = sc.g_full[...]
    nmlp = fl // CHUNK
    for j in range(fl // CHUNK):
        at = slice(j * CHUNK, (j + 1) * CHUNK)
        landed_x(5 + nmlp + j)
        d_hidden = nn(g_full, columns(sc.down_w, j)) * sc.slope[:, at]
        sc.d_hidden[:, at] = d_hidden.astype(BF)
    up_w = weight(sc.up_w)
    rs3 = scatter(sc.rs3_part, sc.rs3_recv, nt(sc.d_hidden[...], up_w))
    for j in range(nmlp):
        at = slice(j * CHUNK, (j + 1) * CHUNK)
        produce(nmlp + j, sc.mnormedT, sc.d_hidden[:, at])
    sc.bup[:, own_ff] = colsum(sc.d_hidden[...])
    issue_x(5)
    rs3.wait_recv()
    g_shard = sc.g_full[own_rows, :].astype(F32)
    sc.vecs[0:1, :] = colsum(g_shard)
    d_mid = norm_back(landed_sum(sc.rs3_recv), i.mlp_norm_gain, sc.hat2, sc.rstd2, 1, 2)
    d_mid = (g_shard + d_mid).astype(BF)
    sc.vecs[3:4, :] = colsum(d_mid)
    ag3 = gather(sc.d_mid, d_mid)
    d_mid = d_mid.astype(F32)
    sc.out_part[...] = nt(sc.act[...], weight(sc.down_w))
    sc.out_part[own_rows, :] = sc.out_part[own_rows, :] + sc.mid_full[own_rows, :].astype(F32) + i.mlp_bdown[...]
    sc.out_low[...] = sc.out_part[...].astype(BF)
    out_rs = over_section(
        lambda t: sc.out_low.at[:, pl.ds(pl.multiple_of(t * wl, LANES), wl)],
        sc.out_recv.at[s],
        sc.out_recv.at[0 : ns - 1],
    )
    sc.out_recv[s] = sc.out_low[:, own_cols]
    to_z[0].merge()
    pump(1)
    to_z[1].merge()
    ag3.wait_recv()

    pump(2)
    two_rows.wait_recv()
    d_att = nt(sc.d_mid[...], weight(sc.two)).astype(BF)
    sc.d_att[...] = d_att
    for n, (b, p) in enumerate(tiles):
        q, k, v = [tile(sc.qkv, b, p, j) for j in range(3)]
        q, d_out = pair(q), pair(tile(sc.d_att, b, p))
        probs = sc.att[n]
        d_probs = nt(d_out, v)
        d_scores = probs * (d_probs - jnp.sum(probs * d_probs, axis=-1, keepdims=True))
        d_scores = d_scores.astype(BF)
        parts = (pick(nn(d_scores, k)) * scale, tn(d_scores, q) * scale, tn(probs.astype(BF), d_out))
        for j in range(3):
            lanes = slice(j * wl + p * LANES, j * wl + (p + 1) * LANES)
            sc.d_qkv[b * LEN : (b + 1) * LEN, lanes] = parts[j].astype(BF)
    rs4 = scatter(sc.rs4_part, sc.rs4_recv, nt(sc.d_qkv[...], weight(sc.qkv_w)))
    produce(2 * nmlp, sc.attendedT, sc.d_mid[:, own_cols])
    for j in range(3):
        produce(2 * nmlp + 1 + j, sc.normedT, sc.d_qkv[:, j * wl : (j + 1) * wl])
    sc.vecs[7:8, own_cols] = colsum(sc.d_qkv[:, 0:wl])
    sc.vecs[8:9, own_cols] = colsum(sc.d_qkv[:, 2 * wl : 3 * wl])
    issue_x(8)
    pump(1)
    rs4.wait_recv()
    d_agg = norm_back(landed_sum(sc.rs4_recv), i.attn_norm_gain, sc.hat1, sc.rstd1, 4, 5)
    d_agg = (sc.d_mid[own_rows, :].astype(F32) + d_agg).astype(BF)
    sc.vecs[6:7, :] = colsum(d_agg)
    ag4 = gather(sc.d_agg, d_agg)
    pump(2)
    ag4.wait_recv()

    awo_rows.wait_recv()
    produce(2 * nmlp + 4, sc.contextT, sc.d_agg[:, own_cols])
    d_context = nt(sc.d_agg[...], weight(sc.awo)).astype(BF)
    sc.vecs[9:10, own_cols] = colsum(d_context)
    value_basis = sc.bv[...].astype(BF)
    cross = jnp.zeros((CHUNK, wl), F32)
    grad_pix = jnp.zeros((tokens, CHUNK), F32)
    for h in range(hl):
        masked = d_context * (head_of == h).astype(F32).astype(BF)
        pulled = nt(masked, value_basis)
        cross = cross + tn(sc.mixed[h], masked)
        pix = sc.pix[...].astype(F32)
        high, low = split(pulled * pix)
        d_weights = nn(high, fold) + nn(low, fold)
        probs = sc.probs[h]
        d_scores = probs * (d_weights - jnp.sum(probs * d_weights, axis=-1, keepdims=True))
        srep = nt(d_scores.astype(BF), fold)
        sc.key_src[h : h + 1, :] = colsum(srep * pix)
        grad_pix = grad_pix + sc.wrep[h].astype(F32) * pulled
        grad_pix = grad_pix + srep * sc.score_rows[h : h + 1, :]
    key_push = push(sc.key_src, sc.key_recv)
    for t in range(nd):
        sc.m_src[t] = cross[t * blk : (t + 1) * blk].astype(sc.m_src.dtype)
    m_rs = over_dp(lambda t: sc.m_src.at[t], sc.m_recv.at[r], sc.m_recv.at[0 : nd - 1])
    sc.m_recv[r] = sc.m_src[r]
    grad_pix = grad_pix.astype(BF)
    pw = CP // ns
    for t in range(ns):
        sc.pix_src[t] = nt(sc.place[t * pw : (t + 1) * pw, :], grad_pix).astype(BF)
    pix_rs = over_section(lambda t: sc.pix_src.at[t], sc.pix_recv.at[s], sc.pix_recv.at[0 : ns - 1])
    sc.pix_recv[s] = sc.pix_src[s]
    for t in range(nd):
        sc.small_src[t, 0:10] = sc.vecs[0:10, t * rows : (t + 1) * rows]
        for j in range(FF // D):
            start = (t * (FF // D) + j) * rows
            sc.small_src[t, 10 + j : 11 + j] = sc.bup[:, start : start + rows]
    small_rs = over_dp(lambda t: sc.small_src.at[t], sc.small_recv.at[r], sc.small_recv.at[0 : nd - 1])
    sc.small_recv[r] = sc.small_src[r]

    issue_x(10)
    pump(2)
    m_rs.wait_recv()
    sc.m_own[...] = summed(sc.m_recv, nd).astype(sc.m_own.dtype)
    m_ag = push(sc.m_own, sc.m_all)
    key_push.wait_recv()
    key_terms = summed(sc.key_recv, nd)
    wide = jnp.concatenate([jnp.broadcast_to(key_terms[h : h + 1], (HEAD, CHUNK)) for h in range(hl)], axis=0)
    d_key = nt(sc.basis[...], wide.astype(BF))
    d_query = jnp.sum(sc.wk[...].astype(F32) * d_key, axis=0, keepdims=True) * scale
    sc.dq_src[...] = d_query
    dq_push = push(sc.dq_src, sc.dq_recv)
    count = len(names)
    sc.final[count] = (d_key * (sc.query_proj[...] * scale)).astype(BF)
    publish(sc.final.at[count], o.singles, lambda q: q * wl)
    issue_x(last)
    for c in range(early):
        middle_early(c)
    pump(2)
    small_rs.wait_recv()
    sc.sec_small[s] = summed(sc.small_recv, nd)
    small_ag = over_section(lambda t: sc.sec_small.at[s], sc.sec_small.at[s], sc.sec_small.at[0 : ns - 1])
    def section_total(ref):
        total = ref[0].astype(F32)
        for k in range(1, ns):
            total = total + ref[k].astype(F32)
        return total

    pump(1)
    m_ag.wait_recv()
    for t in range(nd):
        sc.cross[t * blk : (t + 1) * blk] = sc.m_all[t].astype(F32)
    cross = sc.cross[...].astype(BF)
    sc.final[count + 1] = nn(sc.basis[...], cross).astype(BF)
    publish(sc.final.at[count + 1], o.singles, lambda q: 1 * D + q * wl)
    key_low = jnp.concatenate([key_terms, jnp.zeros((16 - hl, CHUNK), F32)], axis=0).astype(BF)
    grad_basis = nt(cross, sc.wv[...]) + tn(key_low, sc.key_query[...])
    sc.basis_recv[s] = grad_basis.astype(BF)
    basis_sum = over_section(lambda t: sc.basis_recv.at[s], sc.basis_recv.at[s], sc.basis_recv.at[0 : ns - 1])
    dq_push.wait_recv()
    sc.d_query[...] = jnp.broadcast_to(summed(sc.dq_recv, nd), sc.d_query.shape)
    dq_gather = over_section(lambda t: sc.d_query, o.d_query.at[s], o.d_query.at[0 : ns - 1])
    local(sc.d_query, o.d_query.at[s], 5)

    pump(2)
    finish_up_to(last - 2 * halved)
    for c in range(early):
        finish_early(c)
    finish_up_to(last - 3)
    finish_up_to(last - 2)
    finish_up_to(last - 1)
    out_rs.wait_recv()
    sc.activations[...] = section_total(sc.out_recv).astype(BF)
    local(sc.activations, o.activations, 6)
    pix_rs.wait_recv()
    sc.patches_out[...] = section_total(sc.pix_recv).astype(BF)
    local(sc.patches_out, o.patches, 7)
    small_ag.wait_recv()
    sc.small_out[...] = summed(sc.sec_small, ns)
    local(sc.small_out, o.small, 8)
    relay_until(2)
    basis_sum.wait_recv()
    sc.basis_out[...] = section_total(sc.basis_recv)
    local(sc.basis_out, o.basis, 9)
    dq_gather.wait_recv()
    relay_until(0)
    await_landed(sc.final, published[0][1])
    await_landed(sc.final, published[2][1])
    for out, _ in published[0:3]:
        await_sent(sc.final, out)
    await_local(sc.final, 3)
    await_local(sc.query_rows, 4)
    await_local(sc.d_query, 5)
    await_local(sc.activations, 6)
    await_local(sc.patches_out, 7)
    await_local(sc.small_out, 8)
    await_local(sc.basis_out, 9)
    for wait in pending:
        wait()
    assert used.send <= send.shape[0] and used.recv <= recv.shape[0], used


def scratch(ns, nd, tokens):
    nz, rows = nd // 2, D // nd
    wl, fl, hl = D // ns, FF // ns, HEADS // ns
    shard, zq, blk = tokens // ns, nz // ns, CHUNK // nd
    chunks = 2 * (fl // CHUNK) + 5
    v = pltpu.VMEM
    shapes = dict(
        wq=v((rows, wl), BF),
        wk=v((rows, wl), BF),
        wv=v((rows, wl), BF),
        qkv_w=v((nz, 2, rows, 3 * wl), BF),
        up_w=v((nz, 2, rows, fl), BF),
        down_w=v((nz, 2, rows, fl), BF),
        awo_c=v((nz, 2, rows, wl), BF),
        two_c=v((nz, 2, rows, wl), BF),
        awo=v((zq, 2, rows, D), BF),
        two=v((zq, 2, rows, D), BF),
        g_full=v((tokens, D), BF),
        place=v((CP, CHUNK), BF),
        pix=v((tokens, CHUNK), BF),
        fold=v((CHUNK, LANES), BF),
        basis=v((rows, CHUNK), BF),
        vecs=v((16, D), F32),
        bup=v((1, FF), F32),
        query_proj=v((1, wl), F32),
        key_query=v((16, rows), BF),
        score_rows=v((hl, CHUNK), F32),
        bv=v((CHUNK, CHUNK), F32),
        cross=v((CHUNK, CHUNK), F32),
        e_send=v((2, nz, 2, rows, CHUNK), BF),
        e_recv=v((2, nz, 2, rows, CHUNK), BF),
        e_merged=v((2, 2, 2, rows, CHUNK), BF),
        z_merged=v((chunks, 2, rows, CHUNK), BF),
        e_sum=v((2, 2, rows, CHUNK), F32),
        e_out=v((2, rows, CHUNK), BF),
        e_in=v((2, rows, CHUNK), BF),
        probs=v((hl, tokens, LANES), F32),
        wrep=v((hl, tokens, CHUNK), BF),
        mixed=v((hl, tokens, CHUNK), BF),
        context_full=v((tokens, D), BF),
        attended_full=v((tokens, D), BF),
        agg_full=v((tokens, D), BF),
        mid_full=v((tokens, D), BF),
        hat1=v((shard, D), F32),
        hat2=v((shard, D), F32),
        rstd1=v((shard, LANES), F32),
        rstd2=v((shard, LANES), F32),
        normed=v((tokens, D), BF),
        mnormed=v((tokens, D), BF),
        qkv=v((tokens, 3 * wl), BF),
        d_qkv=v((tokens, 3 * wl), BF),
        att=v((tokens // LEN * (wl // LANES), 2 * LEN, LEN), F32),
        attended=v((tokens, wl), BF),
        d_att=v((tokens, wl), BF),
        act=v((tokens, fl), BF),
        slope=v((tokens, fl), F32),
        d_hidden=v((tokens, fl), BF),
        d_mid=v((tokens, D), BF),
        d_agg=v((tokens, D), BF),
        out_part=v((tokens, D), F32),
        out_low=v((tokens, D), BF),
        out_recv=v((ns, tokens, wl), BF),
        pix_src=v((ns, CP // ns, tokens), BF),
        pix_recv=v((ns, CP // ns, tokens), BF),
        small_src=v((nd, 16, rows), F32),
        small_recv=v((nd, 16, rows), F32),
        sec_small=v((ns, 16, rows), F32),
        basis_recv=v((ns, CHUNK, rows), BF),
        x_send=v((chunks, nz, rows, CHUNK), BF),
        x_recv=v((chunks, nz, rows, CHUNK), BF),
        keep=v((chunks, nz, rows, CHUNK), F32),
        z_send=v((chunks, nz, rows, CHUNK), BF),
        z_recv=v((chunks, nz, rows, CHUNK), BF),
        final=v((chunks + 2, rows, CHUNK), BF),
    )
    whole = v((nz, 2, rows, tokens), BF)
    shapes.update(gT=whole, contextT=whole, attendedT=whole, normedT=whole, mnormedT=whole)
    part = v((tokens, D), BF)
    shapes.update(rs3_part=part, rs4_part=part)
    part = v((ns, shard, D), BF)
    shapes.update(rs3_recv=part, rs4_recv=part)
    part = v((hl, CHUNK), F32)
    shapes.update(s_src=part, key_src=part)
    part = v((nd, hl, CHUNK), F32)
    shapes.update(s_recv=part, key_recv=part)
    shapes.update(q_src=v((1, CHUNK), F32), dq_src=v((1, CHUNK), F32))
    part = v((nd, 1, CHUNK), F32)
    shapes.update(q_recv=part, dq_recv=part)
    kind = BF if blk % 16 == 0 else F32
    part = v((nd, blk, CHUNK), kind)
    shapes.update(bv_src=part, bv_recv=part, bv_all=part, m_src=part, m_recv=part, m_all=part)
    part = v((blk, CHUNK), kind)
    shapes.update(bv_own=part, m_own=part)
    shapes.update(
        query_rows=v((16, rows), BF),
        d_query=v((8, wl), F32),
        activations=v((tokens, wl), BF),
        patches_out=v((CP // ns, tokens), BF),
        small_out=v((16, rows), F32),
        basis_out=v((CHUNK, rows), F32),
    )
    dma = pltpu.SemaphoreType.DMA
    shapes.update(send=dma((52,)), recv=dma((160,)), local=dma((28,)))
    return shapes


def fused(ns, nd, near, far):
    tokens = near["patches"].shape[1]
    rows = D // nd
    shapes = scratch(ns, nd, tokens)
    arrays = {**near, **far}
    hbm = pl.BlockSpec(memory_space=pl.ANY)
    outs = dict(
        activations=((tokens, D // ns), BF),
        patches=((CP // ns, tokens), BF),
        basis=((CHUNK, rows), F32),
        query_rows=((16, rows), BF),
        d_query=((ns, 8, D // ns), F32),
        small=((16, rows), F32),
        mlp_up=((rows, FF), BF),
        mlp_down=((rows, FF), BF),
        attn_wqkv=((rows, 3 * D), BF),
        singles=((rows, 4 * D), BF),
    )

    def body(*refs):
        n_in, n_out = len(arrays), len(outs)
        kernel(
            ns,
            nd,
            SimpleNamespace(**dict(zip(arrays, refs[:n_in]))),
            SimpleNamespace(**dict(zip(outs, refs[n_in : n_in + n_out]))),
            SimpleNamespace(**dict(zip(shapes, refs[n_in + n_out :]))),
            list(near),
            refs[n_in + n_out + len(shapes) :],
        )

    result = pl.pallas_call(
        body,
        out_shape=[jax.ShapeDtypeStruct(*a) for a in outs.values()],
        in_specs=[hbm] * len(arrays),
        out_specs=[hbm] * len(outs),
        scratch_shapes=list(shapes.values()) + [pltpu.VMEM(a.shape, a.dtype) for a in near.values()],
        compiler_params=pltpu.CompilerParams(
            collective_id=0, has_side_effects=True, vmem_limit_bytes=60 * 1024 * 1024
        ),
        name="block",
    )(*arrays.values())
    return SimpleNamespace(**dict(zip(outs, result)))


def widen(nd, got, agg_wq):
    rows = D // nd
    arrays = [got.mlp_up, got.mlp_down, got.attn_wqkv, got.singles]
    rest = dict(
        activations=got.activations,
        patches=got.patches,
        basis=got.basis,
        query_rows=got.query_rows,
        d_query=got.d_query,
        small=got.small,
        agg_wq=agg_wq,
    )
    line = (1, rows)
    outs = dict(
        activations=(got.activations.shape, BF),
        patches=(got.patches.shape, BF),
        embed=((CP, rows), F32),
        var=((VARS, rows), F32),
        query=(line, F32),
        wq=((rows, D), F32),
        bq=(line, F32),
        bup=((1, rows * (FF // D)), F32),
    )
    lines = tuple(range(10))
    wide = dict(
        mlp_up=((rows, FF), F32),
        mlp_down=((rows, FF), F32),
        attn_wqkv=((rows, 3 * D), F32),
        agg_wk=((rows, D), F32),
        agg_wv=((rows, D), F32),
        agg_wo=((rows, D), F32),
        attn_wo=((rows, D), F32),
    )
    half, third = FF // 2, 3 * D // 2
    tiles = [(0, at, half, 0, at) for at in (0, half)]
    tiles += [(1, at, half, 1, at) for at in (0, half)]
    tiles += [(2, at, third, 2, at) for at in (0, third)]
    tiles += [(3, n * D, D, 3 + n, 0) for n in range(4)]
    everything = {**wide, **outs}
    shaped = [jax.ShapeDtypeStruct(*a) for a in everything.values()]
    shaped += [jax.ShapeDtypeStruct(line, F32) for _ in lines]
    slim = shaped[len(wide) :]

    def body(*refs):
        sources, refs = refs[: len(arrays)], refs[len(arrays) :]
        rest_in, refs = refs[: len(rest)], refs[len(rest) :]
        targets, refs = refs[: len(wide)], refs[len(wide) :]
        slim_out, refs = refs[: len(slim)], refs[len(slim) :]
        near, refs = refs[: len(arrays)], refs[len(arrays) :]
        far, refs = refs[: len(wide)], refs[len(wide) :]
        rest_near, refs = refs[: len(rest)], refs[len(rest) :]
        slim_near, (ins, outgoing) = refs[: len(slim)], refs[len(slim) :]

        def load(t):
            m, at, width, _, _ = tiles[t]
            cols = pl.ds(at, width)
            return pltpu.make_async_copy(sources[m].at[:, cols], near[m].at[:, cols], ins.at[t])

        def store(t):
            _, _, width, m, at = tiles[t]
            cols = pl.ds(at, width)
            return pltpu.make_async_copy(far[m].at[:, cols], targets[m].at[:, cols], outgoing.at[t])

        def load_rest(n):
            return pltpu.make_async_copy(rest_in[n], rest_near[n], ins.at[len(tiles) + n])

        def store_slim(n):
            return pltpu.make_async_copy(slim_near[n], slim_out[n], outgoing.at[len(tiles) + n])

        def widen_tile(t):
            load(t).wait()
            m, at, width, to, start = tiles[t]
            far[to][:, start : start + width] = near[m][:, at : at + width].astype(F32)
            store(t).start()

        for n in range(len(rest)):
            load_rest(n).start()
        for t in range(len(tiles)):
            load(t).start()
        for t in range(len(tiles) // 2):
            widen_tile(t)
        for n in range(len(rest)):
            load_rest(n).wait()
        i = SimpleNamespace(**dict(zip(rest, rest_near)))
        o = SimpleNamespace(**dict(zip(outs, slim_near)))
        left = slim_near[len(outs) :]
        r = lax.axis_index("dp")
        o.activations[...] = i.activations[...]
        o.patches[...] = i.patches[...]
        o.embed[...] = i.basis[0:CP]
        o.var[...] = i.basis[CP : CP + VARS]
        d_query = jnp.concatenate([i.d_query[k] for k in range(i.d_query.shape[0])], axis=1)
        d_query = jnp.concatenate([d_query, d_query], axis=0)
        d_query = jnp.where(iota(d_query.shape, 0) == 0, d_query, 0.0)
        high, low = split(d_query)
        low, rest_low = split(d_query - high.astype(F32))
        chosen = (iota((rows, D), 1) == iota((rows, D), 0) + r * rows).astype(F32).astype(BF)
        o.bq[...] = (nt(high, chosen) + nt(low, chosen) + nt(rest_low, chosen))[0:1]
        weight = i.agg_wq[...]
        o.query[...] = (nt(high, weight) + nt(low, weight) + nt(rest_low, weight))[0:1]
        first = i.query_rows[...]
        o.wq[...] = tn(first, high) + tn(first, low) + tn(first, rest_low)
        o.bup[...] = jnp.concatenate([i.small[10 + k : 11 + k] for k in range(FF // D)], axis=1)
        for k in lines:
            left[k][...] = i.small[k : k + 1]
        for n in range(len(slim)):
            store_slim(n).start()
        for t in range(len(tiles) // 2, len(tiles)):
            widen_tile(t)
        for t in range(len(tiles)):
            store(t).wait()
        for n in range(len(slim)):
            store_slim(n).wait()

    hbm = pl.BlockSpec(memory_space=pl.ANY)
    dma = pltpu.SemaphoreType.DMA
    result = pl.pallas_call(
        body,
        out_shape=shaped,
        in_specs=[hbm] * (len(arrays) + len(rest)),
        out_specs=[hbm] * len(shaped),
        scratch_shapes=[pltpu.VMEM(a.shape, a.dtype) for a in [*arrays, *shaped[: len(wide)], *rest.values(), *slim]]
        + [dma((len(tiles) + len(rest),)), dma((len(tiles) + len(slim),))],
        compiler_params=pltpu.CompilerParams(vmem_limit_bytes=60 * 1024 * 1024),
        name="widen",
    )(*arrays, *rest.values())
    names = list(everything)
    return SimpleNamespace(**dict(zip(names, result))), [a.reshape(-1) for a in result[len(names) :]]


def on_device(
    ns,
    nd,
    patches,
    var_ids,
    segment_ids,
    embed_weight,
    var_embed,
    agg_query,
    agg_wq,
    agg_bq,
    agg_wk,
    agg_wv,
    agg_bv,
    agg_wo,
    agg_bo,
    attn_norm_gain,
    attn_norm_bias,
    attn_wqkv,
    attn_bq,
    attn_bv,
    attn_wo,
    attn_bo,
    mlp_norm_gain,
    mlp_norm_bias,
    mlp_up,
    mlp_bup,
    mlp_down,
    mlp_bdown,
    cotangent,
):
    near = dict(
        patches=patches,
        var_ids=var_ids,
        segment_ids=segment_ids,
        embed_weight=embed_weight,
        var_embed=var_embed,
        agg_query=agg_query,
        agg_bq=agg_bq,
        agg_bv=agg_bv,
        agg_bo=agg_bo,
        attn_norm_gain=attn_norm_gain,
        attn_norm_bias=attn_norm_bias,
        attn_bq=attn_bq,
        attn_bv=attn_bv,
        attn_bo=attn_bo,
        mlp_norm_gain=mlp_norm_gain,
        mlp_norm_bias=mlp_norm_bias,
        mlp_bup=mlp_bup,
        mlp_bdown=mlp_bdown,
    )
    far = dict(
        agg_wq=agg_wq,
        agg_wk=agg_wk,
        agg_wv=agg_wv,
        agg_wo=agg_wo,
        attn_wqkv=attn_wqkv,
        attn_wo=attn_wo,
        mlp_up=mlp_up,
        mlp_down=mlp_down,
        cotangent=cotangent,
    )
    near = {name: a.reshape(1, -1) if a.ndim == 1 else a for name, a in near.items()}
    near["patches"], near["embed_weight"] = patches.T, embed_weight.T
    got = fused(ns, nd, near, far)
    out, small = widen(nd, got, agg_wq)
    return (
        out.activations,
        out.patches.T,
        out.embed.T,
        out.var,
        out.query.reshape(-1),
        out.wq,
        out.bq.reshape(-1),
        out.agg_wk,
        out.agg_wv,
        small[9],
        out.agg_wo,
        small[6],
        small[4],
        small[5],
        out.attn_wqkv,
        small[7],
        small[8],
        out.attn_wo,
        small[3],
        small[1],
        small[2],
        out.mlp_up,
        out.bup.reshape(-1),
        out.mlp_down,
        small[0],
    )


def solution(mesh):
    in_specs = (
        P("dp", None),
        P(),
        P("dp", None),
        P("dp", None),
        P(),
        P(),
        P("dp", None),
        P(),
        P("dp", None),
        P("dp", None),
        P(),
        P("dp", None),
        P(),
        P(),
        P(),
        P("dp", None),
        P(),
        P(),
        P("dp", None),
        P(),
        P(),
        P(),
        P("dp", None),
        P(),
        P("dp", None),
        P(),
        P("dp", "section"),
    )
    out_specs = (
        P("dp", "section"),
        P("dp", "section"),
        P("dp", None),
        P(None, "dp"),
        P("dp"),
        P("dp", None),
        P("dp"),
        P("dp", None),
        P("dp", None),
        P("dp"),
        P("dp", None),
        P("dp"),
        P("dp"),
        P("dp"),
        P("dp", None),
        P("dp"),
        P("dp"),
        P("dp", None),
        P("dp"),
        P("dp"),
        P("dp"),
        P("dp", None),
        P("dp"),
        P("dp", None),
        P("dp"),
    )
    sizes = (mesh.shape["section"], mesh.shape["dp"])
    return jax.shard_map(
        partial(on_device, *sizes), mesh=mesh, in_specs=in_specs, out_specs=out_specs, check_vma=False
    )
```
